32 devices in a mesh: grp: 2 (over core), blk: 16 (over z, y, x).
Axes of the slice: x: 2, y: 2, z: 4, core: 2. Of those that a mesh axis runs over, the one named last changes fastest.
Arguments:
- cell_input: bfloat16 [2, 2, 1024, 1024], P('grp', None, 'blk'), may hold values from -6 to 6
- lengths: int32 [2, 2], P('grp'), may hold values from 256 to 1024, as said below
- noise_draw: float32 [1, 2, 2, 1024, 512], P(None, 'grp', None, 'blk'), may hold values from -5 to 5
- cotangent: bfloat16 [2, 2, 1024, 1024], P('grp', None, 'blk'), may hold values from -6 to 6
- w_qkv: bfloat16 [1, 1024, 3072], P(None, None, 'blk'), may hold values from -0.1875 to 0.1875
- w_out: bfloat16 [1, 1024, 1024], P(None, None, 'blk'), may hold values from -1 to 1
- w_ffn_in: bfloat16 [1, 1024, 4096], P(None, None, 'blk'), may hold values from -0.1875 to 0.1875
- w_ffn_out: bfloat16 [1, 4096, 1024], P(None, None, 'blk'), may hold values from -0.09375 to 0.09375
- w_latent: bfloat16 [1, 1024, 1024], P(None, None, 'blk'), may hold values from -0.0625 to 0.0625
- w_decode: bfloat16 [1, 512, 1024], P(None, None, 'blk'), may hold values from -0.125 to 0.125
- vectors: bfloat16 [1, 9, 1024], P(None, None, 'blk')
- inner_bias: bfloat16 [1, 5120], P(None, 'blk'), may hold values from -3 to 3
- prior_means: bfloat16 [1, 16, 512], P(None, None, 'blk'), may hold values from -3 to 3
- prior_logvars: bfloat16 [1, 16, 512], P(None, None, 'blk'), may hold values from 2 to 3
Outputs:
- layer_out: float32 [2, 2, 1024, 1024], P('grp', None, 'blk')
- grad_cells: float32 [2, 2, 1024, 1024], P('grp', None, 'blk')
- kl_mean: float32 [], replicated
- grad_qkv: float32 [1, 1024, 3072], P(None, None, 'blk')
- grad_out: float32 [1, 1024, 1024], P(None, None, 'blk')
- grad_ffn_in: float32 [1, 1024, 4096], P(None, None, 'blk')
- grad_ffn_out: float32 [1, 4096, 1024], P(None, None, 'blk')
- grad_latent: float32 [1, 1024, 1024], P(None, None, 'blk')
- grad_decode: float32 [1, 512, 1024], P(None, None, 'blk')
- grad_vectors: float32 [1, 9, 1024], P(None, None, 'blk')
- grad_inner: float32 [1, 5120], P(None, 'blk')
- grad_means: float32 [1, 16, 512], P(None, None, 'blk')
- grad_logvars: float32 [1, 16, 512], P(None, None, 'blk')
The draws below stay inside these ranges and needn't reach their ends.
Inputs may be any that keep to these rules, and one draw needn't show every extreme that they name: In every group one slide has exactly 1024 cells; a slide's cells are the first lengths of its slot.
All inputs are finite; a program needn't handle non-finite values.
Results may differ from the reference program's by a relative error of at most 0.0085.
Values may be sent and summed in bfloat16 or wider, within the bound.
No kernel may reach another device: no remote copies, remote signals or barrier semaphores. Data moves between devices by JAX's collectives and lax.ppermute only.
A program may use at most 256 MiB of HBM per device.

```python
import math
import jax
import jax.numpy as jnp
from jax import lax

D = 1024
HEADS = 16
FF = 4096
LAT = 512
COMP = 16
SLOTS = 2
LAYERS = 1
HEAD_DIM = 64
CAP = 1024
GROUPS = 2


def draw_lengths(key, part):
    key = jax.random.fold_in(key, 7)
    first_key, second_key = jax.random.split(key)
    spans = jax.random.randint(first_key, (GROUPS, SLOTS), CAP // 4, CAP + 1)
    chosen = jax.random.randint(second_key, (GROUPS, 1), 0, SLOTS)
    slot_ids = jnp.arange(SLOTS)[None, :]
    return jnp.where(slot_ids == chosen, CAP, spans).astype(jnp.int32)


def draw_vectors(key, part):
    key = jax.random.fold_in(key, 11)
    spread_vals = 0.25 * jax.random.normal(key, (LAYERS, 9, D), jnp.float32)
    row_ids = jnp.arange(9)
    gain_rows = (row_ids == 0) | (row_ids == 5)
    values = jnp.where(gain_rows[None, :, None], 1.0 + 0.5 * spread_vals, spread_vals)
    return values.astype(jnp.bfloat16)


def block_scale(stream_key, dims, shards, low, largest):
    def one(dim, blocks):
        draws = jax.random.uniform(jax.random.fold_in(jax.random.fold_in(stream_key, 6), dim), (blocks,), jnp.float32, low / len(shards), largest / len(shards))
        return jnp.repeat(jnp.exp(draws), dims[dim] // blocks).reshape((-1,) + (1,) * (len(dims) - dim - 1))

    factor_of = one(*shards[0])
    for cut in shards[1:]:
        factor_of = factor_of * one(*cut)
    return factor_of


def scatter_about(own_key, extent, scale, limit, pieces=(), kind=jnp.bfloat16):
    values = jax.random.normal(own_key, extent, jnp.float32) * scale
    if len(pieces) > 0:
        values = block_scale(own_key, extent, pieces, -0.22, 0.18) * values
    return jnp.clip(values, min=-limit, max=limit).astype(kind)


def setup_inputs(seed: int = 0) -> dict:
    key_list = jax.random.split(jax.random.key(seed), 15)
    return {
        "cell_input": scatter_about(key_list[0], (GROUPS, SLOTS, CAP, D), 1.0, 6.0, ((0, 2), (2, 16))),
        "lengths": draw_lengths(jax.random.fold_in(key_list[14], 71), 0),
        "noise_draw": scatter_about(key_list[2], (LAYERS, GROUPS, SLOTS, CAP, LAT), 1.0, 5.0, ((1, 2), (3, 16)), jnp.float32),
        "cotangent": scatter_about(key_list[3], (GROUPS, SLOTS, CAP, D), 1.0, 6.0, ((0, 2), (2, 16))),
        "w_qkv": scatter_about(key_list[4], (LAYERS, D, 3 * D), D ** -0.5, 0.1875, ((2, 16),)),
        "w_out": scatter_about(key_list[5], (LAYERS, D, D), (max(D // 32, 1)) ** -0.5, 1.0, ((2, 16),)),
        "w_ffn_in": scatter_about(key_list[6], (LAYERS, D, FF), D ** -0.5, 0.1875, ((2, 16),)),
        "w_ffn_out": scatter_about(key_list[7], (LAYERS, FF, D), FF ** -0.5, 0.09375, ((2, 16),)),
        "w_latent": scatter_about(key_list[8], (LAYERS, D, 2 * LAT), (8 * D) ** -0.5, 0.0625, ((2, 16),)),
        "w_decode": scatter_about(key_list[9], (LAYERS, LAT, D), (4 * LAT) ** -0.5, 0.125, ((2, 16),)),
        "vectors": draw_vectors(jax.random.fold_in(key_list[14], 71), 0),
        "inner_bias": scatter_about(key_list[11], (LAYERS, FF + 2 * LAT), 0.5, 3.0, ((1, 16),)),
        "prior_means": scatter_about(key_list[12], (LAYERS, COMP, LAT), 0.5, 3.0, ((2, 16),)),
        "prior_logvars": jnp.clip(2.0 + 1.0 * jax.random.uniform(key_list[13], (LAYERS, COMP, LAT), jnp.float32) ** block_scale(key_list[13], (LAYERS, COMP, LAT), ((2, 16),), -0.2, 0.2), 2.0, 3.0).astype(jnp.bfloat16),
    }


@jax.custom_vjp
def low(v):
    return lax.optimization_barrier(v.astype(jnp.bfloat16)).astype(jnp.float32)

@jax.custom_vjp
def low_back(v):
    return v

def low_keep(v):
    return (low(v), None)

def low_pass(kept, grad):
    return (grad,)

def back_keep(v):
    return (v, None)

def back_low(kept, grad):
    return (low(grad),)
low.defvjp(low_keep, low_pass)
low_back.defvjp(back_keep, back_low)
EPS_NORM = 1e-05
MASKED = -1e+30

def matmul_high(left, right):
    return jnp.dot(left, right, precision=lax.Precision.HIGHEST, preferred_element_type=jnp.float32)

def layer_norm(values, norm_gain, norm_shift):
    centre = values - lax.optimization_barrier(jnp.mean(values, axis=-1, keepdims=True))
    spread = lax.optimization_barrier(jnp.mean(centre * centre, axis=-1, keepdims=True))
    return centre * lax.rsqrt(spread + EPS_NORM) * norm_gain + norm_shift

def mixture_kl(sample, noise_rows, logvar, mean_rows, logvars):
    own_term = lax.optimization_barrier(jnp.sum(-0.5 * noise_rows * noise_rows - 0.5 * logvar, axis=-1))
    offset = sample[:, None, :] - mean_rows[None, :, :]
    component = lax.optimization_barrier(jnp.sum(-0.5 * offset * offset * jnp.exp(-logvars)[None] - 0.5 * logvars[None], axis=-1)) - math.log(mean_rows.shape[0])
    row_peak = lax.optimization_barrier(jnp.max(component, axis=-1, keepdims=True))
    mixture = row_peak[:, 0] + jnp.log(lax.optimization_barrier(jnp.sum(jnp.exp(component - row_peak), axis=-1)))
    return own_term - mixture

def bottleneck(latent, noise_rows, live_rows, mean_rows, logvars):
    lat_width = noise_rows.shape[-1]
    mean_part = latent[:, :lat_width]
    logvar = latent[:, lat_width:]
    sample = mean_part + jnp.exp(0.5 * logvar) * noise_rows
    per_cell = mixture_kl(sample, noise_rows, logvar, mean_rows, logvars)
    return (sample, jnp.sum(jnp.where(live_rows, per_cell, 0.0)) / lat_width)

def slot_attention(packed):
    query_low, keys_low, values_low, length = packed
    key_count = query_low.shape[0]
    heads_q = query_low.reshape(key_count, HEADS, HEAD_DIM)
    heads_k = keys_low.reshape(key_count, HEADS, HEAD_DIM)
    heads_v = values_low.reshape(key_count, HEADS, HEAD_DIM)
    score_scale = 1.0 / math.sqrt(HEAD_DIM)
    scores = jnp.einsum('qhd,khd->hqk', heads_q, heads_k, precision=lax.Precision.HIGHEST) * score_scale
    live_keys = jnp.arange(key_count) < length
    scores = low_back(jnp.where(live_keys[None, None, :], scores, MASKED))
    row_peak = lax.optimization_barrier(jnp.max(scores, axis=-1, keepdims=True))
    weights = jnp.exp(scores - row_peak)
    probs_low = low(weights / lax.optimization_barrier(jnp.sum(weights, axis=-1, keepdims=True)))
    mixed_f = jnp.einsum('hqk,khd->qhd', probs_low, heads_v, precision=lax.Precision.HIGHEST)
    return mixed_f.reshape(key_count, HEADS * HEAD_DIM)

def group_forward(cell_rows, noise_group, lengths_group, params):
    live_rows = (jnp.arange(CAP)[None, :] < lengths_group[:, None]).reshape(SLOTS * CAP)
    hidden = cell_rows.reshape(SLOTS * CAP, D)
    kl_sum = jnp.zeros((), jnp.float32)
    slot_view = (SLOTS, CAP, D)
    for layer_idx in range(LAYERS):
        qkv_w, out_w, in_w, back_w, latent_w, decode_w, vec_rows, inner_rows, mean_rows, logvars = [stacked[layer_idx] for stacked in params]
        normed = low(layer_norm(hidden, vec_rows[0], vec_rows[1]))
        qkv_all = matmul_high(normed, qkv_w)
        query_low = low(low_back(qkv_all[:, :D] + vec_rows[2]))
        keys_low = low(low_back(qkv_all[:, D:2 * D]))
        values_low = low(low_back(qkv_all[:, 2 * D:] + vec_rows[3]))
        mixed_f = lax.map(jax.checkpoint(slot_attention), (query_low.reshape(slot_view), keys_low.reshape(slot_view), values_low.reshape(slot_view), lengths_group))
        mixed_low = low(low_back(mixed_f.reshape(SLOTS * CAP, D)))
        attended = hidden + low_back(matmul_high(mixed_low, out_w)) + vec_rows[4]
        normed_two = low(layer_norm(attended, vec_rows[5], vec_rows[6]))
        inner_act = low_back(matmul_high(normed_two, in_w) + inner_rows[:FF])
        activated = low(jax.nn.gelu(inner_act))
        fed_rows = attended + low_back(matmul_high(activated, back_w)) + vec_rows[7]
        latent = low_back(matmul_high(low(fed_rows), latent_w) + inner_rows[FF:])
        sample, kl_part = bottleneck(latent, noise_group[layer_idx].reshape(SLOTS * CAP, LAT), live_rows, mean_rows, logvars)
        hidden = fed_rows + low_back(matmul_high(low(sample), decode_w)) + vec_rows[8]
        kl_sum = kl_sum + kl_part
    return (hidden.reshape(SLOTS, CAP, D), kl_sum)

def reference(cell_input, lengths, noise_draw, cotangent, w_qkv, w_out, w_ffn_in, w_ffn_out, w_latent, w_decode, vectors, inner_bias, prior_means, prior_logvars):
    params = tuple((array_in.astype(jnp.float32) for array_in in (w_qkv, w_out, w_ffn_in, w_ffn_out, w_latent, w_decode, vectors, inner_bias, prior_means, prior_logvars)))
    noise_groups = jnp.moveaxis(noise_draw.astype(jnp.float32), 1, 0)

    def forward(cells_in, weights_in):

        def per_group(packed):
            return group_forward(packed[0], packed[1], packed[2], weights_in)
        outputs, kl_groups = lax.map(jax.checkpoint(per_group), (cells_in, noise_groups, lengths))
        return (outputs, jnp.sum(kl_groups))
    (layer_out, kl_objective), pullback = jax.vjp(forward, cell_input.astype(jnp.float32), params)
    grad_cells, grad_params = pullback((cotangent.astype(jnp.float32), jnp.ones((), jnp.float32)))
    kl_mean = kl_objective / (GROUPS * SLOTS * CAP)
    return (layer_out, grad_cells, kl_mean, grad_params[0], grad_params[1], grad_params[2], grad_params[3], grad_params[4], grad_params[5], grad_params[6], grad_params[7], grad_params[8], grad_params[9])
```

```python
import math

import jax
import jax.numpy as jnp
import numpy as np
from jax import lax
from jax.experimental import pallas as pl
from jax.experimental.pallas import tpu as pltpu
from jax.sharding import Mesh
from jax.sharding import PartitionSpec as P

HEADS = 16
LAYERS = 1
HEAD_DIM = 64


EPS_NORM = 1e-05
MASKED = -1e30


def to_low(values):
    return values.astype(jnp.bfloat16)


def product(left, right):
    return jnp.dot(left, right, preferred_element_type=jnp.float32)


def product_tn(left, right):
    return lax.dot_general(
        left, right, (((0,), (0,)), ((), ())), preferred_element_type=jnp.float32
    )


def product_nt(left, right):
    return lax.dot_general(
        left, right, (((1,), (1,)), ((), ())), preferred_element_type=jnp.float32
    )


def layer_norm(values, norm_gain, norm_shift):
    centre = values - jnp.mean(values, axis=-1, keepdims=True)
    spread = jnp.mean(centre * centre, axis=-1, keepdims=True)
    return centre * lax.rsqrt(spread + EPS_NORM) * norm_gain + norm_shift


def mixture_kl(sample, noise_rows, logvar, mean_rows, logvars):
    own_term = jnp.sum(-0.5 * noise_rows * noise_rows - 0.5 * logvar, axis=-1)
    offset = sample[:, None, :] - mean_rows[None, :, :]
    component = jnp.sum(
        -0.5 * offset * offset * jnp.exp(-logvars)[None] - 0.5 * logvars[None], axis=-1
    ) - math.log(mean_rows.shape[0])
    row_peak = jnp.max(component, axis=-1, keepdims=True)
    mixture = row_peak[:, 0] + jnp.log(jnp.sum(jnp.exp(component - row_peak), axis=-1))
    return own_term - mixture


def bottleneck(latent, noise_rows, live_rows, mean_rows, logvars):
    lat_width = noise_rows.shape[-1]
    mean_part = latent[:, :lat_width]
    logvar = latent[:, lat_width:]
    sample = mean_part + jnp.exp(0.5 * logvar) * noise_rows
    per_cell = mixture_kl(sample, noise_rows, logvar, mean_rows, logvars)
    return (sample, jnp.sum(jnp.where(live_rows, per_cell, 0.0)) / lat_width)


def slot_scores(query_slots, keys_all, slide_len, score_scale):
    slot_count, query_rows, model_width = query_slots.shape
    heads_q = query_slots.reshape(slot_count, query_rows, HEADS, HEAD_DIM)
    heads_k = keys_all.reshape(slot_count, keys_all.shape[1], HEADS, HEAD_DIM)
    raw_scores = (
        jnp.einsum("sqhd,skhd->shqk", heads_q, heads_k, preferred_element_type=jnp.float32)
        * score_scale
    )
    live_keys = jnp.arange(keys_all.shape[1])[None, :] < slide_len[:, None]
    return jnp.where(live_keys[:, None, None, :], raw_scores, MASKED)


def widen(gathered):
    qkv_w, out_w, in_w, back_w, latent_w, decode_w, vec_rows, inner_rows, mean_rows, logvars = (
        gathered
    )
    return (
        qkv_w,
        out_w,
        in_w,
        back_w,
        latent_w,
        decode_w,
        vec_rows.astype(jnp.float32),
        inner_rows.astype(jnp.float32),
        mean_rows.astype(jnp.float32),
        logvars.astype(jnp.float32),
    )


def gather_weights(layer_parts):
    (
        part_qkv,
        part_out,
        part_in,
        part_back,
        part_latent,
        part_decode,
        part_vectors,
        part_inner,
        part_means,
        part_logvars,
    ) = layer_parts
    return widen(
        (
            lax.all_gather(part_qkv, "blk", axis=1, tiled=True),
            lax.all_gather(part_out, "blk", axis=1, tiled=True),
            lax.all_gather(part_in, "blk", axis=1, tiled=True),
            lax.all_gather(part_back, "blk", axis=1, tiled=True),
            lax.all_gather(part_latent, "blk", axis=1, tiled=True),
            lax.all_gather(part_decode, "blk", axis=1, tiled=True),
            lax.all_gather(part_vectors, "blk", axis=1, tiled=True),
            lax.all_gather(part_inner, "blk", axis=0, tiled=True),
            lax.all_gather(part_means, "blk", axis=1, tiled=True),
            lax.all_gather(part_logvars, "blk", axis=1, tiled=True),
        )
    )


def reduce_grads(grads):
    (
        grad_qkv_w,
        grad_out_w,
        grad_in_w,
        grad_back_w,
        grad_latent_w,
        grad_decode_w,
        grad_vec,
        grad_inner,
        grad_mean_rows,
        grad_logvars,
    ) = grads
    (
        shard_qkv,
        shard_out,
        shard_in,
        shard_back,
        shard_latent,
        shard_decode,
        shard_vec,
        shard_inner,
        shard_means,
        shard_logvars,
    ) = (
        lax.psum_scatter(grad_qkv_w, "blk", scatter_dimension=1, tiled=True),
        lax.psum_scatter(grad_out_w, "blk", scatter_dimension=1, tiled=True),
        lax.psum_scatter(grad_in_w, "blk", scatter_dimension=1, tiled=True),
        lax.psum_scatter(grad_back_w, "blk", scatter_dimension=1, tiled=True),
        lax.psum_scatter(grad_latent_w, "blk", scatter_dimension=1, tiled=True),
        lax.psum_scatter(grad_decode_w, "blk", scatter_dimension=1, tiled=True),
        lax.psum_scatter(grad_vec, "blk", scatter_dimension=1, tiled=True),
        lax.psum_scatter(grad_inner, "blk", scatter_dimension=0, tiled=True),
        lax.psum_scatter(grad_mean_rows, "blk", scatter_dimension=1, tiled=True),
        lax.psum_scatter(grad_logvars, "blk", scatter_dimension=1, tiled=True),
    )
    return lax.psum(
        (
            shard_qkv,
            shard_out,
            shard_in,
            shard_back,
            shard_latent,
            shard_decode,
            shard_vec,
            shard_inner,
            shard_means,
            shard_logvars,
        ),
        "grp",
    )


def layer_forward(hidden, full_weights, noise_rows, live_rows, slide_len, score_scale):
    qkv_w, out_w, in_w, back_w, latent_w, decode_w, vec_rows, inner_rows, mean_rows, logvars = (
        full_weights
    )
    model_width = hidden.shape[1]
    slot_count = slide_len.shape[0]
    slot_span = hidden.shape[0] // slot_count
    ff_width = in_w.shape[1]
    normed = to_low(layer_norm(hidden, vec_rows[0], vec_rows[1]))
    qkv_all = product(normed, qkv_w)
    query_low = to_low(qkv_all[:, :model_width] + vec_rows[2])
    keys_own = to_low(qkv_all[:, model_width : 2 * model_width])
    values_own = to_low(qkv_all[:, 2 * model_width :] + vec_rows[3])
    keys_all, values_all = (
        lax.all_gather(
            keys_own.reshape(slot_count, slot_span, model_width), "blk", axis=1, tiled=True
        ),
        lax.all_gather(
            values_own.reshape(slot_count, slot_span, model_width), "blk", axis=1, tiled=True
        ),
    )
    scores = slot_scores(
        query_low.reshape(slot_count, slot_span, model_width), keys_all, slide_len, score_scale
    )
    row_peak = jnp.max(scores, axis=-1, keepdims=True)
    weights = jnp.exp(scores - row_peak)
    totals = jnp.sum(weights, axis=-1, keepdims=True)
    probs_low = to_low(weights / totals)
    log_total = row_peak + jnp.log(totals)
    heads_v = values_all.reshape(slot_count, values_all.shape[1], HEADS, HEAD_DIM)
    mixed_f = jnp.einsum("shqk,skhd->sqhd", probs_low, heads_v, preferred_element_type=jnp.float32)
    mixed_low = to_low(mixed_f.reshape(slot_count * slot_span, model_width))
    attended = hidden + product(mixed_low, out_w) + vec_rows[4]
    normed_two = to_low(layer_norm(attended, vec_rows[5], vec_rows[6]))
    inner_act = product(normed_two, in_w) + inner_rows[:ff_width]
    activated = to_low(jax.nn.gelu(inner_act))
    fed_rows = attended + product(activated, back_w) + vec_rows[7]
    fed_low = to_low(fed_rows)
    latent = product(fed_low, latent_w) + inner_rows[ff_width:]
    sample, kl_part = bottleneck(latent, noise_rows, live_rows, mean_rows, logvars)
    sample_low = to_low(sample)
    output = fed_rows + product(sample_low, decode_w) + vec_rows[8]
    saved_state = (
        hidden,
        normed,
        query_low,
        keys_own,
        values_own,
        log_total,
        mixed_low,
        attended,
        normed_two,
        inner_act,
        activated,
        fed_low,
        latent,
        sample_low,
    )
    return (output, kl_part, saved_state)


def layer_backward(
    grad_out, full_weights, saved_state, noise_rows, live_rows, slide_len, score_scale
):
    qkv_w, out_w, in_w, back_w, latent_w, decode_w, vec_rows, inner_rows, mean_rows, logvars = (
        full_weights
    )
    (
        hidden,
        normed,
        query_low,
        keys_own,
        values_own,
        log_total,
        mixed_low,
        attended,
        normed_two,
        inner_act,
        activated,
        fed_low,
        latent,
        sample_low,
    ) = saved_state
    model_width = hidden.shape[1]
    row_total = hidden.shape[0]
    slot_count = slide_len.shape[0]
    slot_span = row_total // slot_count
    grad_dec_low = to_low(grad_out)
    grad_decode_w = product_tn(sample_low, grad_dec_low)
    grad_sample = product_nt(grad_dec_low, decode_w)

    def bottle(latent_in, means_in, logvars_in):
        return bottleneck(latent_in, noise_rows, live_rows, means_in, logvars_in)

    ignored, bottle_pull = jax.vjp(bottle, latent, mean_rows, logvars)
    grad_latent_f, grad_mean_rows, grad_logvars = bottle_pull(
        (grad_sample, jnp.ones((), jnp.float32))
    )
    grad_latent_low = to_low(grad_latent_f)
    grad_latent_w = product_tn(fed_low, grad_latent_low)
    grad_fed = grad_out + product_nt(grad_latent_low, latent_w)
    grad_fed_low = to_low(grad_fed)
    grad_back_w = product_tn(activated, grad_fed_low)
    grad_act = product_nt(grad_fed_low, back_w)
    ignored_two, gelu_pull = jax.vjp(jax.nn.gelu, inner_act)
    grad_inner_low = to_low(gelu_pull(grad_act)[0])
    grad_in_w = product_tn(normed_two, grad_inner_low)
    grad_normed_two = product_nt(grad_inner_low, in_w)
    ignored_three, second_pull = jax.vjp(layer_norm, attended, vec_rows[5], vec_rows[6])
    grad_att_norm, grad_gain_two, grad_shift_two = second_pull(grad_normed_two)
    grad_attended = grad_fed + grad_att_norm
    grad_proj_low = to_low(grad_attended)
    grad_out_w = product_tn(mixed_low, grad_proj_low)
    grad_mixed_low = to_low(product_nt(grad_proj_low, out_w))
    keys_all, values_all = (
        lax.all_gather(
            keys_own.reshape(slot_count, slot_span, model_width), "blk", axis=1, tiled=True
        ),
        lax.all_gather(
            values_own.reshape(slot_count, slot_span, model_width), "blk", axis=1, tiled=True
        ),
    )
    grad_mixed_heads = grad_mixed_low.reshape(slot_count, slot_span, HEADS, HEAD_DIM)
    heads_k = keys_all.reshape(slot_count, keys_all.shape[1], HEADS, HEAD_DIM)
    heads_v = values_all.reshape(slot_count, values_all.shape[1], HEADS, HEAD_DIM)
    scores = slot_scores(
        query_low.reshape(slot_count, slot_span, model_width), keys_all, slide_len, score_scale
    )
    probs_f = jnp.exp(scores - log_total)
    grad_probs = jnp.einsum(
        "sqhd,skhd->shqk", grad_mixed_heads, heads_v, preferred_element_type=jnp.float32
    )
    centre = jnp.sum(grad_probs * probs_f, axis=-1, keepdims=True)
    grad_scores_low = to_low(probs_f * (grad_probs - centre))
    grad_query = (
        jnp.einsum("shqk,skhd->sqhd", grad_scores_low, heads_k, preferred_element_type=jnp.float32)
        * score_scale
    )
    grad_query_low = to_low(grad_query.reshape(row_total, model_width))
    rows_all, mixed_all = (
        lax.all_gather(
            query_low.reshape(slot_count, slot_span, model_width), "blk", axis=1, tiled=True
        ),
        lax.all_gather(
            grad_mixed_low.reshape(slot_count, slot_span, model_width), "blk", axis=1, tiled=True
        ),
    )
    total_all, centre_all = (
        lax.all_gather(log_total, "blk", axis=2, tiled=True),
        lax.all_gather(centre, "blk", axis=2, tiled=True),
    )
    query_all = rows_all.reshape(slot_count, rows_all.shape[1], HEADS, HEAD_DIM)
    dmixed_all = mixed_all.reshape(slot_count, mixed_all.shape[1], HEADS, HEAD_DIM)
    own_keys = keys_own.reshape(slot_count, slot_span, HEADS, HEAD_DIM)
    own_values = values_own.reshape(slot_count, slot_span, HEADS, HEAD_DIM)
    own_raw = (
        jnp.einsum("sqhd,skhd->shqk", query_all, own_keys, preferred_element_type=jnp.float32)
        * score_scale
    )
    key_places = lax.axis_index("blk") * slot_span + jnp.arange(slot_span)
    live_own = key_places[None, :] < slide_len[:, None]
    own_scores = jnp.where(live_own[:, None, None, :], own_raw, MASKED)
    own_probs = jnp.exp(own_scores - total_all)
    own_dprobs = jnp.einsum(
        "sqhd,skhd->shqk", dmixed_all, own_values, preferred_element_type=jnp.float32
    )
    own_dscores = to_low(own_probs * (own_dprobs - centre_all))
    grad_keys = (
        jnp.einsum("shqk,sqhd->skhd", own_dscores, query_all, preferred_element_type=jnp.float32)
        * score_scale
    )
    grad_values = jnp.einsum(
        "shqk,sqhd->skhd", to_low(own_probs), dmixed_all, preferred_element_type=jnp.float32
    )
    grad_keys_low = to_low(grad_keys.reshape(row_total, model_width))
    grad_values_low = to_low(grad_values.reshape(row_total, model_width))
    grad_qkv_low = jnp.concatenate([grad_query_low, grad_keys_low, grad_values_low], axis=1)
    grad_qkv_w = product_tn(normed, grad_qkv_low)
    grad_normed = product_nt(grad_qkv_low, qkv_w)
    ignored_four, first_pull = jax.vjp(layer_norm, hidden, vec_rows[0], vec_rows[1])
    grad_hid_norm, grad_gain_one, grad_shift_one = first_pull(grad_normed)
    grad_hidden = grad_attended + grad_hid_norm
    grad_vec = jnp.stack(
        [
            grad_gain_one,
            grad_shift_one,
            jnp.sum(grad_query_low.astype(jnp.float32), axis=0),
            jnp.sum(grad_values_low.astype(jnp.float32), axis=0),
            jnp.sum(grad_attended, axis=0),
            grad_gain_two,
            grad_shift_two,
            jnp.sum(grad_fed, axis=0),
            jnp.sum(grad_out, axis=0),
        ]
    )
    grad_inner = jnp.concatenate(
        [
            jnp.sum(grad_inner_low.astype(jnp.float32), axis=0),
            jnp.sum(grad_latent_low.astype(jnp.float32), axis=0),
        ]
    )
    return (
        grad_hidden,
        (
            grad_qkv_w,
            grad_out_w,
            grad_in_w,
            grad_back_w,
            grad_latent_w,
            grad_decode_w,
            grad_vec,
            grad_inner,
            grad_mean_rows,
            grad_logvars,
        ),
    )


def per_device(
    cell_input,
    lengths,
    noise_draw,
    cotangent,
    w_qkv,
    w_out,
    w_ffn_in,
    w_ffn_out,
    w_latent,
    w_decode,
    vectors,
    inner_bias,
    prior_means,
    prior_logvars,
):
    slot_count = cell_input.shape[1]
    slot_span = cell_input.shape[2]
    model_width = cell_input.shape[3]
    row_total = slot_count * slot_span
    lat_width = noise_draw.shape[-1]
    cycle_size = lax.axis_size("blk")
    score_scale = 1.0 / math.sqrt(HEAD_DIM)
    slide_len = lengths[0]
    positions = lax.axis_index("blk") * slot_span + jnp.arange(slot_span)
    live_rows = (positions[None, :] < slide_len[:, None]).reshape(row_total)
    hidden = cell_input[0].reshape(row_total, model_width).astype(jnp.float32)
    stacks = (
        w_qkv,
        w_out,
        w_ffn_in,
        w_ffn_out,
        w_latent,
        w_decode,
        vectors,
        inner_bias,
        prior_means,
        prior_logvars,
    )
    layer_idx = 0
    full_weights = gather_weights([stacked[layer_idx] for stacked in stacks])
    kept_weights = [full_weights]
    hidden, kl_part, saved_state = layer_forward(
        hidden,
        full_weights,
        noise_draw[layer_idx, 0].reshape(row_total, lat_width),
        live_rows,
        slide_len,
        score_scale,
    )
    saved_layers = [saved_state]
    layer_out = hidden.reshape(1, slot_count, slot_span, model_width)
    kl_total = lax.psum(kl_part, ("grp", "blk"))
    kl_mean = kl_total / (lax.axis_size("grp") * cycle_size * row_total)
    grad_rows = cotangent[0].reshape(row_total, model_width).astype(jnp.float32)
    reduced = [None] * LAYERS
    for layer_idx in reversed(range(LAYERS)):
        full_weights = kept_weights[layer_idx]
        grad_rows, grads = layer_backward(
            grad_rows,
            full_weights,
            saved_layers[layer_idx],
            noise_draw[layer_idx, 0].reshape(row_total, lat_width),
            live_rows,
            slide_len,
            score_scale,
        )
        reduced[layer_idx] = reduce_grads(grads)
    grad_cells = grad_rows.reshape(1, slot_count, slot_span, model_width)
    stacked_grads = [jnp.stack([reduced[0][member]]) for member in range(10)]
    return (
        layer_out,
        grad_cells,
        kl_mean,
        stacked_grads[0],
        stacked_grads[1],
        stacked_grads[2],
        stacked_grads[3],
        stacked_grads[4],
        stacked_grads[5],
        stacked_grads[6],
        stacked_grads[7],
        stacked_grads[8],
        stacked_grads[9],
    )


ZY = ("z", "y")
CHIPS = ("z", "y", "x")
EVERY = ("grp", "z", "y", "x")
PAIR = 2 * HEAD_DIM
VMEM_LIMIT = 48 * 1024 * 1024


def hop(values, axis, step=1):
    size = lax.axis_size(axis)
    return lax.ppermute(values, axis, [(i, i ^ step) for i in range(size)])


def other_core(values):
    return hop(values, "grp")


def swap_groups(values):
    return lax.ppermute(values, ("grp", "x"), [(0, 0), (1, 2), (2, 1), (3, 3)])


def by_core(own, other, axis):
    first = lax.axis_index("grp") == 0
    return jnp.concatenate(
        [jnp.where(first, own, other), jnp.where(first, other, own)], axis=axis
    )


def half_of(values, axis, mine):
    part = values.shape[axis] // 2
    core = lax.axis_index("grp")
    place = core if mine else 1 - core
    return lax.dynamic_slice_in_dim(values, place * part, part, axis)


def flip(place, step):
    high = (place // 2 + step // 2) % 2
    low_bit = (place % 2 + step % 2) % 2
    return high * 2 + low_bit


PLAN_A = (
    (0, 32, 0, 0, 512, 0, 64, 0, 0),
    (0, 32, 1, 0, 512, 0, 64, 32, 0),
    (32, 128, 0, 0, 512, 1, 128, 0, 0),
    (32, 128, 1, 0, 512, 1, 128, 0, 512),
)
SHAPES_A = ((1024, 512), (2048, 1024))
PLAN_B = (
    (0, 64, 0, 0, 512, 0, 64, 0, 0),
    (0, 64, 1, 0, 512, 0, 64, 0, 512),
    (64, 64, 0, 0, 512, 0, 64, 0, 1024),
    (64, 64, 1, 0, 512, 0, 64, 0, 1536),
    (128, 32, 0, 0, 512, 1, 64, 0, 0),
    (128, 32, 1, 0, 512, 1, 64, 32, 0),
    (160, 16, 0, 0, 256, 2, 64, 0, 0),
    (160, 16, 0, 256, 256, 2, 64, 16, 0),
    (160, 16, 1, 0, 256, 2, 64, 32, 0),
    (160, 16, 1, 256, 256, 2, 64, 48, 0),
)
SHAPES_B = ((1024, 2048), (1024, 512), (1024, 256))
PLAN_C = (
    (0, 96, 0, 0, 512, 0, 192, 0, 0),
    (0, 96, 1, 0, 512, 0, 192, 96, 0),
)
SHAPES_C = ((3072, 512),)
BLOCKS = [(dz, dy, dx) for dz in range(4) for dy in range(2) for dx in range(2)]


def run_copies(copies, sems):
    started = []
    for place, (source, target) in enumerate(copies):
        copy = pltpu.make_async_copy(source, target, sems.at[place])
        copy.start()
        started.append(copy)
    for copy in started:
        copy.wait()


def copy_call(body, operands, out_shapes, count):
    anywhere = pl.BlockSpec(memory_space=pl.ANY)
    return pl.pallas_call(
        body,
        out_shape=out_shapes,
        in_specs=[anywhere] * len(operands),
        out_specs=[pl.BlockSpec(memory_space=pltpu.VMEM)] * len(out_shapes),
        scratch_shapes=[pltpu.SemaphoreType.DMA((count,))],
        compiler_params=pltpu.CompilerParams(vmem_limit_bytes=VMEM_LIMIT),
    )(*operands)


def block_rows(entry, step):
    dz, dy, dx = step
    block = (
        flip(lax.axis_index("z"), dz) * 2 + flip(lax.axis_index("y"), dy)
    ) * 2 + flip(lax.axis_index("x"), dx)
    return pl.multiple_of(block * entry[6] + entry[7], 16)


def gather_group(shard, plan, shapes):
    parts = jnp.stack([shard] + [hop(shard, "z", step) for step in (1, 2, 3)])
    left, right = parts[:, :, :512], parts[:, :, 512:]
    left_x = hop(left, "x")
    right_y = hop(right, "y")
    left_two = jnp.stack([left, left_x])
    right_two = jnp.stack([right, right_y])
    left_far = hop(left_two, "y")
    right_far = hop(right_two, "x")

    def body(left_near, left_off, right_near, right_off, *rest):
        outs, sems = rest[:-1], rest[-1]
        copies = []
        for step in BLOCKS:
            dz, dy, dx = step
            for entry in plan:
                row, rows, side, lane, lanes, array, _, _, to_lane = entry
                if side == 0:
                    source = (left_off if dy else left_near).at[dx, dz]
                else:
                    source = (right_off if dx else right_near).at[dy, dz]
                copies.append(
                    (
                        source.at[pl.ds(row, rows), pl.ds(lane, lanes)],
                        outs[array].at[pl.ds(block_rows(entry, step), rows), pl.ds(to_lane, lanes)],
                    )
                )
        run_copies(copies, sems)

    return copy_call(
        body,
        (left_two, left_far, right_two, right_far),
        [jax.ShapeDtypeStruct(shape, shard.dtype) for shape in shapes],
        len(BLOCKS) * len(plan),
    )


def scatter_group(grads, plan, rows_all):
    def body(*refs):
        sources, (left_keep, left_send, right_keep, right_send), sems = (
            refs[: len(grads)],
            refs[len(grads) : -1],
            refs[-1],
        )
        copies = []
        for step in BLOCKS:
            dz, dy, dx = step
            for entry in plan:
                row, rows, side, lane, lanes, array, _, _, at_lane = entry
                if side == 0:
                    target = (left_send if dx else left_keep).at[dy, dz]
                else:
                    target = (right_send if dy else right_keep).at[dx, dz]
                copies.append(
                    (
                        sources[array].at[
                            pl.ds(block_rows(entry, step), rows), pl.ds(at_lane, lanes)
                        ],
                        target.at[pl.ds(row, rows), pl.ds(lane, lanes)],
                    )
                )
        run_copies(copies, sems)

    piece = jax.ShapeDtypeStruct((2, 4, rows_all, 512), jnp.bfloat16)
    left_keep, left_send, right_keep, right_send = copy_call(
        body, grads, [piece] * 4, len(BLOCKS) * len(plan)
    )
    left_came = hop(left_send, "x")
    right_came = hop(right_send, "y")
    left_sum = left_keep.astype(jnp.float32) + left_came.astype(jnp.float32)
    right_sum = right_keep.astype(jnp.float32) + right_came.astype(jnp.float32)
    left_last = hop(to_low(left_sum[1]), "y")
    right_last = hop(to_low(right_sum[1]), "x")
    whole = jnp.concatenate(
        [
            left_sum[0] + left_last.astype(jnp.float32),
            right_sum[0] + right_last.astype(jnp.float32),
        ],
        axis=2,
    )
    travel = to_low(whole)
    total = whole[0]
    for step in (1, 2, 3):
        total = total + hop(travel[step], "z", step).astype(jnp.float32)
    return total


def side_by_side(rows, count):
    part = rows.shape[0] // count
    return jnp.concatenate([rows[i * part : (i + 1) * part] for i in range(count)], axis=1)


def one_below(rows, count):
    part = rows.shape[1] // count
    return jnp.concatenate([rows[:, i * part : (i + 1) * part] for i in range(count)], axis=0)


def place_cells(near, far):
    rows = near.shape[1] - 16

    def body(near_ref, far_ref, cells_ref, small_ref, sems):
        copies = []
        for dz in range(4):
            for dy, ref in ((0, near_ref), (1, far_ref)):
                block = flip(lax.axis_index("z"), dz) * 2 + flip(lax.axis_index("y"), dy)
                copies.append((ref.at[dz, pl.ds(0, rows)], cells_ref.at[block]))
                copies.append((ref.at[dz, pl.ds(rows, 16)], small_ref.at[block]))
        run_copies(copies, sems)

    width = near.shape[2]
    return copy_call(
        body,
        (near, far),
        [
            jax.ShapeDtypeStruct((8, rows, width), near.dtype),
            jax.ShapeDtypeStruct((8, 16, width), near.dtype),
        ],
        16,
    )


def head_lanes(rows):
    return lax.broadcasted_iota(jnp.int32, (rows, PAIR), 1) < HEAD_DIM


def attend_body(own_ref, other_ref, bias_ref, mixed_ref, lse_ref):
    rows = own_ref.shape[0] * own_ref.shape[2]
    own = own_ref[...].reshape(rows, 3 * PAIR)
    other = other_ref[...].reshape(rows, 2 * PAIR)
    keys = jnp.concatenate([own[:, PAIR : 2 * PAIR], other[:, :PAIR]], axis=0)
    values = jnp.concatenate([own[:, 2 * PAIR :], other[:, PAIR:]], axis=0)
    bias = bias_ref[0]
    step = 256
    first_head = head_lanes(step)
    for start in range(0, rows, step):
        query = own[start : start + step, :PAIR]
        outs, totals = [], []
        for head in range(2):
            mine = first_head if head == 0 else jnp.logical_not(first_head)
            part = jnp.where(mine, query, jnp.zeros_like(query))
            scores = product_nt(part, keys) + bias
            peak = jnp.max(scores, axis=-1, keepdims=True)
            weights = jnp.exp(scores - peak)
            total = jnp.sum(weights, axis=-1, keepdims=True)
            outs.append(product(to_low(weights / total), values))
            totals.append(jnp.broadcast_to(peak + jnp.log(total), (step, PAIR)))
        mixed = to_low(jnp.where(first_head, outs[0], outs[1]))
        span = mixed_ref.shape[2]
        mixed_ref[start // span : (start + step) // span, 0] = mixed.reshape(
            step // span, span, PAIR
        )
        lse_ref[0, start : start + step] = jnp.where(first_head, totals[0], totals[1])


def slot_block(shape):
    return pl.BlockSpec((shape[0], 1) + tuple(shape[2:]), lambda s: (0, s, 0, 0))


def plane_block(shape):
    return pl.BlockSpec((1,) + tuple(shape[1:]), lambda s: (s, 0, 0))


def attend(qkv_own, kv_other, bias):
    blocks, slots, span, _ = qkv_own.shape
    rows = blocks * span
    mixed_shape = (blocks, slots, span, PAIR)
    lse_shape = (slots, rows, PAIR)
    return pl.pallas_call(
        attend_body,
        grid=(slots,),
        in_specs=[slot_block(qkv_own.shape), slot_block(kv_other.shape), plane_block(bias.shape)],
        out_specs=[slot_block(mixed_shape), plane_block(lse_shape)],
        out_shape=[
            jax.ShapeDtypeStruct(mixed_shape, jnp.bfloat16),
            jax.ShapeDtypeStruct(lse_shape, jnp.float32),
        ],
        compiler_params=pltpu.CompilerParams(vmem_limit_bytes=VMEM_LIMIT),
    )(qkv_own, kv_other, bias)


def attend_back_body(
    own_ref, other_ref, bias_ref, lse_ref, dmixed_ref, dquery_ref, down_ref, dother_ref, dk_ref, dv_ref
):
    rows = own_ref.shape[0] * own_ref.shape[2]
    own = own_ref[...].reshape(rows, 3 * PAIR)
    other = other_ref[...].reshape(rows, 2 * PAIR)
    keys = jnp.concatenate([own[:, PAIR : 2 * PAIR], other[:, :PAIR]], axis=0)
    values = jnp.concatenate([own[:, 2 * PAIR :], other[:, PAIR:]], axis=0)
    dmixed_all = dmixed_ref[...].reshape(rows, PAIR)
    bias = bias_ref[0]
    step = 256
    first_head = head_lanes(step)
    for start in range(0, rows, step):
        query = own[start : start + step, :PAIR]
        dmixed = dmixed_all[start : start + step]
        dqueries = []
        dkeys = jnp.zeros((2 * rows, PAIR), jnp.float32)
        dvalues = jnp.zeros((2 * rows, PAIR), jnp.float32)
        for head in range(2):
            mine = first_head if head == 0 else jnp.logical_not(first_head)
            part = jnp.where(mine, query, jnp.zeros_like(query))
            dpart = jnp.where(mine, dmixed, jnp.zeros_like(dmixed))
            lse = lse_ref[0, start : start + step, head * HEAD_DIM : head * HEAD_DIM + 1]
            probs = jnp.exp(product_nt(part, keys) + bias - lse)
            dprobs = product_nt(dpart, values)
            centre = jnp.sum(dprobs * probs, axis=-1, keepdims=True)
            dscores = to_low(probs * (dprobs - centre))
            dqueries.append(product(dscores, keys))
            dkeys = dkeys + product_tn(dscores, part)
            dvalues = dvalues + product_tn(to_low(probs), dpart)
        span = dquery_ref.shape[2]
        dquery = to_low(jnp.where(first_head, dqueries[0], dqueries[1]) * (HEAD_DIM**-0.5))
        dquery_ref[start // span : (start + step) // span, 0] = dquery.reshape(
            step // span, span, PAIR
        )
        if start == 0:
            dk_ref[...] = dkeys
            dv_ref[...] = dvalues
        else:
            dk_ref[...] += dkeys
            dv_ref[...] += dvalues
    grid = (own_ref.shape[0], own_ref.shape[2], PAIR)
    down_ref[:, 0, :, :PAIR] = dk_ref[:rows].reshape(grid)
    down_ref[:, 0, :, PAIR:] = dv_ref[:rows].reshape(grid)
    dother_ref[:, 0, :, :PAIR] = dk_ref[rows:].reshape(grid)
    dother_ref[:, 0, :, PAIR:] = dv_ref[rows:].reshape(grid)


def attend_back(qkv_own, kv_other, bias, lse, dmixed):
    blocks, slots, span, _ = qkv_own.shape
    rows = blocks * span
    dkv = (blocks, slots, span, 2 * PAIR)
    return pl.pallas_call(
        attend_back_body,
        grid=(slots,),
        in_specs=[
            slot_block(qkv_own.shape),
            slot_block(kv_other.shape),
            plane_block(bias.shape),
            plane_block(lse.shape),
            slot_block(dmixed.shape),
        ],
        out_specs=[slot_block(dmixed.shape), slot_block(dkv), slot_block(dkv)],
        out_shape=[
            jax.ShapeDtypeStruct(dmixed.shape, jnp.bfloat16),
            jax.ShapeDtypeStruct(dkv, jnp.float32),
            jax.ShapeDtypeStruct(dkv, jnp.float32),
        ],
        scratch_shapes=[
            pltpu.VMEM((2 * rows, PAIR), jnp.float32),
            pltpu.VMEM((2 * rows, PAIR), jnp.float32),
        ],
        compiler_params=pltpu.CompilerParams(vmem_limit_bytes=VMEM_LIMIT),
    )(qkv_own, kv_other, bias, lse, dmixed)


def head_routes(index):
    routes = []
    for core in range(2):
        for chip in range(16):
            head = (3 * chip + index) % 16
            routes.append((core * 16 + chip, (head % 2) * 16 + (head // 2) * 2 + core))
    return routes


def head_roles():
    roles = np.zeros((16, 3), np.int32)
    for chip in range(16):
        for index in range(3):
            block = 3 * chip + index
            roles[block % 16, block // 16] = index
    return roles


def fast_device(
    cell_input,
    lengths,
    noise_draw,
    cotangent,
    w_qkv,
    w_out,
    w_ffn_in,
    w_ffn_out,
    w_latent,
    w_decode,
    vectors,
    inner_bias,
    prior_means,
    prior_logvars,
):
    slots, span, width = cell_input.shape[1:]
    rows = slots * span
    lat = noise_draw.shape[-1]
    comps = prior_means.shape[1]
    ff = w_ffn_out.shape[1]
    core, zi, yi = lax.axis_index("grp"), lax.axis_index("z"), lax.axis_index("y")
    pair = zi * 2 + yi
    head = pair * 2 + core
    low = jnp.bfloat16

    pad = jnp.zeros((width,), low)
    lens = lengths[0]
    lens_low = jnp.concatenate([lens // 32, lens % 32]).astype(low)
    small_rows = jnp.stack(
        [
            jnp.concatenate([vectors.reshape(-1), inner_bias.reshape(-1), pad])[:width],
            jnp.concatenate([prior_means.reshape(-1), prior_logvars.reshape(-1)]),
            jnp.concatenate([lens_low, pad])[:width],
        ]
        + [pad] * 13
    )
    first = swap_groups(jnp.concatenate([cell_input[0].reshape(rows, width), small_rows]))
    near = [first] + [hop(first, "z", step) for step in (1, 2, 3)]
    far = [hop(block, "y") for block in near]
    cells, small_own = place_cells(jnp.stack(near), jnp.stack(far))
    small_other = other_core(small_own)

    qkv_t = w_qkv[0].T.reshape(3, HEAD_DIM, width)
    came = jnp.stack([lax.ppermute(qkv_t[i], EVERY, head_routes(i)) for i in range(3)])
    roles = jnp.asarray(head_roles())[head]
    head_w = jnp.stack([lax.dynamic_index_in_dim(came, roles[j], 0, False) for j in range(3)])
    head_w_other = other_core(head_w)
    pair_w = by_core(head_w[:, None], head_w_other[:, None], 1).reshape(3 * PAIR, width)

    shard_out = side_by_side(half_of(w_out[0], 0, True).T, 2)
    shard_in = half_of(w_ffn_in[0], 1, True).T
    back_rows = half_of(w_ffn_out[0].reshape(16, 2, ff // 32, -1), 1, True)
    shard_back = one_below(back_rows.reshape(ff // 2, -1).T, 2)
    shard_lat = side_by_side(half_of(w_latent[0], 0, True).T, 2)
    shard_dec = side_by_side(half_of(w_decode[0], 0, True).T, 4)
    shard_qkv = side_by_side(half_of(w_qkv[0], 0, True).T, 2)
    out_t, in_t = gather_group(jnp.concatenate([shard_out, shard_in]), PLAN_A, SHAPES_A)
    back_t, lat_t, dec_t = gather_group(
        jnp.concatenate([shard_back, shard_lat, shard_dec]), PLAN_B, SHAPES_B
    )
    (qkv_all_t,) = gather_group(shard_qkv, PLAN_C, SHAPES_C)
    out_t_other, lat_t_other = other_core(out_t), other_core(lat_t)
    dec_t_other, qkv_all_t_other = other_core(dec_t), other_core(qkv_all_t)

    def full_nt(left, own, other):
        return product_nt(half_of(left, 1, True), own) + product_nt(
            half_of(left, 1, False), other
        )

    def full_nn(left, own, other):
        return by_core(product(left, own), product(left, other), 1)

    small = by_core(small_own[:, None], small_other[:, None], 1).reshape(16, 16, width)
    small = small.astype(jnp.float32)
    n_vec = 9 * (width // 16)
    vec_rows = small[:, 0, :n_vec].reshape(16, 9, width // 16)
    vec_rows = vec_rows.transpose(1, 0, 2).reshape(9, width)
    inner_part = small[:, 0, n_vec : n_vec + inner_bias.shape[1]].reshape(-1)
    mean_rows = small[:, 1, :lat].reshape(16, comps, lat // 16)
    mean_rows = mean_rows.transpose(1, 0, 2).reshape(comps, lat)
    logvars = small[:, 1, lat:].reshape(16, comps, lat // 16)
    logvars = logvars.transpose(1, 0, 2).reshape(comps, lat)
    lens_f = first[rows + 2, : 2 * slots].astype(jnp.float32)
    slide_len = (lens_f[:slots] * 32 + lens_f[slots:]).astype(jnp.int32)
    ff_bias = half_of(inner_part[:ff].reshape(16, 2, ff // 32), 1, True).reshape(ff // 2)
    lat_bias = inner_part[ff:]

    cells_f = cells.reshape(8 * rows, width).astype(jnp.float32)
    normed = to_low(layer_norm(cells_f, vec_rows[0], vec_rows[1]))
    pair_q = lax.dynamic_slice_in_dim(vec_rows[2], pair * PAIR, PAIR)
    pair_v = lax.dynamic_slice_in_dim(vec_rows[3], pair * PAIR, PAIR)
    qkv = product_nt(normed, pair_w)
    query = to_low(qkv[:, :PAIR] + pair_q) * jnp.asarray(HEAD_DIM**-0.5, low)
    qkv_own = jnp.concatenate(
        [query, to_low(qkv[:, PAIR : 2 * PAIR]), to_low(qkv[:, 2 * PAIR :] + pair_v)], axis=1
    ).reshape(8, slots, span, 3 * PAIR)
    kv_other = other_core(qkv_own[..., PAIR:])
    starts = jnp.arange(8)[None, :] * 2 + jnp.stack([core, 1 - core])[:, None]
    places = (starts[:, :, None] * span + jnp.arange(span)).reshape(-1)
    bias = jnp.where(places[None, :] < slide_len[:, None], 0.0, MASKED)[:, None, :]
    mixed_pair, lse = attend(qkv_own, kv_other, bias)
    mixed_low = lax.all_to_all(
        mixed_pair.reshape(8, rows, PAIR), ZY, split_axis=0, concat_axis=0, tiled=True
    )
    mixed_low = mixed_low.transpose(1, 0, 2).reshape(rows, width)

    hidden = first[:rows].astype(jnp.float32)
    noise_rows = swap_groups(noise_draw.reshape(rows, lat))
    cot_low = swap_groups(cotangent.reshape(rows, width))
    row_places = head * span + jnp.arange(span)
    live_rows = (row_places[None, :] < slide_len[:, None]).reshape(rows)
    attended = hidden + full_nt(mixed_low, out_t, out_t_other) + vec_rows[4]
    normed_two = to_low(layer_norm(attended, vec_rows[5], vec_rows[6]))
    both_two = jnp.concatenate([normed_two, other_core(normed_two)])
    inner_act = product_nt(both_two, in_t) + ff_bias
    activated = to_low(jax.nn.gelu(inner_act))
    fed_parts = product_nt(activated, back_t)
    fed_rows = attended + (fed_parts[:rows] + other_core(fed_parts[rows:])) + vec_rows[7]
    fed_low = to_low(fed_rows)
    latent = full_nt(fed_low, lat_t, lat_t_other) + lat_bias

    def bottle(latent_in, means_in, logvars_in):
        return bottleneck(latent_in, noise_rows, live_rows, means_in, logvars_in)

    (sample, kl_part), bottle_pull = jax.vjp(bottle, latent, mean_rows, logvars)
    sample_low = to_low(sample)
    output = fed_rows + full_nt(sample_low, dec_t, dec_t_other) + vec_rows[8]
    layer_out = swap_groups(output)

    grad_out = cot_low.astype(jnp.float32)
    grad_sample = full_nn(cot_low, dec_t, dec_t_other)
    grad_latent_f, grad_mean_rows, grad_logvars = bottle_pull(
        (grad_sample, jnp.ones((), jnp.float32))
    )
    grad_latent_low = to_low(grad_latent_f)
    grad_fed = grad_out + full_nn(grad_latent_low, lat_t, lat_t_other)
    grad_fed_low = to_low(grad_fed)
    both_fed = jnp.concatenate([grad_fed_low, other_core(grad_fed_low)])
    grad_act = product(both_fed, back_t)
    ignored, gelu_pull = jax.vjp(jax.nn.gelu, inner_act)
    grad_inner_low = to_low(gelu_pull(grad_act)[0])
    norm_parts = product(grad_inner_low, in_t)
    grad_normed_two = norm_parts[:rows] + other_core(norm_parts[rows:])
    ignored, second_pull = jax.vjp(layer_norm, attended, vec_rows[5], vec_rows[6])
    grad_att_norm, grad_gain_two, grad_shift_two = second_pull(grad_normed_two)
    grad_attended = grad_fed + grad_att_norm
    grad_proj_low = to_low(grad_attended)
    grad_mixed_low = to_low(full_nn(grad_proj_low, out_t, out_t_other))
    dmixed = lax.all_to_all(
        grad_mixed_low.reshape(rows, 8, PAIR).transpose(1, 0, 2),
        ZY,
        split_axis=0,
        concat_axis=0,
        tiled=True,
    ).reshape(8, slots, span, PAIR)

    def weight_grad(left, right):
        return to_low(product_tn(left, right))

    both_cot = jnp.concatenate([cot_low, other_core(cot_low)])
    both_sample = jnp.concatenate([sample_low, other_core(sample_low)])
    both_lat = jnp.concatenate([grad_latent_low, other_core(grad_latent_low)])
    both_fed_low = jnp.concatenate([fed_low, other_core(fed_low)])
    both_proj = jnp.concatenate([grad_proj_low, other_core(grad_proj_low)])
    both_mixed = jnp.concatenate([mixed_low, other_core(mixed_low)])
    sum_b = scatter_group(
        (
            weight_grad(both_fed, activated),
            weight_grad(both_lat, half_of(both_fed_low, 1, True)),
            weight_grad(both_cot, half_of(both_sample, 1, True)),
        ),
        PLAN_B,
        176,
    )
    sum_a = scatter_group(
        (
            weight_grad(both_proj, half_of(both_mixed, 1, True)),
            weight_grad(grad_inner_low, both_two),
        ),
        PLAN_A,
        160,
    )

    dquery, dkv_own, dkv_other = attend_back(qkv_own, kv_other, bias, lse, dmixed)
    dkv = to_low(dkv_own + other_core(dkv_other))
    dqkv = jnp.concatenate([dquery, dkv], axis=3).reshape(8, rows, 3 * PAIR)
    dqkv_rows = lax.all_to_all(dqkv, ZY, split_axis=0, concat_axis=0, tiled=True)
    dqkv_rows = dqkv_rows.reshape(8, rows, 3, PAIR).transpose(2, 1, 0, 3).reshape(3, rows, width)
    grad_query_low, grad_keys_low, grad_values_low = dqkv_rows
    grad_normed = full_nn(
        jnp.concatenate([grad_query_low, grad_keys_low, grad_values_low], axis=1),
        qkv_all_t,
        qkv_all_t_other,
    )
    ignored, first_pull = jax.vjp(layer_norm, hidden, vec_rows[0], vec_rows[1])
    grad_hid_norm, grad_gain_one, grad_shift_one = first_pull(grad_normed)
    grad_cells = swap_groups(grad_attended + grad_hid_norm)

    pair_grad = product_tn(dqkv.reshape(8 * rows, 3 * PAIR), normed)
    pair_grad = pair_grad.reshape(3, 2, HEAD_DIM, width)
    head_grad = half_of(pair_grad, 1, True) + other_core(half_of(pair_grad, 1, False))
    head_grad = to_low(head_grad.reshape(3, HEAD_DIM, width))
    places_of = jnp.argsort(roles)
    back_home = [
        lax.ppermute(
            lax.dynamic_index_in_dim(head_grad, places_of[i], 0, False),
            EVERY,
            [(there, here) for here, there in head_routes(i)],
        )
        for i in range(3)
    ]
    home_grad = jnp.concatenate(back_home)
    grad_qkv = (
        home_grad.astype(jnp.float32) + other_core(home_grad).astype(jnp.float32)
    ).T

    grad_vec = jnp.stack(
        [
            grad_gain_one,
            grad_shift_one,
            jnp.sum(grad_query_low.astype(jnp.float32), axis=0),
            jnp.sum(grad_values_low.astype(jnp.float32), axis=0),
            jnp.sum(grad_attended, axis=0),
            grad_gain_two,
            grad_shift_two,
            jnp.sum(grad_fed, axis=0),
            jnp.sum(grad_out, axis=0),
        ]
    )
    ff_own = jnp.sum(grad_inner_low.astype(jnp.float32), axis=0).reshape(16, 1, ff // 32)
    ff_sums = by_core(ff_own, jnp.zeros_like(ff_own), 1).reshape(16, ff // 16)
    lat_sums = jnp.sum(grad_latent_low.astype(jnp.float32), axis=0)
    inner_sums = jnp.concatenate([ff_sums.reshape(-1), lat_sums]).reshape(16, -1)
    small_sums = jnp.concatenate(
        [
            grad_vec.reshape(9, 16, -1).transpose(1, 0, 2).reshape(16, -1),
            inner_sums,
            grad_mean_rows.reshape(comps, 16, -1).transpose(1, 0, 2).reshape(16, -1),
            grad_logvars.reshape(comps, 16, -1).transpose(1, 0, 2).reshape(16, -1),
            jnp.broadcast_to(kl_part, (16, 128)),
        ],
        axis=1,
    )
    small_width = small_sums.shape[1]
    small_sums = lax.all_to_all(
        small_sums.reshape(16, small_width // 128, 128),
        CHIPS,
        split_axis=0,
        concat_axis=0,
        tiled=True,
    )
    small_sums = jnp.sum(small_sums, axis=0)
    small_sums = (small_sums + other_core(small_sums)).reshape(-1)
    cuts = np.cumsum([n_vec, inner_sums.shape[1], comps * lat // 16, comps * lat // 16])
    vec_out, inner_out, means_out, logvars_out, kl_out = jnp.split(small_sums, cuts)
    kl_mean = kl_out[0] / (32 * rows)

    other_a, other_b = other_core(sum_a), other_core(sum_b)

    def halves(pick, axis):
        return by_core(pick(sum_a, sum_b), pick(other_a, other_b), axis)

    grad_out_w = halves(lambda a, b: one_below(a[:32], 2).T, 0)
    grad_in_w = halves(lambda a, b: a[32:].T, 1)
    grad_back_w = halves(
        lambda a, b: side_by_side(b[:128], 2).T.reshape(16, 1, ff // 32, -1), 1
    ).reshape(ff, -1)
    grad_lat_w = halves(lambda a, b: one_below(b[128:160], 2).T, 0)
    grad_dec_w = halves(lambda a, b: one_below(b[160:], 4).T, 0)
    return (
        layer_out.reshape(1, slots, span, width),
        grad_cells.reshape(1, slots, span, width),
        kl_mean,
        grad_qkv[None],
        grad_out_w[None],
        grad_in_w[None],
        grad_back_w[None],
        grad_lat_w[None],
        grad_dec_w[None],
        vec_out.reshape(1, 9, -1),
        inner_out[None],
        means_out.reshape(1, comps, -1),
        logvars_out.reshape(1, comps, -1),
    )


def solution(mesh):
    chips = mesh.shape["blk"]
    if (mesh.shape["grp"], chips) == (2, HEADS):
        mesh = Mesh(mesh.devices.reshape(2, chips // 4, 2, 2), EVERY)
        blk, run = CHIPS, fast_device
    else:
        blk, run = "blk", per_device
    cells = P("grp", None, blk, None)
    columns = P(None, None, blk)
    return jax.shard_map(
        run,
        mesh=mesh,
        in_specs=(cells, P("grp", None), P(None, "grp", None, blk, None), cells)
        + (columns,) * 7
        + (P(None, blk), columns, columns),
        out_specs=(cells, cells, P()) + (columns,) * 7 + (P(None, blk), columns, columns),
        check_vma=False,
    )
```

```python
import math

import jax
import jax.numpy as jnp
import numpy as np
from jax import lax
from jax.experimental import pallas as pl
from jax.experimental.pallas import tpu as pltpu
from jax.sharding import Mesh
from jax.sharding import PartitionSpec as P

HEADS = 16
LAYERS = 1
HEAD_DIM = 64


EPS_NORM = 1e-05
MASKED = -1e30


def to_low(values):
    return values.astype(jnp.bfloat16)


def product(left, right):
    return jnp.dot(left, right, preferred_element_type=jnp.float32)


def product_tn(left, right):
    return lax.dot_general(
        left, right, (((0,), (0,)), ((), ())), preferred_element_type=jnp.float32
    )


def product_nt(left, right):
    return lax.dot_general(
        left, right, (((1,), (1,)), ((), ())), preferred_element_type=jnp.float32
    )


def layer_norm(values, norm_gain, norm_shift):
    centre = values - jnp.mean(values, axis=-1, keepdims=True)
    spread = jnp.mean(centre * centre, axis=-1, keepdims=True)
    return centre * lax.rsqrt(spread + EPS_NORM) * norm_gain + norm_shift


def mixture_kl(sample, noise_rows, logvar, mean_rows, logvars):
    own_term = jnp.sum(-0.5 * noise_rows * noise_rows - 0.5 * logvar, axis=-1)
    offset = sample[:, None, :] - mean_rows[None, :, :]
    component = jnp.sum(
        -0.5 * offset * offset * jnp.exp(-logvars)[None] - 0.5 * logvars[None], axis=-1
    ) - math.log(mean_rows.shape[0])
    row_peak = jnp.max(component, axis=-1, keepdims=True)
    mixture = row_peak[:, 0] + jnp.log(jnp.sum(jnp.exp(component - row_peak), axis=-1))
    return own_term - mixture


def bottleneck(latent, noise_rows, live_rows, mean_rows, logvars):
    lat_width = noise_rows.shape[-1]
    mean_part = latent[:, :lat_width]
    logvar = latent[:, lat_width:]
    sample = mean_part + jnp.exp(0.5 * logvar) * noise_rows
    per_cell = mixture_kl(sample, noise_rows, logvar, mean_rows, logvars)
    return (sample, jnp.sum(jnp.where(live_rows, per_cell, 0.0)) / lat_width)


def slot_scores(query_slots, keys_all, slide_len, score_scale):
    slot_count, query_rows, model_width = query_slots.shape
    heads_q = query_slots.reshape(slot_count, query_rows, HEADS, HEAD_DIM)
    heads_k = keys_all.reshape(slot_count, keys_all.shape[1], HEADS, HEAD_DIM)
    raw_scores = (
        jnp.einsum("sqhd,skhd->shqk", heads_q, heads_k, preferred_element_type=jnp.float32)
        * score_scale
    )
    live_keys = jnp.arange(keys_all.shape[1])[None, :] < slide_len[:, None]
    return jnp.where(live_keys[:, None, None, :], raw_scores, MASKED)


def widen(gathered):
    qkv_w, out_w, in_w, back_w, latent_w, decode_w, vec_rows, inner_rows, mean_rows, logvars = (
        gathered
    )
    return (
        qkv_w,
        out_w,
        in_w,
        back_w,
        latent_w,
        decode_w,
        vec_rows.astype(jnp.float32),
        inner_rows.astype(jnp.float32),
        mean_rows.astype(jnp.float32),
        logvars.astype(jnp.float32),
    )


def gather_weights(layer_parts):
    (
        part_qkv,
        part_out,
        part_in,
        part_back,
        part_latent,
        part_decode,
        part_vectors,
        part_inner,
        part_means,
        part_logvars,
    ) = layer_parts
    return widen(
        (
            lax.all_gather(part_qkv, "blk", axis=1, tiled=True),
            lax.all_gather(part_out, "blk", axis=1, tiled=True),
            lax.all_gather(part_in, "blk", axis=1, tiled=True),
            lax.all_gather(part_back, "blk", axis=1, tiled=True),
            lax.all_gather(part_latent, "blk", axis=1, tiled=True),
            lax.all_gather(part_decode, "blk", axis=1, tiled=True),
            lax.all_gather(part_vectors, "blk", axis=1, tiled=True),
            lax.all_gather(part_inner, "blk", axis=0, tiled=True),
            lax.all_gather(part_means, "blk", axis=1, tiled=True),
            lax.all_gather(part_logvars, "blk", axis=1, tiled=True),
        )
    )


def reduce_grads(grads):
    (
        grad_qkv_w,
        grad_out_w,
        grad_in_w,
        grad_back_w,
        grad_latent_w,
        grad_decode_w,
        grad_vec,
        grad_inner,
        grad_mean_rows,
        grad_logvars,
    ) = grads
    (
        shard_qkv,
        shard_out,
        shard_in,
        shard_back,
        shard_latent,
        shard_decode,
        shard_vec,
        shard_inner,
        shard_means,
        shard_logvars,
    ) = (
        lax.psum_scatter(grad_qkv_w, "blk", scatter_dimension=1, tiled=True),
        lax.psum_scatter(grad_out_w, "blk", scatter_dimension=1, tiled=True),
        lax.psum_scatter(grad_in_w, "blk", scatter_dimension=1, tiled=True),
        lax.psum_scatter(grad_back_w, "blk", scatter_dimension=1, tiled=True),
        lax.psum_scatter(grad_latent_w, "blk", scatter_dimension=1, tiled=True),
        lax.psum_scatter(grad_decode_w, "blk", scatter_dimension=1, tiled=True),
        lax.psum_scatter(grad_vec, "blk", scatter_dimension=1, tiled=True),
        lax.psum_scatter(grad_inner, "blk", scatter_dimension=0, tiled=True),
        lax.psum_scatter(grad_mean_rows, "blk", scatter_dimension=1, tiled=True),
        lax.psum_scatter(grad_logvars, "blk", scatter_dimension=1, tiled=True),
    )
    return lax.psum(
        (
            shard_qkv,
            shard_out,
            shard_in,
            shard_back,
            shard_latent,
            shard_decode,
            shard_vec,
            shard_inner,
            shard_means,
            shard_logvars,
        ),
        "grp",
    )


def layer_forward(hidden, full_weights, noise_rows, live_rows, slide_len, score_scale):
    qkv_w, out_w, in_w, back_w, latent_w, decode_w, vec_rows, inner_rows, mean_rows, logvars = (
        full_weights
    )
    model_width = hidden.shape[1]
    slot_count = slide_len.shape[0]
    slot_span = hidden.shape[0] // slot_count
    ff_width = in_w.shape[1]
    normed = to_low(layer_norm(hidden, vec_rows[0], vec_rows[1]))
    qkv_all = product(normed, qkv_w)
    query_low = to_low(qkv_all[:, :model_width] + vec_rows[2])
    keys_own = to_low(qkv_all[:, model_width : 2 * model_width])
    values_own = to_low(qkv_all[:, 2 * model_width :] + vec_rows[3])
    keys_all, values_all = (
        lax.all_gather(
            keys_own.reshape(slot_count, slot_span, model_width), "blk", axis=1, tiled=True
        ),
        lax.all_gather(
            values_own.reshape(slot_count, slot_span, model_width), "blk", axis=1, tiled=True
        ),
    )
    scores = slot_scores(
        query_low.reshape(slot_count, slot_span, model_width), keys_all, slide_len, score_scale
    )
    row_peak = jnp.max(scores, axis=-1, keepdims=True)
    weights = jnp.exp(scores - row_peak)
    totals = jnp.sum(weights, axis=-1, keepdims=True)
    probs_low = to_low(weights / totals)
    log_total = row_peak + jnp.log(totals)
    heads_v = values_all.reshape(slot_count, values_all.shape[1], HEADS, HEAD_DIM)
    mixed_f = jnp.einsum("shqk,skhd->sqhd", probs_low, heads_v, preferred_element_type=jnp.float32)
    mixed_low = to_low(mixed_f.reshape(slot_count * slot_span, model_width))
    attended = hidden + product(mixed_low, out_w) + vec_rows[4]
    normed_two = to_low(layer_norm(attended, vec_rows[5], vec_rows[6]))
    inner_act = product(normed_two, in_w) + inner_rows[:ff_width]
    activated = to_low(jax.nn.gelu(inner_act))
    fed_rows = attended + product(activated, back_w) + vec_rows[7]
    fed_low = to_low(fed_rows)
    latent = product(fed_low, latent_w) + inner_rows[ff_width:]
    sample, kl_part = bottleneck(latent, noise_rows, live_rows, mean_rows, logvars)
    sample_low = to_low(sample)
    output = fed_rows + product(sample_low, decode_w) + vec_rows[8]
    saved_state = (
        hidden,
        normed,
        query_low,
        keys_own,
        values_own,
        log_total,
        mixed_low,
        attended,
        normed_two,
        inner_act,
        activated,
        fed_low,
        latent,
        sample_low,
    )
    return (output, kl_part, saved_state)


def layer_backward(
    grad_out, full_weights, saved_state, noise_rows, live_rows, slide_len, score_scale
):
    qkv_w, out_w, in_w, back_w, latent_w, decode_w, vec_rows, inner_rows, mean_rows, logvars = (
        full_weights
    )
    (
        hidden,
        normed,
        query_low,
        keys_own,
        values_own,
        log_total,
        mixed_low,
        attended,
        normed_two,
        inner_act,
        activated,
        fed_low,
        latent,
        sample_low,
    ) = saved_state
    model_width = hidden.shape[1]
    row_total = hidden.shape[0]
    slot_count = slide_len.shape[0]
    slot_span = row_total // slot_count
    grad_dec_low = to_low(grad_out)
    grad_decode_w = product_tn(sample_low, grad_dec_low)
    grad_sample = product_nt(grad_dec_low, decode_w)

    def bottle(latent_in, means_in, logvars_in):
        return bottleneck(latent_in, noise_rows, live_rows, means_in, logvars_in)

    ignored, bottle_pull = jax.vjp(bottle, latent, mean_rows, logvars)
    grad_latent_f, grad_mean_rows, grad_logvars = bottle_pull(
        (grad_sample, jnp.ones((), jnp.float32))
    )
    grad_latent_low = to_low(grad_latent_f)
    grad_latent_w = product_tn(fed_low, grad_latent_low)
    grad_fed = grad_out + product_nt(grad_latent_low, latent_w)
    grad_fed_low = to_low(grad_fed)
    grad_back_w = product_tn(activated, grad_fed_low)
    grad_act = product_nt(grad_fed_low, back_w)
    ignored_two, gelu_pull = jax.vjp(jax.nn.gelu, inner_act)
    grad_inner_low = to_low(gelu_pull(grad_act)[0])
    grad_in_w = product_tn(normed_two, grad_inner_low)
    grad_normed_two = product_nt(grad_inner_low, in_w)
    ignored_three, second_pull = jax.vjp(layer_norm, attended, vec_rows[5], vec_rows[6])
    grad_att_norm, grad_gain_two, grad_shift_two = second_pull(grad_normed_two)
    grad_attended = grad_fed + grad_att_norm
    grad_proj_low = to_low(grad_attended)
    grad_out_w = product_tn(mixed_low, grad_proj_low)
    grad_mixed_low = to_low(product_nt(grad_proj_low, out_w))
    keys_all, values_all = (
        lax.all_gather(
            keys_own.reshape(slot_count, slot_span, model_width), "blk", axis=1, tiled=True
        ),
        lax.all_gather(
            values_own.reshape(slot_count, slot_span, model_width), "blk", axis=1, tiled=True
        ),
    )
    grad_mixed_heads = grad_mixed_low.reshape(slot_count, slot_span, HEADS, HEAD_DIM)
    heads_k = keys_all.reshape(slot_count, keys_all.shape[1], HEADS, HEAD_DIM)
    heads_v = values_all.reshape(slot_count, values_all.shape[1], HEADS, HEAD_DIM)
    scores = slot_scores(
        query_low.reshape(slot_count, slot_span, model_width), keys_all, slide_len, score_scale
    )
    probs_f = jnp.exp(scores - log_total)
    grad_probs = jnp.einsum(
        "sqhd,skhd->shqk", grad_mixed_heads, heads_v, preferred_element_type=jnp.float32
    )
    centre = jnp.sum(grad_probs * probs_f, axis=-1, keepdims=True)
    grad_scores_low = to_low(probs_f * (grad_probs - centre))
    grad_query = (
        jnp.einsum("shqk,skhd->sqhd", grad_scores_low, heads_k, preferred_element_type=jnp.float32)
        * score_scale
    )
    grad_query_low = to_low(grad_query.reshape(row_total, model_width))
    rows_all, mixed_all = (
        lax.all_gather(
            query_low.reshape(slot_count, slot_span, model_width), "blk", axis=1, tiled=True
        ),
        lax.all_gather(
            grad_mixed_low.reshape(slot_count, slot_span, model_width), "blk", axis=1, tiled=True
        ),
    )
    total_all, centre_all = (
        lax.all_gather(log_total, "blk", axis=2, tiled=True),
        lax.all_gather(centre, "blk", axis=2, tiled=True),
    )
    query_all = rows_all.reshape(slot_count, rows_all.shape[1], HEADS, HEAD_DIM)
    dmixed_all = mixed_all.reshape(slot_count, mixed_all.shape[1], HEADS, HEAD_DIM)
    own_keys = keys_own.reshape(slot_count, slot_span, HEADS, HEAD_DIM)
    own_values = values_own.reshape(slot_count, slot_span, HEADS, HEAD_DIM)
    own_raw = (
        jnp.einsum("sqhd,skhd->shqk", query_all, own_keys, preferred_element_type=jnp.float32)
        * score_scale
    )
    key_places = lax.axis_index("blk") * slot_span + jnp.arange(slot_span)
    live_own = key_places[None, :] < slide_len[:, None]
    own_scores = jnp.where(live_own[:, None, None, :], own_raw, MASKED)
    own_probs = jnp.exp(own_scores - total_all)
    own_dprobs = jnp.einsum(
        "sqhd,skhd->shqk", dmixed_all, own_values, preferred_element_type=jnp.float32
    )
    own_dscores = to_low(own_probs * (own_dprobs - centre_all))
    grad_keys = (
        jnp.einsum("shqk,sqhd->skhd", own_dscores, query_all, preferred_element_type=jnp.float32)
        * score_scale
    )
    grad_values = jnp.einsum(
        "shqk,sqhd->skhd", to_low(own_probs), dmixed_all, preferred_element_type=jnp.float32
    )
    grad_keys_low = to_low(grad_keys.reshape(row_total, model_width))
    grad_values_low = to_low(grad_values.reshape(row_total, model_width))
    grad_qkv_low = jnp.concatenate([grad_query_low, grad_keys_low, grad_values_low], axis=1)
    grad_qkv_w = product_tn(normed, grad_qkv_low)
    grad_normed = product_nt(grad_qkv_low, qkv_w)
    ignored_four, first_pull = jax.vjp(layer_norm, hidden, vec_rows[0], vec_rows[1])
    grad_hid_norm, grad_gain_one, grad_shift_one = first_pull(grad_normed)
    grad_hidden = grad_attended + grad_hid_norm
    grad_vec = jnp.stack(
        [
            grad_gain_one,
            grad_shift_one,
            jnp.sum(grad_query_low.astype(jnp.float32), axis=0),
            jnp.sum(grad_values_low.astype(jnp.float32), axis=0),
            jnp.sum(grad_attended, axis=0),
            grad_gain_two,
            grad_shift_two,
            jnp.sum(grad_fed, axis=0),
            jnp.sum(grad_out, axis=0),
        ]
    )
    grad_inner = jnp.concatenate(
        [
            jnp.sum(grad_inner_low.astype(jnp.float32), axis=0),
            jnp.sum(grad_latent_low.astype(jnp.float32), axis=0),
        ]
    )
    return (
        grad_hidden,
        (
            grad_qkv_w,
            grad_out_w,
            grad_in_w,
            grad_back_w,
            grad_latent_w,
            grad_decode_w,
            grad_vec,
            grad_inner,
            grad_mean_rows,
            grad_logvars,
        ),
    )


def per_device(
    cell_input,
    lengths,
    noise_draw,
    cotangent,
    w_qkv,
    w_out,
    w_ffn_in,
    w_ffn_out,
    w_latent,
    w_decode,
    vectors,
    inner_bias,
    prior_means,
    prior_logvars,
):
    slot_count = cell_input.shape[1]
    slot_span = cell_input.shape[2]
    model_width = cell_input.shape[3]
    row_total = slot_count * slot_span
    lat_width = noise_draw.shape[-1]
    cycle_size = lax.axis_size("blk")
    score_scale = 1.0 / math.sqrt(HEAD_DIM)
    slide_len = lengths[0]
    positions = lax.axis_index("blk") * slot_span + jnp.arange(slot_span)
    live_rows = (positions[None, :] < slide_len[:, None]).reshape(row_total)
    hidden = cell_input[0].reshape(row_total, model_width).astype(jnp.float32)
    stacks = (
        w_qkv,
        w_out,
        w_ffn_in,
        w_ffn_out,
        w_latent,
        w_decode,
        vectors,
        inner_bias,
        prior_means,
        prior_logvars,
    )
    layer_idx = 0
    full_weights = gather_weights([stacked[layer_idx] for stacked in stacks])
    kept_weights = [full_weights]
    hidden, kl_part, saved_state = layer_forward(
        hidden,
        full_weights,
        noise_draw[layer_idx, 0].reshape(row_total, lat_width),
        live_rows,
        slide_len,
        score_scale,
    )
    saved_layers = [saved_state]
    layer_out = hidden.reshape(1, slot_count, slot_span, model_width)
    kl_total = lax.psum(kl_part, ("grp", "blk"))
    kl_mean = kl_total / (lax.axis_size("grp") * cycle_size * row_total)
    grad_rows = cotangent[0].reshape(row_total, model_width).astype(jnp.float32)
    reduced = [None] * LAYERS
    for layer_idx in reversed(range(LAYERS)):
        full_weights = kept_weights[layer_idx]
        grad_rows, grads = layer_backward(
            grad_rows,
            full_weights,
            saved_layers[layer_idx],
            noise_draw[layer_idx, 0].reshape(row_total, lat_width),
            live_rows,
            slide_len,
            score_scale,
        )
        reduced[layer_idx] = reduce_grads(grads)
    grad_cells = grad_rows.reshape(1, slot_count, slot_span, model_width)
    stacked_grads = [jnp.stack([reduced[0][member]]) for member in range(10)]
    return (
        layer_out,
        grad_cells,
        kl_mean,
        stacked_grads[0],
        stacked_grads[1],
        stacked_grads[2],
        stacked_grads[3],
        stacked_grads[4],
        stacked_grads[5],
        stacked_grads[6],
        stacked_grads[7],
        stacked_grads[8],
        stacked_grads[9],
    )


EVERY = ("grp", "z", "y", "x")
CHIPS = ("z", "y", "x")
PLANE = ("grp", "y", "x")
PAIR = 2 * HEAD_DIM
SMALL = 16
VMEM_LIMIT = 48 * 1024 * 1024


def hop(values, axis, step=1):
    size = lax.axis_size(axis)
    return lax.ppermute(values, axis, [(i, i ^ step) for i in range(size)])


def other_core(values):
    return hop(values, "grp")


def after(values, done):
    return lax.optimization_barrier((values, done))[0]


def ordered(own, other, axis_name, axis):
    first = lax.axis_index(axis_name) == 0
    return jnp.concatenate(
        [jnp.where(first, own, other), jnp.where(first, other, own)], axis=axis
    )


def half_of(values, axis, axis_name, mine):
    part = values.shape[axis] // 2
    place = lax.axis_index(axis_name)
    place = place if mine else 1 - place
    return lax.dynamic_slice_in_dim(values, place * part, part, axis)


def flip(place, step):
    high = (place // 2 + step // 2) % 2
    low_bit = (place % 2 + step % 2) % 2
    return high * 2 + low_bit


def slide_routes(k):
    return [
        (g * 4 + z, (z // 2) * 4 + 2 * g + ((z % 2) ^ k)) for g in range(2) for z in range(4)
    ]


def pick_slot(slots, k):
    odd = (lax.axis_index("z") + k) % 2 == 1
    return jnp.where(odd, slots[1], slots[0])


def to_slides(slots):
    return jnp.stack(
        [lax.ppermute(pick_slot(slots, k), ("grp", "z"), slide_routes(k)) for k in range(2)]
    )


def from_slides(blocks):
    came = [
        lax.ppermute(
            blocks[k], ("grp", "z"), [(there, here) for here, there in slide_routes(k)]
        )
        for k in range(2)
    ]
    return jnp.stack([pick_slot(came, 0), pick_slot(came, 1)])


def head_routes(index, k):
    routes = []
    for core in range(2):
        for chip in range(16):
            head = (3 * chip + index) % 16
            pair = head // 2
            plane = 2 * core + ((head % 2) ^ k)
            target = (pair // 4) * 16 + plane * 4 + pair % 4
            routes.append((core * 16 + chip, target))
    return routes


def head_roles():
    roles = np.zeros((16, 3), np.int32)
    for chip in range(16):
        for index in range(3):
            block = 3 * chip + index
            roles[block % 16, block // 16] = index
    return roles


def run_copies(copies, sems):
    started = []
    for place, (source, target) in enumerate(copies):
        copy = pltpu.make_async_copy(source, target, sems.at[place])
        copy.start()
        started.append(copy)
    for copy in started:
        copy.wait()


def copy_call(body, operands, out_shapes, count):
    return pl.pallas_call(
        body,
        out_shape=out_shapes,
        in_specs=[pl.BlockSpec(memory_space=pl.ANY)] * len(operands),
        out_specs=[pl.BlockSpec(memory_space=pltpu.VMEM)] * len(out_shapes),
        scratch_shapes=[pltpu.SemaphoreType.DMA((count,))],
        compiler_params=pltpu.CompilerParams(vmem_limit_bytes=VMEM_LIMIT),
    )(*operands)


def low_shape(*shape):
    return jax.ShapeDtypeStruct(shape, jnp.bfloat16)


def wide(values):
    return values.astype(jnp.float32)


def z_hops(values):
    return [hop(values[step - 1], "z", step) for step in (1, 2, 3)]


def plane_hops(values):
    return [
        hop(values[0], "x"),
        hop(values[1], "y"),
        lax.ppermute(values[2], ("y", "x"), [(i, i ^ 3) for i in range(4)]),
    ]


NEAR = ((0, 0), (0, 1), (1, 0), (1, 1))


def z_at(step, part):
    return pl.ds(pl.multiple_of(flip(lax.axis_index("z"), step) * part, part), part)


def chip_place(step):
    return flip(lax.axis_index("y"), step[0]) * 2 + flip(lax.axis_index("x"), step[1])


def place_cells(own, other):
    span, width = own.shape[2] - SMALL, own.shape[3]

    def body(own_ref, other_ref, cells_ref, small_ref, sems):
        core, zi, yi, xi = (lax.axis_index(name) for name in EVERY)
        copies = []
        for dc, ref in ((0, own_ref), (1, other_ref)):
            for dy in range(2):
                for dx in range(2):
                    there = (flip(core, dc), flip(yi, dy), flip(xi, dx))
                    block = (there[0] * 2 + there[1]) * 2 + there[2]
                    for k in range(2):
                        piece = ref.at[dy * 2 + dx, k]
                        copies.append(
                            (piece.at[pl.ds(0, span)], cells_ref.at[block, pl.ds(k * span, span)])
                        )
                        chip = ((there[0] * 2 + (zi + k) % 2) * 2 + there[1]) * 2 + there[2]
                        copies.append((piece.at[pl.ds(span, SMALL)], small_ref.at[chip]))
        run_copies(copies, sems)

    return copy_call(
        body,
        (own, other),
        [low_shape(8, 2 * span, width), low_shape(16, SMALL, width)],
        32,
    )


def wide_shape(*shape):
    return jax.ShapeDtypeStruct(shape, jnp.float32)


def whole_call(body, operands, out_shapes, scratch=()):
    vmem = pl.BlockSpec(memory_space=pltpu.VMEM)
    return pl.pallas_call(
        body,
        out_shape=out_shapes,
        in_specs=[vmem] * len(operands),
        out_specs=[vmem] * len(out_shapes),
        scratch_shapes=list(scratch),
        compiler_params=pltpu.CompilerParams(vmem_limit_bytes=VMEM_LIMIT),
    )(*operands)


def pack_small(vectors, inner_bias, prior_means, prior_logvars, lens):
    def put(part, lanes):
        return jnp.pad(part, ((0, SMALL - part.shape[0]), (0, lanes - part.shape[1])))

    lens_low = jnp.concatenate([lens // 32, lens % 32]).astype(jnp.bfloat16)
    return jnp.concatenate(
        [
            put(vectors, 128),
            put(prior_means, 128),
            put(prior_logvars, 128),
            put(inner_bias, 384),
            put(lens_low[None], 256),
        ],
        axis=1,
    )


def chunk_place(block, step=(0, 0), core_step=0):
    core = flip(lax.axis_index("grp"), core_step)
    return pl.multiple_of(((block * 4 + chip_place(step)) * 2 + core) * 128, 128)


LAT_ROW, FF_ROW, LEN_ROW = 9, 10, 11


def unpack_body(small_ref, vec_ref, means_ref, logvars_ref, inner_ref):
    count = small_ref.shape[0]

    def lanes(row, rows, first, width):
        return jnp.concatenate(
            [wide(small_ref[i, row : row + rows, first : first + width]) for i in range(count)],
            axis=1,
        )

    vec_ref[...] = lanes(0, SMALL, 0, vec_ref.shape[1] // count)
    means_ref[...] = lanes(0, SMALL, 128, means_ref.shape[1] // count)
    logvars_ref[...] = lanes(0, SMALL, 256, means_ref.shape[1] // count)
    inner_ref[...] = lanes(0, 1, 384, inner_ref.shape[1] // count)
    width = vec_ref.shape[1]
    vec_ref[LAT_ROW : LAT_ROW + 1] = inner_ref[:, inner_ref.shape[1] - width :]
    for block in range(4):
        vec_ref[FF_ROW : FF_ROW + 1, block * 128 : block * 128 + 128] = inner_ref[
            :, pl.ds(chunk_place(block), 128)
        ]
    lens = wide(small_ref[0, 0:1, 768:896])
    high = jnp.where(lax.axis_index("z") % 2 == 0, lens[:, 0:1], lens[:, 1:2])
    rest = jnp.where(lax.axis_index("z") % 2 == 0, lens[:, 2:3], lens[:, 3:4])
    vec_ref[LEN_ROW : LEN_ROW + 1] = jnp.broadcast_to(high * 32 + rest, (1, width))


def unpack_small(small, lat, inner):
    count, rows, width = small.shape
    return whole_call(
        unpack_body,
        (small,),
        [wide_shape(rows, width), wide_shape(rows, lat), wide_shape(rows, lat)],
        [pltpu.VMEM((1, inner), jnp.float32)],
    )


def row_stats(values):
    centre = values - jnp.mean(values, axis=-1, keepdims=True)
    scale = lax.rsqrt(jnp.mean(centre * centre, axis=-1, keepdims=True) + EPS_NORM)
    return centre * scale, scale


def norm_back(grad, unit, scale, gain):
    inner = grad * gain
    along = jnp.mean(inner * unit, axis=-1, keepdims=True)
    return scale * (inner - jnp.mean(inner, axis=-1, keepdims=True) - unit * along)


def column_sum(values):
    return jnp.sum(values, axis=0, keepdims=True)


def slide_place(core, block, k, row, span):
    zi = lax.axis_index("z")
    chip = (core * 2 + ((zi + k) & 1)) * 4 + block
    return chip * span + row


def head_lanes(rows):
    return lax.broadcasted_iota(jnp.int32, (rows, PAIR), 1) < HEAD_DIM


def own_pair():
    place = (lax.axis_index("grp") * 2 + lax.axis_index("y")) * 2 + lax.axis_index("x")
    return pl.multiple_of(place * PAIR, PAIR)


def attend_body(cells_ref, vec_ref, head_w_ref, normed_ref, qkv_ref, mixed_ref, lse_ref, bias_ref):
    total_rows = cells_ref.shape[0]
    step = 256
    gain, shift = vec_ref[0:1], vec_ref[1:2]
    bias_q = vec_ref[2:3, pl.ds(own_pair(), PAIR)]
    bias_v = vec_ref[3:4, pl.ds(own_pair(), PAIR)]
    for start in range(0, total_rows, step):
        unit, _ = row_stats(wide(cells_ref[start : start + step]))
        normed = to_low(unit * gain + shift)
        normed_ref[start : start + step] = normed
        qkv = product_nt(normed, head_w_ref[...])
        qkv_ref[start : start + step, :PAIR] = to_low(
            wide(to_low(qkv[:, :PAIR] + bias_q)) * HEAD_DIM**-0.5
        )
        qkv_ref[start : start + step, PAIR : 2 * PAIR] = to_low(qkv[:, PAIR : 2 * PAIR])
        qkv_ref[start : start + step, 2 * PAIR :] = to_low(qkv[:, 2 * PAIR :] + bias_v)
    span = total_rows // 16
    lane = lax.broadcasted_iota(jnp.int32, (1, total_rows), 1)
    place = slide_place(
        lane // (8 * span), (lane // (2 * span)) & 3, (lane // span) & 1, lane & (span - 1), span
    )
    bias = jnp.where(place.astype(jnp.float32) < vec_ref[LEN_ROW : LEN_ROW + 1], 0.0, MASKED)
    bias_ref[...] = bias
    keys = qkv_ref[:, PAIR : 2 * PAIR]
    values = qkv_ref[:, 2 * PAIR :]
    first_head = head_lanes(step)
    for start in range(0, total_rows, step):
        query = qkv_ref[start : start + step, :PAIR]
        outs, totals = [], []
        for head in range(2):
            mine = first_head if head == 0 else jnp.logical_not(first_head)
            part = jnp.where(mine, query, jnp.zeros_like(query))
            scores = product_nt(part, keys) + bias
            peak = jnp.max(scores, axis=-1, keepdims=True)
            weights = jnp.exp(scores - peak)
            total = jnp.sum(weights, axis=-1, keepdims=True)
            outs.append(product(to_low(weights / total), values))
            totals.append(jnp.broadcast_to(peak + jnp.log(total), (step, PAIR)))
        mixed_ref[start : start + step] = to_low(jnp.where(first_head, outs[0], outs[1]))
        lse_ref[start : start + step] = jnp.where(first_head, totals[0], totals[1])


def attend(cells, vec, head_w):
    rows, width = cells.shape
    return whole_call(
        attend_body,
        (cells, vec, head_w),
        [
            low_shape(rows, width),
            low_shape(rows, 3 * PAIR),
            low_shape(rows, PAIR),
            wide_shape(rows, PAIR),
            wide_shape(1, rows),
        ],
    )


def attend_back_body(
    qkv_ref,
    bias_ref,
    lse_ref,
    dmixed_ref,
    normed_ref,
    head_w_ref,
    grad_w_ref,
    near_ref,
    far_ref,
    sums_ref,
    dqkv_ref,
    dk_ref,
    dv_ref,
):
    rows = qkv_ref.shape[0]
    keys = qkv_ref[:, PAIR : 2 * PAIR]
    values = qkv_ref[:, 2 * PAIR :]
    bias = bias_ref[...]
    step = 256
    first_head = head_lanes(step)
    for start in range(0, rows, step):
        query = qkv_ref[start : start + step, :PAIR]
        dmixed = dmixed_ref[start : start + step]
        dqueries = []
        for head in range(2):
            mine = first_head if head == 0 else jnp.logical_not(first_head)
            part = jnp.where(mine, query, jnp.zeros_like(query))
            dpart = jnp.where(mine, dmixed, jnp.zeros_like(dmixed))
            lse = lse_ref[start : start + step, head * HEAD_DIM : head * HEAD_DIM + 1]
            probs = jnp.exp(product_nt(part, keys) + bias - lse)
            dprobs = product_nt(dpart, values)
            centre = jnp.sum(dprobs * probs, axis=-1, keepdims=True)
            dscores = to_low(probs * (dprobs - centre))
            dqueries.append(product(dscores, keys))
            dkeys = product_tn(dscores, part)
            dvalues = product_tn(to_low(probs), dpart)
            if start == 0 and head == 0:
                dk_ref[...] = dkeys
                dv_ref[...] = dvalues
            else:
                dk_ref[...] += dkeys
                dv_ref[...] += dvalues
        dquery = jnp.where(first_head, dqueries[0], dqueries[1]) * (HEAD_DIM**-0.5)
        dqkv_ref[start : start + step, :PAIR] = to_low(dquery)
    dqkv_ref[:, PAIR : 2 * PAIR] = to_low(dk_ref[...])
    dqkv_ref[:, 2 * PAIR :] = to_low(dv_ref[...])
    half = rows // 2
    core = lax.axis_index("grp")
    for ref, first in ((far_ref, (1 - core) * half), (near_ref, core * half)):
        for start in range(0, half, step):
            at = pl.ds(pl.multiple_of(first + start, step), step)
            ref[start : start + step] = product(dqkv_ref[at], head_w_ref[...])
    dqkv = dqkv_ref[...]
    grad_w_ref[...] = to_low(product_tn(dqkv, normed_ref[...]))
    sums_ref[...] = column_sum(wide(dqkv))


def attend_back(qkv, bias, lse, dmixed, normed, head_w):
    rows, width = normed.shape
    return whole_call(
        attend_back_body,
        (qkv, bias, lse, dmixed, normed, head_w),
        [
            low_shape(3 * PAIR, width),
            wide_shape(rows // 2, width),
            wide_shape(rows // 2, width),
            wide_shape(1, 3 * PAIR),
        ],
        [
            pltpu.VMEM((rows, 3 * PAIR), jnp.bfloat16),
            pltpu.VMEM((rows, PAIR), jnp.float32),
            pltpu.VMEM((rows, PAIR), jnp.float32),
        ],
    )


OUT_LANES, LAT_LANES, DEC_LANES = slice(0, 512), slice(512, 1024), slice(1024, 1280)


def project_body(mixed_ref, own_ref, other_ref, hidden_ref, vec_ref, attended_ref, normed_ref):
    core = lax.axis_index("grp")
    total = wide(hidden_ref[...]) + vec_ref[4:5]
    for i in range(4):
        lanes = slice(i * PAIR, (i + 1) * PAIR)
        total = total + product_nt(mixed_ref[core * 4 + i], own_ref[:, lanes])
        total = total + product_nt(mixed_ref[(1 - core) * 4 + i], other_ref[:, lanes])
    attended_ref[...] = total
    unit, _ = row_stats(total)
    normed_ref[...] = to_low(unit * vec_ref[5:6] + vec_ref[6:7])


def project(mixed, own, other, hidden, vec):
    shape = hidden.shape
    return whole_call(
        project_body, (mixed, own, other, hidden, vec), [wide_shape(*shape), low_shape(*shape)]
    )


GELU_SCALE = math.sqrt(2.0 / math.pi)
GELU_CUBE = 0.044715


def stack_rows(refs, target_ref):
    rows = refs[0].shape[0]
    for i, ref in enumerate(refs):
        target_ref[i * rows : (i + 1) * rows] = ref[...]


def stack_z(refs, target_ref):
    rows = refs[0].shape[0]
    for step, ref in enumerate(refs):
        target_ref[z_at(step, rows)] = ref[...]


FF_STEP = 256


def feed_body(*refs):
    rows_in, in_refs, back_refs, vec_ref = refs[:8], refs[8:12], refs[12:16], refs[16]
    act_ref, slope_ref, near_ref, far_ref, in_ref, back_ref, all_ref = refs[17:]
    stack_rows(rows_in, all_ref)
    stack_z(in_refs, in_ref)
    stack_z(back_refs, back_ref)
    half_rows = near_ref.shape[0]
    for first in (half_rows, 0):
        for start in range(first, first + half_rows, 256):
            at = slice(start, start + 256)
            total = None
            for unit in range(0, in_ref.shape[0], FF_STEP):
                lanes = slice(unit, unit + FF_STEP)
                inner = product_nt(all_ref[at], in_ref[lanes]) + vec_ref[FF_ROW : FF_ROW + 1, lanes]
                square = inner * inner
                bend = jnp.tanh(GELU_SCALE * (inner + GELU_CUBE * (inner * square)))
                half = 0.5 * (1.0 + bend)
                act = to_low(inner * half)
                act_ref[at, lanes] = act
                slope_ref[at, lanes] = half + (0.5 * GELU_SCALE) * inner * (1.0 - bend * bend) * (
                    1.0 + (3.0 * GELU_CUBE) * square
                )
                part = product_nt(act, back_ref[:, lanes])
                total = part if total is None else total + part
            ref = far_ref if first else near_ref
            ref[start - first : start - first + 256] = total


def feed(rows_in, in_parts, back_parts, vec):
    rows, width = rows_in[0].shape
    hidden = 4 * in_parts[0].shape[0]
    return whole_call(
        feed_body,
        (*rows_in, *in_parts, *back_parts, vec),
        [
            low_shape(8 * rows, hidden),
            wide_shape(8 * rows, hidden),
            wide_shape(4 * rows, width),
            wide_shape(4 * rows, width),
            low_shape(hidden, width),
            low_shape(width, hidden),
            low_shape(8 * rows, width),
        ],
    )


def feed_back_body(*refs):
    rows_in, (back_ref, in_ref, slope_ref) = refs[:8], refs[8:11]
    du_ref, sums_ref, near_ref, far_ref, all_ref = refs[11:]
    stack_rows(rows_in, all_ref)
    half_rows = near_ref.shape[0]
    sums = [None] * (in_ref.shape[0] // FF_STEP)
    for first in (half_rows, 0):
        for start in range(first, first + half_rows, 256):
            at = slice(start, start + 256)
            total = None
            for i in range(len(sums)):
                lanes = slice(i * FF_STEP, (i + 1) * FF_STEP)
                du = to_low(product(all_ref[at], back_ref[:, lanes]) * slope_ref[at, lanes])
                du_ref[at, lanes] = du
                summed = column_sum(wide(du))
                sums[i] = summed if sums[i] is None else sums[i] + summed
                part = product(du, in_ref[lanes])
                total = part if total is None else total + part
            ref = far_ref if first else near_ref
            ref[start - first : start - first + 256] = total
    for i, summed in enumerate(sums):
        sums_ref[:, i * FF_STEP : (i + 1) * FF_STEP] = summed


def feed_back(rows_in, back_t, in_t, slope):
    rows, width = rows_in[0].shape
    hidden = in_t.shape[0]
    return whole_call(
        feed_back_body,
        (*rows_in, back_t, in_t, slope),
        [
            low_shape(8 * rows, hidden),
            wide_shape(1, hidden),
            wide_shape(4 * rows, width),
            wide_shape(4 * rows, width),
            low_shape(8 * rows, width),
        ],
    )


def combine_body(near_ref, came_ref, keep_ref, *sends):
    rows = keep_ref.shape[0]
    for i, ref in enumerate((keep_ref, *sends)):
        total = near_ref[i * rows : (i + 1) * rows] + came_ref[i * rows : (i + 1) * rows]
        ref[...] = total if i == 0 else to_low(total)


def plane_sum(near, far):
    rows, width = near.shape[0] // 4, near.shape[1]
    keep, *sends = whole_call(
        combine_body,
        (near, other_core(far)),
        [wide_shape(rows, width)] + [low_shape(rows, width)] * 3,
    )
    return keep, *plane_hops(sends)


def plane_rows(values):
    near = [values, *plane_hops([values] * 3)]
    return (*near, *(other_core(part) for part in near))


def z_grad(left, right, part):
    def body(left_ref, right_ref, *outs):
        for step in (1, 2, 3, 0):
            at = z_at(step, part)
            for lane in range(0, right_ref.shape[1], 512):
                lanes = slice(lane, lane + 512)
                outs[step][:, lanes] = to_low(product_tn(left_ref[:, at], right_ref[:, lanes]))

    return whole_call(body, (left, right), [low_shape(part, right.shape[1])] * 4)


def z_sum(refs):
    total = wide(refs[0][...])
    for ref in refs[1:]:
        total = total + wide(ref[...])
    return total


def sum_in_body(*refs):
    refs[-1][...] = z_sum(refs[:-1])


def sum_back_body(*refs):
    parts, outs, total_ref = refs[:4], refs[4:8], refs[8]
    total_ref[...] = z_sum(parts)
    rows = outs[0].shape[0]
    for i, step in enumerate(NEAR):
        at = pl.ds(pl.multiple_of(chip_place(step) * rows, rows), rows)
        outs[i][...] = total_ref[at]


def pick_back_body(weight_ref, *outs):
    for i, step in enumerate(NEAR):
        for block in range(4):
            outs[i][:, block * 128 : (block + 1) * 128] = weight_ref[
                :, pl.ds(chunk_place(block, step), 128)
            ]


def lay_back_body(*refs):
    rows = refs[0].shape[0]
    for i, step in enumerate(NEAR):
        refs[4][pl.ds(pl.multiple_of(chip_place(step) * rows, rows), rows)] = refs[i][...]


def core_order(own, other):
    first = lax.axis_index("grp") == 0
    return jnp.concatenate(
        [jnp.where(first, own, other), jnp.where(first, other, own)], axis=1
    )


def core_halves(values):
    part = values.shape[1] // 2
    first = lax.axis_index("grp") == 0
    low_half, high_half = values[:, :part], values[:, part:]
    return (
        jnp.where(first, low_half, high_half),
        jnp.where(first, high_half, low_half),
    )


def halves_nt(values, own_ref, other_ref, lanes):
    own, other = core_halves(values)
    return product_nt(own, own_ref[:, lanes]) + product_nt(other, other_ref[:, lanes])


def bottle_body(
    attended_ref,
    keep_ref,
    came_x_ref,
    came_y_ref,
    came_far_ref,
    vec_ref,
    own_ref,
    other_ref,
    noise_ref,
    cot_ref,
    means_ref,
    logvars_ref,
    out_ref,
    fed_ref,
    sample_ref,
    dlat_ref,
    dfed_ref,
    dfed_low_ref,
    dmeans_ref,
    dlogvars_ref,
    sums_ref,
):
    rows, width = attended_ref.shape
    lat = noise_ref.shape[1]
    comps = means_ref.shape[0]
    parts = z_sum((keep_ref, came_x_ref, came_y_ref, came_far_ref))
    fed = attended_ref[...] + parts + vec_ref[7:8]
    fed_low = to_low(fed)
    fed_ref[...] = fed_low
    latent = halves_nt(fed_low, own_ref, other_ref, LAT_LANES) + vec_ref[LAT_ROW : LAT_ROW + 1]
    logvar = latent[:, lat:]
    noise = noise_ref[...]
    spread = jnp.exp(0.5 * logvar) * noise
    sample = latent[:, :lat] + spread
    sample_low = to_low(sample)
    sample_ref[...] = sample_low
    out_ref[...] = fed + halves_nt(sample_low, own_ref, other_ref, DEC_LANES) + vec_ref[8:9]
    cot = cot_ref[...]
    dsample = core_order(
        product(cot, own_ref[:, DEC_LANES]), product(cot, other_ref[:, DEC_LANES])
    )

    span = rows // 2
    row = lax.broadcasted_iota(jnp.int32, (rows, 1), 0)
    block = lax.axis_index("y") * 2 + lax.axis_index("x")
    place = slide_place(lax.axis_index("grp"), block, row // span, row & (span - 1), span)
    live = place.astype(jnp.float32) < vec_ref[LEN_ROW : LEN_ROW + 1, 0:1]
    share = jnp.where(live, 1.0 / lat, 0.0)
    own_term = jnp.sum(-0.5 * noise * noise - 0.5 * logvar, axis=-1, keepdims=True)
    logvars = logvars_ref[...]
    inverse = jnp.exp(-logvars)
    terms = []
    for c in range(comps):
        offset = sample - means_ref[c : c + 1]
        terms.append(
            jnp.sum(
                -0.5 * offset * offset * inverse[c : c + 1] - 0.5 * logvars[c : c + 1],
                axis=-1,
                keepdims=True,
            )
            - math.log(comps)
        )
    peak = terms[0]
    for term in terms[1:]:
        peak = jnp.maximum(peak, term)
    weights = [jnp.exp(term - peak) for term in terms]
    total = weights[0]
    for weight in weights[1:]:
        total = total + weight
    kl_cell = own_term - (peak + jnp.log(total))
    kl = jnp.sum(jnp.where(live, kl_cell, 0.0), axis=0, keepdims=True) / lat
    scale = share / total
    for c in range(comps):
        offset = sample - means_ref[c : c + 1]
        slope = offset * inverse[c : c + 1]
        part = weights[c] * scale
        pull = part * slope
        dsample = dsample + pull
        dmeans_ref[c : c + 1] = -column_sum(pull)
        dlogvars_ref[c : c + 1] = column_sum(0.5 * part - 0.5 * (pull * offset))
    dlat = jnp.concatenate([dsample, 0.5 * dsample * spread - 0.5 * share], axis=1)
    dlat_low = to_low(dlat)
    dlat_ref[...] = dlat_low
    grad_out = wide(cot)
    dfed = grad_out + core_order(
        product(dlat_low, own_ref[:, LAT_LANES]), product(dlat_low, other_ref[:, LAT_LANES])
    )
    dfed_ref[...] = dfed
    dfed_low_ref[...] = to_low(dfed)
    sums_ref[...] = jnp.concatenate(
        [
            column_sum(wide(dlat_low)),
            column_sum(dfed),
            column_sum(grad_out),
            jnp.broadcast_to(kl, (1, width)),
            jnp.zeros((4, width), jnp.float32),
        ]
    )


def bottle_call(attended, parts, vec, weights, noise, cot, means, logvars):
    rows, width = attended.shape
    lat = noise.shape[1]
    return whole_call(
        bottle_body,
        (attended, *parts, vec, *weights, noise, cot, means, logvars),
        [
            wide_shape(rows, width),
            low_shape(rows, width),
            low_shape(rows, lat),
            low_shape(rows, width),
            wide_shape(rows, width),
            low_shape(rows, width),
            wide_shape(*means.shape),
            wide_shape(*means.shape),
            wide_shape(8, width),
        ],
    )


def project_back_body(
    keep_ref,
    came_x_ref,
    came_y_ref,
    came_far_ref,
    attended_ref,
    dfed_ref,
    vec_ref,
    own_ref,
    other_ref,
    datt_ref,
    datt_low_ref,
    dmixed_ref,
    sums_ref,
):
    grad = z_sum((keep_ref, came_x_ref, came_y_ref, came_far_ref))
    unit, scale = row_stats(attended_ref[...])
    datt = dfed_ref[...] + norm_back(grad, unit, scale, vec_ref[5:6])
    datt_ref[...] = datt
    datt_low = to_low(datt)
    datt_low_ref[...] = datt_low
    core = lax.axis_index("grp")
    for ref, place in ((own_ref, core), (other_ref, 1 - core)):
        dmixed = to_low(product(datt_low, ref[:, OUT_LANES]))
        for i in range(4):
            dmixed_ref[place * 4 + i] = dmixed[:, i * PAIR : (i + 1) * PAIR]
    sums_ref[...] = jnp.concatenate(
        [
            column_sum(grad * unit),
            column_sum(grad),
            column_sum(datt),
            jnp.zeros((5, datt.shape[1]), jnp.float32),
        ]
    )


def project_back(parts, attended, dfed, vec, own, other):
    rows, width = attended.shape
    return whole_call(
        project_back_body,
        (*parts, attended, dfed, vec, own, other),
        [
            wide_shape(rows, width),
            low_shape(rows, width),
            low_shape(8, rows, PAIR),
            wide_shape(8, width),
        ],
    )


def whole_grads_body(
    datt_ref,
    datt_other_ref,
    mixed_ref,
    mixed_other_ref,
    dlat_ref,
    dlat_other_ref,
    fed_ref,
    fed_other_ref,
    cot_ref,
    cot_other_ref,
    sample_ref,
    sample_other_ref,
    out_ref,
):
    core = lax.axis_index("grp")
    datt = jnp.concatenate([datt_ref[...], datt_other_ref[...]])
    for i in range(4):
        mixed = jnp.concatenate([mixed_ref[core * 4 + i], mixed_other_ref[core * 4 + i]])
        out_ref[:, i * PAIR : (i + 1) * PAIR] = to_low(product_tn(datt, mixed))
    for lanes, left, left_other, right, right_other in (
        (LAT_LANES, dlat_ref, dlat_other_ref, fed_ref, fed_other_ref),
        (DEC_LANES, cot_ref, cot_other_ref, sample_ref, sample_other_ref),
    ):
        grads = jnp.concatenate([left[...], left_other[...]])
        values = jnp.concatenate([core_halves(right[...])[0], core_halves(right_other[...])[0]])
        out_ref[:, lanes] = to_low(product_tn(grads, values))


def whole_grads(pairs):
    operands = []
    for values in pairs:
        operands += [values, other_core(values)]
    width = pairs[0].shape[1]
    return whole_call(whole_grads_body, operands, [low_shape(width, DEC_LANES.stop)])[0]


def back_grad_body(*refs):
    out_ref = refs[8]
    for i, ref in enumerate(refs[:8]):
        for block in range(4):
            place = chunk_place(block, NEAR[i % 4], i // 4)
            out_ref[:, pl.ds(place, 128)] = ref[:, block * 128 : (block + 1) * 128]


def plane_parts_body(own_ref, came_ref, keep_ref, *sends):
    rows = keep_ref.shape[0]
    for i, step in enumerate(NEAR):
        at = pl.ds(pl.multiple_of(chip_place(step) * rows, rows), rows)
        total = own_ref[at] + came_ref[at]
        if i == 0:
            keep_ref[...] = total
        else:
            sends[i - 1][...] = to_low(total)


def plane_parts(own, came):
    rows, width = own.shape[0] // 4, own.shape[1]
    return whole_call(
        plane_parts_body, (own, came), [wide_shape(rows, width)] + [low_shape(rows, width)] * 3
    )


def cells_back_body(
    keep_ref,
    came_x_ref,
    came_y_ref,
    came_far_ref,
    hidden_ref,
    datt_ref,
    vec_ref,
    bottle_sums_ref,
    project_sums_ref,
    head_sums_ref,
    ff_sums_ref,
    dmeans_ref,
    dlogvars_ref,
    grad_ref,
    packed_ref,
    inner_ref,
    rows_ref,
):
    grad = z_sum((keep_ref, came_x_ref, came_y_ref, came_far_ref))
    unit, scale = row_stats(wide(hidden_ref[...]))
    grad_ref[...] = datt_ref[...] + norm_back(grad, unit, scale, vec_ref[0:1])
    width = grad.shape[1]
    count = packed_ref.shape[0]
    inner_ref[...] = jnp.zeros_like(inner_ref)
    for block in range(4):
        inner_ref[:, pl.ds(chunk_place(block), 128)] = ff_sums_ref[
            :, block * 128 : block * 128 + 128
        ]
    inner_ref[:, inner_ref.shape[1] - width :] = bottle_sums_ref[0:1]
    rows_ref[...] = jnp.zeros_like(rows_ref)
    rows_ref[0:1] = column_sum(grad * unit)
    rows_ref[1:2] = column_sum(grad)
    rows_ref[2:3, pl.ds(own_pair(), PAIR)] = head_sums_ref[:, :PAIR]
    rows_ref[3:4, pl.ds(own_pair(), PAIR)] = head_sums_ref[:, 2 * PAIR :]
    rows_ref[4:5] = project_sums_ref[2:3]
    rows_ref[5:7] = project_sums_ref[0:2]
    rows_ref[7:9] = bottle_sums_ref[1:3]
    part = width // count
    pieces = inner_ref.shape[1] // width
    for i in range(pieces):
        rows_ref[9 + i : 10 + i] = jnp.concatenate(
            [
                inner_ref[:, (b * pieces + i) * part : (b * pieces + i + 1) * part]
                for b in range(count)
            ],
            axis=1,
        )
    rows_ref[14:15] = bottle_sums_ref[3:4]
    lat_part = dmeans_ref.shape[1] // count
    for b in range(count):
        packed_ref[b] = jnp.concatenate(
            [
                rows_ref[:, b * part : (b + 1) * part],
                dmeans_ref[:, b * lat_part : (b + 1) * lat_part],
                dlogvars_ref[:, b * lat_part : (b + 1) * lat_part],
            ],
            axis=1,
        )


def cells_back(operands, inner):
    rows, width = operands[0].shape
    return whole_call(
        cells_back_body,
        operands,
        [wide_shape(rows, width), wide_shape(16, SMALL, 128)],
        [pltpu.VMEM((1, inner), jnp.float32), pltpu.VMEM((SMALL, width), jnp.float32)],
    )


def plane_exchange(blocks):
    return lax.all_to_all(blocks, PLANE, split_axis=0, concat_axis=0, tiled=True)


def fast_device(
    cell_input,
    lengths,
    noise_draw,
    cotangent,
    w_qkv,
    w_out,
    w_ffn_in,
    w_ffn_out,
    w_latent,
    w_decode,
    vectors,
    inner_bias,
    prior_means,
    prior_logvars,
):
    slots, span, width = cell_input.shape[1:]
    rows = slots * span
    lat = noise_draw.shape[-1]
    comps = prior_means.shape[1]
    ff = w_ffn_out.shape[1]
    inner = 16 * inner_bias.shape[1]
    core, zi, yi, xi = (lax.axis_index(name) for name in EVERY)
    pair = (core * 2 + yi) * 2 + xi
    odd = zi % 2

    small_rows = pack_small(
        vectors[0], inner_bias, prior_means[0], prior_logvars[0], lengths[0]
    )
    first = to_slides([jnp.concatenate([cell_input[0, s], small_rows]) for s in range(slots)])
    plane_own = jnp.stack([first, *plane_hops([first] * 3)])
    cells, small = place_cells(plane_own, other_core(plane_own))

    qkv_t = w_qkv[0].T.reshape(3, HEAD_DIM, width)
    came = jnp.stack(
        [
            jnp.stack([lax.ppermute(qkv_t[i], EVERY, head_routes(i, k)) for i in range(3)])
            for k in range(2)
        ]
    )
    roles = jnp.asarray(head_roles()).reshape(8, 2, 3)[pair]
    role_of = [jnp.where(odd == k, roles[0], roles[1]) for k in range(2)]
    by_head = [
        jnp.stack([lax.dynamic_index_in_dim(came[k], role_of[k][j], 0, False) for j in range(3)])
        for k in range(2)
    ]
    head_w = jnp.stack(
        [jnp.where(odd == 0, by_head[0], by_head[1]), jnp.where(odd == 0, by_head[1], by_head[0])],
        axis=1,
    ).reshape(3 * PAIR, width)

    shard_o = jnp.concatenate(
        [half_of(w[0], 0, "grp", True).T for w in (w_out, w_latent, w_decode)], axis=1
    )
    whole = lax.all_gather(shard_o, CHIPS, axis=0, tiled=True)

    in_own = half_of(w_ffn_in[0], 1, "grp", True).T
    in_parts = (in_own, *z_hops([after(in_own, first)] * 3))

    back_cols = whole_call(
        pick_back_body, (w_ffn_out[0].T,), [low_shape(width // 16, ff // 8)] * 4
    )
    back_cols = (back_cols[0], *plane_hops(after(back_cols[1:], first)))
    (back_own,) = whole_call(lay_back_body, back_cols, [low_shape(width // 4, ff // 8)])
    back_parts = (back_own, *z_hops([after(back_own, in_parts[1:])] * 3))

    vec, means, logvars = unpack_small(small, lat, inner)
    normed, qkv, mixed_pair, lse, bias = attend(cells.reshape(8 * rows, width), vec, head_w)
    mixed = plane_exchange(mixed_pair.reshape(8, rows, PAIR))
    whole = after(whole, mixed_pair)
    wholes = (whole, other_core(whole))

    hidden = first[:, :span].reshape(rows, width)
    noise_high = to_low(noise_draw[0, 0])
    noise_rest = to_low(noise_draw[0, 0] - wide(noise_high))
    extra = jnp.concatenate(
        [cotangent[0], jnp.concatenate([noise_high, noise_rest], axis=2)], axis=1
    )
    extra = to_slides(after(extra, mixed_pair))
    cot = extra[:, :span].reshape(rows, width)
    noise = extra[:, span:].reshape(rows, width)
    noise = wide(noise[:, :lat]) + wide(noise[:, lat:])

    attended, normed_two = project(mixed, *wholes, hidden, vec)
    rows_two = plane_rows(normed_two)
    act, slope, fed_near, fed_far, in_t, back_t, all_two = feed(
        rows_two, in_parts, back_parts, vec
    )
    output, fed_low, sample_low, dlat_low, dfed, dfed_low, dmeans, dlogvars, bottle_sums = (
        bottle_call(
            attended, plane_sum(fed_near, fed_far), vec, wholes, noise, cot, means, logvars
        )
    )
    layer_out = from_slides(output.reshape(slots, span, width))

    rows_fed = plane_rows(dfed_low)
    du, ff_sums, norm_near, norm_far, all_fed = feed_back(rows_fed, back_t, in_t, slope)
    datt, datt_low, dmixed, project_sums = project_back(
        plane_sum(norm_near, norm_far), attended, dfed, vec, *wholes
    )
    dmixed = plane_exchange(dmixed)

    back_grads = z_grad(all_fed, after(act, du), width // 4)
    back_came = z_hops(back_grads[1:])
    in_grads = z_grad(du, all_two, ff // 32)
    in_came = z_hops(after(in_grads[1:], back_grads))
    sum_whole = lax.psum_scatter(
        whole_grads((datt_low, mixed, dlat_low, fed_low, cot, sample_low)),
        CHIPS,
        scatter_dimension=0,
        tiled=True,
    )

    head_grad, dn_near, dn_far, head_sums = attend_back(
        qkv, bias, lse, dmixed.reshape(8 * rows, PAIR), normed, head_w
    )
    part = width // 16
    back_sums = whole_call(
        sum_back_body,
        (back_grads[0], *after(back_came, dn_far)),
        [wide_shape(part, ff // 8)] * 4,
        [pltpu.VMEM((width // 4, ff // 8), jnp.float32)],
    )
    back_sums = (back_sums[0], *plane_hops(back_sums[1:]))
    back_sums = (*back_sums, *(other_core(total) for total in back_sums))
    (sum_in,) = whole_call(
        sum_in_body,
        (in_grads[0], *after(in_came, dn_far)),
        [wide_shape(ff // 32, width)],
    )
    dn_keep, *dn_sends = plane_parts(dn_near, other_core(dn_far))
    grad_rows, packed = cells_back(
        (
            dn_keep,
            *plane_hops(dn_sends),
            hidden,
            datt,
            vec,
            bottle_sums,
            project_sums,
            head_sums,
            ff_sums,
            dmeans,
            dlogvars,
        ),
        inner,
    )
    grad_cells = from_slides(grad_rows.reshape(slots, span, width))

    head_grad = head_grad.reshape(3, 2, HEAD_DIM, width)
    home = jnp.zeros((3 * HEAD_DIM, width), jnp.float32)
    for k in range(2):
        of_head = jnp.where(odd == k, head_grad[:, 0], head_grad[:, 1])
        role_at = jnp.argsort(role_of[k])
        home = home + jnp.concatenate(
            [
                wide(
                    lax.ppermute(
                        lax.dynamic_index_in_dim(of_head, role_at[i], 0, False),
                        EVERY,
                        [(there, here) for here, there in head_routes(i, k)],
                    )
                )
                for i in range(3)
            ]
        )
    grad_qkv = (home + other_core(home)).T

    small_sums = jnp.sum(
        lax.all_to_all(packed, CHIPS, split_axis=0, concat_axis=0, tiled=True), axis=0
    )
    small_sums = small_sums + other_core(small_sums)
    vec_out = small_sums[:9, :part]
    inner_out = small_sums[9 : 9 + inner // width, :part].reshape(1, -1)
    means_out = small_sums[:, part : part + lat // 16]
    logvars_out = small_sums[:, part + lat // 16 :]
    kl_mean = small_sums[14, 0] / (32 * rows)

    sum_whole = wide(sum_whole)
    whole_other = other_core(sum_whole)
    grad_out_w, grad_lat_w, grad_dec_w = (
        ordered(sum_whole[:, lanes].T, whole_other[:, lanes].T, "grp", 0)
        for lanes in (OUT_LANES, LAT_LANES, DEC_LANES)
    )
    grad_in_w = ordered(sum_in.T, other_core(sum_in).T, "grp", 1)
    grad_back_w = whole_call(back_grad_body, back_sums, [wide_shape(part, ff)])[0].T
    return (
        layer_out.reshape(1, slots, span, width),
        grad_cells.reshape(1, slots, span, width),
        kl_mean,
        grad_qkv[None],
        grad_out_w[None],
        grad_in_w[None],
        grad_back_w[None],
        grad_lat_w[None],
        grad_dec_w[None],
        vec_out[None],
        inner_out,
        means_out[None],
        logvars_out[None],
    )


def solution(mesh):
    chips = mesh.shape["blk"]
    if (mesh.shape["grp"], chips) == (2, HEADS):
        mesh = Mesh(mesh.devices.reshape(2, chips // 4, 2, 2), EVERY)
        blk, run = CHIPS, fast_device
    else:
        blk, run = "blk", per_device
    cells = P("grp", None, blk, None)
    columns = P(None, None, blk)
    return jax.shard_map(
        run,
        mesh=mesh,
        in_specs=(cells, P("grp", None), P(None, "grp", None, blk, None), cells)
        + (columns,) * 7
        + (P(None, blk), columns, columns),
        out_specs=(cells, cells, P()) + (columns,) * 7 + (P(None, blk), columns, columns),
        check_vma=False,
    )
```

```python
import functools
import math

import jax
import jax.numpy as jnp
import numpy as np
from jax import lax
from jax.experimental import pallas as pl
from jax.experimental.pallas import tpu as pltpu
from jax.sharding import Mesh
from jax.sharding import PartitionSpec as P

HEADS = 16
LAYERS = 1
HEAD_DIM = 64


EPS_NORM = 1e-05
MASKED = -1e30


def to_low(values):
    return values.astype(jnp.bfloat16)


def product(left, right):
    return jnp.dot(left, right, preferred_element_type=jnp.float32)


def product_tn(left, right):
    return lax.dot_general(
        left, right, (((0,), (0,)), ((), ())), preferred_element_type=jnp.float32
    )


def product_nt(left, right):
    return lax.dot_general(
        left, right, (((1,), (1,)), ((), ())), preferred_element_type=jnp.float32
    )


def layer_norm(values, norm_gain, norm_shift):
    centre = values - jnp.mean(values, axis=-1, keepdims=True)
    spread = jnp.mean(centre * centre, axis=-1, keepdims=True)
    return centre * lax.rsqrt(spread + EPS_NORM) * norm_gain + norm_shift


def mixture_kl(sample, noise_rows, logvar, mean_rows, logvars):
    own_term = jnp.sum(-0.5 * noise_rows * noise_rows - 0.5 * logvar, axis=-1)
    offset = sample[:, None, :] - mean_rows[None, :, :]
    component = jnp.sum(
        -0.5 * offset * offset * jnp.exp(-logvars)[None] - 0.5 * logvars[None], axis=-1
    ) - math.log(mean_rows.shape[0])
    row_peak = jnp.max(component, axis=-1, keepdims=True)
    mixture = row_peak[:, 0] + jnp.log(jnp.sum(jnp.exp(component - row_peak), axis=-1))
    return own_term - mixture


def bottleneck(latent, noise_rows, live_rows, mean_rows, logvars):
    lat_width = noise_rows.shape[-1]
    mean_part = latent[:, :lat_width]
    logvar = latent[:, lat_width:]
    sample = mean_part + jnp.exp(0.5 * logvar) * noise_rows
    per_cell = mixture_kl(sample, noise_rows, logvar, mean_rows, logvars)
    return (sample, jnp.sum(jnp.where(live_rows, per_cell, 0.0)) / lat_width)


def slot_scores(query_slots, keys_all, slide_len, score_scale):
    slot_count, query_rows, model_width = query_slots.shape
    heads_q = query_slots.reshape(slot_count, query_rows, HEADS, HEAD_DIM)
    heads_k = keys_all.reshape(slot_count, keys_all.shape[1], HEADS, HEAD_DIM)
    raw_scores = (
        jnp.einsum("sqhd,skhd->shqk", heads_q, heads_k, preferred_element_type=jnp.float32)
        * score_scale
    )
    live_keys = jnp.arange(keys_all.shape[1])[None, :] < slide_len[:, None]
    return jnp.where(live_keys[:, None, None, :], raw_scores, MASKED)


def widen(gathered):
    qkv_w, out_w, in_w, back_w, latent_w, decode_w, vec_rows, inner_rows, mean_rows, logvars = (
        gathered
    )
    return (
        qkv_w,
        out_w,
        in_w,
        back_w,
        latent_w,
        decode_w,
        vec_rows.astype(jnp.float32),
        inner_rows.astype(jnp.float32),
        mean_rows.astype(jnp.float32),
        logvars.astype(jnp.float32),
    )


def gather_weights(layer_parts):
    (
        part_qkv,
        part_out,
        part_in,
        part_back,
        part_latent,
        part_decode,
        part_vectors,
        part_inner,
        part_means,
        part_logvars,
    ) = layer_parts
    return widen(
        (
            lax.all_gather(part_qkv, "blk", axis=1, tiled=True),
            lax.all_gather(part_out, "blk", axis=1, tiled=True),
            lax.all_gather(part_in, "blk", axis=1, tiled=True),
            lax.all_gather(part_back, "blk", axis=1, tiled=True),
            lax.all_gather(part_latent, "blk", axis=1, tiled=True),
            lax.all_gather(part_decode, "blk", axis=1, tiled=True),
            lax.all_gather(part_vectors, "blk", axis=1, tiled=True),
            lax.all_gather(part_inner, "blk", axis=0, tiled=True),
            lax.all_gather(part_means, "blk", axis=1, tiled=True),
            lax.all_gather(part_logvars, "blk", axis=1, tiled=True),
        )
    )


def reduce_grads(grads):
    (
        grad_qkv_w,
        grad_out_w,
        grad_in_w,
        grad_back_w,
        grad_latent_w,
        grad_decode_w,
        grad_vec,
        grad_inner,
        grad_mean_rows,
        grad_logvars,
    ) = grads
    (
        shard_qkv,
        shard_out,
        shard_in,
        shard_back,
        shard_latent,
        shard_decode,
        shard_vec,
        shard_inner,
        shard_means,
        shard_logvars,
    ) = (
        lax.psum_scatter(grad_qkv_w, "blk", scatter_dimension=1, tiled=True),
        lax.psum_scatter(grad_out_w, "blk", scatter_dimension=1, tiled=True),
        lax.psum_scatter(grad_in_w, "blk", scatter_dimension=1, tiled=True),
        lax.psum_scatter(grad_back_w, "blk", scatter_dimension=1, tiled=True),
        lax.psum_scatter(grad_latent_w, "blk", scatter_dimension=1, tiled=True),
        lax.psum_scatter(grad_decode_w, "blk", scatter_dimension=1, tiled=True),
        lax.psum_scatter(grad_vec, "blk", scatter_dimension=1, tiled=True),
        lax.psum_scatter(grad_inner, "blk", scatter_dimension=0, tiled=True),
        lax.psum_scatter(grad_mean_rows, "blk", scatter_dimension=1, tiled=True),
        lax.psum_scatter(grad_logvars, "blk", scatter_dimension=1, tiled=True),
    )
    return lax.psum(
        (
            shard_qkv,
            shard_out,
            shard_in,
            shard_back,
            shard_latent,
            shard_decode,
            shard_vec,
            shard_inner,
            shard_means,
            shard_logvars,
        ),
        "grp",
    )


def layer_forward(hidden, full_weights, noise_rows, live_rows, slide_len, score_scale):
    qkv_w, out_w, in_w, back_w, latent_w, decode_w, vec_rows, inner_rows, mean_rows, logvars = (
        full_weights
    )
    model_width = hidden.shape[1]
    slot_count = slide_len.shape[0]
    slot_span = hidden.shape[0] // slot_count
    ff_width = in_w.shape[1]
    normed = to_low(layer_norm(hidden, vec_rows[0], vec_rows[1]))
    qkv_all = product(normed, qkv_w)
    query_low = to_low(qkv_all[:, :model_width] + vec_rows[2])
    keys_own = to_low(qkv_all[:, model_width : 2 * model_width])
    values_own = to_low(qkv_all[:, 2 * model_width :] + vec_rows[3])
    keys_all, values_all = (
        lax.all_gather(
            keys_own.reshape(slot_count, slot_span, model_width), "blk", axis=1, tiled=True
        ),
        lax.all_gather(
            values_own.reshape(slot_count, slot_span, model_width), "blk", axis=1, tiled=True
        ),
    )
    scores = slot_scores(
        query_low.reshape(slot_count, slot_span, model_width), keys_all, slide_len, score_scale
    )
    row_peak = jnp.max(scores, axis=-1, keepdims=True)
    weights = jnp.exp(scores - row_peak)
    totals = jnp.sum(weights, axis=-1, keepdims=True)
    probs_low = to_low(weights / totals)
    log_total = row_peak + jnp.log(totals)
    heads_v = values_all.reshape(slot_count, values_all.shape[1], HEADS, HEAD_DIM)
    mixed_f = jnp.einsum("shqk,skhd->sqhd", probs_low, heads_v, preferred_element_type=jnp.float32)
    mixed_low = to_low(mixed_f.reshape(slot_count * slot_span, model_width))
    attended = hidden + product(mixed_low, out_w) + vec_rows[4]
    normed_two = to_low(layer_norm(attended, vec_rows[5], vec_rows[6]))
    inner_act = product(normed_two, in_w) + inner_rows[:ff_width]
    activated = to_low(jax.nn.gelu(inner_act))
    fed_rows = attended + product(activated, back_w) + vec_rows[7]
    fed_low = to_low(fed_rows)
    latent = product(fed_low, latent_w) + inner_rows[ff_width:]
    sample, kl_part = bottleneck(latent, noise_rows, live_rows, mean_rows, logvars)
    sample_low = to_low(sample)
    output = fed_rows + product(sample_low, decode_w) + vec_rows[8]
    saved_state = (
        hidden,
        normed,
        query_low,
        keys_own,
        values_own,
        log_total,
        mixed_low,
        attended,
        normed_two,
        inner_act,
        activated,
        fed_low,
        latent,
        sample_low,
    )
    return (output, kl_part, saved_state)


def layer_backward(
    grad_out, full_weights, saved_state, noise_rows, live_rows, slide_len, score_scale
):
    qkv_w, out_w, in_w, back_w, latent_w, decode_w, vec_rows, inner_rows, mean_rows, logvars = (
        full_weights
    )
    (
        hidden,
        normed,
        query_low,
        keys_own,
        values_own,
        log_total,
        mixed_low,
        attended,
        normed_two,
        inner_act,
        activated,
        fed_low,
        latent,
        sample_low,
    ) = saved_state
    model_width = hidden.shape[1]
    row_total = hidden.shape[0]
    slot_count = slide_len.shape[0]
    slot_span = row_total // slot_count
    grad_dec_low = to_low(grad_out)
    grad_decode_w = product_tn(sample_low, grad_dec_low)
    grad_sample = product_nt(grad_dec_low, decode_w)

    def bottle(latent_in, means_in, logvars_in):
        return bottleneck(latent_in, noise_rows, live_rows, means_in, logvars_in)

    ignored, bottle_pull = jax.vjp(bottle, latent, mean_rows, logvars)
    grad_latent_f, grad_mean_rows, grad_logvars = bottle_pull(
        (grad_sample, jnp.ones((), jnp.float32))
    )
    grad_latent_low = to_low(grad_latent_f)
    grad_latent_w = product_tn(fed_low, grad_latent_low)
    grad_fed = grad_out + product_nt(grad_latent_low, latent_w)
    grad_fed_low = to_low(grad_fed)
    grad_back_w = product_tn(activated, grad_fed_low)
    grad_act = product_nt(grad_fed_low, back_w)
    ignored_two, gelu_pull = jax.vjp(jax.nn.gelu, inner_act)
    grad_inner_low = to_low(gelu_pull(grad_act)[0])
    grad_in_w = product_tn(normed_two, grad_inner_low)
    grad_normed_two = product_nt(grad_inner_low, in_w)
    ignored_three, second_pull = jax.vjp(layer_norm, attended, vec_rows[5], vec_rows[6])
    grad_att_norm, grad_gain_two, grad_shift_two = second_pull(grad_normed_two)
    grad_attended = grad_fed + grad_att_norm
    grad_proj_low = to_low(grad_attended)
    grad_out_w = product_tn(mixed_low, grad_proj_low)
    grad_mixed_low = to_low(product_nt(grad_proj_low, out_w))
    keys_all, values_all = (
        lax.all_gather(
            keys_own.reshape(slot_count, slot_span, model_width), "blk", axis=1, tiled=True
        ),
        lax.all_gather(
            values_own.reshape(slot_count, slot_span, model_width), "blk", axis=1, tiled=True
        ),
    )
    grad_mixed_heads = grad_mixed_low.reshape(slot_count, slot_span, HEADS, HEAD_DIM)
    heads_k = keys_all.reshape(slot_count, keys_all.shape[1], HEADS, HEAD_DIM)
    heads_v = values_all.reshape(slot_count, values_all.shape[1], HEADS, HEAD_DIM)
    scores = slot_scores(
        query_low.reshape(slot_count, slot_span, model_width), keys_all, slide_len, score_scale
    )
    probs_f = jnp.exp(scores - log_total)
    grad_probs = jnp.einsum(
        "sqhd,skhd->shqk", grad_mixed_heads, heads_v, preferred_element_type=jnp.float32
    )
    centre = jnp.sum(grad_probs * probs_f, axis=-1, keepdims=True)
    grad_scores_low = to_low(probs_f * (grad_probs - centre))
    grad_query = (
        jnp.einsum("shqk,skhd->sqhd", grad_scores_low, heads_k, preferred_element_type=jnp.float32)
        * score_scale
    )
    grad_query_low = to_low(grad_query.reshape(row_total, model_width))
    rows_all, mixed_all = (
        lax.all_gather(
            query_low.reshape(slot_count, slot_span, model_width), "blk", axis=1, tiled=True
        ),
        lax.all_gather(
            grad_mixed_low.reshape(slot_count, slot_span, model_width), "blk", axis=1, tiled=True
        ),
    )
    total_all, centre_all = (
        lax.all_gather(log_total, "blk", axis=2, tiled=True),
        lax.all_gather(centre, "blk", axis=2, tiled=True),
    )
    query_all = rows_all.reshape(slot_count, rows_all.shape[1], HEADS, HEAD_DIM)
    dmixed_all = mixed_all.reshape(slot_count, mixed_all.shape[1], HEADS, HEAD_DIM)
    own_keys = keys_own.reshape(slot_count, slot_span, HEADS, HEAD_DIM)
    own_values = values_own.reshape(slot_count, slot_span, HEADS, HEAD_DIM)
    own_raw = (
        jnp.einsum("sqhd,skhd->shqk", query_all, own_keys, preferred_element_type=jnp.float32)
        * score_scale
    )
    key_places = lax.axis_index("blk") * slot_span + jnp.arange(slot_span)
    live_own = key_places[None, :] < slide_len[:, None]
    own_scores = jnp.where(live_own[:, None, None, :], own_raw, MASKED)
    own_probs = jnp.exp(own_scores - total_all)
    own_dprobs = jnp.einsum(
        "sqhd,skhd->shqk", dmixed_all, own_values, preferred_element_type=jnp.float32
    )
    own_dscores = to_low(own_probs * (own_dprobs - centre_all))
    grad_keys = (
        jnp.einsum("shqk,sqhd->skhd", own_dscores, query_all, preferred_element_type=jnp.float32)
        * score_scale
    )
    grad_values = jnp.einsum(
        "shqk,sqhd->skhd", to_low(own_probs), dmixed_all, preferred_element_type=jnp.float32
    )
    grad_keys_low = to_low(grad_keys.reshape(row_total, model_width))
    grad_values_low = to_low(grad_values.reshape(row_total, model_width))
    grad_qkv_low = jnp.concatenate([grad_query_low, grad_keys_low, grad_values_low], axis=1)
    grad_qkv_w = product_tn(normed, grad_qkv_low)
    grad_normed = product_nt(grad_qkv_low, qkv_w)
    ignored_four, first_pull = jax.vjp(layer_norm, hidden, vec_rows[0], vec_rows[1])
    grad_hid_norm, grad_gain_one, grad_shift_one = first_pull(grad_normed)
    grad_hidden = grad_attended + grad_hid_norm
    grad_vec = jnp.stack(
        [
            grad_gain_one,
            grad_shift_one,
            jnp.sum(grad_query_low.astype(jnp.float32), axis=0),
            jnp.sum(grad_values_low.astype(jnp.float32), axis=0),
            jnp.sum(grad_attended, axis=0),
            grad_gain_two,
            grad_shift_two,
            jnp.sum(grad_fed, axis=0),
            jnp.sum(grad_out, axis=0),
        ]
    )
    grad_inner = jnp.concatenate(
        [
            jnp.sum(grad_inner_low.astype(jnp.float32), axis=0),
            jnp.sum(grad_latent_low.astype(jnp.float32), axis=0),
        ]
    )
    return (
        grad_hidden,
        (
            grad_qkv_w,
            grad_out_w,
            grad_in_w,
            grad_back_w,
            grad_latent_w,
            grad_decode_w,
            grad_vec,
            grad_inner,
            grad_mean_rows,
            grad_logvars,
        ),
    )


def per_device(
    cell_input,
    lengths,
    noise_draw,
    cotangent,
    w_qkv,
    w_out,
    w_ffn_in,
    w_ffn_out,
    w_latent,
    w_decode,
    vectors,
    inner_bias,
    prior_means,
    prior_logvars,
):
    slot_count = cell_input.shape[1]
    slot_span = cell_input.shape[2]
    model_width = cell_input.shape[3]
    row_total = slot_count * slot_span
    lat_width = noise_draw.shape[-1]
    cycle_size = lax.axis_size("blk")
    score_scale = 1.0 / math.sqrt(HEAD_DIM)
    slide_len = lengths[0]
    positions = lax.axis_index("blk") * slot_span + jnp.arange(slot_span)
    live_rows = (positions[None, :] < slide_len[:, None]).reshape(row_total)
    hidden = cell_input[0].reshape(row_total, model_width).astype(jnp.float32)
    stacks = (
        w_qkv,
        w_out,
        w_ffn_in,
        w_ffn_out,
        w_latent,
        w_decode,
        vectors,
        inner_bias,
        prior_means,
        prior_logvars,
    )
    layer_idx = 0
    full_weights = gather_weights([stacked[layer_idx] for stacked in stacks])
    kept_weights = [full_weights]
    hidden, kl_part, saved_state = layer_forward(
        hidden,
        full_weights,
        noise_draw[layer_idx, 0].reshape(row_total, lat_width),
        live_rows,
        slide_len,
        score_scale,
    )
    saved_layers = [saved_state]
    layer_out = hidden.reshape(1, slot_count, slot_span, model_width)
    kl_total = lax.psum(kl_part, ("grp", "blk"))
    kl_mean = kl_total / (lax.axis_size("grp") * cycle_size * row_total)
    grad_rows = cotangent[0].reshape(row_total, model_width).astype(jnp.float32)
    reduced = [None] * LAYERS
    for layer_idx in reversed(range(LAYERS)):
        full_weights = kept_weights[layer_idx]
        grad_rows, grads = layer_backward(
            grad_rows,
            full_weights,
            saved_layers[layer_idx],
            noise_draw[layer_idx, 0].reshape(row_total, lat_width),
            live_rows,
            slide_len,
            score_scale,
        )
        reduced[layer_idx] = reduce_grads(grads)
    grad_cells = grad_rows.reshape(1, slot_count, slot_span, model_width)
    stacked_grads = [jnp.stack([reduced[0][member]]) for member in range(10)]
    return (
        layer_out,
        grad_cells,
        kl_mean,
        stacked_grads[0],
        stacked_grads[1],
        stacked_grads[2],
        stacked_grads[3],
        stacked_grads[4],
        stacked_grads[5],
        stacked_grads[6],
        stacked_grads[7],
        stacked_grads[8],
        stacked_grads[9],
    )


EVERY = ("grp", "z", "y", "x")
CHIPS = ("z", "y", "x")
PLANE = ("grp", "y", "x")
PAIR = 2 * HEAD_DIM
SMALL = 16
VMEM_LIMIT = 20 * 1024 * 1024


def hop(values, axis, step=1):
    size = lax.axis_size(axis)
    return lax.ppermute(values, axis, [(i, i ^ step) for i in range(size)])


def other_core(values):
    return hop(values, "grp")


def after(values, done):
    return lax.optimization_barrier((values, done))[0]


def ordered(own, other, axis_name, axis):
    first = lax.axis_index(axis_name) == 0
    return jnp.concatenate(
        [jnp.where(first, own, other), jnp.where(first, other, own)], axis=axis
    )


def half_of(values, axis, axis_name, mine):
    part = values.shape[axis] // 2
    place = lax.axis_index(axis_name)
    place = place if mine else 1 - place
    return lax.dynamic_slice_in_dim(values, place * part, part, axis)


def flip(place, step):
    high = (place // 2 + step // 2) % 2
    low_bit = (place % 2 + step % 2) % 2
    return high * 2 + low_bit


def slide_routes(k):
    return [
        (g * 4 + z, (z // 2) * 4 + 2 * g + ((z % 2) ^ k)) for g in range(2) for z in range(4)
    ]


def pick_slot(slots, k):
    odd = (lax.axis_index("z") + k) % 2 == 1
    return jnp.where(odd, slots[1], slots[0])


def to_slides(slots):
    return jnp.stack(
        [lax.ppermute(pick_slot(slots, k), ("grp", "z"), slide_routes(k)) for k in range(2)]
    )


def from_slides(blocks):
    came = [
        lax.ppermute(
            blocks[k], ("grp", "z"), [(there, here) for here, there in slide_routes(k)]
        )
        for k in range(2)
    ]
    return jnp.stack([pick_slot(came, 0), pick_slot(came, 1)])


def head_routes(single, k):
    routes = []
    for core in range(2):
        for chip in range(16):
            odd = chip % 2
            block = 3 * chip + (2 - 2 * odd if single else odd)
            pair = (block % 16) // 2
            plane = 2 * core + (odd ^ k)
            target = (pair // 4) * 16 + plane * 4 + pair % 4
            routes.append((core * 16 + chip, target))
    return routes


ARRIVALS = [(single, k) for k in range(2) for single in (False, True)]


def low_shape(*shape):
    return jax.ShapeDtypeStruct(shape, jnp.bfloat16)


def wide(values):
    return values.astype(jnp.float32)


def z_hops(values):
    return [hop(values[step - 1], "z", step) for step in (1, 2, 3)]


def plane_hops(values):
    return [
        hop(values[0], "x"),
        hop(values[1], "y"),
        lax.ppermute(values[2], ("y", "x"), [(i, i ^ 3) for i in range(4)]),
    ]


NEAR = ((0, 0), (0, 1), (1, 0), (1, 1))


def z_at(step, part):
    return pl.ds(pl.multiple_of(flip(lax.axis_index("z"), step) * part, part), part)


def chip_place(step):
    return flip(lax.axis_index("y"), step[0]) * 2 + flip(lax.axis_index("x"), step[1])


def wide_shape(*shape):
    return jax.ShapeDtypeStruct(shape, jnp.float32)


def whole_call(body, operands, out_shapes, scratch=(), left_out=()):
    vmem = pl.BlockSpec(memory_space=pltpu.VMEM)
    specs = [
        pl.BlockSpec(memory_space=pltpu.HBM) if i in left_out else vmem
        for i in range(len(operands))
    ]
    return pl.pallas_call(
        body,
        out_shape=out_shapes,
        in_specs=specs,
        out_specs=[vmem] * len(out_shapes),
        scratch_shapes=list(scratch),
        compiler_params=pltpu.CompilerParams(vmem_limit_bytes=VMEM_LIMIT),
    )(*operands)


def enter_body(cells_ref, lens_ref, vectors_ref, inner_ref, means_ref, logvars_ref, *outs):
    span = cells_ref.shape[0] // 2
    lens = lens_ref[...]
    lens = jnp.concatenate([lens >> 5, lens & 31], axis=1).astype(jnp.float32)
    for k, ref in enumerate(outs):
        slot = (lax.axis_index("z") + k) % 2
        ref[:span] = cells_ref[pl.ds(pl.multiple_of(slot * span, span), span)]
        ref[span:] = jnp.zeros((SMALL, ref.shape[1]), jnp.bfloat16)
        ref[span : span + 9, 0:64] = vectors_ref[...]
        ref[span:, 128:160] = means_ref[...]
        ref[span:, 256:288] = logvars_ref[...]
        ref[span : span + 1, 384:704] = inner_ref[...]
        ref[span : span + 1, 768:772] = to_low(lens)


def chunk_place(block, step=(0, 0), core_step=0):
    core = flip(lax.axis_index("grp"), core_step)
    return pl.multiple_of(((block * 4 + chip_place(step)) * 2 + core) * 128, 128)


LAT_ROW, FF_ROW, LEN_ROW = 9, 10, 11


def unpack(small_ref, vec_ref, means_ref, logvars_ref, inner_ref):
    count = small_ref.shape[0]

    def lanes(row, rows, first, width):
        return jnp.concatenate(
            [wide(small_ref[i, row : row + rows, first : first + width]) for i in range(count)],
            axis=1,
        )

    vec_ref[...] = lanes(0, SMALL, 0, vec_ref.shape[1] // count)
    means_ref[...] = lanes(0, SMALL, 128, means_ref.shape[1] // count)
    logvars_ref[...] = lanes(0, SMALL, 256, means_ref.shape[1] // count)
    inner_ref[...] = lanes(0, 1, 384, inner_ref.shape[1] // count)
    width = vec_ref.shape[1]
    vec_ref[LAT_ROW : LAT_ROW + 1] = inner_ref[:, inner_ref.shape[1] - width :]
    for block in range(4):
        vec_ref[FF_ROW : FF_ROW + 1, block * 128 : block * 128 + 128] = inner_ref[
            :, pl.ds(chunk_place(block), 128)
        ]
    lens = wide(small_ref[0, 0:1, 768:896])
    even = lax.axis_index("z") % 2 == 0
    high = jnp.where(even, lens[:, 0:1], lens[:, 1:2])
    rest = jnp.where(even, lens[:, 2:3], lens[:, 3:4])
    vec_ref[LEN_ROW : LEN_ROW + 1] = jnp.broadcast_to(high * 32 + rest, (1, width))


def row_stats(values):
    centre = values - jnp.mean(values, axis=-1, keepdims=True)
    scale = lax.rsqrt(jnp.mean(centre * centre, axis=-1, keepdims=True) + EPS_NORM)
    return centre * scale, scale


def norm_back(grad, unit, scale, gain):
    inner = grad * gain
    along = jnp.mean(inner * unit, axis=-1, keepdims=True)
    return scale * (inner - jnp.mean(inner, axis=-1, keepdims=True) - unit * along)


def column_sum(values):
    return jnp.sum(values, axis=0, keepdims=True)


def slide_place(core, block, k, row, span):
    zi = lax.axis_index("z")
    chip = (core * 2 + ((zi + k) & 1)) * 4 + block
    return chip * span + row


def head_lanes(rows):
    return lax.broadcasted_iota(jnp.int32, (rows, PAIR), 1) < HEAD_DIM


def own_pair():
    place = (lax.axis_index("grp") * 2 + lax.axis_index("y")) * 2 + lax.axis_index("x")
    return pl.multiple_of(place * PAIR, PAIR)


def head_row(single, k):
    place = (lax.axis_index("grp") * 2 + lax.axis_index("y")) * 2 + lax.axis_index("x")
    parity = (lax.axis_index("z") + k) % 2
    row = 0
    for role in range(3):
        block = 16 * role + 2 * place
        split = (block % 3) // 2
        odd = (block // 3) % 2
        if single:
            here = split * PAIR * role + split * HEAD_DIM * ((odd + parity) % 2)
        else:
            here = (1 - split) * (1 - (odd + parity) % 2) * PAIR * role
        row = row + here
    return pl.multiple_of(row, HEAD_DIM)


def device_place(step, core_step):
    return flip(lax.axis_index("grp"), core_step) * 4 + chip_place(step)


def attend_body(own_ref, other_ref, *refs):
    came, rest = refs[:4], refs[4:]
    vec_ref, means_ref, logvars_ref, normed_ref, qkv_ref, head_w_ref = rest[:6]
    mixed_ref, lse_ref, bias_ref, small_ref, inner_ref = rest[6:]
    span = own_ref.shape[2] - SMALL
    for core_step, ref in enumerate((own_ref, other_ref)):
        for i, step in enumerate(NEAR):
            place = device_place(step, core_step)
            for k in range(2):
                chip = ((place // 4) * 2 + (lax.axis_index("z") + k) % 2) * 4 + place % 4
                small_ref[chip] = ref[i, k, span:]
    unpack(small_ref, vec_ref, means_ref, logvars_ref, inner_ref)
    for ref, (single, k) in zip(came, ARRIVALS):
        head_w_ref[pl.ds(head_row(single, k), ref.shape[0])] = ref[...]
    total_rows = normed_ref.shape[0]
    gain, shift = vec_ref[0:1], vec_ref[1:2]
    bias_q = vec_ref[2:3, pl.ds(own_pair(), PAIR)]
    bias_v = vec_ref[3:4, pl.ds(own_pair(), PAIR)]
    for core_step, ref in enumerate((own_ref, other_ref)):
        for i, step in enumerate(NEAR):
            cells = jnp.concatenate([ref[i, 0, :span], ref[i, 1, :span]])
            unit, _ = row_stats(wide(cells))
            at = device_place(step, core_step) * (2 * span)
            normed_ref[pl.ds(pl.multiple_of(at, 2 * span), 2 * span)] = to_low(unit * gain + shift)
    step = 256
    for start in range(0, total_rows, step):
        qkv = product_nt(normed_ref[start : start + step], head_w_ref[...])
        qkv_ref[start : start + step, :PAIR] = to_low(
            wide(to_low(qkv[:, :PAIR] + bias_q)) * HEAD_DIM**-0.5
        )
        qkv_ref[start : start + step, PAIR : 2 * PAIR] = to_low(qkv[:, PAIR : 2 * PAIR])
        qkv_ref[start : start + step, 2 * PAIR :] = to_low(qkv[:, 2 * PAIR :] + bias_v)
    lane = lax.broadcasted_iota(jnp.int32, (1, total_rows), 1)
    place = slide_place(
        lane // (8 * span), (lane // (2 * span)) & 3, (lane // span) & 1, lane & (span - 1), span
    )
    bias = jnp.where(place.astype(jnp.float32) < vec_ref[LEN_ROW : LEN_ROW + 1], 0.0, MASKED)
    bias_ref[...] = bias
    keys = qkv_ref[:, PAIR : 2 * PAIR]
    values = qkv_ref[:, 2 * PAIR :]
    first_head = head_lanes(step)
    for start in range(0, total_rows, step):
        query = qkv_ref[start : start + step, :PAIR]
        outs, totals = [], []
        for head in range(2):
            mine = first_head if head == 0 else jnp.logical_not(first_head)
            part = jnp.where(mine, query, jnp.zeros_like(query))
            scores = product_nt(part, keys) + bias
            peak = jnp.max(scores, axis=-1, keepdims=True)
            weights = jnp.exp(scores - peak)
            total = jnp.sum(weights, axis=-1, keepdims=True)
            outs.append(product(to_low(weights / total), values))
            totals.append(jnp.broadcast_to(peak + jnp.log(total), (step, PAIR)))
        mixed_ref[start : start + step] = to_low(jnp.where(first_head, outs[0], outs[1]))
        lse_ref[start : start + step] = jnp.where(first_head, totals[0], totals[1])


def attend(own, other, came, lat, inner):
    rows, width = 16 * (own.shape[2] - SMALL), own.shape[3]
    return whole_call(
        attend_body,
        (own, other, *came),
        [
            wide_shape(SMALL, width),
            wide_shape(SMALL, lat),
            wide_shape(SMALL, lat),
            low_shape(rows, width),
            low_shape(rows, 3 * PAIR),
            low_shape(3 * PAIR, width),
            low_shape(rows, PAIR),
            wide_shape(rows, PAIR),
            wide_shape(1, rows),
        ],
        [
            pltpu.VMEM((16, SMALL, width), jnp.bfloat16),
            pltpu.VMEM((1, inner), jnp.float32),
        ],
    )


def side_rows(ref, core_step, start, rows):
    first = flip(lax.axis_index("grp"), core_step) * (ref.shape[0] // 2) + start
    return ref[pl.ds(pl.multiple_of(first, rows), rows)]


def mix_far_body(mixed_ref, out_t_ref, far_ref):
    for start in range(0, far_ref.shape[0], 256):
        far_ref[start : start + 256] = to_low(
            product_nt(side_rows(mixed_ref, 1, start, 256), out_t_ref[...])
        )


def mix_near_body(mixed_ref, out_t_ref, came_ref, keep_ref, *sends):
    rows = keep_ref.shape[0]
    for i, step in enumerate(NEAR):
        first = chip_place(step) * rows
        came = came_ref[pl.ds(pl.multiple_of(first, rows), rows)]
        part = product_nt(side_rows(mixed_ref, 0, first, rows), out_t_ref[...]) + wide(came)
        if i == 0:
            keep_ref[...] = part
        else:
            sends[i - 1][...] = to_low(part)


def part_shapes(rows, width):
    return [wide_shape(rows, width)] + [low_shape(rows, width)] * 3


def mix_out(mixed, out_t, ready):
    rows, width = mixed.shape[0], out_t.shape[0]
    (far,) = whole_call(mix_far_body, (mixed, out_t), [low_shape(rows // 2, width)])
    keep, *sends = whole_call(
        mix_near_body, (mixed, out_t, after(other_core(far), ready)), part_shapes(rows // 8, width)
    )
    return keep, *plane_hops(sends)


def attend_back_body(
    qkv_ref,
    bias_ref,
    lse_ref,
    out_t_ref,
    head_w_ref,
    *refs,
):
    pieces, (dqkv_ref, far_ref, datt_ref) = refs[:8], refs[8:11]
    dmixed_ref, dk_ref, dv_ref, sems = refs[11:]
    rows = qkv_ref.shape[0]
    stack_rows(pieces, datt_ref, sems, lambda i: device_place(NEAR[i % 4], i // 4))
    for start in range(0, rows, 256):
        at = slice(start, start + 256)
        dmixed_ref[at] = to_low(product(datt_ref[at], out_t_ref[...]))
    keys = qkv_ref[:, PAIR : 2 * PAIR]
    values = qkv_ref[:, 2 * PAIR :]
    bias = bias_ref[...]
    step = 256
    first_head = head_lanes(step)
    for start in range(0, rows, step):
        query = qkv_ref[start : start + step, :PAIR]
        dmixed = dmixed_ref[start : start + step]
        dqueries = []
        for head in range(2):
            mine = first_head if head == 0 else jnp.logical_not(first_head)
            part = jnp.where(mine, query, jnp.zeros_like(query))
            dpart = jnp.where(mine, dmixed, jnp.zeros_like(dmixed))
            lse = lse_ref[start : start + step, head * HEAD_DIM : head * HEAD_DIM + 1]
            probs = jnp.exp(product_nt(part, keys) + bias - lse)
            dprobs = product_nt(dpart, values)
            centre = jnp.sum(dprobs * probs, axis=-1, keepdims=True)
            dscores = to_low(probs * (dprobs - centre))
            dqueries.append(product(dscores, keys))
            dkeys = product_tn(dscores, part)
            dvalues = product_tn(to_low(probs), dpart)
            if start == 0 and head == 0:
                dk_ref[...] = dkeys
                dv_ref[...] = dvalues
            else:
                dk_ref[...] += dkeys
                dv_ref[...] += dvalues
        dquery = jnp.where(first_head, dqueries[0], dqueries[1]) * (HEAD_DIM**-0.5)
        dqkv_ref[start : start + step, :PAIR] = to_low(dquery)
    dqkv_ref[:, PAIR : 2 * PAIR] = to_low(dk_ref[...])
    dqkv_ref[:, 2 * PAIR :] = to_low(dv_ref[...])
    for start in range(0, rows // 2, step):
        far_ref[start : start + step] = to_low(
            product(side_rows(dqkv_ref, 1, start, step), head_w_ref[...])
        )


def attend_back(qkv, bias, lse, out_t, head_w, pieces):
    rows, width = qkv.shape[0], head_w.shape[1]
    return whole_call(
        attend_back_body,
        (qkv, bias, lse, out_t, head_w, *pieces),
        [low_shape(rows, 3 * PAIR), low_shape(rows // 2, width), low_shape(rows, width)],
        [
            pltpu.VMEM((rows, PAIR), jnp.bfloat16),
            pltpu.VMEM((rows, PAIR), jnp.float32),
            pltpu.VMEM((rows, PAIR), jnp.float32),
            pltpu.SemaphoreType.DMA((8,)),
        ],
        range(5, 13),
    )


def dnormed_body(dqkv_ref, head_w_ref, came_ref, keep_ref, *sends):
    rows = keep_ref.shape[0]
    for i, step in enumerate(NEAR):
        first = chip_place(step) * rows
        came = came_ref[pl.ds(pl.multiple_of(first, rows), rows)]
        part = product(side_rows(dqkv_ref, 0, first, rows), head_w_ref[...]) + wide(came)
        if i == 0:
            keep_ref[...] = part
        else:
            sends[i - 1][...] = to_low(part)


def dnormed(dqkv, head_w, came):
    rows, width = dqkv.shape[0] // 8, head_w.shape[1]
    return whole_call(dnormed_body, (dqkv, head_w, came), part_shapes(rows, width))


def head_grad_body(dqkv_ref, normed_ref, *refs):
    homes, sums_ref, grad_w_ref = refs[:4], refs[4], refs[5]
    dqkv = dqkv_ref[...]
    sums_ref[...] = column_sum(wide(dqkv))
    grad_w_ref[...] = to_low(product_tn(dqkv, normed_ref[...]))
    for ref, (single, k) in zip(homes, ARRIVALS):
        ref[...] = grad_w_ref[pl.ds(head_row(single, k), ref.shape[0])]


def head_grads(dqkv, normed):
    width = normed.shape[1]
    outs = whole_call(
        head_grad_body,
        (dqkv, normed),
        [low_shape(HEAD_DIM if single else PAIR, width) for single, _ in ARRIVALS]
        + [wide_shape(1, 3 * PAIR)],
        [pltpu.VMEM((3 * PAIR, width), jnp.bfloat16)],
    )
    return outs[:4], outs[4]


def home_body(*refs):
    pair = wide(refs[0][...]) + wide(refs[2][...])
    single = wide(refs[1][...]) + wide(refs[3][...])
    odd = lax.axis_index("x") % 2
    refs[4][pl.ds(pl.multiple_of(odd * HEAD_DIM, HEAD_DIM), PAIR)] = pair
    refs[4][pl.ds(pl.multiple_of((1 - odd) * PAIR, HEAD_DIM), HEAD_DIM)] = single


LAT_LANES, DEC_LANES = slice(0, 512), slice(512, 768)


def project_body(
    keep_ref, came_x_ref, came_y_ref, came_far_ref, blocks_ref, vec_ref, attended_ref, normed_ref, hidden_ref
):
    span = blocks_ref.shape[1] - SMALL
    hidden = jnp.concatenate([blocks_ref[0, :span], blocks_ref[1, :span]])
    hidden_ref[...] = hidden
    parts = z_sum((keep_ref, came_x_ref, came_y_ref, came_far_ref))
    total = wide(hidden) + parts + vec_ref[4:5]
    attended_ref[...] = total
    unit, _ = row_stats(total)
    normed_ref[...] = to_low(unit * vec_ref[5:6] + vec_ref[6:7])


def project(parts, blocks, vec):
    shape = parts[0].shape
    return whole_call(
        project_body,
        (*parts, blocks, vec),
        [wide_shape(*shape), low_shape(*shape), low_shape(*shape)],
    )


GELU_SCALE = math.sqrt(2.0 / math.pi)
GELU_CUBE = 0.044715


def stack_rows(refs, target_ref, sems, order=None):
    rows = refs[0].shape[0]
    copies = []
    for i, ref in enumerate(refs):
        place = i if order is None else order(i)
        target = target_ref.at[pl.ds(pl.multiple_of(place * rows, rows), rows)]
        copies.append(pltpu.make_async_copy(ref, target, sems.at[i]))
    for copy in copies:
        copy.start()
    for copy in copies:
        copy.wait()


FF_STEP = 256


def load_all(rows_in, weights_ref, all_ref, in_ref, back_ref, sems):
    copies = []
    for i, ref in enumerate(rows_in):
        rows = ref.shape[0]
        copies.append((ref, all_ref.at[i * rows : (i + 1) * rows]))
    for z in range(4):
        part = weights_ref.at[z * 256 : z * 256 + 256]
        copies.append((part.at[:128], in_ref.at[z * 128 : (z + 1) * 128]))
        for half in range(2):
            at = z * 256 + half * 128
            copies.append(
                (part.at[128:, half * 512 : half * 512 + 512], back_ref.at[at : at + 128])
            )
    copies = [pltpu.make_async_copy(*copy, sems.at[i]) for i, copy in enumerate(copies)]
    for copy in copies:
        copy.start()
    for copy in copies:
        copy.wait()


def feed_scratch(rows, width, hidden):
    return [
        pltpu.VMEM((rows, width), jnp.bfloat16),
        pltpu.VMEM((hidden, width), jnp.bfloat16),
        pltpu.VMEM((width, hidden), jnp.bfloat16),
        pltpu.SemaphoreType.DMA((16,)),
    ]


def feed_body(*refs, last):
    rows_in, weights_ref, vec_ref, rest = refs[:4], refs[4], refs[5], list(refs[6:])
    came_ref = rest.pop(0) if last else None
    (act_ref, slope_ref), outs = rest[:2], rest[2:-4]
    all_ref, in_ref, back_ref, sems = rest[-4:]
    load_all(rows_in, weights_ref, all_ref, in_ref, back_ref, sems)
    bias = vec_ref[FF_ROW : FF_ROW + 1, : in_ref.shape[0]]
    step = rows_in[0].shape[0] * 2
    for start in range(0, all_ref.shape[0], step):
        at = slice(start, start + step)
        total = None
        for unit in range(0, in_ref.shape[0], FF_STEP):
            lanes = slice(unit, unit + FF_STEP)
            inner = product_nt(all_ref[at], in_ref[lanes]) + bias[:, lanes]
            square = inner * inner
            bend = jnp.tanh(GELU_SCALE * (inner + GELU_CUBE * (inner * square)))
            half = 0.5 * (1.0 + bend)
            act = to_low(inner * half)
            act_ref[at, lanes] = act
            slope_ref[at, lanes] = half + (0.5 * GELU_SCALE) * inner * (1.0 - bend * bend) * (
                1.0 + (3.0 * GELU_CUBE) * square
            )
            part = product_nt(act, back_ref[:, lanes])
            total = part if total is None else total + part
        put_parts(outs, came_ref, start, total)


def put_parts(outs, came_ref, start, total):
    if came_ref is None:
        outs[0][start : start + total.shape[0]] = to_low(total)
        return
    total = total + wide(came_ref[start : start + total.shape[0]])
    rows = outs[0].shape[0]
    for i in range(start // rows, (start + total.shape[0]) // rows):
        piece = total[i * rows - start : (i + 1) * rows - start]
        outs[i][...] = piece if i == 0 else to_low(piece)


def feed_call(body, pieces, weights, more, came, side_shapes):
    rows, width = pieces[0].shape
    last = came is not None
    operands = (*pieces, weights, *more) + ((came,) if last else ())
    outs = part_shapes(rows, width) if last else [low_shape(4 * rows, width)]
    return whole_call(
        functools.partial(body, last=last),
        operands,
        side_shapes + outs,
        feed_scratch(4 * rows, width, 512),
        range(5),
    )


def feed(pieces, weights, vec, came=None):
    count = 4 * pieces[0].shape[0]
    return feed_call(
        feed_body, pieces, weights, (vec,), came, [low_shape(count, 512), wide_shape(count, 512)]
    )


def feed_back_body(*refs, last):
    rows_in, weights_ref, slope_ref, rest = refs[:4], refs[4], refs[5], list(refs[6:])
    came_ref = rest.pop(0) if last else None
    (du_ref, sums_ref), outs = rest[:2], rest[2:-4]
    all_ref, in_ref, back_ref, sems = rest[-4:]
    load_all(rows_in, weights_ref, all_ref, in_ref, back_ref, sems)
    sums = [None] * (in_ref.shape[0] // FF_STEP)
    step = rows_in[0].shape[0] * 2
    for start in range(0, all_ref.shape[0], step):
        at = slice(start, start + step)
        total = None
        for i in range(len(sums)):
            lanes = slice(i * FF_STEP, (i + 1) * FF_STEP)
            du = to_low(product(all_ref[at], back_ref[:, lanes]) * slope_ref[at, lanes])
            du_ref[at, lanes] = du
            summed = column_sum(wide(du))
            sums[i] = summed if sums[i] is None else sums[i] + summed
            part = product(du, in_ref[lanes])
            total = part if total is None else total + part
        put_parts(outs, came_ref, start, total)
    for i, summed in enumerate(sums):
        sums_ref[:, i * FF_STEP : (i + 1) * FF_STEP] = summed


def feed_back(pieces, weights, slope, came=None):
    count = 4 * pieces[0].shape[0]
    return feed_call(
        feed_back_body, pieces, weights, (slope,), came, [low_shape(count, 512), wide_shape(1, 512)]
    )


def plane_rows(values):
    near = [values, *plane_hops([values] * 3)]
    return (*near, *(other_core(part) for part in near))


GRAD_ROWS = 512


def pair_grad_body(*refs):
    fed_in, two_in, whole_ref, halves = refs[:8], refs[8:16], refs[16], refs[17:21]
    out_ref, fed_ref, two_ref, act_ref, du_ref, sems = refs[21:]
    copies = []
    for pieces, target in ((fed_in, fed_ref), (two_in, two_ref), (halves[:2], act_ref), (halves[2:], du_ref)):
        rows = pieces[0].shape[0]
        for i, ref in enumerate(pieces):
            copies.append((ref, target.at[i * rows : (i + 1) * rows]))
    copies = [pltpu.make_async_copy(*copy, sems.at[i]) for i, copy in enumerate(copies)]
    for copy in copies:
        copy.start()
    for copy in copies:
        copy.wait()
    width = whole_ref.shape[1]
    for z in range(out_ref.shape[0] // GRAD_ROWS):
        at = z * GRAD_ROWS
        for lane in range(0, out_ref.shape[1], 512):
            lanes = slice(lane, lane + 512)
            out_ref[at : at + 128, lanes] = to_low(
                product_tn(du_ref[:, z * 128 : (z + 1) * 128], two_ref[:, lanes])
            )
        grad = to_low(product_tn(fed_ref[:, z * 256 : (z + 1) * 256], act_ref[...]))
        out_ref[at + 128 : at + 256] = jnp.concatenate([grad[:128], grad[128:]], axis=1)
        out_ref[at + 256 : at + GRAD_ROWS, :width] = whole_ref[z * 256 : (z + 1) * 256]
        out_ref[at + 256 : at + GRAD_ROWS, width:] = jnp.zeros(
            (256, out_ref.shape[1] - width), jnp.bfloat16
        )


def pair_grads(rows_fed, rows_two, whole, acts, dus):
    rows, width = rows_fed[0].shape
    hidden = acts[0].shape[1]
    return whole_call(
        pair_grad_body,
        (*rows_fed, *rows_two, whole, *acts, *dus),
        [low_shape(4 * GRAD_ROWS, width)],
        [pltpu.VMEM((8 * rows, width), jnp.bfloat16)] * 2
        + [pltpu.VMEM((8 * rows, hidden), jnp.bfloat16)] * 2
        + [pltpu.SemaphoreType.DMA((20,))],
        [*range(16), *range(17, 21)],
    )[0]


def split_grad_body(sum_ref, in_ref, *outs):
    in_ref[...] = wide(sum_ref[:128])
    rows, half = outs[0].shape[0], sum_ref.shape[1] // 2
    for i, step in enumerate(NEAR):
        place = chip_place(step)
        at = pl.ds(pl.multiple_of(128 + (place % 2) * rows, rows), rows)
        lanes = pl.ds(pl.multiple_of((place // 2) * half, half), half)
        outs[i][:, :half] = sum_ref[at, lanes]
        whole = pl.ds(pl.multiple_of(256 + place * rows, rows), rows)
        outs[i][:, half:] = sum_ref[whole, : outs[i].shape[1] - half]


def z_sum(refs):
    total = wide(refs[0][...])
    for ref in refs[1:]:
        total = total + wide(ref[...])
    return total


def pick_body(out_ref, back_ref, pairs_ref, *outs):
    for chip in range(16):
        pair = pl.multiple_of((lax.axis_index("grp") * 4 + chip % 4) * PAIR, PAIR)
        pairs_ref[chip] = out_ref[:, pl.ds(pair, PAIR)]
    for i, step in enumerate(NEAR):
        for block in range(4):
            outs[i][:, block * 128 : (block + 1) * 128] = back_ref[
                :, pl.ds(chunk_place(block, step), 128)
            ]


def lay_body(*refs):
    out_ref = refs[5]
    out_ref[:128] = refs[0][...]
    half = refs[1].shape[1]
    for i, step in enumerate(NEAR):
        place = chip_place(step)
        rows = pl.ds(pl.multiple_of(128 + (place % 2) * 64, 64), 64)
        out_ref[rows, pl.ds(pl.multiple_of((place // 2) * half, half), half)] = refs[1 + i][...]


def core_order(own, other):
    first = lax.axis_index("grp") == 0
    return jnp.concatenate(
        [jnp.where(first, own, other), jnp.where(first, other, own)], axis=1
    )


def core_halves(values):
    part = values.shape[1] // 2
    first = lax.axis_index("grp") == 0
    low_half, high_half = values[:, :part], values[:, part:]
    return (
        jnp.where(first, low_half, high_half),
        jnp.where(first, high_half, low_half),
    )


def halves_nt(values, own_ref, other_ref, lanes):
    own, other = core_halves(values)
    return product_nt(own, own_ref[:, lanes]) + product_nt(other, other_ref[:, lanes])


def bottle_body(
    attended_ref,
    keep_ref,
    came_x_ref,
    came_y_ref,
    came_far_ref,
    vec_ref,
    own_ref,
    other_ref,
    noise_ref,
    cot_ref,
    means_ref,
    logvars_ref,
    out_ref,
    fed_ref,
    sample_ref,
    dlat_ref,
    dfed_ref,
    dfed_low_ref,
    dmeans_ref,
    dlogvars_ref,
    sums_ref,
):
    rows, width = attended_ref.shape
    lat = noise_ref.shape[1]
    comps = means_ref.shape[0]
    parts = z_sum((keep_ref, came_x_ref, came_y_ref, came_far_ref))
    fed = attended_ref[...] + parts + vec_ref[7:8]
    fed_low = to_low(fed)
    fed_ref[...] = fed_low
    latent = halves_nt(fed_low, own_ref, other_ref, LAT_LANES) + vec_ref[LAT_ROW : LAT_ROW + 1]
    logvar = latent[:, lat:]
    noise = noise_ref[...]
    spread = jnp.exp(0.5 * logvar) * noise
    sample = latent[:, :lat] + spread
    sample_low = to_low(sample)
    sample_ref[...] = sample_low
    out_ref[...] = fed + halves_nt(sample_low, own_ref, other_ref, DEC_LANES) + vec_ref[8:9]
    cot = cot_ref[...]
    dsample = core_order(
        product(cot, own_ref[:, DEC_LANES]), product(cot, other_ref[:, DEC_LANES])
    )

    span = rows // 2
    row = lax.broadcasted_iota(jnp.int32, (rows, 1), 0)
    block = lax.axis_index("y") * 2 + lax.axis_index("x")
    place = slide_place(lax.axis_index("grp"), block, row // span, row & (span - 1), span)
    live = place.astype(jnp.float32) < vec_ref[LEN_ROW : LEN_ROW + 1, 0:1]
    share = jnp.where(live, 1.0 / lat, 0.0)
    own_term = jnp.sum(-0.5 * noise * noise - 0.5 * logvar, axis=-1, keepdims=True)
    logvars = logvars_ref[...]
    inverse = jnp.exp(-logvars)
    terms = []
    for c in range(comps):
        offset = sample - means_ref[c : c + 1]
        terms.append(
            jnp.sum(
                -0.5 * offset * offset * inverse[c : c + 1] - 0.5 * logvars[c : c + 1],
                axis=-1,
                keepdims=True,
            )
            - math.log(comps)
        )
    peak = terms[0]
    for term in terms[1:]:
        peak = jnp.maximum(peak, term)
    weights = [jnp.exp(term - peak) for term in terms]
    total = weights[0]
    for weight in weights[1:]:
        total = total + weight
    kl_cell = own_term - (peak + jnp.log(total))
    kl = jnp.sum(jnp.where(live, kl_cell, 0.0), axis=0, keepdims=True) / lat
    scale = share / total
    for c in range(comps):
        offset = sample - means_ref[c : c + 1]
        slope = offset * inverse[c : c + 1]
        part = weights[c] * scale
        pull = part * slope
        dsample = dsample + pull
        dmeans_ref[c : c + 1] = -column_sum(pull)
        dlogvars_ref[c : c + 1] = column_sum(0.5 * part - 0.5 * (pull * offset))
    dlat = jnp.concatenate([dsample, 0.5 * dsample * spread - 0.5 * share], axis=1)
    dlat_low = to_low(dlat)
    dlat_ref[...] = dlat_low
    grad_out = wide(cot)
    dfed = grad_out + core_order(
        product(dlat_low, own_ref[:, LAT_LANES]), product(dlat_low, other_ref[:, LAT_LANES])
    )
    dfed_ref[...] = dfed
    dfed_low_ref[...] = to_low(dfed)
    sums_ref[...] = jnp.concatenate(
        [
            column_sum(wide(dlat_low)),
            column_sum(dfed),
            column_sum(grad_out),
            jnp.broadcast_to(kl, (1, width)),
            jnp.zeros((4, width), jnp.float32),
        ]
    )


def bottle_call(attended, parts, vec, weights, noise, cot, means, logvars):
    rows, width = attended.shape
    lat = noise.shape[1]
    return whole_call(
        bottle_body,
        (attended, *parts, vec, *weights, noise, cot, means, logvars),
        [
            wide_shape(rows, width),
            low_shape(rows, width),
            low_shape(rows, lat),
            low_shape(rows, width),
            wide_shape(rows, width),
            low_shape(rows, width),
            wide_shape(*means.shape),
            wide_shape(*means.shape),
            wide_shape(8, width),
        ],
    )


def project_back_body(
    keep_ref,
    came_x_ref,
    came_y_ref,
    came_far_ref,
    attended_ref,
    dfed_ref,
    vec_ref,
    datt_ref,
    datt_low_ref,
    sums_ref,
):
    grad = z_sum((keep_ref, came_x_ref, came_y_ref, came_far_ref))
    unit, scale = row_stats(attended_ref[...])
    datt = dfed_ref[...] + norm_back(grad, unit, scale, vec_ref[5:6])
    datt_ref[...] = datt
    datt_low_ref[...] = to_low(datt)
    sums_ref[...] = jnp.concatenate(
        [
            column_sum(grad * unit),
            column_sum(grad),
            column_sum(datt),
            jnp.zeros((5, datt.shape[1]), jnp.float32),
        ]
    )


def project_back(parts, attended, dfed, vec):
    rows, width = attended.shape
    return whole_call(
        project_back_body,
        (*parts, attended, dfed, vec),
        [wide_shape(rows, width), low_shape(rows, width), wide_shape(8, width)],
    )


def whole_grads_body(*refs):
    out_ref = refs[-1]
    for lanes, (left, left_other, right, right_other) in (
        (LAT_LANES, refs[:4]),
        (DEC_LANES, refs[4:8]),
    ):
        grads = jnp.concatenate([left[...], left_other[...]])
        values = jnp.concatenate([core_halves(right[...])[0], core_halves(right_other[...])[0]])
        out_ref[:, lanes] = to_low(product_tn(grads, values))


def whole_grads(pairs):
    operands = []
    for values in pairs:
        operands += [values, other_core(values)]
    width = pairs[0].shape[1]
    return whole_call(whole_grads_body, operands, [low_shape(width, DEC_LANES.stop)])[0]


def sum_body(*refs):
    refs[-1][...] = z_sum(refs[:-1])


def last_grad_body(*refs):
    out_ref, wholes = refs[8], refs[9:]
    half = out_ref.shape[1] // 8
    for i, ref in enumerate(refs[:8]):
        for block in range(4):
            place = chunk_place(block, NEAR[i % 4], i // 4)
            out_ref[:, pl.ds(place, 128)] = wide(ref[:, block * 128 : (block + 1) * 128])
    for core in range(2):
        wholes[core][...] = z_sum([ref.at[:, half:] for ref in refs[core * 4 : core * 4 + 4]])


def cells_back_body(
    keep_ref,
    came_x_ref,
    came_y_ref,
    came_far_ref,
    hidden_ref,
    datt_ref,
    vec_ref,
    bottle_sums_ref,
    project_sums_ref,
    head_sums_ref,
    ff_sums_ref,
    ff_more_ref,
    dmeans_ref,
    dlogvars_ref,
    out_grad_ref,
    grad_ref,
    packed_ref,
    inner_ref,
    rows_ref,
):
    grad = z_sum((keep_ref, came_x_ref, came_y_ref, came_far_ref))
    unit, scale = row_stats(wide(hidden_ref[...]))
    grad_ref[...] = datt_ref[...] + norm_back(grad, unit, scale, vec_ref[0:1])
    width = grad.shape[1]
    count = packed_ref.shape[0]
    inner_ref[...] = jnp.zeros_like(inner_ref)
    for block in range(4):
        lanes = slice(block * 128, block * 128 + 128)
        inner_ref[:, pl.ds(chunk_place(block), 128)] = (
            ff_sums_ref[:, lanes] + ff_more_ref[:, lanes]
        )
    inner_ref[:, inner_ref.shape[1] - width :] = bottle_sums_ref[0:1]
    rows_ref[...] = jnp.zeros_like(rows_ref)
    rows_ref[0:1] = column_sum(grad * unit)
    rows_ref[1:2] = column_sum(grad)
    rows_ref[2:3, pl.ds(own_pair(), PAIR)] = head_sums_ref[:, :PAIR]
    rows_ref[3:4, pl.ds(own_pair(), PAIR)] = head_sums_ref[:, 2 * PAIR :]
    rows_ref[4:5] = project_sums_ref[2:3]
    rows_ref[5:7] = project_sums_ref[0:2]
    rows_ref[7:9] = bottle_sums_ref[1:3]
    part = width // count
    pieces = inner_ref.shape[1] // width
    for i in range(pieces):
        rows_ref[9 + i : 10 + i] = jnp.concatenate(
            [
                inner_ref[:, (b * pieces + i) * part : (b * pieces + i + 1) * part]
                for b in range(count)
            ],
            axis=1,
        )
    rows_ref[14:15] = bottle_sums_ref[3:4]
    lat_part = dmeans_ref.shape[1] // count
    for b in range(count):
        sums = jnp.concatenate(
            [
                rows_ref[:, b * part : (b + 1) * part],
                dmeans_ref[:, b * lat_part : (b + 1) * lat_part],
                dlogvars_ref[:, b * lat_part : (b + 1) * lat_part],
            ],
            axis=1,
        )
        high = to_low(sums)
        packed_ref[b, :part] = out_grad_ref[b]
        packed_ref[b, part : part + SMALL] = high
        packed_ref[b, part + SMALL :] = to_low(sums - wide(high))


def last_sum_body(came_ref, out_ref):
    count, rows = came_ref.shape[0], came_ref.shape[1] - 2 * SMALL
    for chip in range(4):
        total = z_sum([came_ref.at[z * 4 + chip, :rows] for z in range(4)])
        out_ref[:rows, chip * PAIR : (chip + 1) * PAIR] = total
    small = z_sum([came_ref.at[i, rows : rows + SMALL] for i in range(count)])
    rest = z_sum([came_ref.at[i, rows + SMALL :] for i in range(count)])
    out_ref[rows:] = jnp.zeros((SMALL, out_ref.shape[1]), jnp.float32)
    out_ref[rows:, :PAIR] = small + rest


def last_body(own_ref, other_ref, grad_ref, small_ref):
    rows, half = grad_ref.shape[0], own_ref.shape[1]
    for ref, place in ((own_ref, 0), (other_ref, 1)):
        core = flip(lax.axis_index("grp"), place)
        grad_ref[:, pl.ds(pl.multiple_of(core * half, half), half)] = ref[:rows]
    small_ref[...] = own_ref[rows:, :PAIR] + other_ref[rows:, :PAIR]


def cells_back(operands, inner):
    rows, width = operands[0].shape
    return whole_call(
        cells_back_body,
        operands,
        [wide_shape(rows, width), low_shape(16, width // 16 + 2 * SMALL, PAIR)],
        [pltpu.VMEM((1, inner), jnp.float32), pltpu.VMEM((SMALL, width), jnp.float32)],
    )


def exchange(blocks, axes):
    return lax.all_to_all(blocks, axes, split_axis=0, concat_axis=0, tiled=True)


def to_all(values, count):
    return jnp.broadcast_to(values[None], (count, *values.shape))


def fast_device(
    cell_input,
    lengths,
    noise_draw,
    cotangent,
    w_qkv,
    w_out,
    w_ffn_in,
    w_ffn_out,
    w_latent,
    w_decode,
    vectors,
    inner_bias,
    prior_means,
    prior_logvars,
):
    slots, span, width = cell_input.shape[1:]
    rows = slots * span
    lat = noise_draw.shape[-1]
    comps = prior_means.shape[1]
    ff = w_ffn_out.shape[1]
    inner = 16 * inner_bias.shape[1]

    blocks = whole_call(
        enter_body,
        (
            cell_input.reshape(rows, width),
            lengths,
            vectors[0],
            inner_bias,
            prior_means[0],
            prior_logvars[0],
        ),
        [low_shape(span + SMALL, width)] * 2,
    )
    first = jnp.stack(
        [lax.ppermute(blocks[k], ("grp", "z"), slide_routes(k)) for k in range(2)]
    )

    qkv_t = w_qkv[0].T
    at_x = lax.axis_index("x") % 2
    head_parts = (
        lax.dynamic_slice_in_dim(qkv_t, at_x * HEAD_DIM, PAIR),
        lax.dynamic_slice_in_dim(qkv_t, (1 - at_x) * PAIR, HEAD_DIM),
    )
    came = [
        lax.ppermute(head_parts[int(single)], EVERY, head_routes(single, k))
        for single, k in ARRIVALS
    ]
    plane_near = jnp.stack([first, hop(first, "x")])
    plane_own = jnp.concatenate([plane_near, hop(after(plane_near, came), "y")])
    plane_other = other_core(plane_own)

    part = width // 16
    out_pairs, *back_cols = whole_call(
        pick_body,
        (w_out[0].T, w_ffn_out[0].T),
        [low_shape(16, part, PAIR)] + [low_shape(part, ff // 8)] * 4,
    )
    out_t = exchange(after(out_pairs, first), CHIPS).reshape(width, PAIR)
    in_own = half_of(w_ffn_in[0], 1, "grp", True).T
    back_cols = (back_cols[0], *plane_hops(after(back_cols[1:], plane_near)))
    (pair_own,) = whole_call(lay_body, (in_own, *back_cols), [low_shape(256, width)])

    shard = jnp.concatenate(
        [half_of(w[0], 0, "grp", True).T for w in (w_latent, w_decode)], axis=1
    )
    shard_width = shard.shape[1]
    whole = lax.all_gather(shard, CHIPS, axis=0, tiled=True)
    pair_w = lax.all_gather(after(pair_own, came), "z", axis=0, tiled=True)

    vec, means, logvars, normed, qkv, head_w, mixed, lse, bias = attend(
        plane_own, plane_other, after(came, pair_own), lat, inner
    )
    mix_parts = mix_out(mixed, out_t, out_t)

    noise_high = to_low(noise_draw[0, 0])
    noise_rest = to_low(noise_draw[0, 0] - wide(noise_high))
    extra = jnp.concatenate(
        [cotangent[0], jnp.concatenate([noise_high, noise_rest], axis=2)], axis=1
    )
    extra = to_slides(after(extra, mixed))
    cot = extra[:, :span].reshape(rows, width)
    noise = extra[:, span:].reshape(rows, width)
    noise = wide(noise[:, :lat]) + wide(noise[:, lat:])

    attended, normed_two, hidden = project(mix_parts, first, vec)
    rows_two = plane_rows(normed_two)
    whole = after(whole, rows_two)
    wholes = (whole, other_core(whole))
    act_far, slope_far, fed_far = feed(rows_two[4:], pair_w, vec)
    act, slope, keep, *sends = feed(rows_two[:4], pair_w, vec, other_core(fed_far))
    fed_parts = (keep, *plane_hops(sends))
    output, fed_low, sample_low, dlat_low, dfed, dfed_low, dmeans, dlogvars, bottle_sums = (
        bottle_call(
            attended, fed_parts, vec, wholes, noise, cot, means, logvars
        )
    )

    rows_fed = plane_rows(dfed_low)
    layer_out = from_slides(after(output, rows_fed).reshape(slots, span, width))
    whole_grad = whole_grads((dlat_low, fed_low, cot, sample_low))
    du_far, ff_far, norm_far = feed_back(rows_fed[4:], pair_w, slope_far)
    du, ff_sums, keep, *sends = feed_back(
        rows_fed[:4], pair_w, slope, after(other_core(norm_far), whole_grad)
    )
    norm_parts = (keep, *plane_hops(sends))
    grads = pair_grads(rows_fed, rows_two, whole_grad, (act, act_far), (du, du_far))
    grads_sum = lax.psum_scatter(grads, "z", scatter_dimension=0, tiled=True)
    datt, datt_low, project_sums = project_back(after(norm_parts, grads), attended, dfed, vec)
    rows_datt = plane_rows(datt_low)
    dqkv, dn_far, all_datt = attend_back(qkv, bias, lse, out_t, head_w, rows_datt)
    dn_keep, *dn_sends = dnormed(dqkv, head_w, other_core(dn_far))
    homes, head_sums = head_grads(dqkv, after(normed, dn_sends))
    dn_parts = (dn_keep, *plane_hops(dn_sends))
    grad_rows, packed = cells_back(
        (
            *dn_parts,
            hidden,
            datt,
            vec,
            bottle_sums,
            project_sums,
            head_sums,
            ff_sums,
            ff_far,
            dmeans,
            dlogvars,
            to_low(product_tn(all_datt, mixed)).reshape(16, part, PAIR),
        ),
        inner,
    )
    grad_cells = from_slides(grad_rows.reshape(slots, span, width))
    sum_in, *sums = whole_call(
        split_grad_body,
        (after(grads_sum, dn_parts),),
        [wide_shape(128, width)] + [low_shape(part, ff // 8 + shard_width)] * 4,
    )
    sums = [sums[0], *plane_hops(sums[1:])]
    sums += [other_core(total) for total in sums]

    homes = [
        lax.ppermute(grad, EVERY, [(there, here) for here, there in head_routes(single, k)])
        for grad, (single, k) in zip(homes, ARRIVALS)
    ]
    (home,) = whole_call(home_body, homes, [wide_shape(3 * HEAD_DIM, width)])
    grad_qkv = (home + other_core(home)).T

    (last,) = whole_call(
        last_sum_body, (exchange(packed, CHIPS),), [wide_shape(part + SMALL, 4 * PAIR)]
    )
    grad_out_w, small_sums = whole_call(
        last_body, (last, other_core(last)), [wide_shape(part, width), wide_shape(SMALL, PAIR)]
    )
    grad_out_w = grad_out_w.T
    vec_out = small_sums[:9, :part]
    inner_out = small_sums[9 : 9 + inner // width, :part].reshape(1, -1)
    means_out = small_sums[:, part : part + lat // 16]
    logvars_out = small_sums[:, part + lat // 16 :]
    kl_mean = small_sums[14, 0] / (32 * rows)

    grad_in_w = ordered(sum_in.T, other_core(sum_in).T, "grp", 1)
    grad_back_w, whole_own, whole_other = whole_call(
        last_grad_body,
        sums,
        [wide_shape(part, ff)] + [wide_shape(part, shard_width)] * 2,
    )
    grad_back_w = grad_back_w.T
    grad_lat_w, grad_dec_w = (
        ordered(whole_own[:, lanes].T, whole_other[:, lanes].T, "grp", 0)
        for lanes in (LAT_LANES, DEC_LANES)
    )
    return (
        layer_out.reshape(1, slots, span, width),
        grad_cells.reshape(1, slots, span, width),
        kl_mean,
        grad_qkv[None],
        grad_out_w[None],
        grad_in_w[None],
        grad_back_w[None],
        grad_lat_w[None],
        grad_dec_w[None],
        vec_out[None],
        inner_out,
        means_out[None],
        logvars_out[None],
    )


def solution(mesh):
    chips = mesh.shape["blk"]
    if (mesh.shape["grp"], chips) == (2, HEADS):
        mesh = Mesh(mesh.devices.reshape(2, chips // 4, 2, 2), EVERY)
        blk, run = CHIPS, fast_device
    else:
        blk, run = "blk", per_device
    cells = P("grp", None, blk, None)
    columns = P(None, None, blk)
    return jax.shard_map(
        run,
        mesh=mesh,
        in_specs=(cells, P("grp", None), P(None, "grp", None, blk, None), cells)
        + (columns,) * 7
        + (P(None, blk), columns, columns),
        out_specs=(cells, cells, P()) + (columns,) * 7 + (P(None, blk), columns, columns),
        check_vma=False,
    )
```

```python
import functools
import math

import jax
import jax.numpy as jnp
import numpy as np
from jax import lax
from jax.experimental import pallas as pl
from jax.experimental.pallas import tpu as pltpu
from jax.sharding import Mesh
from jax.sharding import PartitionSpec as P

HEADS = 16
LAYERS = 1
HEAD_DIM = 64


EPS_NORM = 1e-05
MASKED = -1e30


def to_low(values):
    return values.astype(jnp.bfloat16)


def product(left, right):
    return jnp.dot(left, right, preferred_element_type=jnp.float32)


def product_tn(left, right):
    return lax.dot_general(
        left, right, (((0,), (0,)), ((), ())), preferred_element_type=jnp.float32
    )


def product_nt(left, right):
    return lax.dot_general(
        left, right, (((1,), (1,)), ((), ())), preferred_element_type=jnp.float32
    )


def layer_norm(values, norm_gain, norm_shift):
    centre = values - jnp.mean(values, axis=-1, keepdims=True)
    spread = jnp.mean(centre * centre, axis=-1, keepdims=True)
    return centre * lax.rsqrt(spread + EPS_NORM) * norm_gain + norm_shift


def mixture_kl(sample, noise_rows, logvar, mean_rows, logvars):
    own_term = jnp.sum(-0.5 * noise_rows * noise_rows - 0.5 * logvar, axis=-1)
    offset = sample[:, None, :] - mean_rows[None, :, :]
    component = jnp.sum(
        -0.5 * offset * offset * jnp.exp(-logvars)[None] - 0.5 * logvars[None], axis=-1
    ) - math.log(mean_rows.shape[0])
    row_peak = jnp.max(component, axis=-1, keepdims=True)
    mixture = row_peak[:, 0] + jnp.log(jnp.sum(jnp.exp(component - row_peak), axis=-1))
    return own_term - mixture


def bottleneck(latent, noise_rows, live_rows, mean_rows, logvars):
    lat_width = noise_rows.shape[-1]
    mean_part = latent[:, :lat_width]
    logvar = latent[:, lat_width:]
    sample = mean_part + jnp.exp(0.5 * logvar) * noise_rows
    per_cell = mixture_kl(sample, noise_rows, logvar, mean_rows, logvars)
    return (sample, jnp.sum(jnp.where(live_rows, per_cell, 0.0)) / lat_width)


def slot_scores(query_slots, keys_all, slide_len, score_scale):
    slot_count, query_rows, model_width = query_slots.shape
    heads_q = query_slots.reshape(slot_count, query_rows, HEADS, HEAD_DIM)
    heads_k = keys_all.reshape(slot_count, keys_all.shape[1], HEADS, HEAD_DIM)
    raw_scores = (
        jnp.einsum("sqhd,skhd->shqk", heads_q, heads_k, preferred_element_type=jnp.float32)
        * score_scale
    )
    live_keys = jnp.arange(keys_all.shape[1])[None, :] < slide_len[:, None]
    return jnp.where(live_keys[:, None, None, :], raw_scores, MASKED)


def widen(gathered):
    qkv_w, out_w, in_w, back_w, latent_w, decode_w, vec_rows, inner_rows, mean_rows, logvars = (
        gathered
    )
    return (
        qkv_w,
        out_w,
        in_w,
        back_w,
        latent_w,
        decode_w,
        vec_rows.astype(jnp.float32),
        inner_rows.astype(jnp.float32),
        mean_rows.astype(jnp.float32),
        logvars.astype(jnp.float32),
    )


def gather_weights(layer_parts):
    (
        part_qkv,
        part_out,
        part_in,
        part_back,
        part_latent,
        part_decode,
        part_vectors,
        part_inner,
        part_means,
        part_logvars,
    ) = layer_parts
    return widen(
        (
            lax.all_gather(part_qkv, "blk", axis=1, tiled=True),
            lax.all_gather(part_out, "blk", axis=1, tiled=True),
            lax.all_gather(part_in, "blk", axis=1, tiled=True),
            lax.all_gather(part_back, "blk", axis=1, tiled=True),
            lax.all_gather(part_latent, "blk", axis=1, tiled=True),
            lax.all_gather(part_decode, "blk", axis=1, tiled=True),
            lax.all_gather(part_vectors, "blk", axis=1, tiled=True),
            lax.all_gather(part_inner, "blk", axis=0, tiled=True),
            lax.all_gather(part_means, "blk", axis=1, tiled=True),
            lax.all_gather(part_logvars, "blk", axis=1, tiled=True),
        )
    )


def reduce_grads(grads):
    (
        grad_qkv_w,
        grad_out_w,
        grad_in_w,
        grad_back_w,
        grad_latent_w,
        grad_decode_w,
        grad_vec,
        grad_inner,
        grad_mean_rows,
        grad_logvars,
    ) = grads
    (
        shard_qkv,
        shard_out,
        shard_in,
        shard_back,
        shard_latent,
        shard_decode,
        shard_vec,
        shard_inner,
        shard_means,
        shard_logvars,
    ) = (
        lax.psum_scatter(grad_qkv_w, "blk", scatter_dimension=1, tiled=True),
        lax.psum_scatter(grad_out_w, "blk", scatter_dimension=1, tiled=True),
        lax.psum_scatter(grad_in_w, "blk", scatter_dimension=1, tiled=True),
        lax.psum_scatter(grad_back_w, "blk", scatter_dimension=1, tiled=True),
        lax.psum_scatter(grad_latent_w, "blk", scatter_dimension=1, tiled=True),
        lax.psum_scatter(grad_decode_w, "blk", scatter_dimension=1, tiled=True),
        lax.psum_scatter(grad_vec, "blk", scatter_dimension=1, tiled=True),
        lax.psum_scatter(grad_inner, "blk", scatter_dimension=0, tiled=True),
        lax.psum_scatter(grad_mean_rows, "blk", scatter_dimension=1, tiled=True),
        lax.psum_scatter(grad_logvars, "blk", scatter_dimension=1, tiled=True),
    )
    return lax.psum(
        (
            shard_qkv,
            shard_out,
            shard_in,
            shard_back,
            shard_latent,
            shard_decode,
            shard_vec,
            shard_inner,
            shard_means,
            shard_logvars,
        ),
        "grp",
    )


def layer_forward(hidden, full_weights, noise_rows, live_rows, slide_len, score_scale):
    qkv_w, out_w, in_w, back_w, latent_w, decode_w, vec_rows, inner_rows, mean_rows, logvars = (
        full_weights
    )
    model_width = hidden.shape[1]
    slot_count = slide_len.shape[0]
    slot_span = hidden.shape[0] // slot_count
    ff_width = in_w.shape[1]
    normed = to_low(layer_norm(hidden, vec_rows[0], vec_rows[1]))
    qkv_all = product(normed, qkv_w)
    query_low = to_low(qkv_all[:, :model_width] + vec_rows[2])
    keys_own = to_low(qkv_all[:, model_width : 2 * model_width])
    values_own = to_low(qkv_all[:, 2 * model_width :] + vec_rows[3])
    keys_all, values_all = (
        lax.all_gather(
            keys_own.reshape(slot_count, slot_span, model_width), "blk", axis=1, tiled=True
        ),
        lax.all_gather(
            values_own.reshape(slot_count, slot_span, model_width), "blk", axis=1, tiled=True
        ),
    )
    scores = slot_scores(
        query_low.reshape(slot_count, slot_span, model_width), keys_all, slide_len, score_scale
    )
    row_peak = jnp.max(scores, axis=-1, keepdims=True)
    weights = jnp.exp(scores - row_peak)
    totals = jnp.sum(weights, axis=-1, keepdims=True)
    probs_low = to_low(weights / totals)
    log_total = row_peak + jnp.log(totals)
    heads_v = values_all.reshape(slot_count, values_all.shape[1], HEADS, HEAD_DIM)
    mixed_f = jnp.einsum("shqk,skhd->sqhd", probs_low, heads_v, preferred_element_type=jnp.float32)
    mixed_low = to_low(mixed_f.reshape(slot_count * slot_span, model_width))
    attended = hidden + product(mixed_low, out_w) + vec_rows[4]
    normed_two = to_low(layer_norm(attended, vec_rows[5], vec_rows[6]))
    inner_act = product(normed_two, in_w) + inner_rows[:ff_width]
    activated = to_low(jax.nn.gelu(inner_act))
    fed_rows = attended + product(activated, back_w) + vec_rows[7]
    fed_low = to_low(fed_rows)
    latent = product(fed_low, latent_w) + inner_rows[ff_width:]
    sample, kl_part = bottleneck(latent, noise_rows, live_rows, mean_rows, logvars)
    sample_low = to_low(sample)
    output = fed_rows + product(sample_low, decode_w) + vec_rows[8]
    saved_state = (
        hidden,
        normed,
        query_low,
        keys_own,
        values_own,
        log_total,
        mixed_low,
        attended,
        normed_two,
        inner_act,
        activated,
        fed_low,
        latent,
        sample_low,
    )
    return (output, kl_part, saved_state)


def layer_backward(
    grad_out, full_weights, saved_state, noise_rows, live_rows, slide_len, score_scale
):
    qkv_w, out_w, in_w, back_w, latent_w, decode_w, vec_rows, inner_rows, mean_rows, logvars = (
        full_weights
    )
    (
        hidden,
        normed,
        query_low,
        keys_own,
        values_own,
        log_total,
        mixed_low,
        attended,
        normed_two,
        inner_act,
        activated,
        fed_low,
        latent,
        sample_low,
    ) = saved_state
    model_width = hidden.shape[1]
    row_total = hidden.shape[0]
    slot_count = slide_len.shape[0]
    slot_span = row_total // slot_count
    grad_dec_low = to_low(grad_out)
    grad_decode_w = product_tn(sample_low, grad_dec_low)
    grad_sample = product_nt(grad_dec_low, decode_w)

    def bottle(latent_in, means_in, logvars_in):
        return bottleneck(latent_in, noise_rows, live_rows, means_in, logvars_in)

    ignored, bottle_pull = jax.vjp(bottle, latent, mean_rows, logvars)
    grad_latent_f, grad_mean_rows, grad_logvars = bottle_pull(
        (grad_sample, jnp.ones((), jnp.float32))
    )
    grad_latent_low = to_low(grad_latent_f)
    grad_latent_w = product_tn(fed_low, grad_latent_low)
    grad_fed = grad_out + product_nt(grad_latent_low, latent_w)
    grad_fed_low = to_low(grad_fed)
    grad_back_w = product_tn(activated, grad_fed_low)
    grad_act = product_nt(grad_fed_low, back_w)
    ignored_two, gelu_pull = jax.vjp(jax.nn.gelu, inner_act)
    grad_inner_low = to_low(gelu_pull(grad_act)[0])
    grad_in_w = product_tn(normed_two, grad_inner_low)
    grad_normed_two = product_nt(grad_inner_low, in_w)
    ignored_three, second_pull = jax.vjp(layer_norm, attended, vec_rows[5], vec_rows[6])
    grad_att_norm, grad_gain_two, grad_shift_two = second_pull(grad_normed_two)
    grad_attended = grad_fed + grad_att_norm
    grad_proj_low = to_low(grad_attended)
    grad_out_w = product_tn(mixed_low, grad_proj_low)
    grad_mixed_low = to_low(product_nt(grad_proj_low, out_w))
    keys_all, values_all = (
        lax.all_gather(
            keys_own.reshape(slot_count, slot_span, model_width), "blk", axis=1, tiled=True
        ),
        lax.all_gather(
            values_own.reshape(slot_count, slot_span, model_width), "blk", axis=1, tiled=True
        ),
    )
    grad_mixed_heads = grad_mixed_low.reshape(slot_count, slot_span, HEADS, HEAD_DIM)
    heads_k = keys_all.reshape(slot_count, keys_all.shape[1], HEADS, HEAD_DIM)
    heads_v = values_all.reshape(slot_count, values_all.shape[1], HEADS, HEAD_DIM)
    scores = slot_scores(
        query_low.reshape(slot_count, slot_span, model_width), keys_all, slide_len, score_scale
    )
    probs_f = jnp.exp(scores - log_total)
    grad_probs = jnp.einsum(
        "sqhd,skhd->shqk", grad_mixed_heads, heads_v, preferred_element_type=jnp.float32
    )
    centre = jnp.sum(grad_probs * probs_f, axis=-1, keepdims=True)
    grad_scores_low = to_low(probs_f * (grad_probs - centre))
    grad_query = (
        jnp.einsum("shqk,skhd->sqhd", grad_scores_low, heads_k, preferred_element_type=jnp.float32)
        * score_scale
    )
    grad_query_low = to_low(grad_query.reshape(row_total, model_width))
    rows_all, mixed_all = (
        lax.all_gather(
            query_low.reshape(slot_count, slot_span, model_width), "blk", axis=1, tiled=True
        ),
        lax.all_gather(
            grad_mixed_low.reshape(slot_count, slot_span, model_width), "blk", axis=1, tiled=True
        ),
    )
    total_all, centre_all = (
        lax.all_gather(log_total, "blk", axis=2, tiled=True),
        lax.all_gather(centre, "blk", axis=2, tiled=True),
    )
    query_all = rows_all.reshape(slot_count, rows_all.shape[1], HEADS, HEAD_DIM)
    dmixed_all = mixed_all.reshape(slot_count, mixed_all.shape[1], HEADS, HEAD_DIM)
    own_keys = keys_own.reshape(slot_count, slot_span, HEADS, HEAD_DIM)
    own_values = values_own.reshape(slot_count, slot_span, HEADS, HEAD_DIM)
    own_raw = (
        jnp.einsum("sqhd,skhd->shqk", query_all, own_keys, preferred_element_type=jnp.float32)
        * score_scale
    )
    key_places = lax.axis_index("blk") * slot_span + jnp.arange(slot_span)
    live_own = key_places[None, :] < slide_len[:, None]
    own_scores = jnp.where(live_own[:, None, None, :], own_raw, MASKED)
    own_probs = jnp.exp(own_scores - total_all)
    own_dprobs = jnp.einsum(
        "sqhd,skhd->shqk", dmixed_all, own_values, preferred_element_type=jnp.float32
    )
    own_dscores = to_low(own_probs * (own_dprobs - centre_all))
    grad_keys = (
        jnp.einsum("shqk,sqhd->skhd", own_dscores, query_all, preferred_element_type=jnp.float32)
        * score_scale
    )
    grad_values = jnp.einsum(
        "shqk,sqhd->skhd", to_low(own_probs), dmixed_all, preferred_element_type=jnp.float32
    )
    grad_keys_low = to_low(grad_keys.reshape(row_total, model_width))
    grad_values_low = to_low(grad_values.reshape(row_total, model_width))
    grad_qkv_low = jnp.concatenate([grad_query_low, grad_keys_low, grad_values_low], axis=1)
    grad_qkv_w = product_tn(normed, grad_qkv_low)
    grad_normed = product_nt(grad_qkv_low, qkv_w)
    ignored_four, first_pull = jax.vjp(layer_norm, hidden, vec_rows[0], vec_rows[1])
    grad_hid_norm, grad_gain_one, grad_shift_one = first_pull(grad_normed)
    grad_hidden = grad_attended + grad_hid_norm
    grad_vec = jnp.stack(
        [
            grad_gain_one,
            grad_shift_one,
            jnp.sum(grad_query_low.astype(jnp.float32), axis=0),
            jnp.sum(grad_values_low.astype(jnp.float32), axis=0),
            jnp.sum(grad_attended, axis=0),
            grad_gain_two,
            grad_shift_two,
            jnp.sum(grad_fed, axis=0),
            jnp.sum(grad_out, axis=0),
        ]
    )
    grad_inner = jnp.concatenate(
        [
            jnp.sum(grad_inner_low.astype(jnp.float32), axis=0),
            jnp.sum(grad_latent_low.astype(jnp.float32), axis=0),
        ]
    )
    return (
        grad_hidden,
        (
            grad_qkv_w,
            grad_out_w,
            grad_in_w,
            grad_back_w,
            grad_latent_w,
            grad_decode_w,
            grad_vec,
            grad_inner,
            grad_mean_rows,
            grad_logvars,
        ),
    )


def per_device(
    cell_input,
    lengths,
    noise_draw,
    cotangent,
    w_qkv,
    w_out,
    w_ffn_in,
    w_ffn_out,
    w_latent,
    w_decode,
    vectors,
    inner_bias,
    prior_means,
    prior_logvars,
):
    slot_count = cell_input.shape[1]
    slot_span = cell_input.shape[2]
    model_width = cell_input.shape[3]
    row_total = slot_count * slot_span
    lat_width = noise_draw.shape[-1]
    cycle_size = lax.axis_size("blk")
    score_scale = 1.0 / math.sqrt(HEAD_DIM)
    slide_len = lengths[0]
    positions = lax.axis_index("blk") * slot_span + jnp.arange(slot_span)
    live_rows = (positions[None, :] < slide_len[:, None]).reshape(row_total)
    hidden = cell_input[0].reshape(row_total, model_width).astype(jnp.float32)
    stacks = (
        w_qkv,
        w_out,
        w_ffn_in,
        w_ffn_out,
        w_latent,
        w_decode,
        vectors,
        inner_bias,
        prior_means,
        prior_logvars,
    )
    layer_idx = 0
    full_weights = gather_weights([stacked[layer_idx] for stacked in stacks])
    kept_weights = [full_weights]
    hidden, kl_part, saved_state = layer_forward(
        hidden,
        full_weights,
        noise_draw[layer_idx, 0].reshape(row_total, lat_width),
        live_rows,
        slide_len,
        score_scale,
    )
    saved_layers = [saved_state]
    layer_out = hidden.reshape(1, slot_count, slot_span, model_width)
    kl_total = lax.psum(kl_part, ("grp", "blk"))
    kl_mean = kl_total / (lax.axis_size("grp") * cycle_size * row_total)
    grad_rows = cotangent[0].reshape(row_total, model_width).astype(jnp.float32)
    reduced = [None] * LAYERS
    for layer_idx in reversed(range(LAYERS)):
        full_weights = kept_weights[layer_idx]
        grad_rows, grads = layer_backward(
            grad_rows,
            full_weights,
            saved_layers[layer_idx],
            noise_draw[layer_idx, 0].reshape(row_total, lat_width),
            live_rows,
            slide_len,
            score_scale,
        )
        reduced[layer_idx] = reduce_grads(grads)
    grad_cells = grad_rows.reshape(1, slot_count, slot_span, model_width)
    stacked_grads = [jnp.stack([reduced[0][member]]) for member in range(10)]
    return (
        layer_out,
        grad_cells,
        kl_mean,
        stacked_grads[0],
        stacked_grads[1],
        stacked_grads[2],
        stacked_grads[3],
        stacked_grads[4],
        stacked_grads[5],
        stacked_grads[6],
        stacked_grads[7],
        stacked_grads[8],
        stacked_grads[9],
    )


EVERY = ("grp", "z", "y", "x")
CHIPS = ("z", "y", "x")
PLANE = ("grp", "y", "x")
PAIR = 2 * HEAD_DIM
SMALL = 16
VMEM_LIMIT = 20 * 1024 * 1024


def hop(values, axis, step=1):
    size = lax.axis_size(axis)
    return lax.ppermute(values, axis, [(i, i ^ step) for i in range(size)])


def other_core(values):
    return hop(values, "grp")


def after(values, done):
    return lax.optimization_barrier((values, done))[0]


def ordered(own, other, axis_name, axis):
    first = lax.axis_index(axis_name) == 0
    return jnp.concatenate(
        [jnp.where(first, own, other), jnp.where(first, other, own)], axis=axis
    )


def half_of(values, axis, axis_name, mine):
    part = values.shape[axis] // 2
    place = lax.axis_index(axis_name)
    place = place if mine else 1 - place
    return lax.dynamic_slice_in_dim(values, place * part, part, axis)


def flip(place, step):
    high = (place // 2 + step // 2) % 2
    low_bit = (place % 2 + step % 2) % 2
    return high * 2 + low_bit


def slide_routes(k):
    return [
        (g * 4 + z, (z // 2) * 4 + 2 * g + ((z % 2) ^ k)) for g in range(2) for z in range(4)
    ]


def pick_slot(slots, k):
    odd = (lax.axis_index("z") + k) % 2 == 1
    return jnp.where(odd, slots[1], slots[0])


def to_slides(slots):
    return jnp.stack(
        [lax.ppermute(pick_slot(slots, k), ("grp", "z"), slide_routes(k)) for k in range(2)]
    )


def from_slides(blocks):
    came = [
        lax.ppermute(
            blocks[k], ("grp", "z"), [(there, here) for here, there in slide_routes(k)]
        )
        for k in range(2)
    ]
    return jnp.stack([pick_slot(came, 0), pick_slot(came, 1)])


def head_routes(single, k):
    routes = []
    for core in range(2):
        for chip in range(16):
            odd = chip % 2
            block = 3 * chip + (2 - 2 * odd if single else odd)
            pair = (block % 16) // 2
            plane = 2 * core + (odd ^ k)
            target = (pair // 4) * 16 + plane * 4 + pair % 4
            routes.append((core * 16 + chip, target))
    return routes


ARRIVALS = [(single, k) for k in range(2) for single in (False, True)]


def low_shape(*shape):
    return jax.ShapeDtypeStruct(shape, jnp.bfloat16)


def wide(values):
    return values.astype(jnp.float32)


def z_hops(values):
    return [hop(values[step - 1], "z", step) for step in (1, 2, 3)]


def plane_hops(values):
    return [
        hop(values[0], "x"),
        hop(values[1], "y"),
        lax.ppermute(values[2], ("y", "x"), [(i, i ^ 3) for i in range(4)]),
    ]


NEAR = ((0, 0), (0, 1), (1, 0), (1, 1))


def z_at(step, part):
    return pl.ds(pl.multiple_of(flip(lax.axis_index("z"), step) * part, part), part)


def chip_place(step):
    return flip(lax.axis_index("y"), step[0]) * 2 + flip(lax.axis_index("x"), step[1])


def wide_shape(*shape):
    return jax.ShapeDtypeStruct(shape, jnp.float32)


FLOPS_PER_US = 1.1e9
TIMES = {
    "attend_body": 10.0,
    "feed_body": 3.5,
    "bottle_body": 5.7,
    "feed_back_body": 2.0,
    "pair_grad_body": 3.4,
    "attend_back_body": 9.2,
    "whole_grads_body": 1.3,
    "cells_back_body": 1.4,
}


def took(body):
    inner = body.func if isinstance(body, functools.partial) else body
    return TIMES.get(inner.__name__, 0.8)


def whole_call(
    body, operands, out_shapes, scratch=(), left_out=(), loaded=(), kept=(), early=False
):
    vmem, hbm = pl.BlockSpec(memory_space=pltpu.VMEM), pl.BlockSpec(memory_space=pltpu.HBM)
    n_in, n_out, n_own = len(operands), len(out_shapes), len(scratch)
    left_out, loaded, kept = list(left_out), list(loaded), list(kept)

    def run(*refs):
        ins, outs = list(refs[:n_in]), list(refs[n_in : n_in + n_out])
        own = refs[n_in + n_out : n_in + n_out + n_own]
        rest = refs[n_in + n_out + n_own :]
        in_copies = []
        for at, i in enumerate(loaded):
            in_copies.append(pltpu.make_async_copy(ins[i], rest[at], rest[-1].at[at]))
            ins[i] = rest[at]
        for copy in in_copies:
            copy.start()
        out_copies = {}
        for at, i in enumerate(kept, len(loaded)):
            out_copies[i] = pltpu.make_async_copy(rest[at], outs[i], rest[-1].at[at])
            outs[i] = rest[at]
        for copy in in_copies:
            copy.wait()
        started = []

        def store(i):
            out_copies[i].start()
            started.append(i)

        body(*ins, *outs, *own, **({"store": store} if early else {}))
        for i in out_copies:
            if i not in started:
                out_copies[i].start()
        for copy in out_copies.values():
            copy.wait()

    operands = [
        pltpu.with_memory_space_constraint(part, pltpu.HBM)
        if i in loaded
        else part
        for i, part in enumerate(operands)
    ]
    buffers = [pltpu.VMEM(operands[i].shape, operands[i].dtype) for i in loaded]
    buffers += [pltpu.VMEM(out_shapes[i].shape, out_shapes[i].dtype) for i in kept]
    if buffers:
        buffers.append(pltpu.SemaphoreType.DMA((len(buffers),)))
    out_shapes = [
        pltpu.HBM(part.shape, part.dtype) if i in kept else part
        for i, part in enumerate(out_shapes)
    ]
    return pl.pallas_call(
        run,
        out_shape=out_shapes,
        in_specs=[hbm if i in left_out or i in loaded else vmem for i in range(n_in)],
        out_specs=[hbm if i in kept else vmem for i in range(n_out)],
        scratch_shapes=[*scratch, *buffers],
        compiler_params=pltpu.CompilerParams(vmem_limit_bytes=VMEM_LIMIT),
        cost_estimate=pl.CostEstimate(
            flops=int(took(body) * FLOPS_PER_US), bytes_accessed=0, transcendentals=0
        ),
    )(*operands)


def enter_body(cells_ref, lens_ref, vectors_ref, inner_ref, means_ref, logvars_ref, *outs):
    span = cells_ref.shape[0] // 2
    lens = lens_ref[...]
    lens = jnp.concatenate([lens >> 5, lens & 31], axis=1).astype(jnp.float32)
    for k, ref in enumerate(outs):
        slot = (lax.axis_index("z") + k) % 2
        ref[:span] = cells_ref[pl.ds(pl.multiple_of(slot * span, span), span)]
        ref[span:] = jnp.zeros((SMALL, ref.shape[1]), jnp.bfloat16)
        ref[span : span + 9, 0:64] = vectors_ref[...]
        ref[span:, 128:160] = means_ref[...]
        ref[span:, 256:288] = logvars_ref[...]
        ref[span : span + 1, 384:704] = inner_ref[...]
        ref[span : span + 1, 768:772] = to_low(lens)


def chunk_place(block, step=(0, 0), core_step=0):
    core = flip(lax.axis_index("grp"), core_step)
    return pl.multiple_of(((block * 4 + chip_place(step)) * 2 + core) * 128, 128)


LAT_ROW, FF_ROW, LEN_ROW = 9, 10, 11


def unpack(small_ref, vec_ref, means_ref, logvars_ref, inner_ref):
    count = small_ref.shape[0]

    def lanes(row, rows, first, width):
        return jnp.concatenate(
            [wide(small_ref[i, row : row + rows, first : first + width]) for i in range(count)],
            axis=1,
        )

    vec_ref[...] = lanes(0, SMALL, 0, vec_ref.shape[1] // count)
    means_ref[...] = lanes(0, SMALL, 128, means_ref.shape[1] // count)
    logvars_ref[...] = lanes(0, SMALL, 256, means_ref.shape[1] // count)
    inner_ref[...] = lanes(0, 1, 384, inner_ref.shape[1] // count)
    width = vec_ref.shape[1]
    vec_ref[LAT_ROW : LAT_ROW + 1] = inner_ref[:, inner_ref.shape[1] - width :]
    for block in range(4):
        vec_ref[FF_ROW : FF_ROW + 1, block * 128 : block * 128 + 128] = inner_ref[
            :, pl.ds(chunk_place(block), 128)
        ]
    lens = wide(small_ref[0, 0:1, 768:896])
    even = lax.axis_index("z") % 2 == 0
    high = jnp.where(even, lens[:, 0:1], lens[:, 1:2])
    rest = jnp.where(even, lens[:, 2:3], lens[:, 3:4])
    vec_ref[LEN_ROW : LEN_ROW + 1] = jnp.broadcast_to(high * 32 + rest, (1, width))


def row_stats(values):
    centre = values - jnp.mean(values, axis=-1, keepdims=True)
    scale = lax.rsqrt(jnp.mean(centre * centre, axis=-1, keepdims=True) + EPS_NORM)
    return centre * scale, scale


def norm_back(grad, unit, scale, gain):
    inner = grad * gain
    along = jnp.mean(inner * unit, axis=-1, keepdims=True)
    return scale * (inner - jnp.mean(inner, axis=-1, keepdims=True) - unit * along)


def column_sum(values):
    return jnp.sum(values, axis=0, keepdims=True)


def slide_place(core, block, k, row, span):
    zi = lax.axis_index("z")
    chip = (core * 2 + ((zi + k) & 1)) * 4 + block
    return chip * span + row


def head_lanes(rows):
    return lax.broadcasted_iota(jnp.int32, (rows, PAIR), 1) < HEAD_DIM


def own_pair():
    place = (lax.axis_index("grp") * 2 + lax.axis_index("y")) * 2 + lax.axis_index("x")
    return pl.multiple_of(place * PAIR, PAIR)


def head_row(single, k):
    place = (lax.axis_index("grp") * 2 + lax.axis_index("y")) * 2 + lax.axis_index("x")
    parity = (lax.axis_index("z") + k) % 2
    row = 0
    for role in range(3):
        block = 16 * role + 2 * place
        split = (block % 3) // 2
        odd = (block // 3) % 2
        if single:
            here = split * PAIR * role + split * HEAD_DIM * ((odd + parity) % 2)
        else:
            here = (1 - split) * (1 - (odd + parity) % 2) * PAIR * role
        row = row + here
    return pl.multiple_of(row, HEAD_DIM)


def device_place(step, core_step):
    return flip(lax.axis_index("grp"), core_step) * 4 + chip_place(step)


def attend_body(own_ref, other_ref, *refs):
    came, rest = refs[:4], refs[4:]
    vec_ref, means_ref, logvars_ref, normed_ref, qkv_ref, head_w_ref = rest[:6]
    mixed_ref, lse_ref, bias_ref, small_ref, inner_ref = rest[6:]
    span = own_ref.shape[2] - SMALL
    for core_step, ref in enumerate((own_ref, other_ref)):
        for i, step in enumerate(NEAR):
            place = device_place(step, core_step)
            for k in range(2):
                chip = ((place // 4) * 2 + (lax.axis_index("z") + k) % 2) * 4 + place % 4
                small_ref[chip] = ref[i, k, span:]
    unpack(small_ref, vec_ref, means_ref, logvars_ref, inner_ref)
    for ref, (single, k) in zip(came, ARRIVALS):
        head_w_ref[pl.ds(head_row(single, k), ref.shape[0])] = ref[...]
    total_rows = normed_ref.shape[0]
    gain, shift = vec_ref[0:1], vec_ref[1:2]
    bias_q = vec_ref[2:3, pl.ds(own_pair(), PAIR)]
    bias_v = vec_ref[3:4, pl.ds(own_pair(), PAIR)]
    for core_step, ref in enumerate((own_ref, other_ref)):
        for i, step in enumerate(NEAR):
            cells = jnp.concatenate([ref[i, 0, :span], ref[i, 1, :span]])
            unit, _ = row_stats(wide(cells))
            at = device_place(step, core_step) * (2 * span)
            normed_ref[pl.ds(pl.multiple_of(at, 2 * span), 2 * span)] = to_low(unit * gain + shift)
    step = 256
    for start in range(0, total_rows, step):
        qkv = product_nt(normed_ref[start : start + step], head_w_ref[...])
        qkv_ref[start : start + step, :PAIR] = to_low(
            wide(to_low(qkv[:, :PAIR] + bias_q)) * HEAD_DIM**-0.5
        )
        qkv_ref[start : start + step, PAIR : 2 * PAIR] = to_low(qkv[:, PAIR : 2 * PAIR])
        qkv_ref[start : start + step, 2 * PAIR :] = to_low(qkv[:, 2 * PAIR :] + bias_v)
    lane = lax.broadcasted_iota(jnp.int32, (1, total_rows), 1)
    place = slide_place(
        lane // (8 * span), (lane // (2 * span)) & 3, (lane // span) & 1, lane & (span - 1), span
    )
    bias = jnp.where(place.astype(jnp.float32) < vec_ref[LEN_ROW : LEN_ROW + 1], 0.0, MASKED)
    bias_ref[...] = bias
    keys = qkv_ref[:, PAIR : 2 * PAIR]
    values = qkv_ref[:, 2 * PAIR :]
    first_head = head_lanes(step)
    for start in range(0, total_rows, step):
        query = qkv_ref[start : start + step, :PAIR]
        outs, totals = [], []
        for head in range(2):
            mine = first_head if head == 0 else jnp.logical_not(first_head)
            part = jnp.where(mine, query, jnp.zeros_like(query))
            scores = product_nt(part, keys) + bias
            peak = jnp.max(scores, axis=-1, keepdims=True)
            weights = jnp.exp(scores - peak)
            total = jnp.sum(weights, axis=-1, keepdims=True)
            outs.append(product(to_low(weights / total), values))
            totals.append(jnp.broadcast_to(peak + jnp.log(total), (step, PAIR)))
        mixed_ref[start : start + step] = to_low(jnp.where(first_head, outs[0], outs[1]))
        lse_ref[start : start + step] = jnp.where(first_head, totals[0], totals[1])


def attend(own, other, came, lat, inner):
    rows, width = 16 * (own.shape[2] - SMALL), own.shape[3]
    return whole_call(
        attend_body,
        (own, other, *came),
        [
            wide_shape(SMALL, width),
            wide_shape(SMALL, lat),
            wide_shape(SMALL, lat),
            low_shape(rows, width),
            low_shape(rows, 3 * PAIR),
            low_shape(3 * PAIR, width),
            low_shape(rows, PAIR),
            wide_shape(rows, PAIR),
            wide_shape(1, rows),
        ],
        [
            pltpu.VMEM((16, SMALL, width), jnp.bfloat16),
            pltpu.VMEM((1, inner), jnp.float32),
        ],
        loaded=range(2, 6),
    )


def side_rows(ref, core_step, start, rows):
    first = flip(lax.axis_index("grp"), core_step) * (ref.shape[0] // 2) + start
    return ref[pl.ds(pl.multiple_of(first, rows), rows)]


def mix_far_body(mixed_ref, out_t_ref, far_ref):
    for start in range(0, far_ref.shape[0], 256):
        far_ref[start : start + 256] = to_low(
            product_nt(side_rows(mixed_ref, 1, start, 256), out_t_ref[...])
        )


def mix_near_body(mixed_ref, out_t_ref, came_ref, keep_ref, *sends):
    rows = keep_ref.shape[0]
    for i, step in enumerate(NEAR):
        first = chip_place(step) * rows
        came = came_ref[pl.ds(pl.multiple_of(first, rows), rows)]
        part = product_nt(side_rows(mixed_ref, 0, first, rows), out_t_ref[...]) + wide(came)
        if i == 0:
            keep_ref[...] = part
        else:
            sends[i - 1][...] = to_low(part)


def part_shapes(rows, width):
    return [wide_shape(rows, width)] + [low_shape(rows, width)] * 3


def mix_out(mixed, out_t, ready):
    rows, width = mixed.shape[0], out_t.shape[0]
    (far,) = whole_call(mix_far_body, (mixed, out_t), [low_shape(rows // 2, width)])
    keep, *sends = whole_call(
        mix_near_body, (mixed, out_t, after(other_core(far), ready)), part_shapes(rows // 8, width)
    )
    return keep, *plane_hops(sends)


def out_grad_body(*refs):
    pieces, mixed_ref, out_ref, datt_ref, sems = refs[:8], *refs[8:]
    stack_rows(pieces, datt_ref, sems, lambda i: device_place(NEAR[i % 4], i // 4))
    rows = out_ref.shape[1]
    for chip in range(0, out_ref.shape[0], 4):
        lanes = slice(chip * rows, (chip + 4) * rows)
        grad = to_low(product_tn(datt_ref[:, lanes], mixed_ref[...]))
        out_ref[chip : chip + 4] = grad.reshape(4, rows, PAIR)


def out_grads(pieces, mixed):
    rows, width = pieces[0].shape
    return whole_call(
        out_grad_body,
        (*pieces, mixed),
        [low_shape(16, width // 16, PAIR), low_shape(8 * rows, width)],
        [pltpu.SemaphoreType.DMA((8,))],
        range(8),
    )


def attend_back_body(
    qkv_ref,
    bias_ref,
    lse_ref,
    out_t_ref,
    head_w_ref,
    datt_ref,
    dqkv_ref,
    far_ref,
    dmixed_ref,
    dk_ref,
    dv_ref,
):
    rows = qkv_ref.shape[0]
    for start in range(0, rows, 256):
        at = slice(start, start + 256)
        dmixed_ref[at] = to_low(product(datt_ref[at], out_t_ref[...]))
    keys = qkv_ref[:, PAIR : 2 * PAIR]
    values = qkv_ref[:, 2 * PAIR :]
    bias = bias_ref[...]
    step = 256
    first_head = head_lanes(step)
    for start in range(0, rows, step):
        query = qkv_ref[start : start + step, :PAIR]
        dmixed = dmixed_ref[start : start + step]
        dqueries = []
        for head in range(2):
            mine = first_head if head == 0 else jnp.logical_not(first_head)
            part = jnp.where(mine, query, jnp.zeros_like(query))
            dpart = jnp.where(mine, dmixed, jnp.zeros_like(dmixed))
            lse = lse_ref[start : start + step, head * HEAD_DIM : head * HEAD_DIM + 1]
            probs = jnp.exp(product_nt(part, keys) + bias - lse)
            dprobs = product_nt(dpart, values)
            centre = jnp.sum(dprobs * probs, axis=-1, keepdims=True)
            dscores = to_low(probs * (dprobs - centre))
            dqueries.append(product(dscores, keys))
            dkeys = product_tn(dscores, part)
            dvalues = product_tn(to_low(probs), dpart)
            if start == 0 and head == 0:
                dk_ref[...] = dkeys
                dv_ref[...] = dvalues
            else:
                dk_ref[...] += dkeys
                dv_ref[...] += dvalues
        dquery = jnp.where(first_head, dqueries[0], dqueries[1]) * (HEAD_DIM**-0.5)
        dqkv_ref[start : start + step, :PAIR] = to_low(dquery)
    dqkv_ref[:, PAIR : 2 * PAIR] = to_low(dk_ref[...])
    dqkv_ref[:, 2 * PAIR :] = to_low(dv_ref[...])
    for start in range(0, rows // 2, step):
        far_ref[start : start + step] = to_low(
            product(side_rows(dqkv_ref, 1, start, step), head_w_ref[...])
        )


def attend_back(qkv, bias, lse, out_t, head_w, datt):
    rows, width = qkv.shape[0], head_w.shape[1]
    return whole_call(
        attend_back_body,
        (qkv, bias, lse, out_t, head_w, datt),
        [low_shape(rows, 3 * PAIR), low_shape(rows // 2, width)],
        [
            pltpu.VMEM((rows, PAIR), jnp.bfloat16),
            pltpu.VMEM((rows, PAIR), jnp.float32),
            pltpu.VMEM((rows, PAIR), jnp.float32),
        ],
    )


def dnormed_body(dqkv_ref, head_w_ref, came_ref, keep_ref, *sends):
    rows = keep_ref.shape[0]
    for i, step in enumerate(NEAR):
        first = chip_place(step) * rows
        came = came_ref[pl.ds(pl.multiple_of(first, rows), rows)]
        part = product(side_rows(dqkv_ref, 0, first, rows), head_w_ref[...]) + wide(came)
        if i == 0:
            keep_ref[...] = part
        else:
            sends[i - 1][...] = to_low(part)


def dnormed(dqkv, head_w, came):
    rows, width = dqkv.shape[0] // 8, head_w.shape[1]
    return whole_call(dnormed_body, (dqkv, head_w, came), part_shapes(rows, width))


def head_grad_body(dqkv_ref, normed_ref, *refs):
    homes, sums_ref, grad_w_ref = refs[:4], refs[4], refs[5]
    dqkv = dqkv_ref[...]
    sums_ref[...] = column_sum(wide(dqkv))
    grad_w_ref[...] = to_low(product_tn(dqkv, normed_ref[...]))
    for ref, (single, k) in zip(homes, ARRIVALS):
        ref[...] = grad_w_ref[pl.ds(head_row(single, k), ref.shape[0])]


def head_grads(dqkv, normed):
    width = normed.shape[1]
    outs = whole_call(
        head_grad_body,
        (dqkv, normed),
        [low_shape(HEAD_DIM if single else PAIR, width) for single, _ in ARRIVALS]
        + [wide_shape(1, 3 * PAIR)],
        [pltpu.VMEM((3 * PAIR, width), jnp.bfloat16)],
    )
    return outs[:4], outs[4]


def home_body(*refs):
    pair = wide(refs[0][...]) + wide(refs[2][...])
    single = wide(refs[1][...]) + wide(refs[3][...])
    odd = lax.axis_index("x") % 2
    refs[4][pl.ds(pl.multiple_of(odd * HEAD_DIM, HEAD_DIM), PAIR)] = pair
    refs[4][pl.ds(pl.multiple_of((1 - odd) * PAIR, HEAD_DIM), HEAD_DIM)] = single


LAT_LANES, DEC_LANES = slice(0, 512), slice(512, 768)


def project_body(
    keep_ref, came_x_ref, came_y_ref, came_far_ref, blocks_ref, vec_ref, attended_ref, normed_ref, hidden_ref
):
    span = blocks_ref.shape[1] - SMALL
    hidden = jnp.concatenate([blocks_ref[0, :span], blocks_ref[1, :span]])
    hidden_ref[...] = hidden
    parts = z_sum((keep_ref, came_x_ref, came_y_ref, came_far_ref))
    total = wide(hidden) + parts + vec_ref[4:5]
    attended_ref[...] = total
    unit, _ = row_stats(total)
    normed_ref[...] = to_low(unit * vec_ref[5:6] + vec_ref[6:7])


def project(parts, blocks, vec):
    shape = parts[0].shape
    return whole_call(
        project_body,
        (*parts, blocks, vec),
        [wide_shape(*shape), low_shape(*shape), low_shape(*shape)],
    )


GELU_SCALE = math.sqrt(2.0 / math.pi)
GELU_CUBE = 0.044715


def stack_rows(refs, target_ref, sems, order=None):
    rows = refs[0].shape[0]
    copies = []
    for i, ref in enumerate(refs):
        place = i if order is None else order(i)
        target = target_ref.at[pl.ds(pl.multiple_of(place * rows, rows), rows)]
        copies.append(pltpu.make_async_copy(ref, target, sems.at[i]))
    for copy in copies:
        copy.start()
    for copy in copies:
        copy.wait()


FF_STEP = 256


def load_all(rows_in, weights_ref, all_ref, in_ref, back_ref, sems):
    copies = []
    for i, ref in enumerate(rows_in):
        rows = ref.shape[0]
        copies.append((ref, all_ref.at[i * rows : (i + 1) * rows]))
    for z in range(4):
        part = weights_ref.at[z * 256 : z * 256 + 256]
        copies.append((part.at[:128], in_ref.at[z * 128 : (z + 1) * 128]))
        for half in range(2):
            at = z * 256 + half * 128
            copies.append(
                (part.at[128:, half * 512 : half * 512 + 512], back_ref.at[at : at + 128])
            )
    copies = [pltpu.make_async_copy(*copy, sems.at[i]) for i, copy in enumerate(copies)]
    for copy in copies:
        copy.start()
    for copy in copies:
        copy.wait()


def feed_scratch(rows, width, hidden):
    return [
        pltpu.VMEM((rows, width), jnp.bfloat16),
        pltpu.VMEM((hidden, width), jnp.bfloat16),
        pltpu.VMEM((width, hidden), jnp.bfloat16),
        pltpu.SemaphoreType.DMA((16,)),
    ]


def feed_body(*refs, last):
    rows_in, weights_ref, vec_ref, rest = refs[:4], refs[4], refs[5], list(refs[6:])
    came_ref = rest.pop(0) if last else None
    (act_ref, slope_ref), outs = rest[:2], rest[2:-4]
    all_ref, in_ref, back_ref, sems = rest[-4:]
    load_all(rows_in, weights_ref, all_ref, in_ref, back_ref, sems)
    bias = vec_ref[FF_ROW : FF_ROW + 1, : in_ref.shape[0]]
    step = rows_in[0].shape[0] * 2
    for start in range(0, all_ref.shape[0], step):
        at = slice(start, start + step)
        total = None
        for unit in range(0, in_ref.shape[0], FF_STEP):
            lanes = slice(unit, unit + FF_STEP)
            inner = product_nt(all_ref[at], in_ref[lanes]) + bias[:, lanes]
            square = inner * inner
            bend = jnp.tanh(GELU_SCALE * (inner + GELU_CUBE * (inner * square)))
            half = 0.5 * (1.0 + bend)
            act = to_low(inner * half)
            act_ref[at, lanes] = act
            slope_ref[at, lanes] = half + (0.5 * GELU_SCALE) * inner * (1.0 - bend * bend) * (
                1.0 + (3.0 * GELU_CUBE) * square
            )
            part = product_nt(act, back_ref[:, lanes])
            total = part if total is None else total + part
        put_parts(outs, came_ref, start, total)


def put_parts(outs, came_ref, start, total):
    if came_ref is None:
        outs[0][start : start + total.shape[0]] = to_low(total)
        return
    total = total + wide(came_ref[start : start + total.shape[0]])
    rows = outs[0].shape[0]
    for i in range(start // rows, (start + total.shape[0]) // rows):
        piece = total[i * rows - start : (i + 1) * rows - start]
        outs[i][...] = piece if i == 0 else to_low(piece)


def feed_call(body, pieces, weights, more, came, side_shapes):
    rows, width = pieces[0].shape
    last = came is not None
    operands = (*pieces, weights, *more) + ((came,) if last else ())
    outs = part_shapes(rows, width) if last else [low_shape(4 * rows, width)]
    return whole_call(
        functools.partial(body, last=last),
        operands,
        side_shapes + outs,
        feed_scratch(4 * rows, width, 512),
        range(5),
    )


def feed(pieces, weights, vec, came=None):
    count = 4 * pieces[0].shape[0]
    return feed_call(
        feed_body, pieces, weights, (vec,), came, [low_shape(count, 512), wide_shape(count, 512)]
    )


def feed_back_body(*refs, last):
    rows_in, weights_ref, slope_ref, rest = refs[:4], refs[4], refs[5], list(refs[6:])
    came_ref = rest.pop(0) if last else None
    (du_ref, sums_ref), outs = rest[:2], rest[2:-4]
    all_ref, in_ref, back_ref, sems = rest[-4:]
    load_all(rows_in, weights_ref, all_ref, in_ref, back_ref, sems)
    sums = [None] * (in_ref.shape[0] // FF_STEP)
    step = rows_in[0].shape[0] * 2
    for start in range(0, all_ref.shape[0], step):
        at = slice(start, start + step)
        total = None
        for i in range(len(sums)):
            lanes = slice(i * FF_STEP, (i + 1) * FF_STEP)
            du = to_low(product(all_ref[at], back_ref[:, lanes]) * slope_ref[at, lanes])
            du_ref[at, lanes] = du
            summed = column_sum(wide(du))
            sums[i] = summed if sums[i] is None else sums[i] + summed
            part = product(du, in_ref[lanes])
            total = part if total is None else total + part
        put_parts(outs, came_ref, start, total)
    for i, summed in enumerate(sums):
        sums_ref[:, i * FF_STEP : (i + 1) * FF_STEP] = summed


def feed_back(pieces, weights, slope, came=None):
    count = 4 * pieces[0].shape[0]
    return feed_call(
        feed_back_body,
        pieces,
        weights,
        (slope,),
        came,
        [low_shape(count, 512), wide_shape(1, 512)],
    )


def plane_rows(values):
    near = [values, *plane_hops([values] * 3)]
    return (*near, *(other_core(part) for part in near))


GRAD_ROWS = 448


def pair_grad_body(*refs):
    fed_in, two_in, whole_ref, halves = refs[:8], refs[8:16], refs[16], refs[17:21]
    out_ref, fed_ref, two_ref, act_ref, du_ref, sems = refs[21:]
    copies = []
    for pieces, target in ((fed_in, fed_ref), (two_in, two_ref), (halves[:2], act_ref), (halves[2:], du_ref)):
        rows = pieces[0].shape[0]
        for i, ref in enumerate(pieces):
            copies.append((ref, target.at[i * rows : (i + 1) * rows]))
    copies = [pltpu.make_async_copy(*copy, sems.at[i]) for i, copy in enumerate(copies)]
    for copy in copies:
        copy.start()
    for copy in copies:
        copy.wait()
    width = whole_ref.shape[1]
    for z in range(out_ref.shape[0] // GRAD_ROWS):
        at = z * GRAD_ROWS
        for lane in range(0, out_ref.shape[1], 512):
            lanes = slice(lane, lane + 512)
            out_ref[at : at + 128, lanes] = to_low(
                product_tn(du_ref[:, z * 128 : (z + 1) * 128], two_ref[:, lanes])
            )
        grad = to_low(product_tn(fed_ref[:, z * 256 : (z + 1) * 256], act_ref[...]))
        out_ref[at + 128 : at + 256] = jnp.concatenate([grad[:128], grad[128:]], axis=1)
        out_ref[at + 256 : at + GRAD_ROWS, :width] = whole_ref[z * 256 : z * 256 + 192]
        for piece in range(3):
            out_ref[at + 256 + piece * 64 : at + 320 + piece * 64, width:] = whole_ref[
                z * 256 + 192 : (z + 1) * 256, piece * 256 : (piece + 1) * 256
            ]


def pair_grads(rows_fed, rows_two, whole, acts, dus):
    rows, width = rows_fed[0].shape
    hidden = acts[0].shape[1]
    return whole_call(
        pair_grad_body,
        (*rows_fed, *rows_two, whole, *acts, *dus),
        [low_shape(4 * GRAD_ROWS, width)],
        [pltpu.VMEM((8 * rows, width), jnp.bfloat16)] * 2
        + [pltpu.VMEM((8 * rows, hidden), jnp.bfloat16)] * 2
        + [pltpu.SemaphoreType.DMA((20,))],
        [*range(16), *range(17, 21)],
    )[0]


def split_grad_body(sum_ref, in_ref, *outs):
    in_ref[...] = wide(sum_ref[:128])
    rows, half = outs[0].shape[0], sum_ref.shape[1] // 2
    for i, step in enumerate(NEAR):
        place = chip_place(step)
        at = pl.ds(pl.multiple_of(128 + (place % 2) * rows, rows), rows)
        lanes = pl.ds(pl.multiple_of((place // 2) * half, half), half)
        outs[i][:, :half] = sum_ref[at, lanes]
        first = pl.multiple_of(256 + jnp.minimum(place, 2) * rows, rows)
        whole = sum_ref[pl.ds(first, rows), : outs[i].shape[1] - half]
        fourth = jnp.concatenate(
            [sum_ref[256 + q * rows : 256 + (q + 1) * rows, whole.shape[1] :] for q in range(3)],
            axis=1,
        )
        outs[i][:, half:] = jnp.where(place == 3, fourth, whole)


def z_sum(refs):
    total = wide(refs[0][...])
    for ref in refs[1:]:
        total = total + wide(ref[...])
    return total


def pick_body(out_ref, back_ref, pairs_ref, *outs):
    for chip in range(16):
        pair = pl.multiple_of((lax.axis_index("grp") * 4 + chip % 4) * PAIR, PAIR)
        pairs_ref[chip] = out_ref[:, pl.ds(pair, PAIR)]
    half = outs[0].shape[1]
    for i, (step, lane) in enumerate(zip((0, 1, 2, 1), (0, 0, 0, half))):
        for block in range(4):
            outs[step][:, lane + block * 128 : lane + (block + 1) * 128] = back_ref[
                :, pl.ds(chunk_place(block, NEAR[i]), 128)
            ]


def lay_body(in_ref, own_ref, came_x_ref, came_y_ref, out_ref):
    out_ref[:128] = in_ref[...]
    half = own_ref.shape[1]
    for i, (ref, lane) in enumerate(
        ((own_ref, 0), (came_x_ref, 0), (came_y_ref, 0), (came_y_ref, half))
    ):
        place = chip_place(NEAR[i])
        rows = pl.ds(pl.multiple_of(128 + (place % 2) * 64, 64), 64)
        out_ref[rows, pl.ds(pl.multiple_of((place // 2) * half, half), half)] = ref[
            :, lane : lane + half
        ]


def core_order(own, other):
    first = lax.axis_index("grp") == 0
    return jnp.concatenate(
        [jnp.where(first, own, other), jnp.where(first, other, own)], axis=1
    )


def core_halves(values):
    part = values.shape[1] // 2
    first = lax.axis_index("grp") == 0
    low_half, high_half = values[:, :part], values[:, part:]
    return (
        jnp.where(first, low_half, high_half),
        jnp.where(first, high_half, low_half),
    )


def halves_nt(values, own_ref, other_ref, lanes):
    own, other = core_halves(values)
    return product_nt(own, own_ref[:, lanes]) + product_nt(other, other_ref[:, lanes])


def bottle_body(
    attended_ref,
    keep_ref,
    came_x_ref,
    came_y_ref,
    came_far_ref,
    vec_ref,
    own_ref,
    other_ref,
    noise_ref,
    cot_ref,
    means_ref,
    logvars_ref,
    out_ref,
    fed_ref,
    sample_ref,
    dlat_ref,
    dfed_ref,
    dfed_low_ref,
    dmeans_ref,
    dlogvars_ref,
    sums_ref,
):
    rows, width = attended_ref.shape
    lat = noise_ref.shape[1]
    comps = means_ref.shape[0]
    parts = z_sum((keep_ref, came_x_ref, came_y_ref, came_far_ref))
    fed = attended_ref[...] + parts + vec_ref[7:8]
    fed_low = to_low(fed)
    fed_ref[...] = fed_low
    latent = halves_nt(fed_low, own_ref, other_ref, LAT_LANES) + vec_ref[LAT_ROW : LAT_ROW + 1]
    logvar = latent[:, lat:]
    noise = noise_ref[...]
    spread = jnp.exp(0.5 * logvar) * noise
    sample = latent[:, :lat] + spread
    sample_low = to_low(sample)
    sample_ref[...] = sample_low
    out_ref[...] = fed + halves_nt(sample_low, own_ref, other_ref, DEC_LANES) + vec_ref[8:9]
    cot = cot_ref[...]
    dsample = core_order(
        product(cot, own_ref[:, DEC_LANES]), product(cot, other_ref[:, DEC_LANES])
    )

    span = rows // 2
    row = lax.broadcasted_iota(jnp.int32, (rows, 1), 0)
    block = lax.axis_index("y") * 2 + lax.axis_index("x")
    place = slide_place(lax.axis_index("grp"), block, row // span, row & (span - 1), span)
    live = place.astype(jnp.float32) < vec_ref[LEN_ROW : LEN_ROW + 1, 0:1]
    share = jnp.where(live, 1.0 / lat, 0.0)
    own_term = jnp.sum(-0.5 * noise * noise - 0.5 * logvar, axis=-1, keepdims=True)
    logvars = logvars_ref[...]
    inverse = jnp.exp(-logvars)
    terms = []
    for c in range(comps):
        offset = sample - means_ref[c : c + 1]
        terms.append(
            jnp.sum(
                -0.5 * offset * offset * inverse[c : c + 1] - 0.5 * logvars[c : c + 1],
                axis=-1,
                keepdims=True,
            )
            - math.log(comps)
        )
    peak = terms[0]
    for term in terms[1:]:
        peak = jnp.maximum(peak, term)
    weights = [jnp.exp(term - peak) for term in terms]
    total = weights[0]
    for weight in weights[1:]:
        total = total + weight
    kl_cell = own_term - (peak + jnp.log(total))
    kl = jnp.sum(jnp.where(live, kl_cell, 0.0), axis=0, keepdims=True) / lat
    scale = share / total
    for c in range(comps):
        offset = sample - means_ref[c : c + 1]
        slope = offset * inverse[c : c + 1]
        part = weights[c] * scale
        pull = part * slope
        dsample = dsample + pull
        dmeans_ref[c : c + 1] = -column_sum(pull)
        dlogvars_ref[c : c + 1] = column_sum(0.5 * part - 0.5 * (pull * offset))
    dlat = jnp.concatenate([dsample, 0.5 * dsample * spread - 0.5 * share], axis=1)
    dlat_low = to_low(dlat)
    dlat_ref[...] = dlat_low
    grad_out = wide(cot)
    dfed = grad_out + core_order(
        product(dlat_low, own_ref[:, LAT_LANES]), product(dlat_low, other_ref[:, LAT_LANES])
    )
    dfed_ref[...] = dfed
    dfed_low_ref[...] = to_low(dfed)
    sums_ref[...] = jnp.concatenate(
        [
            column_sum(wide(dlat_low)),
            column_sum(dfed),
            column_sum(grad_out),
            jnp.broadcast_to(kl, (1, width)),
            jnp.zeros((4, width), jnp.float32),
        ]
    )


def bottle_call(attended, parts, vec, weights, noise, cot, means, logvars):
    rows, width = attended.shape
    lat = noise.shape[1]
    return whole_call(
        bottle_body,
        (attended, *parts, vec, *weights, noise, cot, means, logvars),
        [
            wide_shape(rows, width),
            low_shape(rows, width),
            low_shape(rows, lat),
            low_shape(rows, width),
            wide_shape(rows, width),
            low_shape(rows, width),
            wide_shape(*means.shape),
            wide_shape(*means.shape),
            wide_shape(8, width),
        ],
    )


def project_back_body(
    keep_ref,
    came_x_ref,
    came_y_ref,
    came_far_ref,
    attended_ref,
    dfed_ref,
    vec_ref,
    datt_ref,
    datt_low_ref,
    sums_ref,
):
    grad = z_sum((keep_ref, came_x_ref, came_y_ref, came_far_ref))
    unit, scale = row_stats(attended_ref[...])
    datt = dfed_ref[...] + norm_back(grad, unit, scale, vec_ref[5:6])
    datt_ref[...] = datt
    datt_low_ref[...] = to_low(datt)
    sums_ref[...] = jnp.concatenate(
        [
            column_sum(grad * unit),
            column_sum(grad),
            column_sum(datt),
            jnp.zeros((5, datt.shape[1]), jnp.float32),
        ]
    )


def project_back(parts, attended, dfed, vec):
    rows, width = attended.shape
    return whole_call(
        project_back_body,
        (*parts, attended, dfed, vec),
        [wide_shape(rows, width), low_shape(rows, width), wide_shape(8, width)],
    )


def whole_grads_body(*refs):
    out_ref = refs[-1]
    for lanes, (left, left_other, right, right_other) in (
        (LAT_LANES, refs[:4]),
        (DEC_LANES, refs[4:8]),
    ):
        grads = jnp.concatenate([left[...], left_other[...]])
        values = jnp.concatenate([core_halves(right[...])[0], core_halves(right_other[...])[0]])
        out_ref[:, lanes] = to_low(product_tn(grads, values))


def whole_grads(pairs):
    operands = []
    for values in pairs:
        operands += [values, other_core(values)]
    width = pairs[0].shape[1]
    return whole_call(whole_grads_body, operands, [low_shape(width, DEC_LANES.stop)])[0]


def sum_body(*refs):
    refs[-1][...] = z_sum(refs[:-1])


def last_grad_body(*refs):
    out_ref, wholes = refs[8], refs[9:]
    half = out_ref.shape[1] // 8
    for i, ref in enumerate(refs[:8]):
        for block in range(4):
            place = chunk_place(block, NEAR[i % 4], i // 4)
            out_ref[:, pl.ds(place, 128)] = wide(ref[:, block * 128 : (block + 1) * 128])
    for core in range(2):
        wholes[core][...] = z_sum([ref.at[:, half:] for ref in refs[core * 4 : core * 4 + 4]])


def cells_back_body(
    keep_ref,
    came_x_ref,
    came_y_ref,
    came_far_ref,
    hidden_ref,
    datt_ref,
    vec_ref,
    bottle_sums_ref,
    project_sums_ref,
    head_sums_ref,
    ff_sums_ref,
    ff_more_ref,
    dmeans_ref,
    dlogvars_ref,
    out_grad_ref,
    grad_ref,
    packed_ref,
    inner_ref,
    rows_ref,
):
    grad = z_sum((keep_ref, came_x_ref, came_y_ref, came_far_ref))
    unit, scale = row_stats(wide(hidden_ref[...]))
    grad_ref[...] = datt_ref[...] + norm_back(grad, unit, scale, vec_ref[0:1])
    width = grad.shape[1]
    count = packed_ref.shape[0]
    inner_ref[...] = jnp.zeros_like(inner_ref)
    for block in range(4):
        lanes = slice(block * 128, block * 128 + 128)
        inner_ref[:, pl.ds(chunk_place(block), 128)] = (
            ff_sums_ref[:, lanes] + ff_more_ref[:, lanes]
        )
    inner_ref[:, inner_ref.shape[1] - width :] = bottle_sums_ref[0:1]
    rows_ref[...] = jnp.zeros_like(rows_ref)
    rows_ref[0:1] = column_sum(grad * unit)
    rows_ref[1:2] = column_sum(grad)
    rows_ref[2:3, pl.ds(own_pair(), PAIR)] = head_sums_ref[:, :PAIR]
    rows_ref[3:4, pl.ds(own_pair(), PAIR)] = head_sums_ref[:, 2 * PAIR :]
    rows_ref[4:5] = project_sums_ref[2:3]
    rows_ref[5:7] = project_sums_ref[0:2]
    rows_ref[7:9] = bottle_sums_ref[1:3]
    part = width // count
    pieces = inner_ref.shape[1] // width
    for i in range(pieces):
        rows_ref[9 + i : 10 + i] = jnp.concatenate(
            [
                inner_ref[:, (b * pieces + i) * part : (b * pieces + i + 1) * part]
                for b in range(count)
            ],
            axis=1,
        )
    rows_ref[14:15] = bottle_sums_ref[3:4]
    lat_part = dmeans_ref.shape[1] // count
    for b in range(count):
        sums = jnp.concatenate(
            [
                rows_ref[:, b * part : (b + 1) * part],
                dmeans_ref[:, b * lat_part : (b + 1) * lat_part],
                dlogvars_ref[:, b * lat_part : (b + 1) * lat_part],
            ],
            axis=1,
        )
        high = to_low(sums)
        packed_ref[b, :part] = out_grad_ref[b]
        packed_ref[b, part : part + SMALL] = high
        packed_ref[b, part + SMALL :] = to_low(sums - wide(high))


def last_sum_body(came_ref, out_ref):
    count, rows = came_ref.shape[0], came_ref.shape[1] - 2 * SMALL
    for chip in range(4):
        total = z_sum([came_ref.at[z * 4 + chip, :rows] for z in range(4)])
        out_ref[:rows, chip * PAIR : (chip + 1) * PAIR] = total
    small = z_sum([came_ref.at[i, rows : rows + SMALL] for i in range(count)])
    rest = z_sum([came_ref.at[i, rows + SMALL :] for i in range(count)])
    out_ref[rows:] = jnp.zeros((SMALL, out_ref.shape[1]), jnp.float32)
    out_ref[rows:, :PAIR] = small + rest


def last_body(own_ref, other_ref, grad_ref, small_ref):
    rows, half = grad_ref.shape[0], own_ref.shape[1]
    for ref, place in ((own_ref, 0), (other_ref, 1)):
        core = flip(lax.axis_index("grp"), place)
        grad_ref[:, pl.ds(pl.multiple_of(core * half, half), half)] = ref[:rows]
    small_ref[...] = own_ref[rows:, :PAIR] + other_ref[rows:, :PAIR]


def cells_back(operands, inner):
    rows, width = operands[0].shape
    return whole_call(
        cells_back_body,
        operands,
        [wide_shape(rows, width), low_shape(16, width // 16 + 2 * SMALL, PAIR)],
        [pltpu.VMEM((1, inner), jnp.float32), pltpu.VMEM((SMALL, width), jnp.float32)],
    )


def exchange(blocks, axes):
    return lax.all_to_all(blocks, axes, split_axis=0, concat_axis=0, tiled=True)


def to_all(values, count):
    return jnp.broadcast_to(values[None], (count, *values.shape))


def fast_device(
    cell_input,
    lengths,
    noise_draw,
    cotangent,
    w_qkv,
    w_out,
    w_ffn_in,
    w_ffn_out,
    w_latent,
    w_decode,
    vectors,
    inner_bias,
    prior_means,
    prior_logvars,
):
    slots, span, width = cell_input.shape[1:]
    rows = slots * span
    lat = noise_draw.shape[-1]
    comps = prior_means.shape[1]
    ff = w_ffn_out.shape[1]
    inner = 16 * inner_bias.shape[1]

    part = width // 16
    shard = jnp.concatenate(
        [half_of(w[0], 0, "grp", True).T for w in (w_latent, w_decode)], axis=1
    )
    shard_width = shard.shape[1]
    whole = lax.all_gather(shard, CHIPS, axis=0, tiled=True)

    out_pairs, back_own, back_x, back_y = whole_call(
        pick_body,
        after((w_out[0].T, w_ffn_out[0].T), shard),
        [low_shape(16, part, PAIR)]
        + [low_shape(part, ff // 8 * count) for count in (1, 2, 1)],
    )
    out_t = exchange(out_pairs, CHIPS).reshape(width, PAIR)

    blocks = whole_call(
        enter_body,
        (
            after(cell_input.reshape(rows, width), out_pairs),
            lengths,
            vectors[0],
            inner_bias,
            prior_means[0],
            prior_logvars[0],
        ),
        [low_shape(span + SMALL, width)] * 2,
    )
    first = jnp.stack(
        [lax.ppermute(blocks[k], ("grp", "z"), slide_routes(k)) for k in range(2)]
    )

    qkv_t = w_qkv[0].T
    at_x = lax.axis_index("x") % 2
    head_parts = (
        lax.dynamic_slice_in_dim(qkv_t, at_x * HEAD_DIM, PAIR),
        lax.dynamic_slice_in_dim(qkv_t, (1 - at_x) * PAIR, HEAD_DIM),
    )
    came = [
        lax.ppermute(head_parts[int(single)], EVERY, head_routes(single, k))
        for single, k in ARRIVALS
    ]

    in_own = half_of(w_ffn_in[0], 1, "grp", True).T
    noise_high = to_low(noise_draw[0, 0])
    noise_rest = to_low(noise_draw[0, 0] - wide(noise_high))
    extra = jnp.concatenate(
        [cotangent[0], jnp.concatenate([noise_high, noise_rest], axis=2)], axis=1
    )
    size = span + SMALL
    one, two = first[0], first[1]
    one_x = hop(jnp.concatenate([one, back_x]), "x")
    two_y = hop(two, "y")
    sent = jnp.concatenate(
        [one, one_x[:size], jnp.concatenate([back_y, one_x[size:, ff // 8 :]], axis=1)]
    )
    sent_y, sent_x = after((sent, jnp.concatenate([two, two_y])), (came, extra, out_t))
    near_y = hop(sent_y, "y")
    near_x = hop(sent_x, "x")
    plane_own = jnp.concatenate(
        [one, two, one_x[:size], near_x[:size], near_y[:size], two_y]
        + [near_y[size : 2 * size], near_x[size:]]
    ).reshape(4, 2, size, width)
    plane_other = other_core(plane_own)
    (pair_own,) = whole_call(
        lay_body,
        (in_own, back_own, one_x[size:], near_y[2 * size :]),
        [low_shape(256, width)],
    )
    pair_w = lax.all_gather(pair_own, "z", axis=0, tiled=True)

    vec, means, logvars, normed, qkv, head_w, mixed, lse, bias = attend(
        plane_own, plane_other, after(came, pair_own), lat, inner
    )
    mix_parts = mix_out(mixed, out_t, whole)

    extra = to_slides(after(extra, mixed))
    cot = extra[:, :span].reshape(rows, width)
    noise = extra[:, span:].reshape(rows, width)
    noise = wide(noise[:, :lat]) + wide(noise[:, lat:])

    attended, normed_two, hidden = project(mix_parts, first, vec)
    rows_two = plane_rows(normed_two)
    act_far, slope_far, fed_far = feed(rows_two[4:], pair_w, vec)
    act, slope, keep, *sends = feed(rows_two[:4], pair_w, vec, other_core(fed_far))
    fed_parts = (keep, *plane_hops(sends))
    wholes = (whole, other_core(whole))
    output, fed_low, sample_low, dlat_low, dfed, dfed_low, dmeans, dlogvars, bottle_sums = (
        bottle_call(
            attended, fed_parts, vec, wholes, noise, cot, means, logvars
        )
    )

    rows_fed = plane_rows(dfed_low)
    layer_out = wide(
        from_slides(after(to_low(output), rows_fed).reshape(slots, span, width))
    )
    whole_grad = whole_grads((dlat_low, fed_low, cot, sample_low))
    du_far, ff_far, norm_far = feed_back(rows_fed[4:], pair_w, slope_far)
    du, ff_sums, keep, *sends = feed_back(
        rows_fed[:4], pair_w, slope, after(other_core(norm_far), whole_grad)
    )
    norm_parts = (keep, *plane_hops(sends))
    grads = pair_grads(rows_fed, rows_two, whole_grad, (act, act_far), (du, du_far))
    grads_sum = lax.psum_scatter(grads, "z", scatter_dimension=0, tiled=True)
    datt, datt_low, project_sums = project_back(
        after(norm_parts, (grads, layer_out)), attended, dfed, vec
    )
    rows_datt = plane_rows(datt_low)
    out_grad, all_datt = out_grads(rows_datt, mixed)
    dqkv, dn_far = attend_back(qkv, bias, lse, out_t, head_w, all_datt)
    dn_keep, *dn_sends = dnormed(dqkv, head_w, other_core(dn_far))
    homes, head_sums = head_grads(dqkv, after(normed, dn_sends))
    dn_parts = (dn_keep, *plane_hops(dn_sends))
    grad_rows, packed = cells_back(
        (
            *dn_parts,
            hidden,
            datt,
            vec,
            bottle_sums,
            project_sums,
            head_sums,
            ff_sums,
            ff_far,
            dmeans,
            dlogvars,
            out_grad,
        ),
        inner,
    )
    grad_cells = wide(from_slides(to_low(grad_rows).reshape(slots, span, width)))
    sum_in, *sums = whole_call(
        split_grad_body,
        (after(grads_sum, packed),),
        [wide_shape(128, width)] + [low_shape(part, ff // 8 + shard_width)] * 4,
    )
    sums = [sums[0], *plane_hops(sums[1:])]
    sums += [other_core(total) for total in sums]

    (last,) = whole_call(
        last_sum_body, (exchange(packed, CHIPS),), [wide_shape(part + SMALL, 4 * PAIR)]
    )
    grad_out_w, small_sums = whole_call(
        last_body, (last, other_core(last)), [wide_shape(part, width), wide_shape(SMALL, PAIR)]
    )
    grad_out_w = grad_out_w.T
    homes = after(homes, (last, sums[0]))
    homes = [
        lax.ppermute(grad, EVERY, [(there, here) for here, there in head_routes(single, k)])
        for grad, (single, k) in zip(homes, ARRIVALS)
    ]
    (home,) = whole_call(home_body, homes, [wide_shape(3 * HEAD_DIM, width)])
    grad_qkv = (home + other_core(home)).T
    vec_out = small_sums[:9, :part]
    inner_out = small_sums[9 : 9 + inner // width, :part].reshape(1, -1)
    means_out = small_sums[:, part : part + lat // 16]
    logvars_out = small_sums[:, part + lat // 16 :]
    kl_mean = small_sums[14, 0] / (32 * rows)

    grad_in_w = ordered(sum_in.T, other_core(sum_in).T, "grp", 1)
    grad_back_w, whole_own, whole_other = whole_call(
        last_grad_body,
        sums,
        [wide_shape(part, ff)] + [wide_shape(part, shard_width)] * 2,
    )
    grad_back_w = grad_back_w.T
    grad_lat_w, grad_dec_w = (
        ordered(whole_own[:, lanes].T, whole_other[:, lanes].T, "grp", 0)
        for lanes in (LAT_LANES, DEC_LANES)
    )
    return (
        layer_out.reshape(1, slots, span, width),
        grad_cells.reshape(1, slots, span, width),
        kl_mean,
        grad_qkv[None],
        grad_out_w[None],
        grad_in_w[None],
        grad_back_w[None],
        grad_lat_w[None],
        grad_dec_w[None],
        vec_out[None],
        inner_out,
        means_out[None],
        logvars_out[None],
    )


def solution(mesh):
    chips = mesh.shape["blk"]
    if (mesh.shape["grp"], chips) == (2, HEADS):
        mesh = Mesh(mesh.devices.reshape(2, chips // 4, 2, 2), EVERY)
        blk, run = CHIPS, fast_device
    else:
        blk, run = "blk", per_device
    cells = P("grp", None, blk, None)
    columns = P(None, None, blk)
    return jax.shard_map(
        run,
        mesh=mesh,
        in_specs=(cells, P("grp", None), P(None, "grp", None, blk, None), cells)
        + (columns,) * 7
        + (P(None, blk), columns, columns),
        out_specs=(cells, cells, P()) + (columns,) * 7 + (P(None, blk), columns, columns),
        check_vma=False,
    )
```

```python
import functools
import math

import jax
import jax.numpy as jnp
import numpy as np
from jax import lax
from jax.experimental import pallas as pl
from jax.experimental.pallas import tpu as pltpu
from jax.sharding import Mesh
from jax.sharding import PartitionSpec as P

HEADS = 16
LAYERS = 1
HEAD_DIM = 64


EPS_NORM = 1e-05
MASKED = -1e30


def to_low(values):
    return values.astype(jnp.bfloat16)


def product(left, right):
    return jnp.dot(left, right, preferred_element_type=jnp.float32)


def product_tn(left, right):
    return lax.dot_general(
        left, right, (((0,), (0,)), ((), ())), preferred_element_type=jnp.float32
    )


def product_nt(left, right):
    return lax.dot_general(
        left, right, (((1,), (1,)), ((), ())), preferred_element_type=jnp.float32
    )


def layer_norm(values, norm_gain, norm_shift):
    centre = values - jnp.mean(values, axis=-1, keepdims=True)
    spread = jnp.mean(centre * centre, axis=-1, keepdims=True)
    return centre * lax.rsqrt(spread + EPS_NORM) * norm_gain + norm_shift


def mixture_kl(sample, noise_rows, logvar, mean_rows, logvars):
    own_term = jnp.sum(-0.5 * noise_rows * noise_rows - 0.5 * logvar, axis=-1)
    offset = sample[:, None, :] - mean_rows[None, :, :]
    component = jnp.sum(
        -0.5 * offset * offset * jnp.exp(-logvars)[None] - 0.5 * logvars[None], axis=-1
    ) - math.log(mean_rows.shape[0])
    row_peak = jnp.max(component, axis=-1, keepdims=True)
    mixture = row_peak[:, 0] + jnp.log(jnp.sum(jnp.exp(component - row_peak), axis=-1))
    return own_term - mixture


def bottleneck(latent, noise_rows, live_rows, mean_rows, logvars):
    lat_width = noise_rows.shape[-1]
    mean_part = latent[:, :lat_width]
    logvar = latent[:, lat_width:]
    sample = mean_part + jnp.exp(0.5 * logvar) * noise_rows
    per_cell = mixture_kl(sample, noise_rows, logvar, mean_rows, logvars)
    return (sample, jnp.sum(jnp.where(live_rows, per_cell, 0.0)) / lat_width)


def slot_scores(query_slots, keys_all, slide_len, score_scale):
    slot_count, query_rows, model_width = query_slots.shape
    heads_q = query_slots.reshape(slot_count, query_rows, HEADS, HEAD_DIM)
    heads_k = keys_all.reshape(slot_count, keys_all.shape[1], HEADS, HEAD_DIM)
    raw_scores = (
        jnp.einsum("sqhd,skhd->shqk", heads_q, heads_k, preferred_element_type=jnp.float32)
        * score_scale
    )
    live_keys = jnp.arange(keys_all.shape[1])[None, :] < slide_len[:, None]
    return jnp.where(live_keys[:, None, None, :], raw_scores, MASKED)


def widen(gathered):
    qkv_w, out_w, in_w, back_w, latent_w, decode_w, vec_rows, inner_rows, mean_rows, logvars = (
        gathered
    )
    return (
        qkv_w,
        out_w,
        in_w,
        back_w,
        latent_w,
        decode_w,
        vec_rows.astype(jnp.float32),
        inner_rows.astype(jnp.float32),
        mean_rows.astype(jnp.float32),
        logvars.astype(jnp.float32),
    )


def gather_weights(layer_parts):
    (
        part_qkv,
        part_out,
        part_in,
        part_back,
        part_latent,
        part_decode,
        part_vectors,
        part_inner,
        part_means,
        part_logvars,
    ) = layer_parts
    return widen(
        (
            lax.all_gather(part_qkv, "blk", axis=1, tiled=True),
            lax.all_gather(part_out, "blk", axis=1, tiled=True),
            lax.all_gather(part_in, "blk", axis=1, tiled=True),
            lax.all_gather(part_back, "blk", axis=1, tiled=True),
            lax.all_gather(part_latent, "blk", axis=1, tiled=True),
            lax.all_gather(part_decode, "blk", axis=1, tiled=True),
            lax.all_gather(part_vectors, "blk", axis=1, tiled=True),
            lax.all_gather(part_inner, "blk", axis=0, tiled=True),
            lax.all_gather(part_means, "blk", axis=1, tiled=True),
            lax.all_gather(part_logvars, "blk", axis=1, tiled=True),
        )
    )


def reduce_grads(grads):
    (
        grad_qkv_w,
        grad_out_w,
        grad_in_w,
        grad_back_w,
        grad_latent_w,
        grad_decode_w,
        grad_vec,
        grad_inner,
        grad_mean_rows,
        grad_logvars,
    ) = grads
    (
        shard_qkv,
        shard_out,
        shard_in,
        shard_back,
        shard_latent,
        shard_decode,
        shard_vec,
        shard_inner,
        shard_means,
        shard_logvars,
    ) = (
        lax.psum_scatter(grad_qkv_w, "blk", scatter_dimension=1, tiled=True),
        lax.psum_scatter(grad_out_w, "blk", scatter_dimension=1, tiled=True),
        lax.psum_scatter(grad_in_w, "blk", scatter_dimension=1, tiled=True),
        lax.psum_scatter(grad_back_w, "blk", scatter_dimension=1, tiled=True),
        lax.psum_scatter(grad_latent_w, "blk", scatter_dimension=1, tiled=True),
        lax.psum_scatter(grad_decode_w, "blk", scatter_dimension=1, tiled=True),
        lax.psum_scatter(grad_vec, "blk", scatter_dimension=1, tiled=True),
        lax.psum_scatter(grad_inner, "blk", scatter_dimension=0, tiled=True),
        lax.psum_scatter(grad_mean_rows, "blk", scatter_dimension=1, tiled=True),
        lax.psum_scatter(grad_logvars, "blk", scatter_dimension=1, tiled=True),
    )
    return lax.psum(
        (
            shard_qkv,
            shard_out,
            shard_in,
            shard_back,
            shard_latent,
            shard_decode,
            shard_vec,
            shard_inner,
            shard_means,
            shard_logvars,
        ),
        "grp",
    )


def layer_forward(hidden, full_weights, noise_rows, live_rows, slide_len, score_scale):
    qkv_w, out_w, in_w, back_w, latent_w, decode_w, vec_rows, inner_rows, mean_rows, logvars = (
        full_weights
    )
    model_width = hidden.shape[1]
    slot_count = slide_len.shape[0]
    slot_span = hidden.shape[0] // slot_count
    ff_width = in_w.shape[1]
    normed = to_low(layer_norm(hidden, vec_rows[0], vec_rows[1]))
    qkv_all = product(normed, qkv_w)
    query_low = to_low(qkv_all[:, :model_width] + vec_rows[2])
    keys_own = to_low(qkv_all[:, model_width : 2 * model_width])
    values_own = to_low(qkv_all[:, 2 * model_width :] + vec_rows[3])
    keys_all, values_all = (
        lax.all_gather(
            keys_own.reshape(slot_count, slot_span, model_width), "blk", axis=1, tiled=True
        ),
        lax.all_gather(
            values_own.reshape(slot_count, slot_span, model_width), "blk", axis=1, tiled=True
        ),
    )
    scores = slot_scores(
        query_low.reshape(slot_count, slot_span, model_width), keys_all, slide_len, score_scale
    )
    row_peak = jnp.max(scores, axis=-1, keepdims=True)
    weights = jnp.exp(scores - row_peak)
    totals = jnp.sum(weights, axis=-1, keepdims=True)
    probs_low = to_low(weights / totals)
    log_total = row_peak + jnp.log(totals)
    heads_v = values_all.reshape(slot_count, values_all.shape[1], HEADS, HEAD_DIM)
    mixed_f = jnp.einsum("shqk,skhd->sqhd", probs_low, heads_v, preferred_element_type=jnp.float32)
    mixed_low = to_low(mixed_f.reshape(slot_count * slot_span, model_width))
    attended = hidden + product(mixed_low, out_w) + vec_rows[4]
    normed_two = to_low(layer_norm(attended, vec_rows[5], vec_rows[6]))
    inner_act = product(normed_two, in_w) + inner_rows[:ff_width]
    activated = to_low(jax.nn.gelu(inner_act))
    fed_rows = attended + product(activated, back_w) + vec_rows[7]
    fed_low = to_low(fed_rows)
    latent = product(fed_low, latent_w) + inner_rows[ff_width:]
    sample, kl_part = bottleneck(latent, noise_rows, live_rows, mean_rows, logvars)
    sample_low = to_low(sample)
    output = fed_rows + product(sample_low, decode_w) + vec_rows[8]
    saved_state = (
        hidden,
        normed,
        query_low,
        keys_own,
        values_own,
        log_total,
        mixed_low,
        attended,
        normed_two,
        inner_act,
        activated,
        fed_low,
        latent,
        sample_low,
    )
    return (output, kl_part, saved_state)


def layer_backward(
    grad_out, full_weights, saved_state, noise_rows, live_rows, slide_len, score_scale
):
    qkv_w, out_w, in_w, back_w, latent_w, decode_w, vec_rows, inner_rows, mean_rows, logvars = (
        full_weights
    )
    (
        hidden,
        normed,
        query_low,
        keys_own,
        values_own,
        log_total,
        mixed_low,
        attended,
        normed_two,
        inner_act,
        activated,
        fed_low,
        latent,
        sample_low,
    ) = saved_state
    model_width = hidden.shape[1]
    row_total = hidden.shape[0]
    slot_count = slide_len.shape[0]
    slot_span = row_total // slot_count
    grad_dec_low = to_low(grad_out)
    grad_decode_w = product_tn(sample_low, grad_dec_low)
    grad_sample = product_nt(grad_dec_low, decode_w)

    def bottle(latent_in, means_in, logvars_in):
        return bottleneck(latent_in, noise_rows, live_rows, means_in, logvars_in)

    ignored, bottle_pull = jax.vjp(bottle, latent, mean_rows, logvars)
    grad_latent_f, grad_mean_rows, grad_logvars = bottle_pull(
        (grad_sample, jnp.ones((), jnp.float32))
    )
    grad_latent_low = to_low(grad_latent_f)
    grad_latent_w = product_tn(fed_low, grad_latent_low)
    grad_fed = grad_out + product_nt(grad_latent_low, latent_w)
    grad_fed_low = to_low(grad_fed)
    grad_back_w = product_tn(activated, grad_fed_low)
    grad_act = product_nt(grad_fed_low, back_w)
    ignored_two, gelu_pull = jax.vjp(jax.nn.gelu, inner_act)
    grad_inner_low = to_low(gelu_pull(grad_act)[0])
    grad_in_w = product_tn(normed_two, grad_inner_low)
    grad_normed_two = product_nt(grad_inner_low, in_w)
    ignored_three, second_pull = jax.vjp(layer_norm, attended, vec_rows[5], vec_rows[6])
    grad_att_norm, grad_gain_two, grad_shift_two = second_pull(grad_normed_two)
    grad_attended = grad_fed + grad_att_norm
    grad_proj_low = to_low(grad_attended)
    grad_out_w = product_tn(mixed_low, grad_proj_low)
    grad_mixed_low = to_low(product_nt(grad_proj_low, out_w))
    keys_all, values_all = (
        lax.all_gather(
            keys_own.reshape(slot_count, slot_span, model_width), "blk", axis=1, tiled=True
        ),
        lax.all_gather(
            values_own.reshape(slot_count, slot_span, model_width), "blk", axis=1, tiled=True
        ),
    )
    grad_mixed_heads = grad_mixed_low.reshape(slot_count, slot_span, HEADS, HEAD_DIM)
    heads_k = keys_all.reshape(slot_count, keys_all.shape[1], HEADS, HEAD_DIM)
    heads_v = values_all.reshape(slot_count, values_all.shape[1], HEADS, HEAD_DIM)
    scores = slot_scores(
        query_low.reshape(slot_count, slot_span, model_width), keys_all, slide_len, score_scale
    )
    probs_f = jnp.exp(scores - log_total)
    grad_probs = jnp.einsum(
        "sqhd,skhd->shqk", grad_mixed_heads, heads_v, preferred_element_type=jnp.float32
    )
    centre = jnp.sum(grad_probs * probs_f, axis=-1, keepdims=True)
    grad_scores_low = to_low(probs_f * (grad_probs - centre))
    grad_query = (
        jnp.einsum("shqk,skhd->sqhd", grad_scores_low, heads_k, preferred_element_type=jnp.float32)
        * score_scale
    )
    grad_query_low = to_low(grad_query.reshape(row_total, model_width))
    rows_all, mixed_all = (
        lax.all_gather(
            query_low.reshape(slot_count, slot_span, model_width), "blk", axis=1, tiled=True
        ),
        lax.all_gather(
            grad_mixed_low.reshape(slot_count, slot_span, model_width), "blk", axis=1, tiled=True
        ),
    )
    total_all, centre_all = (
        lax.all_gather(log_total, "blk", axis=2, tiled=True),
        lax.all_gather(centre, "blk", axis=2, tiled=True),
    )
    query_all = rows_all.reshape(slot_count, rows_all.shape[1], HEADS, HEAD_DIM)
    dmixed_all = mixed_all.reshape(slot_count, mixed_all.shape[1], HEADS, HEAD_DIM)
    own_keys = keys_own.reshape(slot_count, slot_span, HEADS, HEAD_DIM)
    own_values = values_own.reshape(slot_count, slot_span, HEADS, HEAD_DIM)
    own_raw = (
        jnp.einsum("sqhd,skhd->shqk", query_all, own_keys, preferred_element_type=jnp.float32)
        * score_scale
    )
    key_places = lax.axis_index("blk") * slot_span + jnp.arange(slot_span)
    live_own = key_places[None, :] < slide_len[:, None]
    own_scores = jnp.where(live_own[:, None, None, :], own_raw, MASKED)
    own_probs = jnp.exp(own_scores - total_all)
    own_dprobs = jnp.einsum(
        "sqhd,skhd->shqk", dmixed_all, own_values, preferred_element_type=jnp.float32
    )
    own_dscores = to_low(own_probs * (own_dprobs - centre_all))
    grad_keys = (
        jnp.einsum("shqk,sqhd->skhd", own_dscores, query_all, preferred_element_type=jnp.float32)
        * score_scale
    )
    grad_values = jnp.einsum(
        "shqk,sqhd->skhd", to_low(own_probs), dmixed_all, preferred_element_type=jnp.float32
    )
    grad_keys_low = to_low(grad_keys.reshape(row_total, model_width))
    grad_values_low = to_low(grad_values.reshape(row_total, model_width))
    grad_qkv_low = jnp.concatenate([grad_query_low, grad_keys_low, grad_values_low], axis=1)
    grad_qkv_w = product_tn(normed, grad_qkv_low)
    grad_normed = product_nt(grad_qkv_low, qkv_w)
    ignored_four, first_pull = jax.vjp(layer_norm, hidden, vec_rows[0], vec_rows[1])
    grad_hid_norm, grad_gain_one, grad_shift_one = first_pull(grad_normed)
    grad_hidden = grad_attended + grad_hid_norm
    grad_vec = jnp.stack(
        [
            grad_gain_one,
            grad_shift_one,
            jnp.sum(grad_query_low.astype(jnp.float32), axis=0),
            jnp.sum(grad_values_low.astype(jnp.float32), axis=0),
            jnp.sum(grad_attended, axis=0),
            grad_gain_two,
            grad_shift_two,
            jnp.sum(grad_fed, axis=0),
            jnp.sum(grad_out, axis=0),
        ]
    )
    grad_inner = jnp.concatenate(
        [
            jnp.sum(grad_inner_low.astype(jnp.float32), axis=0),
            jnp.sum(grad_latent_low.astype(jnp.float32), axis=0),
        ]
    )
    return (
        grad_hidden,
        (
            grad_qkv_w,
            grad_out_w,
            grad_in_w,
            grad_back_w,
            grad_latent_w,
            grad_decode_w,
            grad_vec,
            grad_inner,
            grad_mean_rows,
            grad_logvars,
        ),
    )


def per_device(
    cell_input,
    lengths,
    noise_draw,
    cotangent,
    w_qkv,
    w_out,
    w_ffn_in,
    w_ffn_out,
    w_latent,
    w_decode,
    vectors,
    inner_bias,
    prior_means,
    prior_logvars,
):
    slot_count = cell_input.shape[1]
    slot_span = cell_input.shape[2]
    model_width = cell_input.shape[3]
    row_total = slot_count * slot_span
    lat_width = noise_draw.shape[-1]
    cycle_size = lax.axis_size("blk")
    score_scale = 1.0 / math.sqrt(HEAD_DIM)
    slide_len = lengths[0]
    positions = lax.axis_index("blk") * slot_span + jnp.arange(slot_span)
    live_rows = (positions[None, :] < slide_len[:, None]).reshape(row_total)
    hidden = cell_input[0].reshape(row_total, model_width).astype(jnp.float32)
    stacks = (
        w_qkv,
        w_out,
        w_ffn_in,
        w_ffn_out,
        w_latent,
        w_decode,
        vectors,
        inner_bias,
        prior_means,
        prior_logvars,
    )
    layer_idx = 0
    full_weights = gather_weights([stacked[layer_idx] for stacked in stacks])
    kept_weights = [full_weights]
    hidden, kl_part, saved_state = layer_forward(
        hidden,
        full_weights,
        noise_draw[layer_idx, 0].reshape(row_total, lat_width),
        live_rows,
        slide_len,
        score_scale,
    )
    saved_layers = [saved_state]
    layer_out = hidden.reshape(1, slot_count, slot_span, model_width)
    kl_total = lax.psum(kl_part, ("grp", "blk"))
    kl_mean = kl_total / (lax.axis_size("grp") * cycle_size * row_total)
    grad_rows = cotangent[0].reshape(row_total, model_width).astype(jnp.float32)
    reduced = [None] * LAYERS
    for layer_idx in reversed(range(LAYERS)):
        full_weights = kept_weights[layer_idx]
        grad_rows, grads = layer_backward(
            grad_rows,
            full_weights,
            saved_layers[layer_idx],
            noise_draw[layer_idx, 0].reshape(row_total, lat_width),
            live_rows,
            slide_len,
            score_scale,
        )
        reduced[layer_idx] = reduce_grads(grads)
    grad_cells = grad_rows.reshape(1, slot_count, slot_span, model_width)
    stacked_grads = [jnp.stack([reduced[0][member]]) for member in range(10)]
    return (
        layer_out,
        grad_cells,
        kl_mean,
        stacked_grads[0],
        stacked_grads[1],
        stacked_grads[2],
        stacked_grads[3],
        stacked_grads[4],
        stacked_grads[5],
        stacked_grads[6],
        stacked_grads[7],
        stacked_grads[8],
        stacked_grads[9],
    )


EVERY = ("grp", "z", "y", "x")
CHIPS = ("z", "y", "x")
PLANE = ("grp", "y", "x")
PAIR = 2 * HEAD_DIM
SMALL = 16
VMEM_LIMIT = 20 * 1024 * 1024


def hop(values, axis, step=1):
    size = lax.axis_size(axis)
    return lax.ppermute(values, axis, [(i, i ^ step) for i in range(size)])


def other_core(values):
    return hop(values, "grp")


def after(values, done):
    return lax.optimization_barrier((values, done))[0]


def ordered(own, other, axis_name, axis):
    first = lax.axis_index(axis_name) == 0
    return jnp.concatenate(
        [jnp.where(first, own, other), jnp.where(first, other, own)], axis=axis
    )


def half_of(values, axis, axis_name, mine):
    part = values.shape[axis] // 2
    place = lax.axis_index(axis_name)
    place = place if mine else 1 - place
    return lax.dynamic_slice_in_dim(values, place * part, part, axis)


def flip(place, step):
    high = (place // 2 + step // 2) % 2
    low_bit = (place % 2 + step % 2) % 2
    return high * 2 + low_bit


def slide_routes(k):
    return [
        (g * 4 + z, (z // 2) * 4 + 2 * g + ((z % 2) ^ k)) for g in range(2) for z in range(4)
    ]


def pick_slot(slots, k):
    odd = (lax.axis_index("z") + k) % 2 == 1
    return jnp.where(odd, slots[1], slots[0])


def to_slides(slots):
    return jnp.stack(
        [lax.ppermute(pick_slot(slots, k), ("grp", "z"), slide_routes(k)) for k in range(2)]
    )


def from_slides(blocks):
    came = [
        lax.ppermute(
            blocks[k], ("grp", "z"), [(there, here) for here, there in slide_routes(k)]
        )
        for k in range(2)
    ]
    return jnp.stack([pick_slot(came, 0), pick_slot(came, 1)])


def head_routes(single, k):
    routes = []
    for core in range(2):
        for chip in range(16):
            odd = chip % 2
            block = 3 * chip + (2 - 2 * odd if single else odd)
            pair = (block % 16) // 2
            plane = 2 * core + (odd ^ k)
            target = (pair // 4) * 16 + plane * 4 + pair % 4
            routes.append((core * 16 + chip, target))
    return routes


ARRIVALS = [(single, k) for k in range(2) for single in (False, True)]


def low_shape(*shape):
    return jax.ShapeDtypeStruct(shape, jnp.bfloat16)


def wide(values):
    return values.astype(jnp.float32)


def z_hops(values):
    return [hop(values[step - 1], "z", step) for step in (1, 2, 3)]


def plane_hops(values):
    return [
        hop(values[0], "x"),
        hop(values[1], "y"),
        lax.ppermute(values[2], ("y", "x"), [(i, i ^ 3) for i in range(4)]),
    ]


NEAR = ((0, 0), (0, 1), (1, 0), (1, 1))


def z_at(step, part):
    return pl.ds(pl.multiple_of(flip(lax.axis_index("z"), step) * part, part), part)


def chip_place(step):
    return flip(lax.axis_index("y"), step[0]) * 2 + flip(lax.axis_index("x"), step[1])


def pinned(values):
    return [pltpu.with_memory_space_constraint(part, pltpu.HBM) for part in values]


def wide_shape(*shape):
    return jax.ShapeDtypeStruct(shape, jnp.float32)


FLOPS_PER_US = 1.1e9
TIMES = {
    "attend_body": 10.0,
    "feed_body": 3.5,
    "bottle_body": 5.7,
    "feed_back_body": 2.0,
    "pair_grad_body": 3.4,
    "attend_back_body": 9.2,
    "whole_grads_body": 1.3,
    "cells_back_body": 1.4,
}


def took(body):
    inner = body.func if isinstance(body, functools.partial) else body
    return TIMES.get(inner.__name__, 0.8)


def whole_call(
    body, operands, out_shapes, scratch=(), left_out=(), loaded=(), kept=(), early=False, placed=()
):
    vmem, hbm = pl.BlockSpec(memory_space=pltpu.VMEM), pl.BlockSpec(memory_space=pltpu.HBM)
    n_in, n_out, n_own = len(operands), len(out_shapes), len(scratch)
    left_out, loaded, kept = list(left_out), list(loaded), list(kept)

    def run(*refs):
        ins, outs = list(refs[:n_in]), list(refs[n_in : n_in + n_out])
        own = refs[n_in + n_out : n_in + n_out + n_own]
        rest = refs[n_in + n_out + n_own :]
        in_copies = []
        for at, i in enumerate(loaded):
            in_copies.append(pltpu.make_async_copy(ins[i], rest[at], rest[-1].at[at]))
            ins[i] = rest[at]
        for copy in in_copies:
            copy.start()
        out_copies = {}
        for at, i in enumerate(kept, len(loaded)):
            out_copies[i] = pltpu.make_async_copy(rest[at], outs[i], rest[-1].at[at])
            outs[i] = rest[at]
        for copy in in_copies:
            copy.wait()
        started = []

        def store(i):
            out_copies[i].start()
            started.append(i)

        body(*ins, *outs, *own, **({"store": store} if early else {}))
        for i in out_copies:
            if i not in started:
                out_copies[i].start()
        for copy in out_copies.values():
            copy.wait()

    operands = [
        pltpu.with_memory_space_constraint(part, pltpu.HBM)
        if i in loaded
        else part
        for i, part in enumerate(operands)
    ]
    buffers = [pltpu.VMEM(operands[i].shape, operands[i].dtype) for i in loaded]
    buffers += [pltpu.VMEM(out_shapes[i].shape, out_shapes[i].dtype) for i in kept]
    if buffers:
        buffers.append(pltpu.SemaphoreType.DMA((len(buffers),)))
    out_shapes = [
        pltpu.HBM(part.shape, part.dtype) if i in kept or i in placed else part
        for i, part in enumerate(out_shapes)
    ]
    return pl.pallas_call(
        run,
        out_shape=out_shapes,
        in_specs=[hbm if i in left_out or i in loaded else vmem for i in range(n_in)],
        out_specs=[hbm if i in kept or i in placed else vmem for i in range(n_out)],
        scratch_shapes=[*scratch, *buffers],
        compiler_params=pltpu.CompilerParams(vmem_limit_bytes=VMEM_LIMIT),
        cost_estimate=pl.CostEstimate(
            flops=int(took(body) * FLOPS_PER_US), bytes_accessed=0, transcendentals=0
        ),
    )(*operands)


def enter_body(cells_ref, lens_ref, vectors_ref, inner_ref, means_ref, logvars_ref, *outs):
    span = cells_ref.shape[0] // 2
    lens = lens_ref[...]
    lens = jnp.concatenate([lens >> 5, lens & 31], axis=1).astype(jnp.float32)
    for k, ref in enumerate(outs):
        slot = (lax.axis_index("z") + k) % 2
        ref[:span] = cells_ref[pl.ds(pl.multiple_of(slot * span, span), span)]
        ref[span:] = jnp.zeros((SMALL, ref.shape[1]), jnp.bfloat16)
        ref[span : span + 9, 0:64] = vectors_ref[...]
        ref[span:, 128:160] = means_ref[...]
        ref[span:, 256:288] = logvars_ref[...]
        ref[span : span + 1, 384:704] = inner_ref[...]
        ref[span : span + 1, 768:772] = to_low(lens)


def chunk_place(block, step=(0, 0), core_step=0):
    core = flip(lax.axis_index("grp"), core_step)
    return pl.multiple_of(((block * 4 + chip_place(step)) * 2 + core) * 128, 128)


LAT_ROW, FF_ROW, LEN_ROW = 9, 10, 11


def unpack(small_ref, vec_ref, means_ref, logvars_ref, inner_ref):
    count = small_ref.shape[0]

    def lanes(row, rows, first, width):
        return jnp.concatenate(
            [wide(small_ref[i, row : row + rows, first : first + width]) for i in range(count)],
            axis=1,
        )

    vec_ref[...] = lanes(0, SMALL, 0, vec_ref.shape[1] // count)
    means_ref[...] = lanes(0, SMALL, 128, means_ref.shape[1] // count)
    logvars_ref[...] = lanes(0, SMALL, 256, means_ref.shape[1] // count)
    inner_ref[...] = lanes(0, 1, 384, inner_ref.shape[1] // count)
    width = vec_ref.shape[1]
    vec_ref[LAT_ROW : LAT_ROW + 1] = inner_ref[:, inner_ref.shape[1] - width :]
    for block in range(4):
        vec_ref[FF_ROW : FF_ROW + 1, block * 128 : block * 128 + 128] = inner_ref[
            :, pl.ds(chunk_place(block), 128)
        ]
    lens = wide(small_ref[0, 0:1, 768:896])
    even = lax.axis_index("z") % 2 == 0
    high = jnp.where(even, lens[:, 0:1], lens[:, 1:2])
    rest = jnp.where(even, lens[:, 2:3], lens[:, 3:4])
    vec_ref[LEN_ROW : LEN_ROW + 1] = jnp.broadcast_to(high * 32 + rest, (1, width))


def row_stats(values):
    centre = values - jnp.mean(values, axis=-1, keepdims=True)
    scale = lax.rsqrt(jnp.mean(centre * centre, axis=-1, keepdims=True) + EPS_NORM)
    return centre * scale, scale


def norm_back(grad, unit, scale, gain):
    inner = grad * gain
    along = jnp.mean(inner * unit, axis=-1, keepdims=True)
    return scale * (inner - jnp.mean(inner, axis=-1, keepdims=True) - unit * along)


def column_sum(values):
    return jnp.sum(values, axis=0, keepdims=True)


def slide_place(core, block, k, row, span):
    zi = lax.axis_index("z")
    chip = (core * 2 + ((zi + k) & 1)) * 4 + block
    return chip * span + row


def head_lanes(rows):
    return lax.broadcasted_iota(jnp.int32, (rows, PAIR), 1) < HEAD_DIM


def own_pair():
    place = (lax.axis_index("grp") * 2 + lax.axis_index("y")) * 2 + lax.axis_index("x")
    return pl.multiple_of(place * PAIR, PAIR)


def head_row(single, k):
    place = (lax.axis_index("grp") * 2 + lax.axis_index("y")) * 2 + lax.axis_index("x")
    parity = (lax.axis_index("z") + k) % 2
    row = 0
    for role in range(3):
        block = 16 * role + 2 * place
        split = (block % 3) // 2
        odd = (block // 3) % 2
        if single:
            here = split * PAIR * role + split * HEAD_DIM * ((odd + parity) % 2)
        else:
            here = (1 - split) * (1 - (odd + parity) % 2) * PAIR * role
        row = row + here
    return pl.multiple_of(row, HEAD_DIM)


def device_place(step, core_step):
    return flip(lax.axis_index("grp"), core_step) * 4 + chip_place(step)


def attend_body(own_ref, other_ref, *refs):
    came, rest = refs[:4], refs[4:]
    vec_ref, means_ref, logvars_ref, normed_ref, qkv_ref, head_w_ref = rest[:6]
    mixed_ref, lse_ref, bias_ref, small_ref, inner_ref = rest[6:]
    span = own_ref.shape[2] - SMALL
    for core_step, ref in enumerate((own_ref, other_ref)):
        for i, step in enumerate(NEAR):
            place = device_place(step, core_step)
            for k in range(2):
                chip = ((place // 4) * 2 + (lax.axis_index("z") + k) % 2) * 4 + place % 4
                small_ref[chip] = ref[i, k, span:]
    unpack(small_ref, vec_ref, means_ref, logvars_ref, inner_ref)
    for ref, (single, k) in zip(came, ARRIVALS):
        head_w_ref[pl.ds(head_row(single, k), ref.shape[0])] = ref[...]
    total_rows = normed_ref.shape[0]
    gain, shift = vec_ref[0:1], vec_ref[1:2]
    bias_q = vec_ref[2:3, pl.ds(own_pair(), PAIR)]
    bias_v = vec_ref[3:4, pl.ds(own_pair(), PAIR)]
    for core_step, ref in enumerate((own_ref, other_ref)):
        for i, step in enumerate(NEAR):
            cells = jnp.concatenate([ref[i, 0, :span], ref[i, 1, :span]])
            unit, _ = row_stats(wide(cells))
            at = device_place(step, core_step) * (2 * span)
            normed_ref[pl.ds(pl.multiple_of(at, 2 * span), 2 * span)] = to_low(unit * gain + shift)
    step = 256
    for start in range(0, total_rows, step):
        qkv = product_nt(normed_ref[start : start + step], head_w_ref[...])
        qkv_ref[start : start + step, :PAIR] = to_low(
            wide(to_low(qkv[:, :PAIR] + bias_q)) * HEAD_DIM**-0.5
        )
        qkv_ref[start : start + step, PAIR : 2 * PAIR] = to_low(qkv[:, PAIR : 2 * PAIR])
        qkv_ref[start : start + step, 2 * PAIR :] = to_low(qkv[:, 2 * PAIR :] + bias_v)
    lane = lax.broadcasted_iota(jnp.int32, (1, total_rows), 1)
    place = slide_place(
        lane // (8 * span), (lane // (2 * span)) & 3, (lane // span) & 1, lane & (span - 1), span
    )
    bias = jnp.where(place.astype(jnp.float32) < vec_ref[LEN_ROW : LEN_ROW + 1], 0.0, MASKED)
    bias_ref[...] = bias
    keys = qkv_ref[:, PAIR : 2 * PAIR]
    values = qkv_ref[:, 2 * PAIR :]
    first_head = head_lanes(step)
    for start in range(0, total_rows, step):
        query = qkv_ref[start : start + step, :PAIR]
        outs, totals = [], []
        for head in range(2):
            mine = first_head if head == 0 else jnp.logical_not(first_head)
            part = jnp.where(mine, query, jnp.zeros_like(query))
            scores = product_nt(part, keys) + bias
            peak = jnp.max(scores, axis=-1, keepdims=True)
            weights = jnp.exp(scores - peak)
            total = jnp.sum(weights, axis=-1, keepdims=True)
            outs.append(product(to_low(weights / total), values))
            totals.append(jnp.broadcast_to(peak + jnp.log(total), (step, PAIR)))
        mixed_ref[start : start + step] = to_low(jnp.where(first_head, outs[0], outs[1]))
        lse_ref[start : start + step] = jnp.where(first_head, totals[0], totals[1])


def attend(own, other, came, lat, inner):
    rows, width = 16 * (own.shape[2] - SMALL), own.shape[3]
    return whole_call(
        attend_body,
        (own, other, *came),
        [
            wide_shape(SMALL, width),
            wide_shape(SMALL, lat),
            wide_shape(SMALL, lat),
            low_shape(rows, width),
            low_shape(rows, 3 * PAIR),
            low_shape(3 * PAIR, width),
            low_shape(rows, PAIR),
            wide_shape(rows, PAIR),
            wide_shape(1, rows),
        ],
        [
            pltpu.VMEM((16, SMALL, width), jnp.bfloat16),
            pltpu.VMEM((1, inner), jnp.float32),
        ],
        loaded=range(2, 6),
    )


def side_rows(ref, core_step, start, rows):
    first = flip(lax.axis_index("grp"), core_step) * (ref.shape[0] // 2) + start
    return ref[pl.ds(pl.multiple_of(first, rows), rows)]


def mix_far_body(mixed_ref, out_t_ref, far_ref):
    for start in range(0, far_ref.shape[0], 256):
        far_ref[start : start + 256] = to_low(
            product_nt(side_rows(mixed_ref, 1, start, 256), out_t_ref[...])
        )


def mix_near_body(mixed_ref, out_t_ref, came_ref, keep_ref, *sends):
    rows = keep_ref.shape[0]
    for i, step in enumerate(NEAR):
        first = chip_place(step) * rows
        came = came_ref[pl.ds(pl.multiple_of(first, rows), rows)]
        part = product_nt(side_rows(mixed_ref, 0, first, rows), out_t_ref[...]) + wide(came)
        if i == 0:
            keep_ref[...] = part
        else:
            sends[i - 1][...] = to_low(part)


def part_shapes(rows, width):
    return [wide_shape(rows, width)] + [low_shape(rows, width)] * 3


def mix_out(mixed, out_t, ready):
    rows, width = mixed.shape[0], out_t.shape[0]
    (far,) = whole_call(mix_far_body, (mixed, out_t), [low_shape(rows // 2, width)])
    keep, *sends = whole_call(
        mix_near_body, (mixed, out_t, after(other_core(far), ready)), part_shapes(rows // 8, width)
    )
    return keep, *plane_hops(sends)


def out_grad_body(*refs):
    pieces, mixed_ref, out_ref, datt_ref, sems = refs[:8], *refs[8:]
    stack_rows(pieces, datt_ref, sems, lambda i: device_place(NEAR[i % 4], i // 4))
    rows = out_ref.shape[1]
    for chip in range(0, out_ref.shape[0], 4):
        lanes = slice(chip * rows, (chip + 4) * rows)
        grad = to_low(product_tn(datt_ref[:, lanes], mixed_ref[...]))
        out_ref[chip : chip + 4] = grad.reshape(4, rows, PAIR)


def out_grads(pieces, mixed):
    rows, width = pieces[0].shape
    return whole_call(
        out_grad_body,
        (*pieces, mixed),
        [low_shape(16, width // 16, PAIR), low_shape(8 * rows, width)],
        [pltpu.SemaphoreType.DMA((8,))],
        range(8),
    )


def attend_back_body(
    qkv_ref,
    bias_ref,
    lse_ref,
    out_t_ref,
    head_w_ref,
    datt_ref,
    dqkv_ref,
    far_ref,
    dmixed_ref,
    dk_ref,
    dv_ref,
):
    rows = qkv_ref.shape[0]
    for start in range(0, rows, 256):
        at = slice(start, start + 256)
        dmixed_ref[at] = to_low(product(datt_ref[at], out_t_ref[...]))
    keys = qkv_ref[:, PAIR : 2 * PAIR]
    values = qkv_ref[:, 2 * PAIR :]
    bias = bias_ref[...]
    step = 256
    first_head = head_lanes(step)
    for start in range(0, rows, step):
        query = qkv_ref[start : start + step, :PAIR]
        dmixed = dmixed_ref[start : start + step]
        dqueries = []
        for head in range(2):
            mine = first_head if head == 0 else jnp.logical_not(first_head)
            part = jnp.where(mine, query, jnp.zeros_like(query))
            dpart = jnp.where(mine, dmixed, jnp.zeros_like(dmixed))
            lse = lse_ref[start : start + step, head * HEAD_DIM : head * HEAD_DIM + 1]
            probs = jnp.exp(product_nt(part, keys) + bias - lse)
            dprobs = product_nt(dpart, values)
            centre = jnp.sum(dprobs * probs, axis=-1, keepdims=True)
            dscores = to_low(probs * (dprobs - centre))
            dqueries.append(product(dscores, keys))
            dkeys = product_tn(dscores, part)
            dvalues = product_tn(to_low(probs), dpart)
            if start == 0 and head == 0:
                dk_ref[...] = dkeys
                dv_ref[...] = dvalues
            else:
                dk_ref[...] += dkeys
                dv_ref[...] += dvalues
        dquery = jnp.where(first_head, dqueries[0], dqueries[1]) * (HEAD_DIM**-0.5)
        dqkv_ref[start : start + step, :PAIR] = to_low(dquery)
    dqkv_ref[:, PAIR : 2 * PAIR] = to_low(dk_ref[...])
    dqkv_ref[:, 2 * PAIR :] = to_low(dv_ref[...])
    for start in range(0, rows // 2, step):
        far_ref[start : start + step] = to_low(
            product(side_rows(dqkv_ref, 1, start, step), head_w_ref[...])
        )


def attend_back(qkv, bias, lse, out_t, head_w, datt):
    rows, width = qkv.shape[0], head_w.shape[1]
    return whole_call(
        attend_back_body,
        (qkv, bias, lse, out_t, head_w, datt),
        [low_shape(rows, 3 * PAIR), low_shape(rows // 2, width)],
        [
            pltpu.VMEM((rows, PAIR), jnp.bfloat16),
            pltpu.VMEM((rows, PAIR), jnp.float32),
            pltpu.VMEM((rows, PAIR), jnp.float32),
        ],
    )


def dnormed_body(dqkv_ref, head_w_ref, came_ref, keep_ref, *sends):
    rows = keep_ref.shape[0]
    for i, step in enumerate(NEAR):
        first = chip_place(step) * rows
        came = came_ref[pl.ds(pl.multiple_of(first, rows), rows)]
        part = product(side_rows(dqkv_ref, 0, first, rows), head_w_ref[...]) + wide(came)
        if i == 0:
            keep_ref[...] = part
        else:
            sends[i - 1][...] = to_low(part)


def dnormed(dqkv, head_w, came):
    rows, width = dqkv.shape[0] // 8, head_w.shape[1]
    return whole_call(dnormed_body, (dqkv, head_w, came), part_shapes(rows, width))


def head_grad_body(dqkv_ref, normed_ref, *refs):
    homes, sums_ref, grad_w_ref = refs[:4], refs[4], refs[5]
    dqkv = dqkv_ref[...]
    sums_ref[...] = column_sum(wide(dqkv))
    grad_w_ref[...] = to_low(product_tn(dqkv, normed_ref[...]))
    for ref, (single, k) in zip(homes, ARRIVALS):
        ref[...] = grad_w_ref[pl.ds(head_row(single, k), ref.shape[0])]


def head_grads(dqkv, normed):
    width = normed.shape[1]
    outs = whole_call(
        head_grad_body,
        (dqkv, normed),
        [low_shape(HEAD_DIM if single else PAIR, width) for single, _ in ARRIVALS]
        + [wide_shape(1, 3 * PAIR)],
        [pltpu.VMEM((3 * PAIR, width), jnp.bfloat16)],
    )
    return outs[:4], outs[4]


def home_body(*refs):
    pair = wide(refs[0][...]) + wide(refs[2][...])
    single = wide(refs[1][...]) + wide(refs[3][...])
    odd = lax.axis_index("x") % 2
    refs[4][pl.ds(pl.multiple_of(odd * HEAD_DIM, HEAD_DIM), PAIR)] = pair
    refs[4][pl.ds(pl.multiple_of((1 - odd) * PAIR, HEAD_DIM), HEAD_DIM)] = single


LAT_LANES, DEC_LANES = slice(0, 512), slice(512, 768)


def project_body(
    keep_ref, came_x_ref, came_y_ref, came_far_ref, blocks_ref, vec_ref, attended_ref, normed_ref, hidden_ref
):
    span = blocks_ref.shape[1] - SMALL
    hidden = jnp.concatenate([blocks_ref[0, :span], blocks_ref[1, :span]])
    hidden_ref[...] = hidden
    parts = z_sum((keep_ref, came_x_ref, came_y_ref, came_far_ref))
    total = wide(hidden) + parts + vec_ref[4:5]
    attended_ref[...] = total
    unit, _ = row_stats(total)
    normed_ref[...] = to_low(unit * vec_ref[5:6] + vec_ref[6:7])


def project(parts, blocks, vec):
    shape = parts[0].shape
    return whole_call(
        project_body,
        (*parts, blocks, vec),
        [wide_shape(*shape), low_shape(*shape), low_shape(*shape)],
    )


GELU_SCALE = math.sqrt(2.0 / math.pi)
GELU_CUBE = 0.044715


def stack_rows(refs, target_ref, sems, order=None):
    rows = refs[0].shape[0]
    copies = []
    for i, ref in enumerate(refs):
        place = i if order is None else order(i)
        target = target_ref.at[pl.ds(pl.multiple_of(place * rows, rows), rows)]
        copies.append(pltpu.make_async_copy(ref, target, sems.at[i]))
    for copy in copies:
        copy.start()
    for copy in copies:
        copy.wait()


FF_STEP = 256


def load_all(rows_in, weights_ref, all_ref, in_ref, back_ref, sems):
    copies = []
    for i, ref in enumerate(rows_in):
        rows = ref.shape[0]
        copies.append((ref, all_ref.at[i * rows : (i + 1) * rows]))
    for z in range(4):
        part = weights_ref.at[z * 256 : z * 256 + 256]
        copies.append((part.at[:128], in_ref.at[z * 128 : (z + 1) * 128]))
        for half in range(2):
            at = z * 256 + half * 128
            copies.append(
                (part.at[128:, half * 512 : half * 512 + 512], back_ref.at[at : at + 128])
            )
    copies = [pltpu.make_async_copy(*copy, sems.at[i]) for i, copy in enumerate(copies)]
    for copy in copies:
        copy.start()
    for copy in copies:
        copy.wait()


def feed_scratch(rows, width, hidden):
    return [
        pltpu.VMEM((rows, width), jnp.bfloat16),
        pltpu.VMEM((hidden, width), jnp.bfloat16),
        pltpu.VMEM((width, hidden), jnp.bfloat16),
        pltpu.SemaphoreType.DMA((16,)),
    ]


def feed_body(*refs, last):
    rows_in, weights_ref, vec_ref, rest = refs[:4], refs[4], refs[5], list(refs[6:])
    came_ref = rest.pop(0) if last else None
    (act_ref, slope_ref), outs = rest[:2], rest[2:-4]
    all_ref, in_ref, back_ref, sems = rest[-4:]
    load_all(rows_in, weights_ref, all_ref, in_ref, back_ref, sems)
    bias = vec_ref[FF_ROW : FF_ROW + 1, : in_ref.shape[0]]
    step = rows_in[0].shape[0] * 2
    for start in range(0, all_ref.shape[0], step):
        at = slice(start, start + step)
        total = None
        for unit in range(0, in_ref.shape[0], FF_STEP):
            lanes = slice(unit, unit + FF_STEP)
            inner = product_nt(all_ref[at], in_ref[lanes]) + bias[:, lanes]
            square = inner * inner
            bend = jnp.tanh(GELU_SCALE * (inner + GELU_CUBE * (inner * square)))
            half = 0.5 * (1.0 + bend)
            act = to_low(inner * half)
            act_ref[at, lanes] = act
            slope_ref[at, lanes] = half + (0.5 * GELU_SCALE) * inner * (1.0 - bend * bend) * (
                1.0 + (3.0 * GELU_CUBE) * square
            )
            part = product_nt(act, back_ref[:, lanes])
            total = part if total is None else total + part
        put_parts(outs, came_ref, start, total)


def put_parts(outs, came_ref, start, total):
    if came_ref is None:
        outs[0][start : start + total.shape[0]] = to_low(total)
        return
    total = total + wide(came_ref[start : start + total.shape[0]])
    rows = outs[0].shape[0]
    for i in range(start // rows, (start + total.shape[0]) // rows):
        piece = total[i * rows - start : (i + 1) * rows - start]
        outs[i][...] = piece if i == 0 else to_low(piece)


def feed_call(body, pieces, weights, more, came, side_shapes):
    rows, width = pieces[0].shape
    last = came is not None
    operands = (*pieces, weights, *more) + ((came,) if last else ())
    outs = part_shapes(rows, width) if last else [low_shape(4 * rows, width)]
    return whole_call(
        functools.partial(body, last=last),
        operands,
        side_shapes + outs,
        feed_scratch(4 * rows, width, 512),
        range(5),
    )


def feed(pieces, weights, vec, came=None):
    count = 4 * pieces[0].shape[0]
    return feed_call(
        feed_body, pieces, weights, (vec,), came, [low_shape(count, 512), wide_shape(count, 512)]
    )


def feed_back_body(*refs, last):
    rows_in, weights_ref, slope_ref, rest = refs[:4], refs[4], refs[5], list(refs[6:])
    came_ref = rest.pop(0) if last else None
    (du_ref, sums_ref), outs = rest[:2], rest[2:-4]
    all_ref, in_ref, back_ref, sems = rest[-4:]
    load_all(rows_in, weights_ref, all_ref, in_ref, back_ref, sems)
    sums = [None] * (in_ref.shape[0] // FF_STEP)
    step = rows_in[0].shape[0] * 2
    for start in range(0, all_ref.shape[0], step):
        at = slice(start, start + step)
        total = None
        for i in range(len(sums)):
            lanes = slice(i * FF_STEP, (i + 1) * FF_STEP)
            du = to_low(product(all_ref[at], back_ref[:, lanes]) * slope_ref[at, lanes])
            du_ref[at, lanes] = du
            summed = column_sum(wide(du))
            sums[i] = summed if sums[i] is None else sums[i] + summed
            part = product(du, in_ref[lanes])
            total = part if total is None else total + part
        put_parts(outs, came_ref, start, total)
    for i, summed in enumerate(sums):
        sums_ref[:, i * FF_STEP : (i + 1) * FF_STEP] = summed


def feed_back(pieces, weights, slope, came=None):
    count = 4 * pieces[0].shape[0]
    return feed_call(
        feed_back_body,
        pieces,
        weights,
        (slope,),
        came,
        [low_shape(count, 512), wide_shape(1, 512)],
    )


def plane_rows(values):
    near = [values, *plane_hops([values] * 3)]
    return (*near, *(other_core(part) for part in near))


GRAD_ROWS = 448


def pair_grad_body(*refs):
    fed_in, two_in, whole_ref, halves = refs[:8], refs[8:16], refs[16], refs[17:21]
    target_ref, out_ref, fed_ref, two_ref, act_ref, du_ref, sems, out_sems = refs[21:]
    copies = []
    for pieces, target in ((fed_in, fed_ref), (two_in, two_ref), (halves[:2], act_ref), (halves[2:], du_ref)):
        rows = pieces[0].shape[0]
        for i, ref in enumerate(pieces):
            copies.append((ref, target.at[i * rows : (i + 1) * rows]))
    copies = [pltpu.make_async_copy(*copy, sems.at[i]) for i, copy in enumerate(copies)]
    for copy in copies:
        copy.start()
    for copy in copies:
        copy.wait()
    width = whole_ref.shape[1]
    stores = []
    for z in range(out_ref.shape[0] // GRAD_ROWS):
        at = z * GRAD_ROWS
        for lane in range(0, out_ref.shape[1], 512):
            lanes = slice(lane, lane + 512)
            out_ref[at : at + 128, lanes] = to_low(
                product_tn(du_ref[:, z * 128 : (z + 1) * 128], two_ref[:, lanes])
            )
        grad = to_low(product_tn(fed_ref[:, z * 256 : (z + 1) * 256], act_ref[...]))
        out_ref[at + 128 : at + 256] = jnp.concatenate([grad[:128], grad[128:]], axis=1)
        out_ref[at + 256 : at + GRAD_ROWS, :width] = whole_ref[z * 256 : z * 256 + 192]
        for piece in range(3):
            out_ref[at + 256 + piece * 64 : at + 320 + piece * 64, width:] = whole_ref[
                z * 256 + 192 : (z + 1) * 256, piece * 256 : (piece + 1) * 256
            ]
        rows = slice(at, at + GRAD_ROWS)
        stores.append(
            pltpu.make_async_copy(out_ref.at[rows], target_ref.at[rows], out_sems.at[z])
        )
        stores[-1].start()
    for copy in stores:
        copy.wait()


def pair_grads(rows_fed, rows_two, whole, acts, dus):
    rows, width = rows_fed[0].shape
    hidden = acts[0].shape[1]
    return whole_call(
        pair_grad_body,
        (*rows_fed, *rows_two, whole, *acts, *dus),
        [low_shape(4 * GRAD_ROWS, width)],
        [pltpu.VMEM((4 * GRAD_ROWS, width), jnp.bfloat16)]
        + [pltpu.VMEM((8 * rows, width), jnp.bfloat16)] * 2
        + [pltpu.VMEM((8 * rows, hidden), jnp.bfloat16)] * 2
        + [pltpu.SemaphoreType.DMA((20,)), pltpu.SemaphoreType.DMA((4,))],
        [*range(16), *range(17, 21)],
        placed=(0,),
    )[0]


def split_grad_body(sum_ref, in_ref, *outs):
    in_ref[...] = wide(sum_ref[:128])
    rows, half = outs[0].shape[0], sum_ref.shape[1] // 2
    for i, step in enumerate(NEAR):
        place = chip_place(step)
        at = pl.ds(pl.multiple_of(128 + (place % 2) * rows, rows), rows)
        lanes = pl.ds(pl.multiple_of((place // 2) * half, half), half)
        outs[i][:, :half] = sum_ref[at, lanes]
        first = pl.multiple_of(256 + jnp.minimum(place, 2) * rows, rows)
        whole = sum_ref[pl.ds(first, rows), : outs[i].shape[1] - half]
        fourth = jnp.concatenate(
            [sum_ref[256 + q * rows : 256 + (q + 1) * rows, whole.shape[1] :] for q in range(3)],
            axis=1,
        )
        outs[i][:, half:] = jnp.where(place == 3, fourth, whole)


def z_sum(refs):
    total = wide(refs[0][...])
    for ref in refs[1:]:
        total = total + wide(ref[...])
    return total


def pick_body(out_ref, back_ref, pairs_ref, *outs):
    for chip in range(16):
        pair = pl.multiple_of((lax.axis_index("grp") * 4 + chip % 4) * PAIR, PAIR)
        pairs_ref[chip] = out_ref[:, pl.ds(pair, PAIR)]
    half = outs[0].shape[1]
    for i, (step, lane) in enumerate(zip((0, 1, 2, 1), (0, 0, 0, half))):
        for block in range(4):
            outs[step][:, lane + block * 128 : lane + (block + 1) * 128] = back_ref[
                :, pl.ds(chunk_place(block, NEAR[i]), 128)
            ]


def lay_body(in_ref, own_ref, came_x_ref, came_y_ref, out_ref):
    out_ref[:128] = in_ref[...]
    half = own_ref.shape[1]
    for i, (ref, lane) in enumerate(
        ((own_ref, 0), (came_x_ref, 0), (came_y_ref, 0), (came_y_ref, half))
    ):
        place = chip_place(NEAR[i])
        rows = pl.ds(pl.multiple_of(128 + (place % 2) * 64, 64), 64)
        out_ref[rows, pl.ds(pl.multiple_of((place // 2) * half, half), half)] = ref[
            :, lane : lane + half
        ]


def core_order(own, other):
    first = lax.axis_index("grp") == 0
    return jnp.concatenate(
        [jnp.where(first, own, other), jnp.where(first, other, own)], axis=1
    )


def core_halves(values):
    part = values.shape[1] // 2
    first = lax.axis_index("grp") == 0
    low_half, high_half = values[:, :part], values[:, part:]
    return (
        jnp.where(first, low_half, high_half),
        jnp.where(first, high_half, low_half),
    )


def halves_nt(values, own_ref, other_ref, lanes):
    own, other = core_halves(values)
    return product_nt(own, own_ref[:, lanes]) + product_nt(other, other_ref[:, lanes])


def bottle_body(
    attended_ref,
    keep_ref,
    came_x_ref,
    came_y_ref,
    came_far_ref,
    vec_ref,
    own_ref,
    other_ref,
    noise_ref,
    cot_ref,
    means_ref,
    logvars_ref,
    out_ref,
    fed_ref,
    sample_ref,
    dlat_ref,
    dfed_ref,
    dfed_low_ref,
    dmeans_ref,
    dlogvars_ref,
    sums_ref,
):
    rows, width = attended_ref.shape
    lat = noise_ref.shape[1]
    comps = means_ref.shape[0]
    parts = z_sum((keep_ref, came_x_ref, came_y_ref, came_far_ref))
    fed = attended_ref[...] + parts + vec_ref[7:8]
    fed_low = to_low(fed)
    fed_ref[...] = fed_low
    latent = halves_nt(fed_low, own_ref, other_ref, LAT_LANES) + vec_ref[LAT_ROW : LAT_ROW + 1]
    logvar = latent[:, lat:]
    noise = noise_ref[...]
    spread = jnp.exp(0.5 * logvar) * noise
    sample = latent[:, :lat] + spread
    sample_low = to_low(sample)
    sample_ref[...] = sample_low
    out_ref[...] = fed + halves_nt(sample_low, own_ref, other_ref, DEC_LANES) + vec_ref[8:9]
    cot = cot_ref[...]
    dsample = core_order(
        product(cot, own_ref[:, DEC_LANES]), product(cot, other_ref[:, DEC_LANES])
    )

    span = rows // 2
    row = lax.broadcasted_iota(jnp.int32, (rows, 1), 0)
    block = lax.axis_index("y") * 2 + lax.axis_index("x")
    place = slide_place(lax.axis_index("grp"), block, row // span, row & (span - 1), span)
    live = place.astype(jnp.float32) < vec_ref[LEN_ROW : LEN_ROW + 1, 0:1]
    share = jnp.where(live, 1.0 / lat, 0.0)
    own_term = jnp.sum(-0.5 * noise * noise - 0.5 * logvar, axis=-1, keepdims=True)
    logvars = logvars_ref[...]
    inverse = jnp.exp(-logvars)
    terms = []
    for c in range(comps):
        offset = sample - means_ref[c : c + 1]
        terms.append(
            jnp.sum(
                -0.5 * offset * offset * inverse[c : c + 1] - 0.5 * logvars[c : c + 1],
                axis=-1,
                keepdims=True,
            )
            - math.log(comps)
        )
    peak = terms[0]
    for term in terms[1:]:
        peak = jnp.maximum(peak, term)
    weights = [jnp.exp(term - peak) for term in terms]
    total = weights[0]
    for weight in weights[1:]:
        total = total + weight
    kl_cell = own_term - (peak + jnp.log(total))
    kl = jnp.sum(jnp.where(live, kl_cell, 0.0), axis=0, keepdims=True) / lat
    scale = share / total
    for c in range(comps):
        offset = sample - means_ref[c : c + 1]
        slope = offset * inverse[c : c + 1]
        part = weights[c] * scale
        pull = part * slope
        dsample = dsample + pull
        dmeans_ref[c : c + 1] = -column_sum(pull)
        dlogvars_ref[c : c + 1] = column_sum(0.5 * part - 0.5 * (pull * offset))
    dlat = jnp.concatenate([dsample, 0.5 * dsample * spread - 0.5 * share], axis=1)
    dlat_low = to_low(dlat)
    dlat_ref[...] = dlat_low
    grad_out = wide(cot)
    dfed = grad_out + core_order(
        product(dlat_low, own_ref[:, LAT_LANES]), product(dlat_low, other_ref[:, LAT_LANES])
    )
    dfed_ref[...] = dfed
    dfed_low_ref[...] = to_low(dfed)
    sums_ref[...] = jnp.concatenate(
        [
            column_sum(wide(dlat_low)),
            column_sum(dfed),
            column_sum(grad_out),
            jnp.broadcast_to(kl, (1, width)),
            jnp.zeros((4, width), jnp.float32),
        ]
    )


def bottle_call(attended, parts, vec, weights, noise, cot, means, logvars):
    rows, width = attended.shape
    lat = noise.shape[1]
    return whole_call(
        bottle_body,
        (attended, *parts, vec, *weights, noise, cot, means, logvars),
        [
            wide_shape(rows, width),
            low_shape(rows, width),
            low_shape(rows, lat),
            low_shape(rows, width),
            wide_shape(rows, width),
            low_shape(rows, width),
            wide_shape(*means.shape),
            wide_shape(*means.shape),
            wide_shape(8, width),
        ],
    )


def project_back_body(
    keep_ref,
    came_x_ref,
    came_y_ref,
    came_far_ref,
    attended_ref,
    dfed_ref,
    vec_ref,
    sent_ref,
    datt_ref,
    datt_low_ref,
    sums_ref,
):
    grad = z_sum((keep_ref, came_x_ref, came_y_ref, came_far_ref))
    unit, scale = row_stats(attended_ref[...])
    datt = dfed_ref[...] + norm_back(grad, unit, scale, vec_ref[5:6])
    datt_ref[...] = datt
    datt_low_ref[...] = to_low(datt)
    sums_ref[...] = jnp.concatenate(
        [
            column_sum(grad * unit),
            column_sum(grad),
            column_sum(datt),
            jnp.zeros((5, datt.shape[1]), jnp.float32),
        ]
    )


def project_back(parts, attended, dfed, vec, sent):
    rows, width = attended.shape
    return whole_call(
        project_back_body,
        (*parts, attended, dfed, vec, sent),
        [wide_shape(rows, width), low_shape(rows, width), wide_shape(8, width)],
        left_out=(7,),
    )


def whole_grads_body(*refs):
    out_ref = refs[-1]
    for lanes, (left, left_other, right, right_other) in (
        (LAT_LANES, refs[:4]),
        (DEC_LANES, refs[4:8]),
    ):
        grads = jnp.concatenate([left[...], left_other[...]])
        values = jnp.concatenate([core_halves(right[...])[0], core_halves(right_other[...])[0]])
        out_ref[:, lanes] = to_low(product_tn(grads, values))


def whole_grads(pairs):
    operands = []
    for values in pairs:
        operands += [values, other_core(values)]
    width = pairs[0].shape[1]
    return whole_call(whole_grads_body, operands, [low_shape(width, DEC_LANES.stop)])[0]


def sum_body(*refs):
    refs[-1][...] = z_sum(refs[:-1])


def last_grad_body(*refs):
    out_ref, wholes = refs[8], refs[9:]
    half = out_ref.shape[1] // 8
    for i, ref in enumerate(refs[:8]):
        for block in range(4):
            place = chunk_place(block, NEAR[i % 4], i // 4)
            out_ref[:, pl.ds(place, 128)] = wide(ref[:, block * 128 : (block + 1) * 128])
    for core in range(2):
        wholes[core][...] = z_sum([ref.at[:, half:] for ref in refs[core * 4 : core * 4 + 4]])


def cells_back_body(
    keep_ref,
    came_x_ref,
    came_y_ref,
    came_far_ref,
    hidden_ref,
    datt_ref,
    vec_ref,
    bottle_sums_ref,
    project_sums_ref,
    head_sums_ref,
    ff_sums_ref,
    ff_more_ref,
    dmeans_ref,
    dlogvars_ref,
    out_grad_ref,
    grad_ref,
    packed_ref,
    inner_ref,
    rows_ref,
):
    grad = z_sum((keep_ref, came_x_ref, came_y_ref, came_far_ref))
    unit, scale = row_stats(wide(hidden_ref[...]))
    grad_ref[...] = datt_ref[...] + norm_back(grad, unit, scale, vec_ref[0:1])
    width = grad.shape[1]
    count = packed_ref.shape[0]
    inner_ref[...] = jnp.zeros_like(inner_ref)
    for block in range(4):
        lanes = slice(block * 128, block * 128 + 128)
        inner_ref[:, pl.ds(chunk_place(block), 128)] = (
            ff_sums_ref[:, lanes] + ff_more_ref[:, lanes]
        )
    inner_ref[:, inner_ref.shape[1] - width :] = bottle_sums_ref[0:1]
    rows_ref[...] = jnp.zeros_like(rows_ref)
    rows_ref[0:1] = column_sum(grad * unit)
    rows_ref[1:2] = column_sum(grad)
    rows_ref[2:3, pl.ds(own_pair(), PAIR)] = head_sums_ref[:, :PAIR]
    rows_ref[3:4, pl.ds(own_pair(), PAIR)] = head_sums_ref[:, 2 * PAIR :]
    rows_ref[4:5] = project_sums_ref[2:3]
    rows_ref[5:7] = project_sums_ref[0:2]
    rows_ref[7:9] = bottle_sums_ref[1:3]
    part = width // count
    pieces = inner_ref.shape[1] // width
    for i in range(pieces):
        rows_ref[9 + i : 10 + i] = jnp.concatenate(
            [
                inner_ref[:, (b * pieces + i) * part : (b * pieces + i + 1) * part]
                for b in range(count)
            ],
            axis=1,
        )
    rows_ref[14:15] = bottle_sums_ref[3:4]
    lat_part = dmeans_ref.shape[1] // count
    for b in range(count):
        sums = jnp.concatenate(
            [
                rows_ref[:, b * part : (b + 1) * part],
                dmeans_ref[:, b * lat_part : (b + 1) * lat_part],
                dlogvars_ref[:, b * lat_part : (b + 1) * lat_part],
            ],
            axis=1,
        )
        high = to_low(sums)
        packed_ref[b, :part] = out_grad_ref[b]
        packed_ref[b, part : part + SMALL] = high
        packed_ref[b, part + SMALL :] = to_low(sums - wide(high))


def last_sum_body(came_ref, out_ref):
    count, rows = came_ref.shape[0], came_ref.shape[1] - 2 * SMALL
    for chip in range(4):
        total = z_sum([came_ref.at[z * 4 + chip, :rows] for z in range(4)])
        out_ref[:rows, chip * PAIR : (chip + 1) * PAIR] = total
    small = z_sum([came_ref.at[i, rows : rows + SMALL] for i in range(count)])
    rest = z_sum([came_ref.at[i, rows + SMALL :] for i in range(count)])
    out_ref[rows:] = jnp.zeros((SMALL, out_ref.shape[1]), jnp.float32)
    out_ref[rows:, :PAIR] = small + rest


def last_body(own_ref, other_ref, grad_ref, small_ref):
    rows, half = grad_ref.shape[0], own_ref.shape[1]
    for ref, place in ((own_ref, 0), (other_ref, 1)):
        core = flip(lax.axis_index("grp"), place)
        grad_ref[:, pl.ds(pl.multiple_of(core * half, half), half)] = ref[:rows]
    small_ref[...] = own_ref[rows:, :PAIR] + other_ref[rows:, :PAIR]


def cells_back(operands, inner):
    rows, width = operands[0].shape
    return whole_call(
        cells_back_body,
        operands,
        [wide_shape(rows, width), low_shape(16, width // 16 + 2 * SMALL, PAIR)],
        [pltpu.VMEM((1, inner), jnp.float32), pltpu.VMEM((SMALL, width), jnp.float32)],
    )


def exchange(blocks, axes):
    return lax.all_to_all(blocks, axes, split_axis=0, concat_axis=0, tiled=True)


def to_all(values, count):
    return jnp.broadcast_to(values[None], (count, *values.shape))


def fast_device(
    cell_input,
    lengths,
    noise_draw,
    cotangent,
    w_qkv,
    w_out,
    w_ffn_in,
    w_ffn_out,
    w_latent,
    w_decode,
    vectors,
    inner_bias,
    prior_means,
    prior_logvars,
):
    slots, span, width = cell_input.shape[1:]
    rows = slots * span
    lat = noise_draw.shape[-1]
    comps = prior_means.shape[1]
    ff = w_ffn_out.shape[1]
    inner = 16 * inner_bias.shape[1]

    part = width // 16
    shard = jnp.concatenate(
        [half_of(w[0], 0, "grp", True).T for w in (w_latent, w_decode)], axis=1
    )
    shard_width = shard.shape[1]
    whole = lax.all_gather(shard, CHIPS, axis=0, tiled=True)

    out_pairs, back_own, back_x, back_y = whole_call(
        pick_body,
        after((w_out[0].T, w_ffn_out[0].T), shard),
        [low_shape(16, part, PAIR)]
        + [low_shape(part, ff // 8 * count) for count in (1, 2, 1)],
    )
    out_t = exchange(out_pairs, CHIPS).reshape(width, PAIR)

    blocks = whole_call(
        enter_body,
        (
            after(cell_input.reshape(rows, width), out_pairs),
            lengths,
            vectors[0],
            inner_bias,
            prior_means[0],
            prior_logvars[0],
        ),
        [low_shape(span + SMALL, width)] * 2,
    )
    first = jnp.stack(
        [lax.ppermute(blocks[k], ("grp", "z"), slide_routes(k)) for k in range(2)]
    )

    qkv_t = w_qkv[0].T
    at_x = lax.axis_index("x") % 2
    head_parts = (
        lax.dynamic_slice_in_dim(qkv_t, at_x * HEAD_DIM, PAIR),
        lax.dynamic_slice_in_dim(qkv_t, (1 - at_x) * PAIR, HEAD_DIM),
    )
    came = [
        lax.ppermute(head_parts[int(single)], EVERY, head_routes(single, k))
        for single, k in ARRIVALS
    ]

    in_own = half_of(w_ffn_in[0], 1, "grp", True).T
    noise_high = to_low(noise_draw[0, 0])
    noise_rest = to_low(noise_draw[0, 0] - wide(noise_high))
    extra = jnp.concatenate(
        [cotangent[0], jnp.concatenate([noise_high, noise_rest], axis=2)], axis=1
    )
    size = span + SMALL
    one, two = first[0], first[1]
    one_x = hop(jnp.concatenate([one, back_x]), "x")
    two_y = hop(two, "y")
    sent = jnp.concatenate(
        [one, one_x[:size], jnp.concatenate([back_y, one_x[size:, ff // 8 :]], axis=1)]
    )
    sent_y, sent_x = after((sent, jnp.concatenate([two, two_y])), (came[:2], extra, out_t))
    near_y = hop(sent_y, "y")
    near_x = hop(sent_x, "x")
    plane_own = jnp.concatenate(
        [one, two, one_x[:size], near_x[:size], near_y[:size], two_y]
        + [near_y[size : 2 * size], near_x[size:]]
    ).reshape(4, 2, size, width)
    plane_own, came = lax.optimization_barrier((plane_own, came))
    plane_other = other_core(plane_own)
    (pair_own,) = whole_call(
        lay_body,
        (in_own, back_own, one_x[size:], near_y[2 * size :]),
        [low_shape(256, width)],
    )
    pair_w = lax.all_gather(pair_own, "z", axis=0, tiled=True)

    vec, means, logvars, normed, qkv, head_w, mixed, lse, bias = attend(
        plane_own, plane_other, after(came, pair_own), lat, inner
    )
    mix_parts = mix_out(mixed, out_t, whole)

    extra = to_slides(after(extra, mixed))
    cot = extra[:, :span].reshape(rows, width)
    noise = extra[:, span:].reshape(rows, width)
    noise = wide(noise[:, :lat]) + wide(noise[:, lat:])

    attended, normed_two, hidden = project(mix_parts, first, vec)
    rows_two = plane_rows(normed_two)
    act_far, slope_far, fed_far = feed(pinned(rows_two[4:]), pinned([pair_w])[0], vec)
    act, slope, keep, *sends = feed(
        pinned(rows_two[:4]), pinned([pair_w])[0], vec, other_core(fed_far)
    )
    fed_parts = (keep, *plane_hops(sends))
    wholes = (whole, other_core(whole))
    output, fed_low, sample_low, dlat_low, dfed, dfed_low, dmeans, dlogvars, bottle_sums = (
        bottle_call(
            attended, fed_parts, vec, wholes, noise, cot, means, logvars
        )
    )

    rows_fed = plane_rows(dfed_low)
    layer_out = from_slides(after(to_low(output), rows_fed).reshape(slots, span, width))
    whole_grad = whole_grads((dlat_low, fed_low, cot, sample_low))
    du_far, ff_far, norm_far = feed_back(rows_fed[4:], pair_w, slope_far)
    du, ff_sums, keep, *sends = feed_back(
        rows_fed[:4], pair_w, slope, after(other_core(norm_far), whole_grad)
    )
    norm_parts = (keep, *plane_hops(sends))
    grads = pair_grads(rows_fed, pinned(rows_two), whole_grad, (act, act_far), (du, du_far))
    grads_sum = lax.psum_scatter(grads, "z", scatter_dimension=0, tiled=True)
    datt, datt_low, project_sums = project_back(
        after(norm_parts, grads), attended, dfed, vec, layer_out
    )
    rows_datt = plane_rows(datt_low)
    out_grad, all_datt = out_grads(rows_datt, mixed)
    dqkv, dn_far = attend_back(qkv, bias, lse, out_t, head_w, all_datt)
    dn_keep, *dn_sends = dnormed(dqkv, head_w, other_core(dn_far))
    homes, head_sums = head_grads(dqkv, after(normed, dn_sends))
    dn_parts = (dn_keep, *plane_hops(dn_sends))
    grad_rows, packed = cells_back(
        (
            *dn_parts,
            hidden,
            datt,
            vec,
            bottle_sums,
            project_sums,
            head_sums,
            ff_sums,
            ff_far,
            dmeans,
            dlogvars,
            out_grad,
        ),
        inner,
    )
    grad_cells = wide(from_slides(to_low(grad_rows).reshape(slots, span, width)))
    sum_in, *sums = whole_call(
        split_grad_body,
        (after(grads_sum, packed),),
        [wide_shape(128, width)] + [low_shape(part, ff // 8 + shard_width)] * 4,
    )
    sums = [sums[0], *plane_hops(sums[1:])]
    sums += [other_core(total) for total in sums]

    (last,) = whole_call(
        last_sum_body, (exchange(packed, CHIPS),), [wide_shape(part + SMALL, 4 * PAIR)]
    )
    grad_out_w, small_sums = whole_call(
        last_body, (last, other_core(last)), [wide_shape(part, width), wide_shape(SMALL, PAIR)]
    )
    grad_out_w = grad_out_w.T
    homes = [
        lax.ppermute(grad, EVERY, [(there, here) for here, there in head_routes(single, k)])
        for grad, (single, k) in zip(homes, ARRIVALS)
    ]
    (home,) = whole_call(
        home_body, after(homes, (packed, sums[1:4])), [wide_shape(3 * HEAD_DIM, width)]
    )
    grad_qkv = (home + other_core(home)).T
    vec_out = small_sums[:9, :part]
    inner_out = small_sums[9 : 9 + inner // width, :part].reshape(1, -1)
    means_out = small_sums[:, part : part + lat // 16]
    logvars_out = small_sums[:, part + lat // 16 :]
    kl_mean = small_sums[14, 0] / (32 * rows)

    grad_in_w = ordered(sum_in.T, other_core(sum_in).T, "grp", 1)
    grad_back_w, whole_own, whole_other = whole_call(
        last_grad_body,
        sums,
        [wide_shape(part, ff)] + [wide_shape(part, shard_width)] * 2,
    )
    grad_back_w = grad_back_w.T
    grad_lat_w, grad_dec_w = (
        ordered(whole_own[:, lanes].T, whole_other[:, lanes].T, "grp", 0)
        for lanes in (LAT_LANES, DEC_LANES)
    )
    return (
        wide(layer_out).reshape(1, slots, span, width),
        grad_cells.reshape(1, slots, span, width),
        kl_mean,
        grad_qkv[None],
        grad_out_w[None],
        grad_in_w[None],
        grad_back_w[None],
        grad_lat_w[None],
        grad_dec_w[None],
        vec_out[None],
        inner_out,
        means_out[None],
        logvars_out[None],
    )


def solution(mesh):
    chips = mesh.shape["blk"]
    if (mesh.shape["grp"], chips) == (2, HEADS):
        mesh = Mesh(mesh.devices.reshape(2, chips // 4, 2, 2), EVERY)
        blk, run = CHIPS, fast_device
    else:
        blk, run = "blk", per_device
    cells = P("grp", None, blk, None)
    columns = P(None, None, blk)
    return jax.shard_map(
        run,
        mesh=mesh,
        in_specs=(cells, P("grp", None), P(None, "grp", None, blk, None), cells)
        + (columns,) * 7
        + (P(None, blk), columns, columns),
        out_specs=(cells, cells, P()) + (columns,) * 7 + (P(None, blk), columns, columns),
        check_vma=False,
    )
```

```python
import functools
import math

import jax
import jax.numpy as jnp
import numpy as np
from jax import lax
from jax.experimental import pallas as pl
from jax.experimental.pallas import tpu as pltpu
from jax.sharding import Mesh
from jax.sharding import PartitionSpec as P

HEADS = 16
LAYERS = 1
HEAD_DIM = 64


EPS_NORM = 1e-05
MASKED = -1e30


def to_low(values):
    return values.astype(jnp.bfloat16)


def product(left, right):
    return jnp.dot(left, right, preferred_element_type=jnp.float32)


def product_tn(left, right):
    return lax.dot_general(
        left, right, (((0,), (0,)), ((), ())), preferred_element_type=jnp.float32
    )


def product_nt(left, right):
    return lax.dot_general(
        left, right, (((1,), (1,)), ((), ())), preferred_element_type=jnp.float32
    )


def layer_norm(values, norm_gain, norm_shift):
    centre = values - jnp.mean(values, axis=-1, keepdims=True)
    spread = jnp.mean(centre * centre, axis=-1, keepdims=True)
    return centre * lax.rsqrt(spread + EPS_NORM) * norm_gain + norm_shift


def mixture_kl(sample, noise_rows, logvar, mean_rows, logvars):
    own_term = jnp.sum(-0.5 * noise_rows * noise_rows - 0.5 * logvar, axis=-1)
    offset = sample[:, None, :] - mean_rows[None, :, :]
    component = jnp.sum(
        -0.5 * offset * offset * jnp.exp(-logvars)[None] - 0.5 * logvars[None], axis=-1
    ) - math.log(mean_rows.shape[0])
    row_peak = jnp.max(component, axis=-1, keepdims=True)
    mixture = row_peak[:, 0] + jnp.log(jnp.sum(jnp.exp(component - row_peak), axis=-1))
    return own_term - mixture


def bottleneck(latent, noise_rows, live_rows, mean_rows, logvars):
    lat_width = noise_rows.shape[-1]
    mean_part = latent[:, :lat_width]
    logvar = latent[:, lat_width:]
    sample = mean_part + jnp.exp(0.5 * logvar) * noise_rows
    per_cell = mixture_kl(sample, noise_rows, logvar, mean_rows, logvars)
    return (sample, jnp.sum(jnp.where(live_rows, per_cell, 0.0)) / lat_width)


def slot_scores(query_slots, keys_all, slide_len, score_scale):
    slot_count, query_rows, model_width = query_slots.shape
    heads_q = query_slots.reshape(slot_count, query_rows, HEADS, HEAD_DIM)
    heads_k = keys_all.reshape(slot_count, keys_all.shape[1], HEADS, HEAD_DIM)
    raw_scores = (
        jnp.einsum("sqhd,skhd->shqk", heads_q, heads_k, preferred_element_type=jnp.float32)
        * score_scale
    )
    live_keys = jnp.arange(keys_all.shape[1])[None, :] < slide_len[:, None]
    return jnp.where(live_keys[:, None, None, :], raw_scores, MASKED)


def widen(gathered):
    qkv_w, out_w, in_w, back_w, latent_w, decode_w, vec_rows, inner_rows, mean_rows, logvars = (
        gathered
    )
    return (
        qkv_w,
        out_w,
        in_w,
        back_w,
        latent_w,
        decode_w,
        vec_rows.astype(jnp.float32),
        inner_rows.astype(jnp.float32),
        mean_rows.astype(jnp.float32),
        logvars.astype(jnp.float32),
    )


def gather_weights(layer_parts):
    (
        part_qkv,
        part_out,
        part_in,
        part_back,
        part_latent,
        part_decode,
        part_vectors,
        part_inner,
        part_means,
        part_logvars,
    ) = layer_parts
    return widen(
        (
            lax.all_gather(part_qkv, "blk", axis=1, tiled=True),
            lax.all_gather(part_out, "blk", axis=1, tiled=True),
            lax.all_gather(part_in, "blk", axis=1, tiled=True),
            lax.all_gather(part_back, "blk", axis=1, tiled=True),
            lax.all_gather(part_latent, "blk", axis=1, tiled=True),
            lax.all_gather(part_decode, "blk", axis=1, tiled=True),
            lax.all_gather(part_vectors, "blk", axis=1, tiled=True),
            lax.all_gather(part_inner, "blk", axis=0, tiled=True),
            lax.all_gather(part_means, "blk", axis=1, tiled=True),
            lax.all_gather(part_logvars, "blk", axis=1, tiled=True),
        )
    )


def reduce_grads(grads):
    (
        grad_qkv_w,
        grad_out_w,
        grad_in_w,
        grad_back_w,
        grad_latent_w,
        grad_decode_w,
        grad_vec,
        grad_inner,
        grad_mean_rows,
        grad_logvars,
    ) = grads
    (
        shard_qkv,
        shard_out,
        shard_in,
        shard_back,
        shard_latent,
        shard_decode,
        shard_vec,
        shard_inner,
        shard_means,
        shard_logvars,
    ) = (
        lax.psum_scatter(grad_qkv_w, "blk", scatter_dimension=1, tiled=True),
        lax.psum_scatter(grad_out_w, "blk", scatter_dimension=1, tiled=True),
        lax.psum_scatter(grad_in_w, "blk", scatter_dimension=1, tiled=True),
        lax.psum_scatter(grad_back_w, "blk", scatter_dimension=1, tiled=True),
        lax.psum_scatter(grad_latent_w, "blk", scatter_dimension=1, tiled=True),
        lax.psum_scatter(grad_decode_w, "blk", scatter_dimension=1, tiled=True),
        lax.psum_scatter(grad_vec, "blk", scatter_dimension=1, tiled=True),
        lax.psum_scatter(grad_inner, "blk", scatter_dimension=0, tiled=True),
        lax.psum_scatter(grad_mean_rows, "blk", scatter_dimension=1, tiled=True),
        lax.psum_scatter(grad_logvars, "blk", scatter_dimension=1, tiled=True),
    )
    return lax.psum(
        (
            shard_qkv,
            shard_out,
            shard_in,
            shard_back,
            shard_latent,
            shard_decode,
            shard_vec,
            shard_inner,
            shard_means,
            shard_logvars,
        ),
        "grp",
    )


def layer_forward(hidden, full_weights, noise_rows, live_rows, slide_len, score_scale):
    qkv_w, out_w, in_w, back_w, latent_w, decode_w, vec_rows, inner_rows, mean_rows, logvars = (
        full_weights
    )
    model_width = hidden.shape[1]
    slot_count = slide_len.shape[0]
    slot_span = hidden.shape[0] // slot_count
    ff_width = in_w.shape[1]
    normed = to_low(layer_norm(hidden, vec_rows[0], vec_rows[1]))
    qkv_all = product(normed, qkv_w)
    query_low = to_low(qkv_all[:, :model_width] + vec_rows[2])
    keys_own = to_low(qkv_all[:, model_width : 2 * model_width])
    values_own = to_low(qkv_all[:, 2 * model_width :] + vec_rows[3])
    keys_all, values_all = (
        lax.all_gather(
            keys_own.reshape(slot_count, slot_span, model_width), "blk", axis=1, tiled=True
        ),
        lax.all_gather(
            values_own.reshape(slot_count, slot_span, model_width), "blk", axis=1, tiled=True
        ),
    )
    scores = slot_scores(
        query_low.reshape(slot_count, slot_span, model_width), keys_all, slide_len, score_scale
    )
    row_peak = jnp.max(scores, axis=-1, keepdims=True)
    weights = jnp.exp(scores - row_peak)
    totals = jnp.sum(weights, axis=-1, keepdims=True)
    probs_low = to_low(weights / totals)
    log_total = row_peak + jnp.log(totals)
    heads_v = values_all.reshape(slot_count, values_all.shape[1], HEADS, HEAD_DIM)
    mixed_f = jnp.einsum("shqk,skhd->sqhd", probs_low, heads_v, preferred_element_type=jnp.float32)
    mixed_low = to_low(mixed_f.reshape(slot_count * slot_span, model_width))
    attended = hidden + product(mixed_low, out_w) + vec_rows[4]
    normed_two = to_low(layer_norm(attended, vec_rows[5], vec_rows[6]))
    inner_act = product(normed_two, in_w) + inner_rows[:ff_width]
    activated = to_low(jax.nn.gelu(inner_act))
    fed_rows = attended + product(activated, back_w) + vec_rows[7]
    fed_low = to_low(fed_rows)
    latent = product(fed_low, latent_w) + inner_rows[ff_width:]
    sample, kl_part = bottleneck(latent, noise_rows, live_rows, mean_rows, logvars)
    sample_low = to_low(sample)
    output = fed_rows + product(sample_low, decode_w) + vec_rows[8]
    saved_state = (
        hidden,
        normed,
        query_low,
        keys_own,
        values_own,
        log_total,
        mixed_low,
        attended,
        normed_two,
        inner_act,
        activated,
        fed_low,
        latent,
        sample_low,
    )
    return (output, kl_part, saved_state)


def layer_backward(
    grad_out, full_weights, saved_state, noise_rows, live_rows, slide_len, score_scale
):
    qkv_w, out_w, in_w, back_w, latent_w, decode_w, vec_rows, inner_rows, mean_rows, logvars = (
        full_weights
    )
    (
        hidden,
        normed,
        query_low,
        keys_own,
        values_own,
        log_total,
        mixed_low,
        attended,
        normed_two,
        inner_act,
        activated,
        fed_low,
        latent,
        sample_low,
    ) = saved_state
    model_width = hidden.shape[1]
    row_total = hidden.shape[0]
    slot_count = slide_len.shape[0]
    slot_span = row_total // slot_count
    grad_dec_low = to_low(grad_out)
    grad_decode_w = product_tn(sample_low, grad_dec_low)
    grad_sample = product_nt(grad_dec_low, decode_w)

    def bottle(latent_in, means_in, logvars_in):
        return bottleneck(latent_in, noise_rows, live_rows, means_in, logvars_in)

    ignored, bottle_pull = jax.vjp(bottle, latent, mean_rows, logvars)
    grad_latent_f, grad_mean_rows, grad_logvars = bottle_pull(
        (grad_sample, jnp.ones((), jnp.float32))
    )
    grad_latent_low = to_low(grad_latent_f)
    grad_latent_w = product_tn(fed_low, grad_latent_low)
    grad_fed = grad_out + product_nt(grad_latent_low, latent_w)
    grad_fed_low = to_low(grad_fed)
    grad_back_w = product_tn(activated, grad_fed_low)
    grad_act = product_nt(grad_fed_low, back_w)
    ignored_two, gelu_pull = jax.vjp(jax.nn.gelu, inner_act)
    grad_inner_low = to_low(gelu_pull(grad_act)[0])
    grad_in_w = product_tn(normed_two, grad_inner_low)
    grad_normed_two = product_nt(grad_inner_low, in_w)
    ignored_three, second_pull = jax.vjp(layer_norm, attended, vec_rows[5], vec_rows[6])
    grad_att_norm, grad_gain_two, grad_shift_two = second_pull(grad_normed_two)
    grad_attended = grad_fed + grad_att_norm
    grad_proj_low = to_low(grad_attended)
    grad_out_w = product_tn(mixed_low, grad_proj_low)
    grad_mixed_low = to_low(product_nt(grad_proj_low, out_w))
    keys_all, values_all = (
        lax.all_gather(
            keys_own.reshape(slot_count, slot_span, model_width), "blk", axis=1, tiled=True
        ),
        lax.all_gather(
            values_own.reshape(slot_count, slot_span, model_width), "blk", axis=1, tiled=True
        ),
    )
    grad_mixed_heads = grad_mixed_low.reshape(slot_count, slot_span, HEADS, HEAD_DIM)
    heads_k = keys_all.reshape(slot_count, keys_all.shape[1], HEADS, HEAD_DIM)
    heads_v = values_all.reshape(slot_count, values_all.shape[1], HEADS, HEAD_DIM)
    scores = slot_scores(
        query_low.reshape(slot_count, slot_span, model_width), keys_all, slide_len, score_scale
    )
    probs_f = jnp.exp(scores - log_total)
    grad_probs = jnp.einsum(
        "sqhd,skhd->shqk", grad_mixed_heads, heads_v, preferred_element_type=jnp.float32
    )
    centre = jnp.sum(grad_probs * probs_f, axis=-1, keepdims=True)
    grad_scores_low = to_low(probs_f * (grad_probs - centre))
    grad_query = (
        jnp.einsum("shqk,skhd->sqhd", grad_scores_low, heads_k, preferred_element_type=jnp.float32)
        * score_scale
    )
    grad_query_low = to_low(grad_query.reshape(row_total, model_width))
    rows_all, mixed_all = (
        lax.all_gather(
            query_low.reshape(slot_count, slot_span, model_width), "blk", axis=1, tiled=True
        ),
        lax.all_gather(
            grad_mixed_low.reshape(slot_count, slot_span, model_width), "blk", axis=1, tiled=True
        ),
    )
    total_all, centre_all = (
        lax.all_gather(log_total, "blk", axis=2, tiled=True),
        lax.all_gather(centre, "blk", axis=2, tiled=True),
    )
    query_all = rows_all.reshape(slot_count, rows_all.shape[1], HEADS, HEAD_DIM)
    dmixed_all = mixed_all.reshape(slot_count, mixed_all.shape[1], HEADS, HEAD_DIM)
    own_keys = keys_own.reshape(slot_count, slot_span, HEADS, HEAD_DIM)
    own_values = values_own.reshape(slot_count, slot_span, HEADS, HEAD_DIM)
    own_raw = (
        jnp.einsum("sqhd,skhd->shqk", query_all, own_keys, preferred_element_type=jnp.float32)
        * score_scale
    )
    key_places = lax.axis_index("blk") * slot_span + jnp.arange(slot_span)
    live_own = key_places[None, :] < slide_len[:, None]
    own_scores = jnp.where(live_own[:, None, None, :], own_raw, MASKED)
    own_probs = jnp.exp(own_scores - total_all)
    own_dprobs = jnp.einsum(
        "sqhd,skhd->shqk", dmixed_all, own_values, preferred_element_type=jnp.float32
    )
    own_dscores = to_low(own_probs * (own_dprobs - centre_all))
    grad_keys = (
        jnp.einsum("shqk,sqhd->skhd", own_dscores, query_all, preferred_element_type=jnp.float32)
        * score_scale
    )
    grad_values = jnp.einsum(
        "shqk,sqhd->skhd", to_low(own_probs), dmixed_all, preferred_element_type=jnp.float32
    )
    grad_keys_low = to_low(grad_keys.reshape(row_total, model_width))
    grad_values_low = to_low(grad_values.reshape(row_total, model_width))
    grad_qkv_low = jnp.concatenate([grad_query_low, grad_keys_low, grad_values_low], axis=1)
    grad_qkv_w = product_tn(normed, grad_qkv_low)
    grad_normed = product_nt(grad_qkv_low, qkv_w)
    ignored_four, first_pull = jax.vjp(layer_norm, hidden, vec_rows[0], vec_rows[1])
    grad_hid_norm, grad_gain_one, grad_shift_one = first_pull(grad_normed)
    grad_hidden = grad_attended + grad_hid_norm
    grad_vec = jnp.stack(
        [
            grad_gain_one,
            grad_shift_one,
            jnp.sum(grad_query_low.astype(jnp.float32), axis=0),
            jnp.sum(grad_values_low.astype(jnp.float32), axis=0),
            jnp.sum(grad_attended, axis=0),
            grad_gain_two,
            grad_shift_two,
            jnp.sum(grad_fed, axis=0),
            jnp.sum(grad_out, axis=0),
        ]
    )
    grad_inner = jnp.concatenate(
        [
            jnp.sum(grad_inner_low.astype(jnp.float32), axis=0),
            jnp.sum(grad_latent_low.astype(jnp.float32), axis=0),
        ]
    )
    return (
        grad_hidden,
        (
            grad_qkv_w,
            grad_out_w,
            grad_in_w,
            grad_back_w,
            grad_latent_w,
            grad_decode_w,
            grad_vec,
            grad_inner,
            grad_mean_rows,
            grad_logvars,
        ),
    )


def per_device(
    cell_input,
    lengths,
    noise_draw,
    cotangent,
    w_qkv,
    w_out,
    w_ffn_in,
    w_ffn_out,
    w_latent,
    w_decode,
    vectors,
    inner_bias,
    prior_means,
    prior_logvars,
):
    slot_count = cell_input.shape[1]
    slot_span = cell_input.shape[2]
    model_width = cell_input.shape[3]
    row_total = slot_count * slot_span
    lat_width = noise_draw.shape[-1]
    cycle_size = lax.axis_size("blk")
    score_scale = 1.0 / math.sqrt(HEAD_DIM)
    slide_len = lengths[0]
    positions = lax.axis_index("blk") * slot_span + jnp.arange(slot_span)
    live_rows = (positions[None, :] < slide_len[:, None]).reshape(row_total)
    hidden = cell_input[0].reshape(row_total, model_width).astype(jnp.float32)
    stacks = (
        w_qkv,
        w_out,
        w_ffn_in,
        w_ffn_out,
        w_latent,
        w_decode,
        vectors,
        inner_bias,
        prior_means,
        prior_logvars,
    )
    layer_idx = 0
    full_weights = gather_weights([stacked[layer_idx] for stacked in stacks])
    kept_weights = [full_weights]
    hidden, kl_part, saved_state = layer_forward(
        hidden,
        full_weights,
        noise_draw[layer_idx, 0].reshape(row_total, lat_width),
        live_rows,
        slide_len,
        score_scale,
    )
    saved_layers = [saved_state]
    layer_out = hidden.reshape(1, slot_count, slot_span, model_width)
    kl_total = lax.psum(kl_part, ("grp", "blk"))
    kl_mean = kl_total / (lax.axis_size("grp") * cycle_size * row_total)
    grad_rows = cotangent[0].reshape(row_total, model_width).astype(jnp.float32)
    reduced = [None] * LAYERS
    for layer_idx in reversed(range(LAYERS)):
        full_weights = kept_weights[layer_idx]
        grad_rows, grads = layer_backward(
            grad_rows,
            full_weights,
            saved_layers[layer_idx],
            noise_draw[layer_idx, 0].reshape(row_total, lat_width),
            live_rows,
            slide_len,
            score_scale,
        )
        reduced[layer_idx] = reduce_grads(grads)
    grad_cells = grad_rows.reshape(1, slot_count, slot_span, model_width)
    stacked_grads = [jnp.stack([reduced[0][member]]) for member in range(10)]
    return (
        layer_out,
        grad_cells,
        kl_mean,
        stacked_grads[0],
        stacked_grads[1],
        stacked_grads[2],
        stacked_grads[3],
        stacked_grads[4],
        stacked_grads[5],
        stacked_grads[6],
        stacked_grads[7],
        stacked_grads[8],
        stacked_grads[9],
    )


EVERY = ("grp", "z", "y", "x")
CHIPS = ("z", "y", "x")
PLANE = ("grp", "y", "x")
PAIR = 2 * HEAD_DIM
SMALL = 16
VMEM_LIMIT = 20 * 1024 * 1024


def hop(values, axis, step=1):
    size = lax.axis_size(axis)
    return lax.ppermute(values, axis, [(i, i ^ step) for i in range(size)])


def other_core(values):
    return hop(values, "grp")


def after(values, done):
    return lax.optimization_barrier((values, done))[0]


def ordered(own, other, axis_name, axis):
    first = lax.axis_index(axis_name) == 0
    return jnp.concatenate(
        [jnp.where(first, own, other), jnp.where(first, other, own)], axis=axis
    )


def half_of(values, axis, axis_name, mine):
    part = values.shape[axis] // 2
    place = lax.axis_index(axis_name)
    place = place if mine else 1 - place
    return lax.dynamic_slice_in_dim(values, place * part, part, axis)


def flip(place, step):
    high = (place // 2 + step // 2) % 2
    low_bit = (place % 2 + step % 2) % 2
    return high * 2 + low_bit


def slide_routes(k):
    return [
        (g * 4 + z, (z // 2) * 4 + 2 * g + ((z % 2) ^ k)) for g in range(2) for z in range(4)
    ]


def pick_slot(slots, k):
    odd = (lax.axis_index("z") + k) % 2 == 1
    return jnp.where(odd, slots[1], slots[0])


def to_slides(slots):
    return jnp.stack(
        [lax.ppermute(pick_slot(slots, k), ("grp", "z"), slide_routes(k)) for k in range(2)]
    )


def from_slides(blocks):
    came = [
        lax.ppermute(
            blocks[k], ("grp", "z"), [(there, here) for here, there in slide_routes(k)]
        )
        for k in range(2)
    ]
    return jnp.stack([pick_slot(came, 0), pick_slot(came, 1)])


def head_routes(single, k):
    routes = []
    for core in range(2):
        for chip in range(16):
            odd = chip % 2
            block = 3 * chip + (2 - 2 * odd if single else odd)
            pair = (block % 16) // 2
            plane = 2 * core + (odd ^ k)
            target = (pair // 4) * 16 + plane * 4 + pair % 4
            routes.append((core * 16 + chip, target))
    return routes


ARRIVALS = [(single, k) for k in range(2) for single in (False, True)]


def low_shape(*shape):
    return jax.ShapeDtypeStruct(shape, jnp.bfloat16)


def wide(values):
    return values.astype(jnp.float32)


def z_hops(values):
    return [hop(values[step - 1], "z", step) for step in (1, 2, 3)]


def plane_hops(values):
    return [
        hop(values[0], "x"),
        hop(values[1], "y"),
        lax.ppermute(values[2], ("y", "x"), [(i, i ^ 3) for i in range(4)]),
    ]


NEAR = ((0, 0), (0, 1), (1, 0), (1, 1))


def z_at(step, part):
    return pl.ds(pl.multiple_of(flip(lax.axis_index("z"), step) * part, part), part)


def chip_place(step):
    return flip(lax.axis_index("y"), step[0]) * 2 + flip(lax.axis_index("x"), step[1])


def pinned(values):
    return [pltpu.with_memory_space_constraint(part, pltpu.HBM) for part in values]


def wide_shape(*shape):
    return jax.ShapeDtypeStruct(shape, jnp.float32)


FLOPS_PER_US = 1.1e9
TIMES = {
    "attend_body": 10.0,
    "feed_body": 3.5,
    "bottle_body": 5.7,
    "feed_back_body": 2.0,
    "pair_grad_body": 3.4,
    "attend_back_body": 9.2,
    "whole_grads_body": 1.3,
    "cells_back_body": 1.4,
}


def took(body):
    inner = body.func if isinstance(body, functools.partial) else body
    return TIMES.get(inner.__name__, 0.8)


def whole_call(
    body, operands, out_shapes, scratch=(), left_out=(), loaded=(), kept=(), early=False, placed=()
):
    vmem, hbm = pl.BlockSpec(memory_space=pltpu.VMEM), pl.BlockSpec(memory_space=pltpu.HBM)
    n_in, n_out, n_own = len(operands), len(out_shapes), len(scratch)
    left_out, loaded, kept = list(left_out), list(loaded), list(kept)

    def run(*refs):
        ins, outs = list(refs[:n_in]), list(refs[n_in : n_in + n_out])
        own = refs[n_in + n_out : n_in + n_out + n_own]
        rest = refs[n_in + n_out + n_own :]
        in_copies = []
        for at, i in enumerate(loaded):
            in_copies.append(pltpu.make_async_copy(ins[i], rest[at], rest[-1].at[at]))
            ins[i] = rest[at]
        for copy in in_copies:
            copy.start()
        out_copies = {}
        for at, i in enumerate(kept, len(loaded)):
            out_copies[i] = pltpu.make_async_copy(rest[at], outs[i], rest[-1].at[at])
            outs[i] = rest[at]
        for copy in in_copies:
            copy.wait()
        started = []

        def store(i):
            out_copies[i].start()
            started.append(i)

        body(*ins, *outs, *own, **({"store": store} if early else {}))
        for i in out_copies:
            if i not in started:
                out_copies[i].start()
        for copy in out_copies.values():
            copy.wait()

    operands = [
        pltpu.with_memory_space_constraint(part, pltpu.HBM)
        if i in loaded
        else part
        for i, part in enumerate(operands)
    ]
    buffers = [pltpu.VMEM(operands[i].shape, operands[i].dtype) for i in loaded]
    buffers += [pltpu.VMEM(out_shapes[i].shape, out_shapes[i].dtype) for i in kept]
    if buffers:
        buffers.append(pltpu.SemaphoreType.DMA((len(buffers),)))
    out_shapes = [
        pltpu.HBM(part.shape, part.dtype) if i in kept or i in placed else part
        for i, part in enumerate(out_shapes)
    ]
    return pl.pallas_call(
        run,
        out_shape=out_shapes,
        in_specs=[hbm if i in left_out or i in loaded else vmem for i in range(n_in)],
        out_specs=[hbm if i in kept or i in placed else vmem for i in range(n_out)],
        scratch_shapes=[*scratch, *buffers],
        compiler_params=pltpu.CompilerParams(vmem_limit_bytes=VMEM_LIMIT),
        cost_estimate=pl.CostEstimate(
            flops=int(took(body) * FLOPS_PER_US), bytes_accessed=0, transcendentals=0
        ),
    )(*operands)


def enter_body(cells_ref, lens_ref, vectors_ref, inner_ref, means_ref, logvars_ref, *outs):
    span = cells_ref.shape[0] // 2
    lens = lens_ref[...]
    lens = jnp.concatenate([lens >> 5, lens & 31], axis=1).astype(jnp.float32)
    for k, ref in enumerate(outs):
        slot = (lax.axis_index("z") + k) % 2
        ref[:span] = cells_ref[pl.ds(pl.multiple_of(slot * span, span), span)]
        ref[span:] = jnp.zeros((SMALL, ref.shape[1]), jnp.bfloat16)
        ref[span : span + 9, 0:64] = vectors_ref[...]
        ref[span:, 128:160] = means_ref[...]
        ref[span:, 256:288] = logvars_ref[...]
        ref[span : span + 1, 384:704] = inner_ref[...]
        ref[span : span + 1, 768:772] = to_low(lens)


def chunk_place(block, step=(0, 0), core_step=0):
    core = flip(lax.axis_index("grp"), core_step)
    return pl.multiple_of(((block * 4 + chip_place(step)) * 2 + core) * 128, 128)


LAT_ROW, FF_ROW, LEN_ROW = 9, 10, 11


def unpack(small_ref, vec_ref, means_ref, logvars_ref, inner_ref):
    count = small_ref.shape[0]

    def lanes(row, rows, first, width):
        return jnp.concatenate(
            [wide(small_ref[i, row : row + rows, first : first + width]) for i in range(count)],
            axis=1,
        )

    vec_ref[...] = lanes(0, SMALL, 0, vec_ref.shape[1] // count)
    means_ref[...] = lanes(0, SMALL, 128, means_ref.shape[1] // count)
    logvars_ref[...] = lanes(0, SMALL, 256, means_ref.shape[1] // count)
    inner_ref[...] = lanes(0, 1, 384, inner_ref.shape[1] // count)
    width = vec_ref.shape[1]
    vec_ref[LAT_ROW : LAT_ROW + 1] = inner_ref[:, inner_ref.shape[1] - width :]
    for block in range(4):
        vec_ref[FF_ROW : FF_ROW + 1, block * 128 : block * 128 + 128] = inner_ref[
            :, pl.ds(chunk_place(block), 128)
        ]
    lens = wide(small_ref[0, 0:1, 768:896])
    even = lax.axis_index("z") % 2 == 0
    high = jnp.where(even, lens[:, 0:1], lens[:, 1:2])
    rest = jnp.where(even, lens[:, 2:3], lens[:, 3:4])
    vec_ref[LEN_ROW : LEN_ROW + 1] = jnp.broadcast_to(high * 32 + rest, (1, width))


def row_stats(values):
    centre = values - jnp.mean(values, axis=-1, keepdims=True)
    scale = lax.rsqrt(jnp.mean(centre * centre, axis=-1, keepdims=True) + EPS_NORM)
    return centre * scale, scale


def norm_back(grad, unit, scale, gain):
    inner = grad * gain
    along = jnp.mean(inner * unit, axis=-1, keepdims=True)
    return scale * (inner - jnp.mean(inner, axis=-1, keepdims=True) - unit * along)


def column_sum(values):
    return jnp.sum(values, axis=0, keepdims=True)


def slide_place(core, block, k, row, span):
    zi = lax.axis_index("z")
    chip = (core * 2 + ((zi + k) & 1)) * 4 + block
    return chip * span + row


def head_lanes(rows):
    return lax.broadcasted_iota(jnp.int32, (rows, PAIR), 1) < HEAD_DIM


def own_pair():
    place = (lax.axis_index("grp") * 2 + lax.axis_index("y")) * 2 + lax.axis_index("x")
    return pl.multiple_of(place * PAIR, PAIR)


def head_row(single, k):
    place = (lax.axis_index("grp") * 2 + lax.axis_index("y")) * 2 + lax.axis_index("x")
    parity = (lax.axis_index("z") + k) % 2
    row = 0
    for role in range(3):
        block = 16 * role + 2 * place
        split = (block % 3) // 2
        odd = (block // 3) % 2
        if single:
            here = split * PAIR * role + split * HEAD_DIM * ((odd + parity) % 2)
        else:
            here = (1 - split) * (1 - (odd + parity) % 2) * PAIR * role
        row = row + here
    return pl.multiple_of(row, HEAD_DIM)


def device_place(step, core_step):
    return flip(lax.axis_index("grp"), core_step) * 4 + chip_place(step)


def attend_body(own_ref, other_ref, *refs):
    came, rest = refs[:4], refs[4:]
    vec_ref, means_ref, logvars_ref, normed_ref, qkv_ref, head_w_ref = rest[:6]
    mixed_ref, lse_ref, bias_ref, small_ref, inner_ref = rest[6:]
    span = own_ref.shape[2] - SMALL
    for core_step, ref in enumerate((own_ref, other_ref)):
        for i, step in enumerate(NEAR):
            place = device_place(step, core_step)
            for k in range(2):
                chip = ((place // 4) * 2 + (lax.axis_index("z") + k) % 2) * 4 + place % 4
                small_ref[chip] = ref[i, k, span:]
    unpack(small_ref, vec_ref, means_ref, logvars_ref, inner_ref)
    for ref, (single, k) in zip(came, ARRIVALS):
        head_w_ref[pl.ds(head_row(single, k), ref.shape[0])] = ref[...]
    total_rows = normed_ref.shape[0]
    gain, shift = vec_ref[0:1], vec_ref[1:2]
    bias_q = vec_ref[2:3, pl.ds(own_pair(), PAIR)]
    bias_v = vec_ref[3:4, pl.ds(own_pair(), PAIR)]
    for core_step, ref in enumerate((own_ref, other_ref)):
        for i, step in enumerate(NEAR):
            cells = jnp.concatenate([ref[i, 0, :span], ref[i, 1, :span]])
            unit, _ = row_stats(wide(cells))
            at = device_place(step, core_step) * (2 * span)
            normed_ref[pl.ds(pl.multiple_of(at, 2 * span), 2 * span)] = to_low(unit * gain + shift)
    step = 256
    for start in range(0, total_rows, step):
        qkv = product_nt(normed_ref[start : start + step], head_w_ref[...])
        qkv_ref[start : start + step, :PAIR] = to_low(
            wide(to_low(qkv[:, :PAIR] + bias_q)) * HEAD_DIM**-0.5
        )
        qkv_ref[start : start + step, PAIR : 2 * PAIR] = to_low(qkv[:, PAIR : 2 * PAIR])
        qkv_ref[start : start + step, 2 * PAIR :] = to_low(qkv[:, 2 * PAIR :] + bias_v)
    lane = lax.broadcasted_iota(jnp.int32, (1, total_rows), 1)
    place = slide_place(
        lane // (8 * span), (lane // (2 * span)) & 3, (lane // span) & 1, lane & (span - 1), span
    )
    bias = jnp.where(place.astype(jnp.float32) < vec_ref[LEN_ROW : LEN_ROW + 1], 0.0, MASKED)
    bias_ref[...] = bias
    keys = qkv_ref[:, PAIR : 2 * PAIR]
    values = qkv_ref[:, 2 * PAIR :]
    first_head = head_lanes(step)
    for start in range(0, total_rows, step):
        query = qkv_ref[start : start + step, :PAIR]
        outs, totals = [], []
        for head in range(2):
            mine = first_head if head == 0 else jnp.logical_not(first_head)
            part = jnp.where(mine, query, jnp.zeros_like(query))
            scores = product_nt(part, keys) + bias
            peak = jnp.max(scores, axis=-1, keepdims=True)
            weights = jnp.exp(scores - peak)
            total = jnp.sum(weights, axis=-1, keepdims=True)
            outs.append(product(to_low(weights / total), values))
            totals.append(jnp.broadcast_to(peak + jnp.log(total), (step, PAIR)))
        mixed_ref[start : start + step] = to_low(jnp.where(first_head, outs[0], outs[1]))
        lse_ref[start : start + step] = jnp.where(first_head, totals[0], totals[1])


def attend(own, other, came, lat, inner):
    rows, width = 16 * (own.shape[2] - SMALL), own.shape[3]
    return whole_call(
        attend_body,
        (own, other, *came),
        [
            wide_shape(SMALL, width),
            wide_shape(SMALL, lat),
            wide_shape(SMALL, lat),
            low_shape(rows, width),
            low_shape(rows, 3 * PAIR),
            low_shape(3 * PAIR, width),
            low_shape(rows, PAIR),
            wide_shape(rows, PAIR),
            wide_shape(1, rows),
        ],
        [
            pltpu.VMEM((16, SMALL, width), jnp.bfloat16),
            pltpu.VMEM((1, inner), jnp.float32),
        ],
        loaded=range(2, 6),
    )


def side_rows(ref, core_step, start, rows):
    first = flip(lax.axis_index("grp"), core_step) * (ref.shape[0] // 2) + start
    return ref[pl.ds(pl.multiple_of(first, rows), rows)]


def mix_far_body(mixed_ref, out_t_ref, far_ref):
    for start in range(0, far_ref.shape[0], 256):
        far_ref[start : start + 256] = to_low(
            product_nt(side_rows(mixed_ref, 1, start, 256), out_t_ref[...])
        )


def mix_near_body(mixed_ref, out_t_ref, came_ref, keep_ref, *sends):
    rows = keep_ref.shape[0]
    for i, step in enumerate(NEAR):
        first = chip_place(step) * rows
        came = came_ref[pl.ds(pl.multiple_of(first, rows), rows)]
        part = product_nt(side_rows(mixed_ref, 0, first, rows), out_t_ref[...]) + wide(came)
        if i == 0:
            keep_ref[...] = part
        else:
            sends[i - 1][...] = to_low(part)


def part_shapes(rows, width):
    return [wide_shape(rows, width)] + [low_shape(rows, width)] * 3


def mix_out(mixed, out_t, ready):
    rows, width = mixed.shape[0], out_t.shape[0]
    (far,) = whole_call(mix_far_body, (mixed, out_t), [low_shape(rows // 2, width)])
    keep, *sends = whole_call(
        mix_near_body, (mixed, out_t, after(other_core(far), ready)), part_shapes(rows // 8, width)
    )
    return keep, *plane_hops(sends)


def out_grad_body(*refs):
    pieces, mixed_ref, out_ref, datt_ref, sems = refs[:8], *refs[8:]
    stack_rows(pieces, datt_ref, sems, lambda i: device_place(NEAR[i % 4], i // 4))
    rows = out_ref.shape[1]
    for chip in range(0, out_ref.shape[0], 4):
        lanes = slice(chip * rows, (chip + 4) * rows)
        grad = to_low(product_tn(datt_ref[:, lanes], mixed_ref[...]))
        out_ref[chip : chip + 4] = grad.reshape(4, rows, PAIR)


def out_grads(pieces, mixed):
    rows, width = pieces[0].shape
    return whole_call(
        out_grad_body,
        (*pieces, mixed),
        [low_shape(16, width // 16, PAIR), low_shape(8 * rows, width)],
        [pltpu.SemaphoreType.DMA((8,))],
        range(8),
    )


def attend_back_body(
    qkv_ref,
    bias_ref,
    lse_ref,
    out_t_ref,
    head_w_ref,
    datt_ref,
    dqkv_ref,
    far_ref,
    dmixed_ref,
    dk_ref,
    dv_ref,
):
    rows = qkv_ref.shape[0]
    for start in range(0, rows, 256):
        at = slice(start, start + 256)
        dmixed_ref[at] = to_low(product(datt_ref[at], out_t_ref[...]))
    keys = qkv_ref[:, PAIR : 2 * PAIR]
    values = qkv_ref[:, 2 * PAIR :]
    bias = bias_ref[...]
    step = 256
    first_head = head_lanes(step)
    for start in range(0, rows, step):
        query = qkv_ref[start : start + step, :PAIR]
        dmixed = dmixed_ref[start : start + step]
        dqueries = []
        for head in range(2):
            mine = first_head if head == 0 else jnp.logical_not(first_head)
            part = jnp.where(mine, query, jnp.zeros_like(query))
            dpart = jnp.where(mine, dmixed, jnp.zeros_like(dmixed))
            lse = lse_ref[start : start + step, head * HEAD_DIM : head * HEAD_DIM + 1]
            probs = jnp.exp(product_nt(part, keys) + bias - lse)
            dprobs = product_nt(dpart, values)
            centre = jnp.sum(dprobs * probs, axis=-1, keepdims=True)
            dscores = to_low(probs * (dprobs - centre))
            dqueries.append(product(dscores, keys))
            dkeys = product_tn(dscores, part)
            dvalues = product_tn(to_low(probs), dpart)
            if start == 0 and head == 0:
                dk_ref[...] = dkeys
                dv_ref[...] = dvalues
            else:
                dk_ref[...] += dkeys
                dv_ref[...] += dvalues
        dquery = jnp.where(first_head, dqueries[0], dqueries[1]) * (HEAD_DIM**-0.5)
        dqkv_ref[start : start + step, :PAIR] = to_low(dquery)
    dqkv_ref[:, PAIR : 2 * PAIR] = to_low(dk_ref[...])
    dqkv_ref[:, 2 * PAIR :] = to_low(dv_ref[...])
    for start in range(0, rows // 2, step):
        far_ref[start : start + step] = to_low(
            product(side_rows(dqkv_ref, 1, start, step), head_w_ref[...])
        )


def attend_back(qkv, bias, lse, out_t, head_w, datt):
    rows, width = qkv.shape[0], head_w.shape[1]
    return whole_call(
        attend_back_body,
        (qkv, bias, lse, out_t, head_w, datt),
        [low_shape(rows, 3 * PAIR), low_shape(rows // 2, width)],
        [
            pltpu.VMEM((rows, PAIR), jnp.bfloat16),
            pltpu.VMEM((rows, PAIR), jnp.float32),
            pltpu.VMEM((rows, PAIR), jnp.float32),
        ],
    )


def dnormed_body(dqkv_ref, head_w_ref, came_ref, keep_ref, *sends):
    rows = keep_ref.shape[0]
    for i, step in enumerate(NEAR):
        first = chip_place(step) * rows
        came = came_ref[pl.ds(pl.multiple_of(first, rows), rows)]
        part = product(side_rows(dqkv_ref, 0, first, rows), head_w_ref[...]) + wide(came)
        if i == 0:
            keep_ref[...] = part
        else:
            sends[i - 1][...] = to_low(part)


def dnormed(dqkv, head_w, came):
    rows, width = dqkv.shape[0] // 8, head_w.shape[1]
    return whole_call(dnormed_body, (dqkv, head_w, came), part_shapes(rows, width))


def head_grad_body(dqkv_ref, normed_ref, *refs):
    homes, sums_ref, grad_w_ref = refs[:4], refs[4], refs[5]
    dqkv = dqkv_ref[...]
    sums_ref[...] = column_sum(wide(dqkv))
    grad_w_ref[...] = to_low(product_tn(dqkv, normed_ref[...]))
    for ref, (single, k) in zip(homes, ARRIVALS):
        ref[...] = grad_w_ref[pl.ds(head_row(single, k), ref.shape[0])]


def head_grads(dqkv, normed):
    width = normed.shape[1]
    outs = whole_call(
        head_grad_body,
        (dqkv, normed),
        [low_shape(HEAD_DIM if single else PAIR, width) for single, _ in ARRIVALS]
        + [wide_shape(1, 3 * PAIR)],
        [pltpu.VMEM((3 * PAIR, width), jnp.bfloat16)],
    )
    return outs[:4], outs[4]


def home_body(*refs):
    pair = wide(refs[0][...]) + wide(refs[2][...])
    single = wide(refs[1][...]) + wide(refs[3][...])
    odd = lax.axis_index("x") % 2
    refs[4][pl.ds(pl.multiple_of(odd * HEAD_DIM, HEAD_DIM), PAIR)] = pair
    refs[4][pl.ds(pl.multiple_of((1 - odd) * PAIR, HEAD_DIM), HEAD_DIM)] = single


LAT_LANES, DEC_LANES = slice(0, 512), slice(512, 768)


def project_body(
    keep_ref, came_x_ref, came_y_ref, came_far_ref, blocks_ref, vec_ref, attended_ref, normed_ref, hidden_ref
):
    span = blocks_ref.shape[1] - SMALL
    hidden = jnp.concatenate([blocks_ref[0, :span], blocks_ref[1, :span]])
    hidden_ref[...] = hidden
    parts = z_sum((keep_ref, came_x_ref, came_y_ref, came_far_ref))
    total = wide(hidden) + parts + vec_ref[4:5]
    attended_ref[...] = total
    unit, _ = row_stats(total)
    normed_ref[...] = to_low(unit * vec_ref[5:6] + vec_ref[6:7])


def project(parts, blocks, vec):
    shape = parts[0].shape
    return whole_call(
        project_body,
        (*parts, blocks, vec),
        [wide_shape(*shape), low_shape(*shape), low_shape(*shape)],
    )


GELU_SCALE = math.sqrt(2.0 / math.pi)
GELU_CUBE = 0.044715


def stack_rows(refs, target_ref, sems, order=None):
    rows = refs[0].shape[0]
    copies = []
    for i, ref in enumerate(refs):
        place = i if order is None else order(i)
        target = target_ref.at[pl.ds(pl.multiple_of(place * rows, rows), rows)]
        copies.append(pltpu.make_async_copy(ref, target, sems.at[i]))
    for copy in copies:
        copy.start()
    for copy in copies:
        copy.wait()


FF_STEP = 256


def load_all(rows_in, weights_ref, all_ref, in_ref, back_ref, sems):
    copies = []
    for i, ref in enumerate(rows_in):
        rows = ref.shape[0]
        copies.append((ref, all_ref.at[i * rows : (i + 1) * rows]))
    for z in range(4):
        part = weights_ref.at[z * 256 : z * 256 + 256]
        copies.append((part.at[:128], in_ref.at[z * 128 : (z + 1) * 128]))
        for half in range(2):
            at = z * 256 + half * 128
            copies.append(
                (part.at[128:, half * 512 : half * 512 + 512], back_ref.at[at : at + 128])
            )
    copies = [pltpu.make_async_copy(*copy, sems.at[i]) for i, copy in enumerate(copies)]
    for copy in copies:
        copy.start()
    for copy in copies:
        copy.wait()


def feed_scratch(rows, width, hidden):
    return [
        pltpu.VMEM((rows, width), jnp.bfloat16),
        pltpu.VMEM((hidden, width), jnp.bfloat16),
        pltpu.VMEM((width, hidden), jnp.bfloat16),
        pltpu.SemaphoreType.DMA((16,)),
    ]


def feed_body(*refs, last):
    rows_in, weights_ref, vec_ref, rest = refs[:4], refs[4], refs[5], list(refs[6:])
    came_ref = rest.pop(0) if last else None
    (act_ref, slope_ref), outs = rest[:2], rest[2:-4]
    all_ref, in_ref, back_ref, sems = rest[-4:]
    load_all(rows_in, weights_ref, all_ref, in_ref, back_ref, sems)
    bias = vec_ref[FF_ROW : FF_ROW + 1, : in_ref.shape[0]]
    step = rows_in[0].shape[0] * 2
    for start in range(0, all_ref.shape[0], step):
        at = slice(start, start + step)
        total = None
        for unit in range(0, in_ref.shape[0], FF_STEP):
            lanes = slice(unit, unit + FF_STEP)
            inner = product_nt(all_ref[at], in_ref[lanes]) + bias[:, lanes]
            square = inner * inner
            bend = jnp.tanh(GELU_SCALE * (inner + GELU_CUBE * (inner * square)))
            half = 0.5 * (1.0 + bend)
            act = to_low(inner * half)
            act_ref[at, lanes] = act
            slope_ref[at, lanes] = half + (0.5 * GELU_SCALE) * inner * (1.0 - bend * bend) * (
                1.0 + (3.0 * GELU_CUBE) * square
            )
            part = product_nt(act, back_ref[:, lanes])
            total = part if total is None else total + part
        put_parts(outs, came_ref, start, total)


def put_parts(outs, came_ref, start, total):
    if came_ref is None:
        outs[0][start : start + total.shape[0]] = to_low(total)
        return
    total = total + wide(came_ref[start : start + total.shape[0]])
    rows = outs[0].shape[0]
    for i in range(start // rows, (start + total.shape[0]) // rows):
        piece = total[i * rows - start : (i + 1) * rows - start]
        outs[i][...] = piece if i == 0 else to_low(piece)


def feed_call(body, pieces, weights, more, came, side_shapes):
    rows, width = pieces[0].shape
    last = came is not None
    operands = (*pieces, weights, *more) + ((came,) if last else ())
    outs = part_shapes(rows, width) if last else [low_shape(4 * rows, width)]
    return whole_call(
        functools.partial(body, last=last),
        operands,
        side_shapes + outs,
        feed_scratch(4 * rows, width, 512),
        range(5),
    )


def feed(pieces, weights, vec, came=None):
    count = 4 * pieces[0].shape[0]
    return feed_call(
        feed_body, pieces, weights, (vec,), came, [low_shape(count, 512), wide_shape(count, 512)]
    )


def feed_back_body(*refs, last):
    rows_in, weights_ref, slope_ref, rest = refs[:4], refs[4], refs[5], list(refs[6:])
    came_ref = rest.pop(0) if last else None
    (du_ref, sums_ref), outs = rest[:2], rest[2:-4]
    all_ref, in_ref, back_ref, sems = rest[-4:]
    load_all(rows_in, weights_ref, all_ref, in_ref, back_ref, sems)
    sums = [None] * (in_ref.shape[0] // FF_STEP)
    step = rows_in[0].shape[0] * 2
    for start in range(0, all_ref.shape[0], step):
        at = slice(start, start + step)
        total = None
        for i in range(len(sums)):
            lanes = slice(i * FF_STEP, (i + 1) * FF_STEP)
            du = to_low(product(all_ref[at], back_ref[:, lanes]) * slope_ref[at, lanes])
            du_ref[at, lanes] = du
            summed = column_sum(wide(du))
            sums[i] = summed if sums[i] is None else sums[i] + summed
            part = product(du, in_ref[lanes])
            total = part if total is None else total + part
        put_parts(outs, came_ref, start, total)
    for i, summed in enumerate(sums):
        sums_ref[:, i * FF_STEP : (i + 1) * FF_STEP] = summed


def feed_back(pieces, weights, slope, came=None):
    count = 4 * pieces[0].shape[0]
    return feed_call(
        feed_back_body,
        pieces,
        weights,
        (slope,),
        came,
        [low_shape(count, 512), wide_shape(1, 512)],
    )


def plane_rows(values):
    near = [values, *plane_hops([values] * 3)]
    return (*near, *(other_core(part) for part in near))


GRAD_ROWS = 448


def pair_grad_body(*refs):
    fed_in, two_in, whole_ref, halves = refs[:8], refs[8:16], refs[16], refs[17:21]
    target_ref, out_ref, fed_ref, two_ref, act_ref, du_ref, sems, out_sems = refs[21:]
    copies = []
    for pieces, target in ((fed_in, fed_ref), (two_in, two_ref), (halves[:2], act_ref), (halves[2:], du_ref)):
        rows = pieces[0].shape[0]
        for i, ref in enumerate(pieces):
            copies.append((ref, target.at[i * rows : (i + 1) * rows]))
    copies = [pltpu.make_async_copy(*copy, sems.at[i]) for i, copy in enumerate(copies)]
    for copy in copies:
        copy.start()
    for copy in copies:
        copy.wait()
    width = whole_ref.shape[1]
    stores = []
    for z in range(out_ref.shape[0] // GRAD_ROWS):
        at = z * GRAD_ROWS
        for lane in range(0, out_ref.shape[1], 512):
            lanes = slice(lane, lane + 512)
            out_ref[at : at + 128, lanes] = to_low(
                product_tn(du_ref[:, z * 128 : (z + 1) * 128], two_ref[:, lanes])
            )
        grad = to_low(product_tn(fed_ref[:, z * 256 : (z + 1) * 256], act_ref[...]))
        out_ref[at + 128 : at + 256] = jnp.concatenate([grad[:128], grad[128:]], axis=1)
        out_ref[at + 256 : at + GRAD_ROWS, :width] = whole_ref[z * 256 : z * 256 + 192]
        for piece in range(3):
            out_ref[at + 256 + piece * 64 : at + 320 + piece * 64, width:] = whole_ref[
                z * 256 + 192 : (z + 1) * 256, piece * 256 : (piece + 1) * 256
            ]
        rows = slice(at, at + GRAD_ROWS)
        stores.append(
            pltpu.make_async_copy(out_ref.at[rows], target_ref.at[rows], out_sems.at[z])
        )
        stores[-1].start()
    for copy in stores:
        copy.wait()


def pair_grads(rows_fed, rows_two, whole, acts, dus):
    rows, width = rows_fed[0].shape
    hidden = acts[0].shape[1]
    return whole_call(
        pair_grad_body,
        (*rows_fed, *rows_two, whole, *acts, *dus),
        [low_shape(4 * GRAD_ROWS, width)],
        [pltpu.VMEM((4 * GRAD_ROWS, width), jnp.bfloat16)]
        + [pltpu.VMEM((8 * rows, width), jnp.bfloat16)] * 2
        + [pltpu.VMEM((8 * rows, hidden), jnp.bfloat16)] * 2
        + [pltpu.SemaphoreType.DMA((20,)), pltpu.SemaphoreType.DMA((4,))],
        [*range(16), *range(17, 21)],
        placed=(0,),
    )[0]


def split_grad_body(sum_ref, in_ref, *outs):
    in_ref[...] = wide(sum_ref[:128])
    rows, half = outs[0].shape[0], sum_ref.shape[1] // 2
    for i, step in enumerate(NEAR):
        place = chip_place(step)
        at = pl.ds(pl.multiple_of(128 + (place % 2) * rows, rows), rows)
        lanes = pl.ds(pl.multiple_of((place // 2) * half, half), half)
        outs[i][:, :half] = sum_ref[at, lanes]
        first = pl.multiple_of(256 + jnp.minimum(place, 2) * rows, rows)
        whole = sum_ref[pl.ds(first, rows), : outs[i].shape[1] - half]
        fourth = jnp.concatenate(
            [sum_ref[256 + q * rows : 256 + (q + 1) * rows, whole.shape[1] :] for q in range(3)],
            axis=1,
        )
        outs[i][:, half:] = jnp.where(place == 3, fourth, whole)


def z_sum(refs):
    total = wide(refs[0][...])
    for ref in refs[1:]:
        total = total + wide(ref[...])
    return total


def pick_body(out_ref, back_ref, pairs_ref, *outs):
    for chip in range(16):
        pair = pl.multiple_of((lax.axis_index("grp") * 4 + chip % 4) * PAIR, PAIR)
        pairs_ref[chip] = out_ref[:, pl.ds(pair, PAIR)]
    half = outs[0].shape[1]
    for i, (step, lane) in enumerate(zip((0, 1, 2, 1), (0, 0, 0, half))):
        for block in range(4):
            outs[step][:, lane + block * 128 : lane + (block + 1) * 128] = back_ref[
                :, pl.ds(chunk_place(block, NEAR[i]), 128)
            ]


def lay_body(in_ref, own_ref, came_x_ref, came_y_ref, out_ref):
    out_ref[:128] = in_ref[...]
    half = own_ref.shape[1]
    for i, (ref, lane) in enumerate(
        ((own_ref, 0), (came_x_ref, 0), (came_y_ref, 0), (came_y_ref, half))
    ):
        place = chip_place(NEAR[i])
        rows = pl.ds(pl.multiple_of(128 + (place % 2) * 64, 64), 64)
        out_ref[rows, pl.ds(pl.multiple_of((place // 2) * half, half), half)] = ref[
            :, lane : lane + half
        ]


def core_order(own, other):
    first = lax.axis_index("grp") == 0
    return jnp.concatenate(
        [jnp.where(first, own, other), jnp.where(first, other, own)], axis=1
    )


def core_halves(values):
    part = values.shape[1] // 2
    first = lax.axis_index("grp") == 0
    low_half, high_half = values[:, :part], values[:, part:]
    return (
        jnp.where(first, low_half, high_half),
        jnp.where(first, high_half, low_half),
    )


def halves_nt(values, own_ref, other_ref, lanes):
    own, other = core_halves(values)
    return product_nt(own, own_ref[:, lanes]) + product_nt(other, other_ref[:, lanes])


def bottle_body(
    attended_ref,
    keep_ref,
    came_x_ref,
    came_y_ref,
    came_far_ref,
    vec_ref,
    own_ref,
    other_ref,
    noise_ref,
    cot_ref,
    means_ref,
    logvars_ref,
    out_ref,
    fed_ref,
    sample_ref,
    dlat_ref,
    dfed_ref,
    dfed_low_ref,
    dmeans_ref,
    dlogvars_ref,
    sums_ref,
):
    rows, width = attended_ref.shape
    lat = noise_ref.shape[1]
    comps = means_ref.shape[0]
    parts = z_sum((keep_ref, came_x_ref, came_y_ref, came_far_ref))
    fed = attended_ref[...] + parts + vec_ref[7:8]
    fed_low = to_low(fed)
    fed_ref[...] = fed_low
    latent = halves_nt(fed_low, own_ref, other_ref, LAT_LANES) + vec_ref[LAT_ROW : LAT_ROW + 1]
    logvar = latent[:, lat:]
    noise = noise_ref[...]
    spread = jnp.exp(0.5 * logvar) * noise
    sample = latent[:, :lat] + spread
    sample_low = to_low(sample)
    sample_ref[...] = sample_low
    out_ref[...] = to_low(
        fed + halves_nt(sample_low, own_ref, other_ref, DEC_LANES) + vec_ref[8:9]
    )
    cot = cot_ref[...]
    dsample = core_order(
        product(cot, own_ref[:, DEC_LANES]), product(cot, other_ref[:, DEC_LANES])
    )

    span = rows // 2
    row = lax.broadcasted_iota(jnp.int32, (rows, 1), 0)
    block = lax.axis_index("y") * 2 + lax.axis_index("x")
    place = slide_place(lax.axis_index("grp"), block, row // span, row & (span - 1), span)
    live = place.astype(jnp.float32) < vec_ref[LEN_ROW : LEN_ROW + 1, 0:1]
    share = jnp.where(live, 1.0 / lat, 0.0)
    own_term = jnp.sum(-0.5 * noise * noise - 0.5 * logvar, axis=-1, keepdims=True)
    logvars = logvars_ref[...]
    inverse = jnp.exp(-logvars)
    terms = []
    for c in range(comps):
        offset = sample - means_ref[c : c + 1]
        terms.append(
            jnp.sum(
                -0.5 * offset * offset * inverse[c : c + 1] - 0.5 * logvars[c : c + 1],
                axis=-1,
                keepdims=True,
            )
            - math.log(comps)
        )
    peak = terms[0]
    for term in terms[1:]:
        peak = jnp.maximum(peak, term)
    weights = [jnp.exp(term - peak) for term in terms]
    total = weights[0]
    for weight in weights[1:]:
        total = total + weight
    kl_cell = own_term - (peak + jnp.log(total))
    kl = jnp.sum(jnp.where(live, kl_cell, 0.0), axis=0, keepdims=True) / lat
    scale = share / total
    for c in range(comps):
        offset = sample - means_ref[c : c + 1]
        slope = offset * inverse[c : c + 1]
        part = weights[c] * scale
        pull = part * slope
        dsample = dsample + pull
        dmeans_ref[c : c + 1] = -column_sum(pull)
        dlogvars_ref[c : c + 1] = column_sum(0.5 * part - 0.5 * (pull * offset))
    dlat = jnp.concatenate([dsample, 0.5 * dsample * spread - 0.5 * share], axis=1)
    dlat_low = to_low(dlat)
    dlat_ref[...] = dlat_low
    grad_out = wide(cot)
    dfed = grad_out + core_order(
        product(dlat_low, own_ref[:, LAT_LANES]), product(dlat_low, other_ref[:, LAT_LANES])
    )
    dfed_ref[...] = dfed
    dfed_low_ref[...] = to_low(dfed)
    sums_ref[...] = jnp.concatenate(
        [
            column_sum(wide(dlat_low)),
            column_sum(dfed),
            column_sum(grad_out),
            jnp.broadcast_to(kl, (1, width)),
            jnp.zeros((4, width), jnp.float32),
        ]
    )


def bottle_call(attended, parts, vec, weights, noise, cot, means, logvars):
    rows, width = attended.shape
    lat = noise.shape[1]
    return whole_call(
        bottle_body,
        (attended, *parts, vec, *weights, noise, cot, means, logvars),
        [
            low_shape(rows, width),
            low_shape(rows, width),
            low_shape(rows, lat),
            low_shape(rows, width),
            wide_shape(rows, width),
            low_shape(rows, width),
            wide_shape(*means.shape),
            wide_shape(*means.shape),
            wide_shape(8, width),
        ],
    )


def project_back_body(
    keep_ref,
    came_x_ref,
    came_y_ref,
    came_far_ref,
    attended_ref,
    dfed_ref,
    vec_ref,
    sent_ref,
    datt_ref,
    datt_low_ref,
    sums_ref,
):
    grad = z_sum((keep_ref, came_x_ref, came_y_ref, came_far_ref))
    unit, scale = row_stats(attended_ref[...])
    datt = dfed_ref[...] + norm_back(grad, unit, scale, vec_ref[5:6])
    datt_ref[...] = datt
    datt_low_ref[...] = to_low(datt)
    sums_ref[...] = jnp.concatenate(
        [
            column_sum(grad * unit),
            column_sum(grad),
            column_sum(datt),
            jnp.zeros((5, datt.shape[1]), jnp.float32),
        ]
    )


def project_back(parts, attended, dfed, vec, sent):
    rows, width = attended.shape
    return whole_call(
        project_back_body,
        (*parts, attended, dfed, vec, sent),
        [wide_shape(rows, width), low_shape(rows, width), wide_shape(8, width)],
        left_out=(7,),
    )


def whole_grads_body(*refs):
    out_ref = refs[-1]
    for lanes, (left, left_other, right, right_other) in (
        (LAT_LANES, refs[:4]),
        (DEC_LANES, refs[4:8]),
    ):
        grads = jnp.concatenate([left[...], left_other[...]])
        values = jnp.concatenate([core_halves(right[...])[0], core_halves(right_other[...])[0]])
        out_ref[:, lanes] = to_low(product_tn(grads, values))


def whole_grads(pairs):
    operands = []
    for values in pairs:
        operands += [values, other_core(values)]
    width = pairs[0].shape[1]
    return whole_call(whole_grads_body, operands, [low_shape(width, DEC_LANES.stop)])[0]


def sum_body(*refs):
    refs[-1][...] = z_sum(refs[:-1])


def last_grad_body(*refs):
    out_ref, lat_ref, dec_ref = refs[8:]
    half = out_ref.shape[1] // 8
    for i, ref in enumerate(refs[:8]):
        for block in range(4):
            place = chunk_place(block, NEAR[i % 4], i // 4)
            out_ref[:, pl.ds(place, 128)] = wide(ref[:, block * 128 : (block + 1) * 128])
    for i in range(2):
        total = z_sum([ref.at[:, half:] for ref in refs[i * 4 : i * 4 + 4]])
        lat_ref[:, core_lanes(i, lat_ref.shape[1] // 2)] = total[:, LAT_LANES]
        dec_ref[:, core_lanes(i, dec_ref.shape[1] // 2)] = total[:, DEC_LANES]


def cells_back_body(
    keep_ref,
    came_x_ref,
    came_y_ref,
    came_far_ref,
    hidden_ref,
    datt_ref,
    vec_ref,
    bottle_sums_ref,
    project_sums_ref,
    head_sums_ref,
    ff_sums_ref,
    ff_more_ref,
    dmeans_ref,
    dlogvars_ref,
    out_grad_ref,
    grad_ref,
    packed_ref,
    inner_ref,
    rows_ref,
):
    grad = z_sum((keep_ref, came_x_ref, came_y_ref, came_far_ref))
    unit, scale = row_stats(wide(hidden_ref[...]))
    grad_ref[...] = to_low(datt_ref[...] + norm_back(grad, unit, scale, vec_ref[0:1]))
    width = grad.shape[1]
    count = packed_ref.shape[0]
    inner_ref[...] = jnp.zeros_like(inner_ref)
    for block in range(4):
        lanes = slice(block * 128, block * 128 + 128)
        inner_ref[:, pl.ds(chunk_place(block), 128)] = (
            ff_sums_ref[:, lanes] + ff_more_ref[:, lanes]
        )
    inner_ref[:, inner_ref.shape[1] - width :] = bottle_sums_ref[0:1]
    rows_ref[...] = jnp.zeros_like(rows_ref)
    rows_ref[0:1] = column_sum(grad * unit)
    rows_ref[1:2] = column_sum(grad)
    rows_ref[2:3, pl.ds(own_pair(), PAIR)] = head_sums_ref[:, :PAIR]
    rows_ref[3:4, pl.ds(own_pair(), PAIR)] = head_sums_ref[:, 2 * PAIR :]
    rows_ref[4:5] = project_sums_ref[2:3]
    rows_ref[5:7] = project_sums_ref[0:2]
    rows_ref[7:9] = bottle_sums_ref[1:3]
    part = width // count
    pieces = inner_ref.shape[1] // width
    for i in range(pieces):
        rows_ref[9 + i : 10 + i] = jnp.concatenate(
            [
                inner_ref[:, (b * pieces + i) * part : (b * pieces + i + 1) * part]
                for b in range(count)
            ],
            axis=1,
        )
    rows_ref[14:15] = bottle_sums_ref[3:4]
    lat_part = dmeans_ref.shape[1] // count
    for b in range(count):
        sums = jnp.concatenate(
            [
                rows_ref[:, b * part : (b + 1) * part],
                dmeans_ref[:, b * lat_part : (b + 1) * lat_part],
                dlogvars_ref[:, b * lat_part : (b + 1) * lat_part],
            ],
            axis=1,
        )
        high = to_low(sums)
        packed_ref[b, :part] = out_grad_ref[b]
        packed_ref[b, part : part + SMALL] = high
        packed_ref[b, part + SMALL :] = to_low(sums - wide(high))


def last_sum_body(came_ref, out_ref):
    count, rows = came_ref.shape[0], came_ref.shape[1] - 2 * SMALL
    for chip in range(4):
        total = z_sum([came_ref.at[z * 4 + chip, :rows] for z in range(4)])
        out_ref[:rows, chip * PAIR : (chip + 1) * PAIR] = total
    small = z_sum([came_ref.at[i, rows : rows + SMALL] for i in range(count)])
    rest = z_sum([came_ref.at[i, rows + SMALL :] for i in range(count)])
    out_ref[rows:] = jnp.zeros((SMALL, out_ref.shape[1]), jnp.float32)
    out_ref[rows:, :PAIR] = small + rest


def core_lanes(core_step, width):
    core = flip(lax.axis_index("grp"), core_step)
    return pl.ds(pl.multiple_of(core * width, width), width)


def last_body(own_ref, other_ref, grad_ref, vec_ref, inner_ref, means_ref, logvars_ref, kl_ref):
    rows = grad_ref.shape[0]
    for i, ref in enumerate((own_ref, other_ref)):
        grad_ref[:, core_lanes(i, own_ref.shape[1])] = ref[:rows]
    small = own_ref[rows:, :PAIR] + other_ref[rows:, :PAIR]
    part = vec_ref.shape[1]
    vec_ref[...] = small[:9, :part]
    pieces = inner_ref.shape[1] // part
    inner_ref[...] = jnp.concatenate(
        [small[9 + i : 10 + i, :part] for i in range(pieces)], axis=1
    )
    lat = means_ref.shape[1]
    means_ref[...] = small[:, part : part + lat]
    logvars_ref[...] = small[:, part + lat :]
    kl_ref[...] = small[14:15, :1]


def in_grad_body(own_ref, other_ref, out_ref):
    for i, ref in enumerate((own_ref, other_ref)):
        out_ref[:, core_lanes(i, ref.shape[0])] = ref[...].T


def cells_back(operands, inner):
    rows, width = operands[0].shape
    return whole_call(
        cells_back_body,
        operands,
        [low_shape(rows, width), low_shape(16, width // 16 + 2 * SMALL, PAIR)],
        [pltpu.VMEM((1, inner), jnp.float32), pltpu.VMEM((SMALL, width), jnp.float32)],
    )


def exchange(blocks, axes):
    return lax.all_to_all(blocks, axes, split_axis=0, concat_axis=0, tiled=True)


def to_all(values, count):
    return jnp.broadcast_to(values[None], (count, *values.shape))


def fast_device(
    cell_input,
    lengths,
    noise_draw,
    cotangent,
    w_qkv,
    w_out,
    w_ffn_in,
    w_ffn_out,
    w_latent,
    w_decode,
    vectors,
    inner_bias,
    prior_means,
    prior_logvars,
):
    slots, span, width = cell_input.shape[1:]
    rows = slots * span
    lat = noise_draw.shape[-1]
    comps = prior_means.shape[1]
    ff = w_ffn_out.shape[1]
    inner = 16 * inner_bias.shape[1]

    part = width // 16
    shard = jnp.concatenate(
        [half_of(w[0], 0, "grp", True).T for w in (w_latent, w_decode)], axis=1
    )
    shard_width = shard.shape[1]
    whole = lax.all_gather(shard, CHIPS, axis=0, tiled=True)

    out_pairs, back_own, back_x, back_y = whole_call(
        pick_body,
        after((w_out[0].T, w_ffn_out[0].T), shard),
        [low_shape(16, part, PAIR)]
        + [low_shape(part, ff // 8 * count) for count in (1, 2, 1)],
    )
    out_t = exchange(out_pairs, CHIPS).reshape(width, PAIR)

    blocks = whole_call(
        enter_body,
        (
            after(cell_input.reshape(rows, width), out_pairs),
            lengths,
            vectors[0],
            inner_bias,
            prior_means[0],
            prior_logvars[0],
        ),
        [low_shape(span + SMALL, width)] * 2,
    )
    first = jnp.stack(
        [lax.ppermute(blocks[k], ("grp", "z"), slide_routes(k)) for k in range(2)]
    )

    qkv_t = w_qkv[0].T
    at_x = lax.axis_index("x") % 2
    head_parts = (
        lax.dynamic_slice_in_dim(qkv_t, at_x * HEAD_DIM, PAIR),
        lax.dynamic_slice_in_dim(qkv_t, (1 - at_x) * PAIR, HEAD_DIM),
    )
    came = [
        lax.ppermute(head_parts[int(single)], EVERY, head_routes(single, k))
        for single, k in ARRIVALS
    ]

    in_own = half_of(w_ffn_in[0], 1, "grp", True).T
    noise_high = to_low(noise_draw[0, 0])
    noise_rest = to_low(noise_draw[0, 0] - wide(noise_high))
    extra = jnp.concatenate(
        [cotangent[0], jnp.concatenate([noise_high, noise_rest], axis=2)], axis=1
    )
    size = span + SMALL
    one, two = first[0], first[1]
    one_x = hop(jnp.concatenate([one, back_x]), "x")
    two_y = hop(two, "y")
    sent = jnp.concatenate(
        [one, one_x[:size], jnp.concatenate([back_y, one_x[size:, ff // 8 :]], axis=1)]
    )
    sent_y, sent_x = after((sent, jnp.concatenate([two, two_y])), (came[:2], extra, out_t))
    near_y = hop(sent_y, "y")
    near_x = hop(sent_x, "x")
    plane_own = jnp.concatenate(
        [one, two, one_x[:size], near_x[:size], near_y[:size], two_y]
        + [near_y[size : 2 * size], near_x[size:]]
    ).reshape(4, 2, size, width)
    plane_own, came = lax.optimization_barrier((plane_own, came))
    plane_other = other_core(plane_own)
    (pair_own,) = whole_call(
        lay_body,
        (in_own, back_own, one_x[size:], near_y[2 * size :]),
        [low_shape(256, width)],
    )
    pair_w = lax.all_gather(pair_own, "z", axis=0, tiled=True)

    vec, means, logvars, normed, qkv, head_w, mixed, lse, bias = attend(
        plane_own, plane_other, after(came, pair_own), lat, inner
    )
    mix_parts = mix_out(mixed, out_t, whole)

    extra = to_slides(after(extra, mixed))
    cot = extra[:, :span].reshape(rows, width)
    noise = extra[:, span:].reshape(rows, width)
    noise = wide(noise[:, :lat]) + wide(noise[:, lat:])

    attended, normed_two, hidden = project(mix_parts, first, vec)
    rows_two = plane_rows(normed_two)
    act_far, slope_far, fed_far = feed(pinned(rows_two[4:]), pinned([pair_w])[0], vec)
    act, slope, keep, *sends = feed(
        pinned(rows_two[:4]), pinned([pair_w])[0], vec, other_core(fed_far)
    )
    fed_parts = (keep, *plane_hops(sends))
    wholes = (whole, other_core(whole))
    output, fed_low, sample_low, dlat_low, dfed, dfed_low, dmeans, dlogvars, bottle_sums = (
        bottle_call(
            attended, fed_parts, vec, wholes, noise, cot, means, logvars
        )
    )

    rows_fed = plane_rows(dfed_low)
    layer_out = from_slides(after(output, rows_fed).reshape(slots, span, width))
    whole_grad = whole_grads((dlat_low, fed_low, cot, sample_low))
    du_far, ff_far, norm_far = feed_back(rows_fed[4:], pair_w, slope_far)
    du, ff_sums, keep, *sends = feed_back(
        rows_fed[:4], pair_w, slope, after(other_core(norm_far), whole_grad)
    )
    norm_parts = (keep, *plane_hops(sends))
    grads = pair_grads(rows_fed, pinned(rows_two), whole_grad, (act, act_far), (du, du_far))
    grads_sum = lax.psum_scatter(grads, "z", scatter_dimension=0, tiled=True)
    datt, datt_low, project_sums = project_back(
        after(norm_parts, grads), attended, dfed, vec, layer_out
    )
    rows_datt = plane_rows(datt_low)
    out_grad, all_datt = out_grads(rows_datt, mixed)
    dqkv, dn_far = attend_back(qkv, bias, lse, out_t, head_w, all_datt)
    dn_keep, *dn_sends = dnormed(dqkv, head_w, other_core(dn_far))
    homes, head_sums = head_grads(dqkv, after(normed, dn_sends))
    dn_parts = (dn_keep, *plane_hops(dn_sends))
    grad_rows, packed = cells_back(
        (
            *dn_parts,
            hidden,
            datt,
            vec,
            bottle_sums,
            project_sums,
            head_sums,
            ff_sums,
            ff_far,
            dmeans,
            dlogvars,
            out_grad,
        ),
        inner,
    )
    grad_cells = from_slides(grad_rows.reshape(slots, span, width))
    sum_in, *sums = whole_call(
        split_grad_body,
        (after(grads_sum, packed),),
        [wide_shape(128, width)] + [low_shape(part, ff // 8 + shard_width)] * 4,
    )
    sums = [sums[0], *plane_hops(sums[1:])]
    sums += [other_core(total) for total in sums]

    (last,) = whole_call(
        last_sum_body,
        (after(exchange(packed, CHIPS), (sums[1:4], grad_cells)),),
        [wide_shape(part + SMALL, 4 * PAIR)],
    )
    grad_out_w, vec_out, inner_out, means_out, logvars_out, kl_sum = whole_call(
        last_body,
        (last, other_core(last)),
        [
            wide_shape(part, width),
            wide_shape(9, part),
            wide_shape(1, inner // 16),
            wide_shape(comps, lat // 16),
            wide_shape(comps, lat // 16),
            wide_shape(1, 1),
        ],
    )
    kl_mean = kl_sum[0, 0] / (32 * rows)

    homes = [
        lax.ppermute(grad, EVERY, [(there, here) for here, there in head_routes(single, k)])
        for grad, (single, k) in zip(homes, ARRIVALS)
    ]
    (home,) = whole_call(
        home_body, after(homes, (packed, sums[1:4])), [wide_shape(3 * HEAD_DIM, width)]
    )
    grad_qkv = (home + other_core(home)).T

    (grad_in_w,) = whole_call(
        in_grad_body, (sum_in, other_core(sum_in)), [wide_shape(width, ff // 16)]
    )
    grad_back_w, grad_lat_w, grad_dec_w = whole_call(
        last_grad_body,
        after(sums, grad_in_w),
        [wide_shape(part, ff), wide_shape(part, width), wide_shape(part, lat)],
    )
    return (
        wide(layer_out).reshape(1, slots, span, width),
        wide(grad_cells).reshape(1, slots, span, width),
        kl_mean,
        grad_qkv[None],
        grad_out_w.T[None],
        grad_in_w[None],
        grad_back_w.T[None],
        grad_lat_w.T[None],
        grad_dec_w.T[None],
        vec_out[None],
        inner_out,
        means_out[None],
        logvars_out[None],
    )


def solution(mesh):
    chips = mesh.shape["blk"]
    if (mesh.shape["grp"], chips) == (2, HEADS):
        mesh = Mesh(mesh.devices.reshape(2, chips // 4, 2, 2), EVERY)
        blk, run = CHIPS, fast_device
    else:
        blk, run = "blk", per_device
    cells = P("grp", None, blk, None)
    columns = P(None, None, blk)
    return jax.shard_map(
        run,
        mesh=mesh,
        in_specs=(cells, P("grp", None), P(None, "grp", None, blk, None), cells)
        + (columns,) * 7
        + (P(None, blk), columns, columns),
        out_specs=(cells, cells, P()) + (columns,) * 7 + (P(None, blk), columns, columns),
        check_vma=False,
    )
```

```python
import functools
import math

import jax
import jax.numpy as jnp
import numpy as np
from jax import lax
from jax.experimental import pallas as pl
from jax.experimental.pallas import tpu as pltpu
from jax.sharding import Mesh
from jax.sharding import PartitionSpec as P

HEADS = 16
LAYERS = 1
HEAD_DIM = 64


EPS_NORM = 1e-05
MASKED = -1e30


def to_low(values):
    return values.astype(jnp.bfloat16)


def product(left, right):
    return jnp.dot(left, right, preferred_element_type=jnp.float32)


def product_tn(left, right):
    return lax.dot_general(
        left, right, (((0,), (0,)), ((), ())), preferred_element_type=jnp.float32
    )


def product_nt(left, right):
    return lax.dot_general(
        left, right, (((1,), (1,)), ((), ())), preferred_element_type=jnp.float32
    )


def layer_norm(values, norm_gain, norm_shift):
    centre = values - jnp.mean(values, axis=-1, keepdims=True)
    spread = jnp.mean(centre * centre, axis=-1, keepdims=True)
    return centre * lax.rsqrt(spread + EPS_NORM) * norm_gain + norm_shift


def mixture_kl(sample, noise_rows, logvar, mean_rows, logvars):
    own_term = jnp.sum(-0.5 * noise_rows * noise_rows - 0.5 * logvar, axis=-1)
    offset = sample[:, None, :] - mean_rows[None, :, :]
    component = jnp.sum(
        -0.5 * offset * offset * jnp.exp(-logvars)[None] - 0.5 * logvars[None], axis=-1
    ) - math.log(mean_rows.shape[0])
    row_peak = jnp.max(component, axis=-1, keepdims=True)
    mixture = row_peak[:, 0] + jnp.log(jnp.sum(jnp.exp(component - row_peak), axis=-1))
    return own_term - mixture


def bottleneck(latent, noise_rows, live_rows, mean_rows, logvars):
    lat_width = noise_rows.shape[-1]
    mean_part = latent[:, :lat_width]
    logvar = latent[:, lat_width:]
    sample = mean_part + jnp.exp(0.5 * logvar) * noise_rows
    per_cell = mixture_kl(sample, noise_rows, logvar, mean_rows, logvars)
    return (sample, jnp.sum(jnp.where(live_rows, per_cell, 0.0)) / lat_width)


def slot_scores(query_slots, keys_all, slide_len, score_scale):
    slot_count, query_rows, model_width = query_slots.shape
    heads_q = query_slots.reshape(slot_count, query_rows, HEADS, HEAD_DIM)
    heads_k = keys_all.reshape(slot_count, keys_all.shape[1], HEADS, HEAD_DIM)
    raw_scores = (
        jnp.einsum("sqhd,skhd->shqk", heads_q, heads_k, preferred_element_type=jnp.float32)
        * score_scale
    )
    live_keys = jnp.arange(keys_all.shape[1])[None, :] < slide_len[:, None]
    return jnp.where(live_keys[:, None, None, :], raw_scores, MASKED)


def widen(gathered):
    qkv_w, out_w, in_w, back_w, latent_w, decode_w, vec_rows, inner_rows, mean_rows, logvars = (
        gathered
    )
    return (
        qkv_w,
        out_w,
        in_w,
        back_w,
        latent_w,
        decode_w,
        vec_rows.astype(jnp.float32),
        inner_rows.astype(jnp.float32),
        mean_rows.astype(jnp.float32),
        logvars.astype(jnp.float32),
    )


def gather_weights(layer_parts):
    (
        part_qkv,
        part_out,
        part_in,
        part_back,
        part_latent,
        part_decode,
        part_vectors,
        part_inner,
        part_means,
        part_logvars,
    ) = layer_parts
    return widen(
        (
            lax.all_gather(part_qkv, "blk", axis=1, tiled=True),
            lax.all_gather(part_out, "blk", axis=1, tiled=True),
            lax.all_gather(part_in, "blk", axis=1, tiled=True),
            lax.all_gather(part_back, "blk", axis=1, tiled=True),
            lax.all_gather(part_latent, "blk", axis=1, tiled=True),
            lax.all_gather(part_decode, "blk", axis=1, tiled=True),
            lax.all_gather(part_vectors, "blk", axis=1, tiled=True),
            lax.all_gather(part_inner, "blk", axis=0, tiled=True),
            lax.all_gather(part_means, "blk", axis=1, tiled=True),
            lax.all_gather(part_logvars, "blk", axis=1, tiled=True),
        )
    )


def reduce_grads(grads):
    (
        grad_qkv_w,
        grad_out_w,
        grad_in_w,
        grad_back_w,
        grad_latent_w,
        grad_decode_w,
        grad_vec,
        grad_inner,
        grad_mean_rows,
        grad_logvars,
    ) = grads
    (
        shard_qkv,
        shard_out,
        shard_in,
        shard_back,
        shard_latent,
        shard_decode,
        shard_vec,
        shard_inner,
        shard_means,
        shard_logvars,
    ) = (
        lax.psum_scatter(grad_qkv_w, "blk", scatter_dimension=1, tiled=True),
        lax.psum_scatter(grad_out_w, "blk", scatter_dimension=1, tiled=True),
        lax.psum_scatter(grad_in_w, "blk", scatter_dimension=1, tiled=True),
        lax.psum_scatter(grad_back_w, "blk", scatter_dimension=1, tiled=True),
        lax.psum_scatter(grad_latent_w, "blk", scatter_dimension=1, tiled=True),
        lax.psum_scatter(grad_decode_w, "blk", scatter_dimension=1, tiled=True),
        lax.psum_scatter(grad_vec, "blk", scatter_dimension=1, tiled=True),
        lax.psum_scatter(grad_inner, "blk", scatter_dimension=0, tiled=True),
        lax.psum_scatter(grad_mean_rows, "blk", scatter_dimension=1, tiled=True),
        lax.psum_scatter(grad_logvars, "blk", scatter_dimension=1, tiled=True),
    )
    return lax.psum(
        (
            shard_qkv,
            shard_out,
            shard_in,
            shard_back,
            shard_latent,
            shard_decode,
            shard_vec,
            shard_inner,
            shard_means,
            shard_logvars,
        ),
        "grp",
    )


def layer_forward(hidden, full_weights, noise_rows, live_rows, slide_len, score_scale):
    qkv_w, out_w, in_w, back_w, latent_w, decode_w, vec_rows, inner_rows, mean_rows, logvars = (
        full_weights
    )
    model_width = hidden.shape[1]
    slot_count = slide_len.shape[0]
    slot_span = hidden.shape[0] // slot_count
    ff_width = in_w.shape[1]
    normed = to_low(layer_norm(hidden, vec_rows[0], vec_rows[1]))
    qkv_all = product(normed, qkv_w)
    query_low = to_low(qkv_all[:, :model_width] + vec_rows[2])
    keys_own = to_low(qkv_all[:, model_width : 2 * model_width])
    values_own = to_low(qkv_all[:, 2 * model_width :] + vec_rows[3])
    keys_all, values_all = (
        lax.all_gather(
            keys_own.reshape(slot_count, slot_span, model_width), "blk", axis=1, tiled=True
        ),
        lax.all_gather(
            values_own.reshape(slot_count, slot_span, model_width), "blk", axis=1, tiled=True
        ),
    )
    scores = slot_scores(
        query_low.reshape(slot_count, slot_span, model_width), keys_all, slide_len, score_scale
    )
    row_peak = jnp.max(scores, axis=-1, keepdims=True)
    weights = jnp.exp(scores - row_peak)
    totals = jnp.sum(weights, axis=-1, keepdims=True)
    probs_low = to_low(weights / totals)
    log_total = row_peak + jnp.log(totals)
    heads_v = values_all.reshape(slot_count, values_all.shape[1], HEADS, HEAD_DIM)
    mixed_f = jnp.einsum("shqk,skhd->sqhd", probs_low, heads_v, preferred_element_type=jnp.float32)
    mixed_low = to_low(mixed_f.reshape(slot_count * slot_span, model_width))
    attended = hidden + product(mixed_low, out_w) + vec_rows[4]
    normed_two = to_low(layer_norm(attended, vec_rows[5], vec_rows[6]))
    inner_act = product(normed_two, in_w) + inner_rows[:ff_width]
    activated = to_low(jax.nn.gelu(inner_act))
    fed_rows = attended + product(activated, back_w) + vec_rows[7]
    fed_low = to_low(fed_rows)
    latent = product(fed_low, latent_w) + inner_rows[ff_width:]
    sample, kl_part = bottleneck(latent, noise_rows, live_rows, mean_rows, logvars)
    sample_low = to_low(sample)
    output = fed_rows + product(sample_low, decode_w) + vec_rows[8]
    saved_state = (
        hidden,
        normed,
        query_low,
        keys_own,
        values_own,
        log_total,
        mixed_low,
        attended,
        normed_two,
        inner_act,
        activated,
        fed_low,
        latent,
        sample_low,
    )
    return (output, kl_part, saved_state)


def layer_backward(
    grad_out, full_weights, saved_state, noise_rows, live_rows, slide_len, score_scale
):
    qkv_w, out_w, in_w, back_w, latent_w, decode_w, vec_rows, inner_rows, mean_rows, logvars = (
        full_weights
    )
    (
        hidden,
        normed,
        query_low,
        keys_own,
        values_own,
        log_total,
        mixed_low,
        attended,
        normed_two,
        inner_act,
        activated,
        fed_low,
        latent,
        sample_low,
    ) = saved_state
    model_width = hidden.shape[1]
    row_total = hidden.shape[0]
    slot_count = slide_len.shape[0]
    slot_span = row_total // slot_count
    grad_dec_low = to_low(grad_out)
    grad_decode_w = product_tn(sample_low, grad_dec_low)
    grad_sample = product_nt(grad_dec_low, decode_w)

    def bottle(latent_in, means_in, logvars_in):
        return bottleneck(latent_in, noise_rows, live_rows, means_in, logvars_in)

    ignored, bottle_pull = jax.vjp(bottle, latent, mean_rows, logvars)
    grad_latent_f, grad_mean_rows, grad_logvars = bottle_pull(
        (grad_sample, jnp.ones((), jnp.float32))
    )
    grad_latent_low = to_low(grad_latent_f)
    grad_latent_w = product_tn(fed_low, grad_latent_low)
    grad_fed = grad_out + product_nt(grad_latent_low, latent_w)
    grad_fed_low = to_low(grad_fed)
    grad_back_w = product_tn(activated, grad_fed_low)
    grad_act = product_nt(grad_fed_low, back_w)
    ignored_two, gelu_pull = jax.vjp(jax.nn.gelu, inner_act)
    grad_inner_low = to_low(gelu_pull(grad_act)[0])
    grad_in_w = product_tn(normed_two, grad_inner_low)
    grad_normed_two = product_nt(grad_inner_low, in_w)
    ignored_three, second_pull = jax.vjp(layer_norm, attended, vec_rows[5], vec_rows[6])
    grad_att_norm, grad_gain_two, grad_shift_two = second_pull(grad_normed_two)
    grad_attended = grad_fed + grad_att_norm
    grad_proj_low = to_low(grad_attended)
    grad_out_w = product_tn(mixed_low, grad_proj_low)
    grad_mixed_low = to_low(product_nt(grad_proj_low, out_w))
    keys_all, values_all = (
        lax.all_gather(
            keys_own.reshape(slot_count, slot_span, model_width), "blk", axis=1, tiled=True
        ),
        lax.all_gather(
            values_own.reshape(slot_count, slot_span, model_width), "blk", axis=1, tiled=True
        ),
    )
    grad_mixed_heads = grad_mixed_low.reshape(slot_count, slot_span, HEADS, HEAD_DIM)
    heads_k = keys_all.reshape(slot_count, keys_all.shape[1], HEADS, HEAD_DIM)
    heads_v = values_all.reshape(slot_count, values_all.shape[1], HEADS, HEAD_DIM)
    scores = slot_scores(
        query_low.reshape(slot_count, slot_span, model_width), keys_all, slide_len, score_scale
    )
    probs_f = jnp.exp(scores - log_total)
    grad_probs = jnp.einsum(
        "sqhd,skhd->shqk", grad_mixed_heads, heads_v, preferred_element_type=jnp.float32
    )
    centre = jnp.sum(grad_probs * probs_f, axis=-1, keepdims=True)
    grad_scores_low = to_low(probs_f * (grad_probs - centre))
    grad_query = (
        jnp.einsum("shqk,skhd->sqhd", grad_scores_low, heads_k, preferred_element_type=jnp.float32)
        * score_scale
    )
    grad_query_low = to_low(grad_query.reshape(row_total, model_width))
    rows_all, mixed_all = (
        lax.all_gather(
            query_low.reshape(slot_count, slot_span, model_width), "blk", axis=1, tiled=True
        ),
        lax.all_gather(
            grad_mixed_low.reshape(slot_count, slot_span, model_width), "blk", axis=1, tiled=True
        ),
    )
    total_all, centre_all = (
        lax.all_gather(log_total, "blk", axis=2, tiled=True),
        lax.all_gather(centre, "blk", axis=2, tiled=True),
    )
    query_all = rows_all.reshape(slot_count, rows_all.shape[1], HEADS, HEAD_DIM)
    dmixed_all = mixed_all.reshape(slot_count, mixed_all.shape[1], HEADS, HEAD_DIM)
    own_keys = keys_own.reshape(slot_count, slot_span, HEADS, HEAD_DIM)
    own_values = values_own.reshape(slot_count, slot_span, HEADS, HEAD_DIM)
    own_raw = (
        jnp.einsum("sqhd,skhd->shqk", query_all, own_keys, preferred_element_type=jnp.float32)
        * score_scale
    )
    key_places = lax.axis_index("blk") * slot_span + jnp.arange(slot_span)
    live_own = key_places[None, :] < slide_len[:, None]
    own_scores = jnp.where(live_own[:, None, None, :], own_raw, MASKED)
    own_probs = jnp.exp(own_scores - total_all)
    own_dprobs = jnp.einsum(
        "sqhd,skhd->shqk", dmixed_all, own_values, preferred_element_type=jnp.float32
    )
    own_dscores = to_low(own_probs * (own_dprobs - centre_all))
    grad_keys = (
        jnp.einsum("shqk,sqhd->skhd", own_dscores, query_all, preferred_element_type=jnp.float32)
        * score_scale
    )
    grad_values = jnp.einsum(
        "shqk,sqhd->skhd", to_low(own_probs), dmixed_all, preferred_element_type=jnp.float32
    )
    grad_keys_low = to_low(grad_keys.reshape(row_total, model_width))
    grad_values_low = to_low(grad_values.reshape(row_total, model_width))
    grad_qkv_low = jnp.concatenate([grad_query_low, grad_keys_low, grad_values_low], axis=1)
    grad_qkv_w = product_tn(normed, grad_qkv_low)
    grad_normed = product_nt(grad_qkv_low, qkv_w)
    ignored_four, first_pull = jax.vjp(layer_norm, hidden, vec_rows[0], vec_rows[1])
    grad_hid_norm, grad_gain_one, grad_shift_one = first_pull(grad_normed)
    grad_hidden = grad_attended + grad_hid_norm
    grad_vec = jnp.stack(
        [
            grad_gain_one,
            grad_shift_one,
            jnp.sum(grad_query_low.astype(jnp.float32), axis=0),
            jnp.sum(grad_values_low.astype(jnp.float32), axis=0),
            jnp.sum(grad_attended, axis=0),
            grad_gain_two,
            grad_shift_two,
            jnp.sum(grad_fed, axis=0),
            jnp.sum(grad_out, axis=0),
        ]
    )
    grad_inner = jnp.concatenate(
        [
            jnp.sum(grad_inner_low.astype(jnp.float32), axis=0),
            jnp.sum(grad_latent_low.astype(jnp.float32), axis=0),
        ]
    )
    return (
        grad_hidden,
        (
            grad_qkv_w,
            grad_out_w,
            grad_in_w,
            grad_back_w,
            grad_latent_w,
            grad_decode_w,
            grad_vec,
            grad_inner,
            grad_mean_rows,
            grad_logvars,
        ),
    )


def per_device(
    cell_input,
    lengths,
    noise_draw,
    cotangent,
    w_qkv,
    w_out,
    w_ffn_in,
    w_ffn_out,
    w_latent,
    w_decode,
    vectors,
    inner_bias,
    prior_means,
    prior_logvars,
):
    slot_count = cell_input.shape[1]
    slot_span = cell_input.shape[2]
    model_width = cell_input.shape[3]
    row_total = slot_count * slot_span
    lat_width = noise_draw.shape[-1]
    cycle_size = lax.axis_size("blk")
    score_scale = 1.0 / math.sqrt(HEAD_DIM)
    slide_len = lengths[0]
    positions = lax.axis_index("blk") * slot_span + jnp.arange(slot_span)
    live_rows = (positions[None, :] < slide_len[:, None]).reshape(row_total)
    hidden = cell_input[0].reshape(row_total, model_width).astype(jnp.float32)
    stacks = (
        w_qkv,
        w_out,
        w_ffn_in,
        w_ffn_out,
        w_latent,
        w_decode,
        vectors,
        inner_bias,
        prior_means,
        prior_logvars,
    )
    layer_idx = 0
    full_weights = gather_weights([stacked[layer_idx] for stacked in stacks])
    kept_weights = [full_weights]
    hidden, kl_part, saved_state = layer_forward(
        hidden,
        full_weights,
        noise_draw[layer_idx, 0].reshape(row_total, lat_width),
        live_rows,
        slide_len,
        score_scale,
    )
    saved_layers = [saved_state]
    layer_out = hidden.reshape(1, slot_count, slot_span, model_width)
    kl_total = lax.psum(kl_part, ("grp", "blk"))
    kl_mean = kl_total / (lax.axis_size("grp") * cycle_size * row_total)
    grad_rows = cotangent[0].reshape(row_total, model_width).astype(jnp.float32)
    reduced = [None] * LAYERS
    for layer_idx in reversed(range(LAYERS)):
        full_weights = kept_weights[layer_idx]
        grad_rows, grads = layer_backward(
            grad_rows,
            full_weights,
            saved_layers[layer_idx],
            noise_draw[layer_idx, 0].reshape(row_total, lat_width),
            live_rows,
            slide_len,
            score_scale,
        )
        reduced[layer_idx] = reduce_grads(grads)
    grad_cells = grad_rows.reshape(1, slot_count, slot_span, model_width)
    stacked_grads = [jnp.stack([reduced[0][member]]) for member in range(10)]
    return (
        layer_out,
        grad_cells,
        kl_mean,
        stacked_grads[0],
        stacked_grads[1],
        stacked_grads[2],
        stacked_grads[3],
        stacked_grads[4],
        stacked_grads[5],
        stacked_grads[6],
        stacked_grads[7],
        stacked_grads[8],
        stacked_grads[9],
    )


EVERY = ("grp", "z", "y", "x")
CHIPS = ("z", "y", "x")
PLANE = ("grp", "y", "x")
PAIR = 2 * HEAD_DIM
SMALL = 16
VMEM_LIMIT = 20 * 1024 * 1024


def hop(values, axis, step=1):
    size = lax.axis_size(axis)
    return lax.ppermute(values, axis, [(i, i ^ step) for i in range(size)])


def other_core(values):
    return hop(values, "grp")


def after(values, done):
    return lax.optimization_barrier((values, done))[0]


def ordered(own, other, axis_name, axis):
    first = lax.axis_index(axis_name) == 0
    return jnp.concatenate(
        [jnp.where(first, own, other), jnp.where(first, other, own)], axis=axis
    )


def half_of(values, axis, axis_name, mine):
    part = values.shape[axis] // 2
    place = lax.axis_index(axis_name)
    place = place if mine else 1 - place
    return lax.dynamic_slice_in_dim(values, place * part, part, axis)


def flip(place, step):
    high = (place // 2 + step // 2) % 2
    low_bit = (place % 2 + step % 2) % 2
    return high * 2 + low_bit


def slide_routes(k):
    return [
        (g * 4 + z, (z // 2) * 4 + 2 * g + ((z % 2) ^ k)) for g in range(2) for z in range(4)
    ]


def pick_slot(slots, k):
    odd = (lax.axis_index("z") + k) % 2 == 1
    return jnp.where(odd, slots[1], slots[0])


def to_slides(slots):
    return jnp.stack(
        [lax.ppermute(pick_slot(slots, k), ("grp", "z"), slide_routes(k)) for k in range(2)]
    )


def from_slides(blocks):
    came = [
        lax.ppermute(
            blocks[k], ("grp", "z"), [(there, here) for here, there in slide_routes(k)]
        )
        for k in range(2)
    ]
    return jnp.stack([pick_slot(came, 0), pick_slot(came, 1)])


def head_routes(single, k):
    routes = []
    for core in range(2):
        for chip in range(16):
            odd = chip % 2
            block = 3 * chip + (2 - 2 * odd if single else odd)
            pair = (block % 16) // 2
            plane = 2 * core + (odd ^ k)
            target = (pair // 4) * 16 + plane * 4 + pair % 4
            routes.append((core * 16 + chip, target))
    return routes


ARRIVALS = [(single, k) for k in range(2) for single in (False, True)]


def low_shape(*shape):
    return jax.ShapeDtypeStruct(shape, jnp.bfloat16)


def wide(values):
    return values.astype(jnp.float32)


def z_hops(values):
    return [hop(values[step - 1], "z", step) for step in (1, 2, 3)]


def plane_hops(values):
    return [
        hop(values[0], "x"),
        hop(values[1], "y"),
        lax.ppermute(values[2], ("y", "x"), [(i, i ^ 3) for i in range(4)]),
    ]


NEAR = ((0, 0), (0, 1), (1, 0), (1, 1))


def z_at(step, part):
    return pl.ds(pl.multiple_of(flip(lax.axis_index("z"), step) * part, part), part)


def chip_place(step):
    return flip(lax.axis_index("y"), step[0]) * 2 + flip(lax.axis_index("x"), step[1])


def pinned(values):
    return [pltpu.with_memory_space_constraint(part, pltpu.HBM) for part in values]


def wide_shape(*shape):
    return jax.ShapeDtypeStruct(shape, jnp.float32)


FLOPS_PER_US = 1.5e9
TIMES = {
    "attend_body": 10.0,
    "feed_body": 3.5,
    "bottle_body": 5.7,
    "feed_back_body": 2.0,
    "pair_grad_body": 3.4,
    "attend_back_body": 9.2,
    "whole_grads_body": 1.3,
    "cells_back_body": 1.4,
}


def took(body):
    inner = body.func if isinstance(body, functools.partial) else body
    return TIMES.get(inner.__name__, 0.8)


def whole_call(
    body, operands, out_shapes, scratch=(), left_out=(), loaded=(), kept=(), early=False, placed=()
):
    vmem, hbm = pl.BlockSpec(memory_space=pltpu.VMEM), pl.BlockSpec(memory_space=pltpu.HBM)
    n_in, n_out, n_own = len(operands), len(out_shapes), len(scratch)
    left_out, loaded, kept = list(left_out), list(loaded), list(kept)

    def run(*refs):
        ins, outs = list(refs[:n_in]), list(refs[n_in : n_in + n_out])
        own = refs[n_in + n_out : n_in + n_out + n_own]
        rest = refs[n_in + n_out + n_own :]
        in_copies = []
        for at, i in enumerate(loaded):
            in_copies.append(pltpu.make_async_copy(ins[i], rest[at], rest[-1].at[at]))
            ins[i] = rest[at]
        for copy in in_copies:
            copy.start()
        out_copies = {}
        for at, i in enumerate(kept, len(loaded)):
            out_copies[i] = pltpu.make_async_copy(rest[at], outs[i], rest[-1].at[at])
            outs[i] = rest[at]
        for copy in in_copies:
            copy.wait()
        started = []

        def store(i):
            out_copies[i].start()
            started.append(i)

        body(*ins, *outs, *own, **({"store": store} if early else {}))
        for i in out_copies:
            if i not in started:
                out_copies[i].start()
        for copy in out_copies.values():
            copy.wait()

    operands = [
        pltpu.with_memory_space_constraint(part, pltpu.HBM)
        if i in loaded
        else part
        for i, part in enumerate(operands)
    ]
    buffers = [pltpu.VMEM(operands[i].shape, operands[i].dtype) for i in loaded]
    buffers += [pltpu.VMEM(out_shapes[i].shape, out_shapes[i].dtype) for i in kept]
    if buffers:
        buffers.append(pltpu.SemaphoreType.DMA((len(buffers),)))
    out_shapes = [
        pltpu.HBM(part.shape, part.dtype) if i in kept or i in placed else part
        for i, part in enumerate(out_shapes)
    ]
    return pl.pallas_call(
        run,
        out_shape=out_shapes,
        in_specs=[hbm if i in left_out or i in loaded else vmem for i in range(n_in)],
        out_specs=[hbm if i in kept or i in placed else vmem for i in range(n_out)],
        scratch_shapes=[*scratch, *buffers],
        compiler_params=pltpu.CompilerParams(vmem_limit_bytes=VMEM_LIMIT),
        cost_estimate=pl.CostEstimate(
            flops=int(took(body) * FLOPS_PER_US), bytes_accessed=0, transcendentals=0
        ),
    )(*operands)


def enter_body(cells_ref, lens_ref, vectors_ref, inner_ref, means_ref, logvars_ref, *outs):
    span = cells_ref.shape[0] // 2
    lens = lens_ref[...]
    lens = jnp.concatenate([lens >> 5, lens & 31], axis=1).astype(jnp.float32)
    for k, ref in enumerate(outs):
        slot = (lax.axis_index("z") + k) % 2
        ref[:span] = cells_ref[pl.ds(pl.multiple_of(slot * span, span), span)]
        ref[span:] = jnp.zeros((SMALL, ref.shape[1]), jnp.bfloat16)
        ref[span : span + 9, 0:64] = vectors_ref[...]
        ref[span:, 128:160] = means_ref[...]
        ref[span:, 256:288] = logvars_ref[...]
        ref[span : span + 1, 384:704] = inner_ref[...]
        ref[span : span + 1, 768:772] = to_low(lens)


def chunk_place(block, step=(0, 0), core_step=0):
    core = flip(lax.axis_index("grp"), core_step)
    return pl.multiple_of(((block * 4 + chip_place(step)) * 2 + core) * 128, 128)


LAT_ROW, FF_ROW, LEN_ROW = 9, 10, 11


def unpack(small_ref, vec_ref, means_ref, logvars_ref, inner_ref):
    count = small_ref.shape[0]

    def lanes(row, rows, first, width):
        return jnp.concatenate(
            [wide(small_ref[i, row : row + rows, first : first + width]) for i in range(count)],
            axis=1,
        )

    vec_ref[...] = lanes(0, SMALL, 0, vec_ref.shape[1] // count)
    means_ref[...] = lanes(0, SMALL, 128, means_ref.shape[1] // count)
    logvars_ref[...] = lanes(0, SMALL, 256, means_ref.shape[1] // count)
    inner_ref[...] = lanes(0, 1, 384, inner_ref.shape[1] // count)
    width = vec_ref.shape[1]
    vec_ref[LAT_ROW : LAT_ROW + 1] = inner_ref[:, inner_ref.shape[1] - width :]
    for block in range(4):
        vec_ref[FF_ROW : FF_ROW + 1, block * 128 : block * 128 + 128] = inner_ref[
            :, pl.ds(chunk_place(block), 128)
        ]
    lens = wide(small_ref[0, 0:1, 768:896])
    even = lax.axis_index("z") % 2 == 0
    high = jnp.where(even, lens[:, 0:1], lens[:, 1:2])
    rest = jnp.where(even, lens[:, 2:3], lens[:, 3:4])
    vec_ref[LEN_ROW : LEN_ROW + 1] = jnp.broadcast_to(high * 32 + rest, (1, width))


def row_stats(values):
    centre = values - jnp.mean(values, axis=-1, keepdims=True)
    scale = lax.rsqrt(jnp.mean(centre * centre, axis=-1, keepdims=True) + EPS_NORM)
    return centre * scale, scale


def norm_back(grad, unit, scale, gain):
    inner = grad * gain
    along = jnp.mean(inner * unit, axis=-1, keepdims=True)
    return scale * (inner - jnp.mean(inner, axis=-1, keepdims=True) - unit * along)


def column_sum(values):
    return jnp.sum(values, axis=0, keepdims=True)


def slide_place(core, block, k, row, span):
    zi = lax.axis_index("z")
    chip = (core * 2 + ((zi + k) & 1)) * 4 + block
    return chip * span + row


def head_lanes(rows):
    return lax.broadcasted_iota(jnp.int32, (rows, PAIR), 1) < HEAD_DIM


def own_pair():
    place = (lax.axis_index("grp") * 2 + lax.axis_index("y")) * 2 + lax.axis_index("x")
    return pl.multiple_of(place * PAIR, PAIR)


def head_row(single, k):
    place = (lax.axis_index("grp") * 2 + lax.axis_index("y")) * 2 + lax.axis_index("x")
    parity = (lax.axis_index("z") + k) % 2
    row = 0
    for role in range(3):
        block = 16 * role + 2 * place
        split = (block % 3) // 2
        odd = (block // 3) % 2
        if single:
            here = split * PAIR * role + split * HEAD_DIM * ((odd + parity) % 2)
        else:
            here = (1 - split) * (1 - (odd + parity) % 2) * PAIR * role
        row = row + here
    return pl.multiple_of(row, HEAD_DIM)


def device_place(step, core_step):
    return flip(lax.axis_index("grp"), core_step) * 4 + chip_place(step)


def attend_body(own_ref, other_ref, *refs):
    came, rest = refs[:4], refs[4:]
    vec_ref, means_ref, logvars_ref, normed_ref, qkv_ref, head_w_ref = rest[:6]
    mixed_ref, lse_ref, bias_ref, small_ref, inner_ref = rest[6:]
    span = own_ref.shape[2] - SMALL
    for core_step, ref in enumerate((own_ref, other_ref)):
        for i, step in enumerate(NEAR):
            place = device_place(step, core_step)
            for k in range(2):
                chip = ((place // 4) * 2 + (lax.axis_index("z") + k) % 2) * 4 + place % 4
                small_ref[chip] = ref[i, k, span:]
    unpack(small_ref, vec_ref, means_ref, logvars_ref, inner_ref)
    for ref, (single, k) in zip(came, ARRIVALS):
        head_w_ref[pl.ds(head_row(single, k), ref.shape[0])] = ref[...]
    total_rows = normed_ref.shape[0]
    gain, shift = vec_ref[0:1], vec_ref[1:2]
    bias_q = vec_ref[2:3, pl.ds(own_pair(), PAIR)]
    bias_v = vec_ref[3:4, pl.ds(own_pair(), PAIR)]
    for core_step, ref in enumerate((own_ref, other_ref)):
        for i, step in enumerate(NEAR):
            cells = jnp.concatenate([ref[i, 0, :span], ref[i, 1, :span]])
            unit, _ = row_stats(wide(cells))
            at = device_place(step, core_step) * (2 * span)
            normed_ref[pl.ds(pl.multiple_of(at, 2 * span), 2 * span)] = to_low(unit * gain + shift)
    step = 256
    for start in range(0, total_rows, step):
        qkv = product_nt(normed_ref[start : start + step], head_w_ref[...])
        qkv_ref[start : start + step, :PAIR] = to_low(
            wide(to_low(qkv[:, :PAIR] + bias_q)) * HEAD_DIM**-0.5
        )
        qkv_ref[start : start + step, PAIR : 2 * PAIR] = to_low(qkv[:, PAIR : 2 * PAIR])
        qkv_ref[start : start + step, 2 * PAIR :] = to_low(qkv[:, 2 * PAIR :] + bias_v)
    lane = lax.broadcasted_iota(jnp.int32, (1, total_rows), 1)
    place = slide_place(
        lane // (8 * span), (lane // (2 * span)) & 3, (lane // span) & 1, lane & (span - 1), span
    )
    bias = jnp.where(place.astype(jnp.float32) < vec_ref[LEN_ROW : LEN_ROW + 1], 0.0, MASKED)
    bias_ref[...] = bias
    keys = qkv_ref[:, PAIR : 2 * PAIR]
    values = qkv_ref[:, 2 * PAIR :]
    first_head = head_lanes(step)
    for start in range(0, total_rows, step):
        query = qkv_ref[start : start + step, :PAIR]
        outs, totals = [], []
        for head in range(2):
            mine = first_head if head == 0 else jnp.logical_not(first_head)
            part = jnp.where(mine, query, jnp.zeros_like(query))
            scores = product_nt(part, keys) + bias
            peak = jnp.max(scores, axis=-1, keepdims=True)
            weights = jnp.exp(scores - peak)
            total = jnp.sum(weights, axis=-1, keepdims=True)
            outs.append(product(to_low(weights / total), values))
            totals.append(jnp.broadcast_to(peak + jnp.log(total), (step, PAIR)))
        mixed_ref[start : start + step] = to_low(jnp.where(first_head, outs[0], outs[1]))
        lse_ref[start : start + step] = jnp.where(first_head, totals[0], totals[1])


def attend(own, other, came, lat, inner):
    rows, width = 16 * (own.shape[2] - SMALL), own.shape[3]
    return whole_call(
        attend_body,
        (own, other, *came),
        [
            wide_shape(SMALL, width),
            wide_shape(SMALL, lat),
            wide_shape(SMALL, lat),
            low_shape(rows, width),
            low_shape(rows, 3 * PAIR),
            low_shape(3 * PAIR, width),
            low_shape(rows, PAIR),
            wide_shape(rows, PAIR),
            wide_shape(1, rows),
        ],
        [
            pltpu.VMEM((16, SMALL, width), jnp.bfloat16),
            pltpu.VMEM((1, inner), jnp.float32),
        ],
        loaded=range(2, 6),
    )


def side_rows(ref, core_step, start, rows):
    first = flip(lax.axis_index("grp"), core_step) * (ref.shape[0] // 2) + start
    return ref[pl.ds(pl.multiple_of(first, rows), rows)]


def mix_far_body(mixed_ref, out_t_ref, far_ref):
    for start in range(0, far_ref.shape[0], 256):
        far_ref[start : start + 256] = to_low(
            product_nt(side_rows(mixed_ref, 1, start, 256), out_t_ref[...])
        )


def mix_near_body(mixed_ref, out_t_ref, came_ref, keep_ref, *sends):
    rows = keep_ref.shape[0]
    for i, step in enumerate(NEAR):
        first = chip_place(step) * rows
        came = came_ref[pl.ds(pl.multiple_of(first, rows), rows)]
        part = product_nt(side_rows(mixed_ref, 0, first, rows), out_t_ref[...]) + wide(came)
        if i == 0:
            keep_ref[...] = part
        else:
            sends[i - 1][...] = to_low(part)


def part_shapes(rows, width):
    return [wide_shape(rows, width)] + [low_shape(rows, width)] * 3


def mix_out(mixed, out_t, ready):
    rows, width = mixed.shape[0], out_t.shape[0]
    (far,) = whole_call(mix_far_body, (mixed, out_t), [low_shape(rows // 2, width)])
    keep, *sends = whole_call(
        mix_near_body, (mixed, out_t, after(other_core(far), ready)), part_shapes(rows // 8, width)
    )
    return keep, *plane_hops(sends)


def out_grad_body(*refs):
    pieces, mixed_ref, out_ref, datt_ref, sems = refs[:8], *refs[8:]
    stack_rows(pieces, datt_ref, sems, lambda i: device_place(NEAR[i % 4], i // 4))
    rows = out_ref.shape[1]
    for chip in range(0, out_ref.shape[0], 4):
        lanes = slice(chip * rows, (chip + 4) * rows)
        grad = to_low(product_tn(datt_ref[:, lanes], mixed_ref[...]))
        out_ref[chip : chip + 4] = grad.reshape(4, rows, PAIR)


def out_grads(pieces, mixed):
    rows, width = pieces[0].shape
    return whole_call(
        out_grad_body,
        (*pieces, mixed),
        [low_shape(16, width // 16, PAIR), low_shape(8 * rows, width)],
        [pltpu.SemaphoreType.DMA((8,))],
        range(8),
    )


def attend_back_body(
    qkv_ref,
    bias_ref,
    lse_ref,
    out_t_ref,
    head_w_ref,
    datt_ref,
    dqkv_ref,
    far_ref,
    dmixed_ref,
    dk_ref,
    dv_ref,
):
    rows = qkv_ref.shape[0]
    for start in range(0, rows, 256):
        at = slice(start, start + 256)
        dmixed_ref[at] = to_low(product(datt_ref[at], out_t_ref[...]))
    keys = qkv_ref[:, PAIR : 2 * PAIR]
    values = qkv_ref[:, 2 * PAIR :]
    bias = bias_ref[...]
    step = 256
    first_head = head_lanes(step)
    for start in range(0, rows, step):
        query = qkv_ref[start : start + step, :PAIR]
        dmixed = dmixed_ref[start : start + step]
        dqueries = []
        for head in range(2):
            mine = first_head if head == 0 else jnp.logical_not(first_head)
            part = jnp.where(mine, query, jnp.zeros_like(query))
            dpart = jnp.where(mine, dmixed, jnp.zeros_like(dmixed))
            lse = lse_ref[start : start + step, head * HEAD_DIM : head * HEAD_DIM + 1]
            probs = jnp.exp(product_nt(part, keys) + bias - lse)
            dprobs = product_nt(dpart, values)
            centre = jnp.sum(dprobs * probs, axis=-1, keepdims=True)
            dscores = to_low(probs * (dprobs - centre))
            dqueries.append(product(dscores, keys))
            dkeys = product_tn(dscores, part)
            dvalues = product_tn(to_low(probs), dpart)
            if start == 0 and head == 0:
                dk_ref[...] = dkeys
                dv_ref[...] = dvalues
            else:
                dk_ref[...] += dkeys
                dv_ref[...] += dvalues
        dquery = jnp.where(first_head, dqueries[0], dqueries[1]) * (HEAD_DIM**-0.5)
        dqkv_ref[start : start + step, :PAIR] = to_low(dquery)
    dqkv_ref[:, PAIR : 2 * PAIR] = to_low(dk_ref[...])
    dqkv_ref[:, 2 * PAIR :] = to_low(dv_ref[...])
    for start in range(0, rows // 2, step):
        far_ref[start : start + step] = to_low(
            product(side_rows(dqkv_ref, 1, start, step), head_w_ref[...])
        )


def attend_back(qkv, bias, lse, out_t, head_w, datt):
    rows, width = qkv.shape[0], head_w.shape[1]
    return whole_call(
        attend_back_body,
        (qkv, bias, lse, out_t, head_w, datt),
        [low_shape(rows, 3 * PAIR), low_shape(rows // 2, width)],
        [
            pltpu.VMEM((rows, PAIR), jnp.bfloat16),
            pltpu.VMEM((rows, PAIR), jnp.float32),
            pltpu.VMEM((rows, PAIR), jnp.float32),
        ],
    )


def dnormed_body(dqkv_ref, head_w_ref, came_ref, keep_ref, *sends):
    rows = keep_ref.shape[0]
    for i, step in enumerate(NEAR):
        first = chip_place(step) * rows
        came = came_ref[pl.ds(pl.multiple_of(first, rows), rows)]
        part = product(side_rows(dqkv_ref, 0, first, rows), head_w_ref[...]) + wide(came)
        if i == 0:
            keep_ref[...] = part
        else:
            sends[i - 1][...] = to_low(part)


def dnormed(dqkv, head_w, came):
    rows, width = dqkv.shape[0] // 8, head_w.shape[1]
    return whole_call(dnormed_body, (dqkv, head_w, came), part_shapes(rows, width))


def head_grad_body(dqkv_ref, normed_ref, *refs):
    homes, sums_ref, grad_w_ref = refs[:4], refs[4], refs[5]
    dqkv = dqkv_ref[...]
    sums_ref[...] = column_sum(wide(dqkv))
    grad_w_ref[...] = to_low(product_tn(dqkv, normed_ref[...]))
    for ref, (single, k) in zip(homes, ARRIVALS):
        ref[...] = grad_w_ref[pl.ds(head_row(single, k), ref.shape[0])]


def head_grads(dqkv, normed):
    width = normed.shape[1]
    outs = whole_call(
        head_grad_body,
        (dqkv, normed),
        [low_shape(HEAD_DIM if single else PAIR, width) for single, _ in ARRIVALS]
        + [wide_shape(1, 3 * PAIR)],
        [pltpu.VMEM((3 * PAIR, width), jnp.bfloat16)],
    )
    return outs[:4], outs[4]


def home_body(*refs):
    pair = wide(refs[0][...]) + wide(refs[2][...])
    single = wide(refs[1][...]) + wide(refs[3][...])
    odd = lax.axis_index("x") % 2
    refs[4][pl.ds(pl.multiple_of(odd * HEAD_DIM, HEAD_DIM), PAIR)] = pair
    refs[4][pl.ds(pl.multiple_of((1 - odd) * PAIR, HEAD_DIM), HEAD_DIM)] = single


LAT_LANES, DEC_LANES = slice(0, 512), slice(512, 768)


def project_body(
    keep_ref, came_x_ref, came_y_ref, came_far_ref, blocks_ref, vec_ref, attended_ref, normed_ref, hidden_ref
):
    span = blocks_ref.shape[1] - SMALL
    hidden = jnp.concatenate([blocks_ref[0, :span], blocks_ref[1, :span]])
    hidden_ref[...] = hidden
    parts = z_sum((keep_ref, came_x_ref, came_y_ref, came_far_ref))
    total = wide(hidden) + parts + vec_ref[4:5]
    attended_ref[...] = total
    unit, _ = row_stats(total)
    normed_ref[...] = to_low(unit * vec_ref[5:6] + vec_ref[6:7])


def project(parts, blocks, vec):
    shape = parts[0].shape
    return whole_call(
        project_body,
        (*parts, blocks, vec),
        [wide_shape(*shape), low_shape(*shape), low_shape(*shape)],
    )


GELU_SCALE = math.sqrt(2.0 / math.pi)
GELU_CUBE = 0.044715


def stack_rows(refs, target_ref, sems, order=None):
    rows = refs[0].shape[0]
    copies = []
    for i, ref in enumerate(refs):
        place = i if order is None else order(i)
        target = target_ref.at[pl.ds(pl.multiple_of(place * rows, rows), rows)]
        copies.append(pltpu.make_async_copy(ref, target, sems.at[i]))
    for copy in copies:
        copy.start()
    for copy in copies:
        copy.wait()


FF_STEP = 256


def load_all(rows_in, weights_ref, all_ref, in_ref, back_ref, sems):
    copies = []
    for i, ref in enumerate(rows_in):
        rows = ref.shape[0]
        copies.append((ref, all_ref.at[i * rows : (i + 1) * rows]))
    for z in range(4):
        part = weights_ref.at[z * 256 : z * 256 + 256]
        copies.append((part.at[:128], in_ref.at[z * 128 : (z + 1) * 128]))
        for half in range(2):
            at = z * 256 + half * 128
            copies.append(
                (part.at[128:, half * 512 : half * 512 + 512], back_ref.at[at : at + 128])
            )
    copies = [pltpu.make_async_copy(*copy, sems.at[i]) for i, copy in enumerate(copies)]
    for copy in copies:
        copy.start()
    for copy in copies:
        copy.wait()


def feed_scratch(rows, width, hidden):
    return [
        pltpu.VMEM((rows, width), jnp.bfloat16),
        pltpu.VMEM((hidden, width), jnp.bfloat16),
        pltpu.VMEM((width, hidden), jnp.bfloat16),
        pltpu.SemaphoreType.DMA((16,)),
    ]


def feed_body(*refs, last):
    rows_in, weights_ref, vec_ref, rest = refs[:4], refs[4], refs[5], list(refs[6:])
    came_ref = rest.pop(0) if last else None
    (act_ref, slope_ref), outs = rest[:2], rest[2:-4]
    all_ref, in_ref, back_ref, sems = rest[-4:]
    load_all(rows_in, weights_ref, all_ref, in_ref, back_ref, sems)
    bias = vec_ref[FF_ROW : FF_ROW + 1, : in_ref.shape[0]]
    step = rows_in[0].shape[0] * 2
    for start in range(0, all_ref.shape[0], step):
        at = slice(start, start + step)
        total = None
        for unit in range(0, in_ref.shape[0], FF_STEP):
            lanes = slice(unit, unit + FF_STEP)
            inner = product_nt(all_ref[at], in_ref[lanes]) + bias[:, lanes]
            square = inner * inner
            bend = jnp.tanh(GELU_SCALE * (inner + GELU_CUBE * (inner * square)))
            half = 0.5 * (1.0 + bend)
            act = to_low(inner * half)
            act_ref[at, lanes] = act
            slope_ref[at, lanes] = half + (0.5 * GELU_SCALE) * inner * (1.0 - bend * bend) * (
                1.0 + (3.0 * GELU_CUBE) * square
            )
            part = product_nt(act, back_ref[:, lanes])
            total = part if total is None else total + part
        put_parts(outs, came_ref, start, total)


def put_parts(outs, came_ref, start, total):
    if came_ref is None:
        outs[0][start : start + total.shape[0]] = to_low(total)
        return
    total = total + wide(came_ref[start : start + total.shape[0]])
    rows = outs[0].shape[0]
    for i in range(start // rows, (start + total.shape[0]) // rows):
        piece = total[i * rows - start : (i + 1) * rows - start]
        outs[i][...] = piece if i == 0 else to_low(piece)


def feed_call(body, pieces, weights, more, came, side_shapes):
    rows, width = pieces[0].shape
    last = came is not None
    operands = (*pieces, weights, *more) + ((came,) if last else ())
    outs = part_shapes(rows, width) if last else [low_shape(4 * rows, width)]
    return whole_call(
        functools.partial(body, last=last),
        operands,
        side_shapes + outs,
        feed_scratch(4 * rows, width, 512),
        range(5),
    )


def feed(pieces, weights, vec, came=None):
    count = 4 * pieces[0].shape[0]
    return feed_call(
        feed_body, pieces, weights, (vec,), came, [low_shape(count, 512), wide_shape(count, 512)]
    )


def feed_back_body(*refs, last):
    rows_in, weights_ref, slope_ref, rest = refs[:4], refs[4], refs[5], list(refs[6:])
    came_ref = rest.pop(0) if last else None
    (du_ref, sums_ref), outs = rest[:2], rest[2:-4]
    all_ref, in_ref, back_ref, sems = rest[-4:]
    load_all(rows_in, weights_ref, all_ref, in_ref, back_ref, sems)
    sums = [None] * (in_ref.shape[0] // FF_STEP)
    step = rows_in[0].shape[0] * 2
    for start in range(0, all_ref.shape[0], step):
        at = slice(start, start + step)
        total = None
        for i in range(len(sums)):
            lanes = slice(i * FF_STEP, (i + 1) * FF_STEP)
            du = to_low(product(all_ref[at], back_ref[:, lanes]) * slope_ref[at, lanes])
            du_ref[at, lanes] = du
            summed = column_sum(wide(du))
            sums[i] = summed if sums[i] is None else sums[i] + summed
            part = product(du, in_ref[lanes])
            total = part if total is None else total + part
        put_parts(outs, came_ref, start, total)
    for i, summed in enumerate(sums):
        sums_ref[:, i * FF_STEP : (i + 1) * FF_STEP] = summed


def feed_back(pieces, weights, slope, came=None):
    count = 4 * pieces[0].shape[0]
    return feed_call(
        feed_back_body,
        pieces,
        weights,
        (slope,),
        came,
        [low_shape(count, 512), wide_shape(1, 512)],
    )


def plane_rows(values):
    near = [values, *plane_hops([values] * 3)]
    return (*near, *(other_core(part) for part in near))


GRAD_ROWS = 448


def pair_grad_body(*refs):
    fed_in, two_in, whole_ref, halves = refs[:8], refs[8:16], refs[16], refs[17:21]
    target_ref, out_ref, fed_ref, two_ref, act_ref, du_ref, sems, out_sems = refs[21:]
    copies = []
    for pieces, target in ((fed_in, fed_ref), (two_in, two_ref), (halves[:2], act_ref), (halves[2:], du_ref)):
        rows = pieces[0].shape[0]
        for i, ref in enumerate(pieces):
            copies.append((ref, target.at[i * rows : (i + 1) * rows]))
    copies = [pltpu.make_async_copy(*copy, sems.at[i]) for i, copy in enumerate(copies)]
    for copy in copies:
        copy.start()
    for copy in copies:
        copy.wait()
    width = whole_ref.shape[1]
    stores = []
    for z in range(out_ref.shape[0] // GRAD_ROWS):
        at = z * GRAD_ROWS
        for lane in range(0, out_ref.shape[1], 512):
            lanes = slice(lane, lane + 512)
            out_ref[at : at + 128, lanes] = to_low(
                product_tn(du_ref[:, z * 128 : (z + 1) * 128], two_ref[:, lanes])
            )
        grad = to_low(product_tn(fed_ref[:, z * 256 : (z + 1) * 256], act_ref[...]))
        out_ref[at + 128 : at + 256] = jnp.concatenate([grad[:128], grad[128:]], axis=1)
        out_ref[at + 256 : at + GRAD_ROWS, :width] = whole_ref[z * 256 : z * 256 + 192]
        for piece in range(3):
            out_ref[at + 256 + piece * 64 : at + 320 + piece * 64, width:] = whole_ref[
                z * 256 + 192 : (z + 1) * 256, piece * 256 : (piece + 1) * 256
            ]
        rows = slice(at, at + GRAD_ROWS)
        stores.append(
            pltpu.make_async_copy(out_ref.at[rows], target_ref.at[rows], out_sems.at[z])
        )
        stores[-1].start()
    for copy in stores:
        copy.wait()


def pair_grads(rows_fed, rows_two, whole, acts, dus):
    rows, width = rows_fed[0].shape
    hidden = acts[0].shape[1]
    return whole_call(
        pair_grad_body,
        (*rows_fed, *rows_two, whole, *acts, *dus),
        [low_shape(4 * GRAD_ROWS, width)],
        [pltpu.VMEM((4 * GRAD_ROWS, width), jnp.bfloat16)]
        + [pltpu.VMEM((8 * rows, width), jnp.bfloat16)] * 2
        + [pltpu.VMEM((8 * rows, hidden), jnp.bfloat16)] * 2
        + [pltpu.SemaphoreType.DMA((20,)), pltpu.SemaphoreType.DMA((4,))],
        [*range(16), *range(17, 21)],
        placed=(0,),
    )[0]


def split_grad_body(sum_ref, in_ref, *outs):
    in_ref[...] = wide(sum_ref[:128])
    rows, half = outs[0].shape[0], sum_ref.shape[1] // 2
    for i, step in enumerate(NEAR):
        place = chip_place(step)
        at = pl.ds(pl.multiple_of(128 + (place % 2) * rows, rows), rows)
        lanes = pl.ds(pl.multiple_of((place // 2) * half, half), half)
        outs[i][:, :half] = sum_ref[at, lanes]
        first = pl.multiple_of(256 + jnp.minimum(place, 2) * rows, rows)
        whole = sum_ref[pl.ds(first, rows), : outs[i].shape[1] - half]
        fourth = jnp.concatenate(
            [sum_ref[256 + q * rows : 256 + (q + 1) * rows, whole.shape[1] :] for q in range(3)],
            axis=1,
        )
        outs[i][:, half:] = jnp.where(place == 3, fourth, whole)


def z_sum(refs):
    total = wide(refs[0][...])
    for ref in refs[1:]:
        total = total + wide(ref[...])
    return total


def pick_body(out_ref, back_ref, pairs_ref, *outs):
    for chip in range(16):
        pair = pl.multiple_of((lax.axis_index("grp") * 4 + chip % 4) * PAIR, PAIR)
        pairs_ref[chip] = out_ref[:, pl.ds(pair, PAIR)]
    half = outs[0].shape[1]
    for i, (step, lane) in enumerate(zip((0, 1, 2, 1), (0, 0, 0, half))):
        for block in range(4):
            outs[step][:, lane + block * 128 : lane + (block + 1) * 128] = back_ref[
                :, pl.ds(chunk_place(block, NEAR[i]), 128)
            ]


def lay_body(in_ref, own_ref, came_x_ref, came_y_ref, out_ref):
    out_ref[:128] = in_ref[...]
    half = own_ref.shape[1]
    for i, (ref, lane) in enumerate(
        ((own_ref, 0), (came_x_ref, 0), (came_y_ref, 0), (came_y_ref, half))
    ):
        place = chip_place(NEAR[i])
        rows = pl.ds(pl.multiple_of(128 + (place % 2) * 64, 64), 64)
        out_ref[rows, pl.ds(pl.multiple_of((place // 2) * half, half), half)] = ref[
            :, lane : lane + half
        ]


def core_order(own, other):
    first = lax.axis_index("grp") == 0
    return jnp.concatenate(
        [jnp.where(first, own, other), jnp.where(first, other, own)], axis=1
    )


def core_halves(values):
    part = values.shape[1] // 2
    first = lax.axis_index("grp") == 0
    low_half, high_half = values[:, :part], values[:, part:]
    return (
        jnp.where(first, low_half, high_half),
        jnp.where(first, high_half, low_half),
    )


def halves_nt(values, own_ref, other_ref, lanes):
    own, other = core_halves(values)
    return product_nt(own, own_ref[:, lanes]) + product_nt(other, other_ref[:, lanes])


def bottle_body(
    attended_ref,
    keep_ref,
    came_x_ref,
    came_y_ref,
    came_far_ref,
    vec_ref,
    own_ref,
    other_ref,
    extra_ref,
    more_ref,
    means_ref,
    logvars_ref,
    out_ref,
    fed_ref,
    sample_ref,
    dlat_ref,
    dfed_ref,
    dfed_low_ref,
    dmeans_ref,
    dlogvars_ref,
    sums_ref,
    cot_ref,
):
    rows, width = attended_ref.shape
    lat = means_ref.shape[1]
    span = rows // 2
    comps = means_ref.shape[0]
    parts = z_sum((keep_ref, came_x_ref, came_y_ref, came_far_ref))
    fed = attended_ref[...] + parts + vec_ref[7:8]
    fed_low = to_low(fed)
    fed_ref[...] = fed_low
    latent = halves_nt(fed_low, own_ref, other_ref, LAT_LANES) + vec_ref[LAT_ROW : LAT_ROW + 1]
    logvar = latent[:, lat:]
    noise = jnp.concatenate([extra_ref[span:], more_ref[span:]])
    noise = wide(noise[:, :lat]) + wide(noise[:, lat:])
    spread = jnp.exp(0.5 * logvar) * noise
    sample = latent[:, :lat] + spread
    sample_low = to_low(sample)
    sample_ref[...] = sample_low
    out_ref[...] = to_low(
        fed + halves_nt(sample_low, own_ref, other_ref, DEC_LANES) + vec_ref[8:9]
    )
    cot = jnp.concatenate([extra_ref[:span], more_ref[:span]])
    cot_ref[...] = cot
    dsample = core_order(
        product(cot, own_ref[:, DEC_LANES]), product(cot, other_ref[:, DEC_LANES])
    )

    row = lax.broadcasted_iota(jnp.int32, (rows, 1), 0)
    block = lax.axis_index("y") * 2 + lax.axis_index("x")
    place = slide_place(lax.axis_index("grp"), block, row // span, row & (span - 1), span)
    live = place.astype(jnp.float32) < vec_ref[LEN_ROW : LEN_ROW + 1, 0:1]
    share = jnp.where(live, 1.0 / lat, 0.0)
    own_term = jnp.sum(-0.5 * noise * noise - 0.5 * logvar, axis=-1, keepdims=True)
    logvars = logvars_ref[...]
    inverse = jnp.exp(-logvars)
    falls = -0.5 * inverse
    levels = -0.5 * jnp.sum(logvars, axis=-1, keepdims=True) - math.log(comps)
    terms = []
    for c in range(comps):
        offset = sample - means_ref[c : c + 1]
        drop = jnp.sum(offset * offset * falls[c : c + 1], axis=-1, keepdims=True)
        terms.append(drop + levels[c : c + 1])
    peak = terms[0]
    for term in terms[1:]:
        peak = jnp.maximum(peak, term)
    weights = [jnp.exp(term - peak) for term in terms]
    total = weights[0]
    for weight in weights[1:]:
        total = total + weight
    kl_cell = own_term - (peak + jnp.log(total))
    kl = jnp.sum(jnp.where(live, kl_cell, 0.0), axis=0, keepdims=True) / lat
    scale = share / total
    for c in range(comps):
        offset = sample - means_ref[c : c + 1]
        slope = offset * inverse[c : c + 1]
        part = weights[c] * scale
        pull = part * slope
        dsample = dsample + pull
        dmeans_ref[c : c + 1] = -column_sum(pull)
        dlogvars_ref[c : c + 1] = column_sum(0.5 * part - 0.5 * (pull * offset))
    dlat = jnp.concatenate([dsample, 0.5 * dsample * spread - 0.5 * share], axis=1)
    dlat_low = to_low(dlat)
    dlat_ref[...] = dlat_low
    grad_out = wide(cot)
    dfed = grad_out + core_order(
        product(dlat_low, own_ref[:, LAT_LANES]), product(dlat_low, other_ref[:, LAT_LANES])
    )
    dfed_ref[...] = dfed
    dfed_low_ref[...] = to_low(dfed)
    sums_ref[...] = jnp.concatenate(
        [
            column_sum(wide(dlat_low)),
            column_sum(dfed),
            column_sum(grad_out),
            jnp.broadcast_to(kl, (1, width)),
            jnp.zeros((4, width), jnp.float32),
        ]
    )


def bottle_call(attended, parts, vec, weights, extra, means, logvars):
    rows, width = attended.shape
    lat = means.shape[1]
    return whole_call(
        bottle_body,
        (attended, *parts, vec, *weights, *extra, means, logvars),
        [
            low_shape(rows, width),
            low_shape(rows, width),
            low_shape(rows, lat),
            low_shape(rows, width),
            wide_shape(rows, width),
            low_shape(rows, width),
            wide_shape(*means.shape),
            wide_shape(*means.shape),
            wide_shape(8, width),
            low_shape(rows, width),
        ],
    )


def project_back_body(
    keep_ref,
    came_x_ref,
    came_y_ref,
    came_far_ref,
    attended_ref,
    dfed_ref,
    vec_ref,
    sent_ref,
    datt_ref,
    datt_low_ref,
    sums_ref,
):
    grad = z_sum((keep_ref, came_x_ref, came_y_ref, came_far_ref))
    unit, scale = row_stats(attended_ref[...])
    datt = dfed_ref[...] + norm_back(grad, unit, scale, vec_ref[5:6])
    datt_ref[...] = datt
    datt_low_ref[...] = to_low(datt)
    sums_ref[...] = jnp.concatenate(
        [
            column_sum(grad * unit),
            column_sum(grad),
            column_sum(datt),
            jnp.zeros((5, datt.shape[1]), jnp.float32),
        ]
    )


def project_back(parts, attended, dfed, vec, sent):
    rows, width = attended.shape
    return whole_call(
        project_back_body,
        (*parts, attended, dfed, vec, sent),
        [wide_shape(rows, width), low_shape(rows, width), wide_shape(8, width)],
        left_out=(7,),
    )


def whole_grads_body(*refs):
    out_ref = refs[-1]
    for lanes, (left, left_other, right, right_other) in (
        (LAT_LANES, refs[:4]),
        (DEC_LANES, refs[4:8]),
    ):
        grads = jnp.concatenate([left[...], left_other[...]])
        values = jnp.concatenate([core_halves(right[...])[0], core_halves(right_other[...])[0]])
        out_ref[:, lanes] = to_low(product_tn(grads, values))


def whole_grads(pairs):
    operands = []
    for values in pairs:
        operands += [values, other_core(values)]
    width = pairs[0].shape[1]
    return whole_call(whole_grads_body, operands, [low_shape(width, DEC_LANES.stop)])[0]


def sum_body(*refs):
    refs[-1][...] = z_sum(refs[:-1])


def last_grad_body(*refs):
    out_ref, lat_ref, dec_ref = refs[8:]
    half = out_ref.shape[1] // 8
    for i, ref in enumerate(refs[:8]):
        for block in range(4):
            place = chunk_place(block, NEAR[i % 4], i // 4)
            out_ref[:, pl.ds(place, 128)] = wide(ref[:, block * 128 : (block + 1) * 128])
    for i in range(2):
        total = z_sum([ref.at[:, half:] for ref in refs[i * 4 : i * 4 + 4]])
        lat_ref[:, core_lanes(i, lat_ref.shape[1] // 2)] = total[:, LAT_LANES]
        dec_ref[:, core_lanes(i, dec_ref.shape[1] // 2)] = total[:, DEC_LANES]


def cells_back_body(
    keep_ref,
    came_x_ref,
    came_y_ref,
    came_far_ref,
    hidden_ref,
    datt_ref,
    vec_ref,
    bottle_sums_ref,
    project_sums_ref,
    head_sums_ref,
    ff_sums_ref,
    ff_more_ref,
    dmeans_ref,
    dlogvars_ref,
    out_grad_ref,
    grad_ref,
    packed_ref,
    inner_ref,
    rows_ref,
):
    grad = z_sum((keep_ref, came_x_ref, came_y_ref, came_far_ref))
    unit, scale = row_stats(wide(hidden_ref[...]))
    grad_ref[...] = to_low(datt_ref[...] + norm_back(grad, unit, scale, vec_ref[0:1]))
    width = grad.shape[1]
    count = packed_ref.shape[0]
    inner_ref[...] = jnp.zeros_like(inner_ref)
    for block in range(4):
        lanes = slice(block * 128, block * 128 + 128)
        inner_ref[:, pl.ds(chunk_place(block), 128)] = (
            ff_sums_ref[:, lanes] + ff_more_ref[:, lanes]
        )
    inner_ref[:, inner_ref.shape[1] - width :] = bottle_sums_ref[0:1]
    rows_ref[...] = jnp.zeros_like(rows_ref)
    rows_ref[0:1] = column_sum(grad * unit)
    rows_ref[1:2] = column_sum(grad)
    rows_ref[2:3, pl.ds(own_pair(), PAIR)] = head_sums_ref[:, :PAIR]
    rows_ref[3:4, pl.ds(own_pair(), PAIR)] = head_sums_ref[:, 2 * PAIR :]
    rows_ref[4:5] = project_sums_ref[2:3]
    rows_ref[5:7] = project_sums_ref[0:2]
    rows_ref[7:9] = bottle_sums_ref[1:3]
    part = width // count
    pieces = inner_ref.shape[1] // width
    for i in range(pieces):
        rows_ref[9 + i : 10 + i] = jnp.concatenate(
            [
                inner_ref[:, (b * pieces + i) * part : (b * pieces + i + 1) * part]
                for b in range(count)
            ],
            axis=1,
        )
    rows_ref[14:15] = bottle_sums_ref[3:4]
    lat_part = dmeans_ref.shape[1] // count
    for b in range(count):
        sums = jnp.concatenate(
            [
                rows_ref[:, b * part : (b + 1) * part],
                dmeans_ref[:, b * lat_part : (b + 1) * lat_part],
                dlogvars_ref[:, b * lat_part : (b + 1) * lat_part],
            ],
            axis=1,
        )
        high = to_low(sums)
        packed_ref[b, :part] = out_grad_ref[b]
        packed_ref[b, part : part + SMALL] = high
        packed_ref[b, part + SMALL :] = to_low(sums - wide(high))


def last_sum_body(came_ref, out_ref):
    count, rows = came_ref.shape[0], came_ref.shape[1] - 2 * SMALL
    for chip in range(4):
        total = z_sum([came_ref.at[z * 4 + chip, :rows] for z in range(4)])
        out_ref[:rows, chip * PAIR : (chip + 1) * PAIR] = total
    small = z_sum([came_ref.at[i, rows : rows + SMALL] for i in range(count)])
    rest = z_sum([came_ref.at[i, rows + SMALL :] for i in range(count)])
    out_ref[rows:] = jnp.zeros((SMALL, out_ref.shape[1]), jnp.float32)
    out_ref[rows:, :PAIR] = small + rest


def core_lanes(core_step, width):
    core = flip(lax.axis_index("grp"), core_step)
    return pl.ds(pl.multiple_of(core * width, width), width)


def last_body(own_ref, other_ref, grad_ref, vec_ref, inner_ref, means_ref, logvars_ref, kl_ref):
    rows = grad_ref.shape[0]
    for i, ref in enumerate((own_ref, other_ref)):
        grad_ref[:, core_lanes(i, own_ref.shape[1])] = ref[:rows]
    small = own_ref[rows:, :PAIR] + other_ref[rows:, :PAIR]
    part = vec_ref.shape[1]
    vec_ref[...] = small[:9, :part]
    pieces = inner_ref.shape[1] // part
    inner_ref[...] = jnp.concatenate(
        [small[9 + i : 10 + i, :part] for i in range(pieces)], axis=1
    )
    lat = means_ref.shape[1]
    means_ref[...] = small[:, part : part + lat]
    logvars_ref[...] = small[:, part + lat :]
    kl_ref[...] = small[14:15, :1]


def in_grad_body(own_ref, other_ref, out_ref):
    for i, ref in enumerate((own_ref, other_ref)):
        out_ref[:, core_lanes(i, ref.shape[0])] = ref[...].T


def cells_back(operands, inner):
    rows, width = operands[0].shape
    return whole_call(
        cells_back_body,
        operands,
        [low_shape(rows, width), low_shape(16, width // 16 + 2 * SMALL, PAIR)],
        [pltpu.VMEM((1, inner), jnp.float32), pltpu.VMEM((SMALL, width), jnp.float32)],
    )


def exchange(blocks, axes):
    return lax.all_to_all(blocks, axes, split_axis=0, concat_axis=0, tiled=True)


def to_all(values, count):
    return jnp.broadcast_to(values[None], (count, *values.shape))


def fast_device(
    cell_input,
    lengths,
    noise_draw,
    cotangent,
    w_qkv,
    w_out,
    w_ffn_in,
    w_ffn_out,
    w_latent,
    w_decode,
    vectors,
    inner_bias,
    prior_means,
    prior_logvars,
):
    slots, span, width = cell_input.shape[1:]
    rows = slots * span
    lat = noise_draw.shape[-1]
    comps = prior_means.shape[1]
    ff = w_ffn_out.shape[1]
    inner = 16 * inner_bias.shape[1]

    part = width // 16
    shard = jnp.concatenate(
        [half_of(w[0], 0, "grp", True).T for w in (w_latent, w_decode)], axis=1
    )
    shard_width = shard.shape[1]
    whole = lax.all_gather(shard, CHIPS, axis=0, tiled=True)

    out_pairs, back_own, back_x, back_y = whole_call(
        pick_body,
        after((w_out[0].T, w_ffn_out[0].T), shard),
        [low_shape(16, part, PAIR)]
        + [low_shape(part, ff // 8 * count) for count in (1, 2, 1)],
    )
    out_t = exchange(out_pairs, CHIPS).reshape(width, PAIR)

    blocks = whole_call(
        enter_body,
        (
            after(cell_input.reshape(rows, width), out_pairs),
            lengths,
            vectors[0],
            inner_bias,
            prior_means[0],
            prior_logvars[0],
        ),
        [low_shape(span + SMALL, width)] * 2,
    )
    first = jnp.stack(
        [lax.ppermute(blocks[k], ("grp", "z"), slide_routes(k)) for k in range(2)]
    )

    qkv_t = w_qkv[0].T
    at_x = lax.axis_index("x") % 2
    head_parts = (
        lax.dynamic_slice_in_dim(qkv_t, at_x * HEAD_DIM, PAIR),
        lax.dynamic_slice_in_dim(qkv_t, (1 - at_x) * PAIR, HEAD_DIM),
    )
    came = [
        lax.ppermute(head_parts[int(single)], EVERY, head_routes(single, k))
        for single, k in ARRIVALS
    ]

    in_own = half_of(w_ffn_in[0], 1, "grp", True).T
    noise_high = to_low(noise_draw[0, 0])
    noise_rest = to_low(noise_draw[0, 0] - wide(noise_high))
    extra = jnp.concatenate(
        [cotangent[0], jnp.concatenate([noise_high, noise_rest], axis=2)], axis=1
    )
    size = span + SMALL
    one, two = first[0], first[1]
    one_x = hop(jnp.concatenate([one, back_x]), "x")
    two_y = hop(two, "y")
    sent = jnp.concatenate(
        [one, one_x[:size], jnp.concatenate([back_y, one_x[size:, ff // 8 :]], axis=1)]
    )
    sent_y, sent_x = after((sent, jnp.concatenate([two, two_y])), (came[:2], extra, out_t))
    near_y = hop(sent_y, "y")
    near_x = hop(sent_x, "x")
    plane_own = jnp.concatenate(
        [one, two, one_x[:size], near_x[:size], near_y[:size], two_y]
        + [near_y[size : 2 * size], near_x[size:]]
    ).reshape(4, 2, size, width)
    plane_own, came = lax.optimization_barrier((plane_own, came))
    plane_other = other_core(plane_own)
    (pair_own,) = whole_call(
        lay_body,
        (in_own, back_own, one_x[size:], near_y[2 * size :]),
        [low_shape(256, width)],
    )
    pair_w = lax.all_gather(pair_own, "z", axis=0, tiled=True)

    vec, means, logvars, normed, qkv, head_w, mixed, lse, bias = attend(
        plane_own, plane_other, after(came, pair_own), lat, inner
    )
    mix_parts = mix_out(mixed, out_t, whole)

    extra = after(extra, mixed)
    extra = [
        lax.ppermute(pick_slot(extra, k), ("grp", "z"), slide_routes(k)) for k in range(2)
    ]

    attended, normed_two, hidden = project(mix_parts, first, vec)
    rows_two = plane_rows(normed_two)
    act_far, slope_far, fed_far = feed(pinned(rows_two[4:]), pinned([pair_w])[0], vec)
    act, slope, keep, *sends = feed(
        pinned(rows_two[:4]), pinned([pair_w])[0], vec, other_core(fed_far)
    )
    fed_parts = (keep, *plane_hops(sends))
    wholes = (whole, other_core(whole))
    output, fed_low, sample_low, dlat_low, dfed, dfed_low, dmeans, dlogvars, bottle_sums, cot = (
        bottle_call(
            attended, fed_parts, vec, wholes, extra, means, logvars
        )
    )

    rows_fed = plane_rows(dfed_low)
    layer_out = from_slides(after(output, rows_fed).reshape(slots, span, width))
    whole_grad = whole_grads((dlat_low, fed_low, cot, sample_low))
    du_far, ff_far, norm_far = feed_back(rows_fed[4:], pair_w, slope_far)
    du, ff_sums, keep, *sends = feed_back(
        rows_fed[:4], pair_w, slope, after(other_core(norm_far), whole_grad)
    )
    norm_parts = (keep, *plane_hops(sends))
    grads = pair_grads(rows_fed, pinned(rows_two), whole_grad, (act, act_far), (du, du_far))
    grads_sum = lax.psum_scatter(grads, "z", scatter_dimension=0, tiled=True)
    datt, datt_low, project_sums = project_back(
        after(norm_parts, grads), attended, dfed, vec, layer_out
    )
    rows_datt = plane_rows(datt_low)
    out_grad, all_datt = out_grads(rows_datt, mixed)
    dqkv, dn_far = attend_back(qkv, bias, lse, out_t, head_w, all_datt)
    dn_keep, *dn_sends = dnormed(dqkv, head_w, other_core(dn_far))
    homes, head_sums = head_grads(dqkv, after(normed, dn_sends))
    dn_parts = (dn_keep, *plane_hops(dn_sends))
    grad_rows, packed = cells_back(
        (
            *dn_parts,
            hidden,
            datt,
            vec,
            bottle_sums,
            project_sums,
            head_sums,
            ff_sums,
            ff_far,
            dmeans,
            dlogvars,
            out_grad,
        ),
        inner,
    )
    grad_cells = from_slides(grad_rows.reshape(slots, span, width))
    sum_in, *sums = whole_call(
        split_grad_body,
        (after(grads_sum, packed),),
        [wide_shape(128, width)] + [low_shape(part, ff // 8 + shard_width)] * 4,
    )
    sums = [sums[0], *plane_hops(sums[1:])]
    sums += [other_core(total) for total in sums]

    (last,) = whole_call(
        last_sum_body,
        (after(exchange(packed, CHIPS), (sums[1:4], grad_cells)),),
        [wide_shape(part + SMALL, 4 * PAIR)],
    )
    grad_out_w, vec_out, inner_out, means_out, logvars_out, kl_sum = whole_call(
        last_body,
        (last, other_core(last)),
        [
            wide_shape(part, width),
            wide_shape(9, part),
            wide_shape(1, inner // 16),
            wide_shape(comps, lat // 16),
            wide_shape(comps, lat // 16),
            wide_shape(1, 1),
        ],
    )
    kl_mean = kl_sum[0, 0] / (32 * rows)

    homes = [
        lax.ppermute(grad, EVERY, [(there, here) for here, there in head_routes(single, k)])
        for grad, (single, k) in zip(homes, ARRIVALS)
    ]
    (home,) = whole_call(
        home_body, after(homes, (packed, sums[1:4])), [wide_shape(3 * HEAD_DIM, width)]
    )
    grad_qkv = (home + other_core(home)).T

    (grad_in_w,) = whole_call(
        in_grad_body, (sum_in, other_core(sum_in)), [wide_shape(width, ff // 16)]
    )
    grad_back_w, grad_lat_w, grad_dec_w = whole_call(
        last_grad_body,
        after(sums, grad_in_w),
        [wide_shape(part, ff), wide_shape(part, width), wide_shape(part, lat)],
    )
    return (
        wide(layer_out).reshape(1, slots, span, width),
        wide(grad_cells).reshape(1, slots, span, width),
        kl_mean,
        grad_qkv[None],
        grad_out_w.T[None],
        grad_in_w[None],
        grad_back_w.T[None],
        grad_lat_w.T[None],
        grad_dec_w.T[None],
        vec_out[None],
        inner_out,
        means_out[None],
        logvars_out[None],
    )


def solution(mesh):
    chips = mesh.shape["blk"]
    if (mesh.shape["grp"], chips) == (2, HEADS):
        mesh = Mesh(mesh.devices.reshape(2, chips // 4, 2, 2), EVERY)
        blk, run = CHIPS, fast_device
    else:
        blk, run = "blk", per_device
    cells = P("grp", None, blk, None)
    columns = P(None, None, blk)
    return jax.shard_map(
        run,
        mesh=mesh,
        in_specs=(cells, P("grp", None), P(None, "grp", None, blk, None), cells)
        + (columns,) * 7
        + (P(None, blk), columns, columns),
        out_specs=(cells, cells, P()) + (columns,) * 7 + (P(None, blk), columns, columns),
        check_vma=False,
    )
```
